32 devices in a mesh: dp: 4 (over y, x), pipe: 4 (over z), expert: 2 (over core).
Axes of the slice: x: 2, y: 2, z: 4, core: 2. Of those that a mesh axis runs over, the one named last changes fastest.
Arguments:
- tokens: bfloat16 [4, 1024, 5120], P('pipe', ('dp', 'expert')), may hold values from -6 to 6
- cotangent: bfloat16 [4, 1024, 5120], P('pipe', ('dp', 'expert')), may hold values from -6 to 6
- gain: float32 [4, 5120], P('pipe'), may hold values from 0.1 to 1.9
- w_gate: bfloat16 [4, 2, 5120, 768], P('pipe', 'expert', 'dp'), may hold values from -0.078125 to 0.078125
- w_up: bfloat16 [4, 2, 5120, 768], P('pipe', 'expert', 'dp'), may hold values from -0.078125 to 0.078125
- w_down: bfloat16 [4, 2, 768, 5120], P('pipe', 'expert', None, 'dp'), may hold values from -0.21875 to 0.21875
- route: int32 [4, 4, 128, 1], P('pipe', None, ('dp', 'expert')), may hold values from 0 to 1; in each aligned block of 16 rows (0 to 15, 16 to 31, ..., all dimensions but the last counted through in order) at most 12 rows name the same one
Outputs:
- out_tokens: bfloat16 [4, 1024, 5120], P('pipe', ('dp', 'expert'))
- grad_tokens: bfloat16 [4, 1024, 5120], P('pipe', ('dp', 'expert'))
- grad_gain: float32 [4, 5120], P('pipe')
- grad_gate: bfloat16 [4, 2, 5120, 768], P('pipe', 'expert', 'dp')
- grad_up: bfloat16 [4, 2, 5120, 768], P('pipe', 'expert', 'dp')
- grad_down: bfloat16 [4, 2, 768, 5120], P('pipe', 'expert', None, 'dp')
The draws below stay inside these ranges and needn't reach their ends.
Inputs may be any that keep to these rules, and one draw needn't show every extreme that they name: route[l, m, t, 0] is the expert of tile t at layer l for micro-batch m. Among the 16 tiles of one device for one layer and one micro-batch (aligned blocks), no expert is named more than 12 times; every expert is named somewhere.
All inputs are finite; a program needn't handle non-finite values.
Results may differ from the reference program's by a relative error of at most 0.034.
Values may be sent and summed in bfloat16 or wider, within the bound.
No kernel may reach another device: no remote copies, remote signals or barrier semaphores. Data moves between devices by JAX's collectives and lax.ppermute only.
A program may use at most 128 MiB of HBM per device.

```python
import math
import jax
import jax.numpy as jnp
import numpy as np
from jax import lax

D = 5120
FF = 768
TILE = 8
TILES_MB = 16
PASSES = 2
EXPERTS = 2
CAP = 12
ROWS = 1024
TILES = 128
N_DP = 4
N_PIPE = 4


def levels(stream_key, extent, split, least, top_value):
    def one(axis_at, parts):
        heights = jax.random.uniform(jax.random.fold_in(jax.random.fold_in(stream_key, 6), axis_at), (parts,), jnp.float32, least / len(split), top_value / len(split))
        return jnp.repeat(jnp.exp(heights), extent[axis_at] // parts).reshape((-1,) + (1,) * (len(extent) - axis_at - 1))

    level = one(*split[0])
    for cut in split[1:]:
        level = level * one(*cut)
    return level


def routed_block(own_key, own, number, rows, amount, top, most, skew):
    sequence = jax.random.permutation(own_key, amount)
    heavy_load, usual = portions_of(amount, rows * top, most, skew, True), portions_of(amount, rows * top, most, skew, False)
    places = jnp.arange(amount)

    def named(lengths, rotation):
        used = int((lengths > 0).sum())
        fixed = max(1, used // 4)
        shifted = fixed + (places - fixed + rotation * (used - fixed)) % max(1, amount - fixed)
        return jnp.zeros((amount,), jnp.int32).at[sequence[jnp.where(places < fixed, places, shifted)]].set(jnp.asarray(lengths, jnp.int32))

    lengths = jnp.where(number % 4 == 0, named(heavy_load, number // 4), named(usual, number - number // 4 - 1))
    mixed = jax.random.permutation(jax.random.fold_in(own, 3), amount)
    donor, taker = mixed[0:amount // 2 * 2:2], mixed[1:amount // 2 * 2:2]
    slack = jnp.minimum(lengths[donor] - 1, most - lengths[taker]) // 2
    slack = jnp.where((donor == sequence[0]) | (taker == sequence[0]) | (lengths[taker] == 0), 0, jnp.maximum(slack, 0))
    shifted = jax.random.randint(jax.random.fold_in(own, 4), (amount // 2,), 0, 1 << 20) % (slack + 1)
    lengths = lengths.at[donor].add(-shifted).at[taker].add(shifted)
    labels = jnp.searchsorted(jnp.cumsum(lengths), jnp.arange(rows * top), side="right").astype(jnp.int32)
    grid = labels.reshape(top, rows).T
    grid = grid[jax.random.permutation(jax.random.fold_in(own, 1), rows)]
    rotation = jax.random.randint(jax.random.fold_in(own, 2), (rows, 1), 0, top)
    return jnp.take_along_axis(grid, (jnp.arange(top)[None, :] + rotation) % top, axis=1)


def portions_of(number_of, total, limit, slope, full):
    portions = [(1 << 20) // math.isqrt(rank ** slope) + 1 for rank in range(1, number_of + 1)]
    largest = limit if full else min(limit, max(-(-total // number_of), total * portions[0] // sum(portions)))
    least = 1 if total - largest >= number_of - 1 else 0
    holding, surplus = [largest] + [least] * (number_of - 1), total - largest - least * (number_of - 1)
    while surplus > 0:
        candidates = [i for i in range(1, number_of) if holding[i] < largest] or [i for i in range(1, number_of) if holding[i] < limit]
        pool, budget = sum([portions[i] for i in candidates]), surplus
        for i in candidates:
            extra = min(limit - holding[i], max(1, budget * portions[i] // pool), surplus)
            holding[i] = holding[i] + extra
            surplus = surplus - extra
    return np.array(holding)


def gaussian(key, extent, scale, limit, pieces=(), kind=jnp.bfloat16):
    array = jax.random.normal(key, extent, jnp.float32) * scale
    if len(pieces) > 0:
        array = levels(key, extent, pieces, -0.22, 0.18) * array
    return jnp.clip(array, min=-limit, max=limit).astype(kind)


def setup_inputs(seed: int = 0) -> dict:
    streams_of = jax.random.split(jax.random.key(seed), 8)
    tokens = gaussian(streams_of[0], (N_PIPE, ROWS, D), 1.0, 6.0, ((0, 4), (1, 8)))
    cotangent = gaussian(streams_of[1], (N_PIPE, ROWS, D), 1.0, 6.0, ((0, 4), (1, 8)))
    gain = jnp.clip(1.0 + 0.18 * jax.random.normal(streams_of[2], (N_PIPE, D), jnp.float32), 0.1, 1.9)
    w_gate = gaussian(streams_of[3], (N_PIPE, EXPERTS, D, FF), D ** -0.5, 0.078125, ((0, 4), (1, 2), (2, 4)))
    w_up = gaussian(streams_of[4], (N_PIPE, EXPERTS, D, FF), D ** -0.5, 0.078125, ((0, 4), (1, 2), (2, 4)))
    w_down = gaussian(streams_of[5], (N_PIPE, EXPERTS, FF, D), FF ** -0.5, 0.21875, ((0, 4), (1, 2), (3, 4)))
    route_keys = jax.random.split(jax.random.fold_in(streams_of[6], 1), N_PIPE * N_PIPE * TILES // TILES_MB)
    route_turns = jax.random.permutation(jax.random.fold_in(streams_of[6], 3), N_PIPE * N_PIPE * TILES // TILES_MB)
    route = jax.vmap(lambda own, number: routed_block(jax.random.fold_in(streams_of[6], 2), own, number, TILES_MB, EXPERTS, 1, CAP, 2))(route_keys, route_turns).reshape((N_PIPE, N_PIPE, TILES, 1))
    return dict(tokens=tokens, cotangent=cotangent, gain=gain, w_gate=w_gate, w_up=w_up, w_down=w_down, route=route)


epsilon = 1e-06

def contract_last(former, latter):
    return lax.dot_general(former, latter, (((1,), (1,)), ((), ())), preferred_element_type=jnp.float32)

def contract_first(former, latter):
    return lax.dot_general(former, latter, (((0,), (0,)), ((), ())), preferred_element_type=jnp.float32)

def normalize(hidden, gain_row):
    widened = hidden.astype(jnp.float32)
    inverse = lax.rsqrt(lax.optimization_barrier(jnp.mean(widened * widened, axis=-1, keepdims=True)) + epsilon)
    scaled = widened * inverse
    return ((scaled * gain_row).astype(jnp.bfloat16), scaled, inverse)

def hidden_pair(rows_now, gate_weight, up_weight):
    quarter = rows_now.shape[1] // N_DP
    gate_pre = jnp.zeros((rows_now.shape[0], gate_weight.shape[1]), jnp.float32)
    up_pre = jnp.zeros((rows_now.shape[0], up_weight.shape[1]), jnp.float32)
    for part_index in range(N_DP):
        lower = part_index * quarter
        upper = lower + quarter
        gate_part = jnp.dot(rows_now[:, lower:upper], gate_weight[lower:upper], preferred_element_type=jnp.float32).astype(jnp.bfloat16)
        up_part = jnp.dot(rows_now[:, lower:upper], up_weight[lower:upper], preferred_element_type=jnp.float32).astype(jnp.bfloat16)
        gate_part, up_part = lax.optimization_barrier((gate_part, up_part))
        gate_pre = gate_pre + gate_part.astype(jnp.float32)
        up_pre = up_pre + up_part.astype(jnp.float32)
    return (gate_pre, up_pre)

def expert_forward(rows_now, gate_weight, up_weight, down_weight):
    gate_pre, up_pre = hidden_pair(rows_now, gate_weight, up_weight)
    activated = (jax.nn.silu(gate_pre) * up_pre).astype(jnp.bfloat16)
    return jnp.dot(activated, down_weight, preferred_element_type=jnp.float32).astype(jnp.bfloat16)

def expert_backward(rows_now, grad_now, gate_weight, up_weight, down_weight):
    gate_pre, up_pre = hidden_pair(rows_now, gate_weight, up_weight)
    sigmoid_gate = jax.nn.sigmoid(gate_pre)
    silu_gate = gate_pre * sigmoid_gate
    activated = (silu_gate * up_pre).astype(jnp.bfloat16)
    quarter = grad_now.shape[1] // N_DP
    grad_act = jnp.zeros(gate_pre.shape, jnp.float32)
    for part_index in range(N_DP):
        lower = part_index * quarter
        upper = lower + quarter
        partial_value = contract_last(grad_now[:, lower:upper], down_weight[:, lower:upper]).astype(jnp.bfloat16)
        grad_act = grad_act + lax.optimization_barrier(partial_value).astype(jnp.float32)
    grad_gate_pre = (grad_act * up_pre * sigmoid_gate * (1.0 + gate_pre * (1.0 - sigmoid_gate))).astype(jnp.bfloat16)
    grad_up_pre = (grad_act * silu_gate).astype(jnp.bfloat16)
    back_rows = (contract_last(grad_gate_pre, gate_weight) + contract_last(grad_up_pre, up_weight)).astype(jnp.bfloat16)
    grad_gate = contract_first(rows_now, grad_gate_pre)
    grad_up = contract_first(rows_now, grad_up_pre)
    grad_down = contract_first(activated, grad_now)
    return (back_rows, grad_gate, grad_up, grad_down)

def segments(tile_experts):
    tile_count = tile_experts.shape[0]
    per_block = math.gcd(tile_count, 8)
    block_count = tile_count // per_block
    blocked = tile_experts.reshape(block_count, per_block)
    lowest = blocked[:, 0].astype(jnp.int32)
    spread = (blocked[:, -1] - lowest + 1).astype(jnp.int32)
    begins = (jnp.cumsum(spread) - spread).astype(jnp.int32)
    seg_count = block_count + EXPERTS - 1
    positions = jnp.arange(seg_count, dtype=jnp.int32)
    owner_block = lax.optimization_barrier(jnp.sum((begins[None, :] <= positions[:, None]).astype(jnp.int32), axis=1)).astype(jnp.int32) - 1
    owner_block = jnp.clip(owner_block, 0, block_count - 1).astype(jnp.int32)
    expert_of = jnp.clip(lowest[owner_block] + positions - begins[owner_block], 0, EXPERTS - 1).astype(jnp.int32)
    usable = positions < jnp.sum(spread).astype(jnp.int32)
    return (per_block, block_count, owner_block, expert_of, usable)

def grouped_forward(tiles_sorted, tile_experts, gate_weight, up_weight, down_weight):
    per_block, block_count, owner_block, expert_of, usable = segments(tile_experts)
    model_width = tiles_sorted.shape[-1]
    blocks = tiles_sorted.reshape(block_count, per_block * TILE, model_width)
    row_owner = jnp.repeat(tile_experts.reshape(block_count, per_block), TILE, axis=1)

    def visit(result_buf, segment):
        block_index, expert_index, allowed = segment
        rows_now = blocks[block_index]
        chosen = (row_owner[block_index] == expert_index) & allowed
        produced = expert_forward(rows_now, gate_weight[expert_index], up_weight[expert_index], down_weight[expert_index]).astype(jnp.float32)
        result_buf = result_buf.at[block_index].add(jnp.where(chosen[:, None], produced, jnp.zeros_like(produced)))
        return (result_buf, None)
    start_buf = jnp.zeros((block_count, per_block * TILE, model_width), jnp.float32)
    result_buf, unused = lax.scan(visit, start_buf, (owner_block, expert_of, usable))
    return result_buf.reshape(-1, TILE, model_width).astype(jnp.bfloat16)

def grouped_backward(tiles_sorted, grads_sorted, tile_experts, gate_weight, up_weight, down_weight, sums):
    per_block, block_count, owner_block, expert_of, usable = segments(tile_experts)
    model_width = tiles_sorted.shape[-1]
    blocks = tiles_sorted.reshape(block_count, per_block * TILE, model_width)
    grad_blocks = grads_sorted.reshape(block_count, per_block * TILE, model_width)
    row_owner = jnp.repeat(tile_experts.reshape(block_count, per_block), TILE, axis=1)

    def visit(carry, segment):
        result_buf, acc_gate, acc_up, acc_down = carry
        block_index, expert_index, allowed = segment
        rows_now = blocks[block_index]
        chosen = (row_owner[block_index] == expert_index) & allowed
        grad_all = grad_blocks[block_index]
        grad_now = jnp.where(chosen[:, None], grad_all, jnp.zeros_like(grad_all))
        back_rows, part_gate, part_up, part_down = expert_backward(rows_now, grad_now, gate_weight[expert_index], up_weight[expert_index], down_weight[expert_index])
        back_wide = back_rows.astype(jnp.float32)
        result_buf = result_buf.at[block_index].add(jnp.where(chosen[:, None], back_wide, jnp.zeros_like(back_wide)))
        acc_gate = acc_gate.at[expert_index].add(part_gate)
        acc_up = acc_up.at[expert_index].add(part_up)
        acc_down = acc_down.at[expert_index].add(part_down)
        return ((result_buf, acc_gate, acc_up, acc_down), None)
    start_buf = jnp.zeros((block_count, per_block * TILE, model_width), jnp.float32)
    carry, unused = lax.scan(visit, (start_buf,) + tuple(sums), (owner_block, expert_of, usable))
    back_sorted = carry[0].reshape(-1, TILE, model_width).astype(jnp.bfloat16)
    return (back_sorted, carry[1:])

def layer_forward(hidden, gain_row, gate_weight, up_weight, down_weight, route_row):
    normed, scaled, inverse = normalize(hidden, gain_row)
    sort_order = jnp.argsort(route_row, stable=True).astype(jnp.int32)
    restore = jnp.argsort(sort_order, stable=True).astype(jnp.int32)
    tile_blocks = normed.reshape(-1, TILE, normed.shape[-1])
    produced = grouped_forward(tile_blocks[sort_order], route_row[sort_order], gate_weight, up_weight, down_weight)
    ffn_rows = produced[restore].reshape(hidden.shape)
    return (hidden.astype(jnp.float32) + ffn_rows.astype(jnp.float32)).astype(jnp.bfloat16)

def layer_backward(hidden, grad_rows, gain_row, gate_weight, up_weight, down_weight, route_row, sums):
    normed, scaled, inverse = normalize(hidden, gain_row)
    sort_order = jnp.argsort(route_row, stable=True).astype(jnp.int32)
    restore = jnp.argsort(sort_order, stable=True).astype(jnp.int32)
    tile_blocks = normed.reshape(-1, TILE, normed.shape[-1])
    grad_tiles = grad_rows.reshape(-1, TILE, grad_rows.shape[-1])
    back_sorted, sums = grouped_backward(tile_blocks[sort_order], grad_tiles[sort_order], route_row[sort_order], gate_weight, up_weight, down_weight, sums)
    grad_normed = back_sorted[restore].reshape(hidden.shape).astype(jnp.float32)
    gain_part = lax.optimization_barrier(jnp.sum(grad_normed * scaled, axis=0))
    grad_scaled = grad_normed * gain_row
    grad_wide = inverse * (grad_scaled - scaled * lax.optimization_barrier(jnp.mean(grad_scaled * scaled, axis=-1, keepdims=True)))
    grad_in = (grad_rows.astype(jnp.float32) + grad_wide).astype(jnp.bfloat16)
    return (grad_in, gain_part, sums)

def reference(tokens, cotangent, gain, w_gate, w_up, w_down, route):
    pipe_count = tokens.shape[0]
    stored = {}
    finals = [None] * pipe_count
    for micro_index in range(pipe_count):
        hidden = tokens[micro_index]
        for pass_index in range(PASSES):
            layer_index = (micro_index + pass_index) % pipe_count
            stored[micro_index, pass_index] = hidden
            hidden = layer_forward(hidden, gain[layer_index], w_gate[layer_index], w_up[layer_index], w_down[layer_index], route[layer_index, micro_index, :, 0])
        finals[(micro_index + PASSES - 1) % pipe_count] = hidden
    acc_gate = [jnp.zeros(w_gate.shape[1:], jnp.float32) for layer_index in range(pipe_count)]
    acc_up = [jnp.zeros(w_up.shape[1:], jnp.float32) for layer_index in range(pipe_count)]
    acc_down = [jnp.zeros(w_down.shape[1:], jnp.float32) for layer_index in range(pipe_count)]
    acc_gain = [jnp.zeros(gain.shape[1:], jnp.float32) for layer_index in range(pipe_count)]
    entry_grads = [None] * pipe_count
    for micro_index in range(pipe_count):
        grad_rows = cotangent[(micro_index + PASSES - 1) % pipe_count]
        for pass_index in reversed(range(PASSES)):
            layer_index = (micro_index + pass_index) % pipe_count
            grad_rows, gain_part, sums = layer_backward(stored[micro_index, pass_index], grad_rows, gain[layer_index], w_gate[layer_index], w_up[layer_index], w_down[layer_index], route[layer_index, micro_index, :, 0], (acc_gate[layer_index], acc_up[layer_index], acc_down[layer_index]))
            acc_gate[layer_index], acc_up[layer_index], acc_down[layer_index] = sums
            acc_gain[layer_index] = acc_gain[layer_index] + gain_part
        entry_grads[micro_index] = grad_rows
    return (jnp.stack(finals), jnp.stack(entry_grads), jnp.stack(acc_gain), jnp.stack([item.astype(jnp.bfloat16) for item in acc_gate]), jnp.stack([item.astype(jnp.bfloat16) for item in acc_up]), jnp.stack([item.astype(jnp.bfloat16) for item in acc_down]))
```

```python
import jax
import jax.numpy as jnp
from jax import lax
from jax.sharding import PartitionSpec as P

TILE = 8
PASSES = 2
PAIR = 2


epsilon = 1e-06
bf16 = jnp.bfloat16
f32 = jnp.float32


def dot(former, latter, contract):
    return lax.dot_general(
        former, latter, ((contract[:1], contract[1:]), ((), ())), preferred_element_type=f32
    )


def partner_route(size, step):
    return [(i, i ^ step) for i in range(size)]


def swap(block, axis, step):
    return lax.ppermute(block, axis, partner_route(lax.axis_size(axis), step))


def shifted(block, axis, distance):
    size = lax.axis_size(axis)
    return lax.ppermute(block, axis, [(i, (i + distance) % size) for i in range(size)])


def quarter_of(rows, index, width):
    return lax.dynamic_slice_in_dim(rows, index * width, width, axis=-1)


def to_quarters(rows, dp_count):
    width = rows.shape[-1] // dp_count
    here = lax.axis_index("dp")
    return jnp.concatenate(
        [quarter_of(rows, here, width)]
        + [swap(quarter_of(rows, here ^ step, width), "dp", step) for step in range(1, dp_count)]
    )


def from_quarters(parts, dp_count):
    here = lax.axis_index("dp")
    rows = parts.shape[0] // dp_count
    width = parts.shape[1]
    whole = jnp.zeros((rows, width * dp_count), parts.dtype)
    for step in range(dp_count):
        part = parts[step * rows : (step + 1) * rows]
        if step:
            part = swap(part, "dp", step)
        whole = lax.dynamic_update_slice_in_dim(whole, part, (here ^ step) * width, axis=1)
    return whole


def sum_parts(parts, dp_count):
    rows = parts.shape[0] // dp_count
    total = parts[:rows].astype(f32)
    for step in range(1, dp_count):
        total = total + swap(parts[step * rows : (step + 1) * rows], "dp", step).astype(f32)
    return total


def gather_rows(rows, dp_count):
    return jnp.concatenate([rows] + [swap(rows, "dp", step) for step in range(1, dp_count)])


def pick(mask, own, other):
    return jnp.where(mask, own, other)


def body(tokens, cotangent, gain, w_gate, w_up, w_down, route):
    pipe_count = lax.axis_size("pipe")
    dp_count = lax.axis_size("dp")
    section = lax.axis_index("pipe")
    expert = lax.axis_index("expert")
    here = lax.axis_index("dp")
    width = tokens.shape[-1] // dp_count
    features = tokens.shape[-1]
    hidden_units = w_gate.shape[-1]
    gain_part = lax.dynamic_slice_in_dim(gain[0], here * width, width)

    own_tokens = tokens[0]
    hidden = to_quarters(own_tokens, dp_count)
    weights_own = (w_gate[0, 0], w_up[0, 0], w_down[0, 0])
    weights_other = tuple(swap(weight, "expert", 1) for weight in weights_own)
    micro = [(section - k + pipe_count) % pipe_count for k in range(PASSES)]
    route_rows = jnp.stack(
        [lax.dynamic_index_in_dim(route[0, :, :, 0], m, 0, keepdims=False) for m in micro], axis=1
    )
    route_all = gather_rows(route_rows, dp_count)
    masks = [
        jnp.repeat(route_all[:, k] == expert, TILE)[:, None] for k in range(PASSES)
    ]
    grad = to_quarters(cotangent[0], dp_count)

    def scale_of(square_sum):
        return lax.rsqrt(square_sum / features + epsilon)

    wide = own_tokens.astype(f32)
    inverse = scale_of(jnp.sum(wide * wide, axis=-1, keepdims=True))
    kept = []
    rows = own_tokens.shape[0]
    for k in range(PASSES):
        mask = masks[k]
        wide = hidden.astype(f32)
        if k:
            squares = jnp.sum(wide * wide, axis=-1, keepdims=True)
            inverse = scale_of(sum_parts(squares, dp_count))
        gained = (wide * gain_part).astype(bf16)
        gate, up = (
            sum_parts(
                pick(
                    mask,
                    dot(gained, weights_own[i], (1, 0)),
                    dot(gained, weights_other[i], (1, 0)),
                ).astype(bf16),
                dp_count,
            )
            * inverse
            for i in range(2)
        )
        sigmoid = jax.nn.sigmoid(gate)
        activated = gather_rows((gate * sigmoid * up).astype(bf16), dp_count)
        ffn = pick(
            mask,
            dot(activated, weights_own[2], (1, 0)),
            dot(activated, weights_other[2], (1, 0)),
        ).astype(bf16)
        next_hidden = (wide + ffn.astype(f32)).astype(bf16)
        kept.append((hidden, gained, inverse, gate, up, sigmoid, activated))
        if k + 1 < PASSES:
            hidden = shifted(next_hidden, "pipe", 1)
    out_rows = from_quarters(next_hidden, dp_count)

    sums = [[], [], []]
    gain_sum = jnp.zeros((width,), f32)
    for k in reversed(range(PASSES)):
        hidden, gained, inverse, gate, up, sigmoid, activated = kept[k]
        mask = masks[k]
        grad_act = sum_parts(
            pick(
                mask, dot(grad, weights_own[2], (1, 1)), dot(grad, weights_other[2], (1, 1))
            ).astype(bf16),
            dp_count,
        )
        gate_grad = grad_act * up * sigmoid * (1.0 + gate * (1.0 - sigmoid)) * inverse
        up_grad = grad_act * gate * sigmoid * inverse
        shrink = jnp.sum(gate_grad * gate + up_grad * up, axis=-1, keepdims=True) * (
            inverse / features
        )
        gate_grad = gather_rows(gate_grad.astype(bf16), dp_count)
        up_grad = gather_rows(up_grad.astype(bf16), dp_count)
        shrink = gather_rows(shrink, dp_count)
        back = pick(
            mask,
            dot(gate_grad, weights_own[0], (1, 1)) + dot(up_grad, weights_own[1], (1, 1)),
            dot(gate_grad, weights_other[0], (1, 1)) + dot(up_grad, weights_other[1], (1, 1)),
        )
        wide = hidden.astype(f32)
        gain_sum = gain_sum + jnp.sum(back * wide, axis=0)
        grad_in = (grad.astype(f32) + back * gain_part - wide * shrink).astype(bf16)
        sums[0].append((gained, gate_grad, mask))
        sums[1].append((gained, up_grad, mask))
        sums[2].append((activated, grad, mask))
        if k > 0:
            grad = shifted(grad_in, "pipe", -1)
    entry = from_quarters(grad_in, dp_count)

    def weight_grad(pairs, wanted):
        return sum(
            dot(left, jnp.where(mask == wanted, right, jnp.zeros_like(right)), (0, 0))
            for left, right, mask in pairs
        )

    grads = []
    for pairs in sums:
        received = swap(weight_grad(pairs, False).astype(bf16), "expert", 1)
        grads.append((weight_grad(pairs, True) + received.astype(f32)).astype(bf16))
    gain_all = lax.all_gather(lax.psum(gain_sum, "expert"), "dp", tiled=True)
    return (
        out_rows[None],
        entry[None],
        gain_all[None],
        grads[0][None, None],
        grads[1][None, None],
        grads[2][None, None],
    )


def start_shifted(block, axis, distance):
    devices = range(lax.axis_size(axis))
    route = [((i - distance) % len(devices), i) for i in devices]
    return lax.ppermute(block, axis, route)


def start_contract_last(former, latter):
    return lax.dot_general(
        former, latter, (((1,), (1,)), ((), ())), preferred_element_type=jnp.float32
    )


def start_contract_first(former, latter):
    return lax.dot_general(
        former, latter, (((0,), (0,)), ((), ())), preferred_element_type=jnp.float32
    )


def start_normalize(hidden, gain_row):
    widened = hidden.astype(jnp.float32)
    inverse = lax.rsqrt(jnp.mean(widened * widened, axis=-1, keepdims=True) + epsilon)
    scaled = widened * inverse
    return ((scaled * gain_row).astype(jnp.bfloat16), scaled, inverse)


def start_slot_matrix(route_now, expert_count, capacity):
    tile_count = route_now.shape[0]
    expert_ids = jnp.arange(expert_count, dtype=jnp.int32)
    member = (route_now[None, :] == expert_ids[:, None]).astype(jnp.int32)
    earlier = jnp.cumsum(member, axis=1) - member
    rank_ids = jnp.arange(capacity, dtype=jnp.int32)
    placed = member[:, None, :] * (earlier[:, None, :] == rank_ids[None, :, None]).astype(jnp.int32)
    return placed.reshape(expert_count * capacity, tile_count)


def start_into_slots(placed, rows, tile_rows, dp_count):
    width = rows.shape[-1]
    tile_blocks = rows.reshape(placed.shape[1], tile_rows, dp_count, width // dp_count)
    return jnp.einsum(
        "st,trqd->qsrd",
        placed.astype(jnp.bfloat16),
        tile_blocks,
        preferred_element_type=jnp.float32,
    ).astype(jnp.bfloat16)


def start_from_slots(placed, slot_rows):
    merged = jnp.einsum(
        "st,qsrd->trqd", placed.astype(jnp.bfloat16), slot_rows, preferred_element_type=jnp.float32
    ).astype(jnp.bfloat16)
    return merged.reshape(merged.shape[0] * merged.shape[1], -1)


def start_send_out(slot_rows):
    quarter = slot_rows.shape[-1]
    flat = slot_rows.reshape((-1,) + slot_rows.shape[2:])
    arrived = lax.all_to_all(flat, ("dp", "expert"), split_axis=0, concat_axis=0, tiled=True)
    return arrived.reshape(-1, quarter)


def start_send_back(part_rows, dp_count, tile_rows):
    quarter = part_rows.shape[-1]
    flat = part_rows.reshape(-1, tile_rows, quarter)
    returned = lax.all_to_all(flat, ("dp", "expert"), split_axis=0, concat_axis=0, tiled=True)
    return returned.reshape(dp_count, -1, tile_rows, quarter)


def start_widen_rounded(values):
    return lax.optimization_barrier(values.astype(jnp.bfloat16)).astype(jnp.float32)


def start_expert_forward(received, gate_weight, up_weight, down_weight):
    gate_terms = start_widen_rounded(jnp.dot(received, gate_weight, preferred_element_type=jnp.float32))
    up_terms = start_widen_rounded(jnp.dot(received, up_weight, preferred_element_type=jnp.float32))
    gate_pre, up_pre = (
        lax.psum(gate_terms.astype(jnp.bfloat16), "dp").astype(jnp.float32),
        lax.psum(up_terms.astype(jnp.bfloat16), "dp").astype(jnp.float32),
    )
    activated = (jax.nn.silu(gate_pre) * up_pre).astype(jnp.bfloat16)
    part_rows = jnp.dot(activated, down_weight, preferred_element_type=jnp.float32).astype(
        jnp.bfloat16
    )
    return (part_rows, (gate_pre, up_pre, activated))


def start_expert_backward(
    received, grad_recv, kept_state, gate_weight, up_weight, down_weight, grad_sums
):
    gate_pre, up_pre, activated = kept_state
    grad_terms = start_widen_rounded(start_contract_last(grad_recv, down_weight))
    grad_act = lax.psum(grad_terms.astype(jnp.bfloat16), "dp").astype(jnp.float32)
    sigmoid_gate = jax.nn.sigmoid(gate_pre)
    silu_gate = gate_pre * sigmoid_gate
    grad_gate_pre = (
        grad_act * up_pre * sigmoid_gate * (1.0 + gate_pre * (1.0 - sigmoid_gate))
    ).astype(jnp.bfloat16)
    grad_up_pre = (grad_act * silu_gate).astype(jnp.bfloat16)
    back_rows = (
        start_contract_last(grad_gate_pre, gate_weight) + start_contract_last(grad_up_pre, up_weight)
    ).astype(jnp.bfloat16)
    grad_gate = grad_sums[0] + start_contract_first(received, grad_gate_pre)
    grad_up = grad_sums[1] + start_contract_first(received, grad_up_pre)
    grad_down = grad_sums[2] + start_contract_first(activated, grad_recv)
    return (back_rows, (grad_gate, grad_up, grad_down))


def start_body(tokens, cotangent, gain, w_gate, w_up, w_down, route):
    pipe_count = lax.axis_size("pipe")
    dp_count = lax.axis_size("dp")
    expert_count = lax.axis_size("expert")
    section_index = lax.axis_index("pipe")
    gain_row = gain[0]
    gate_weight = w_gate[0, 0]
    up_weight = w_up[0, 0]
    down_weight = w_down[0, 0]
    route_table = route[0, :, :, 0]
    tile_count = route_table.shape[1]
    capacity = max(2, 3 * tile_count // (2 * expert_count))
    hidden = tokens[0]
    saved_ticks = []
    out_rows = hidden
    for pass_index in range(PASSES):
        micro_index = (section_index - pass_index + pipe_count) % pipe_count
        route_now = lax.dynamic_index_in_dim(route_table, micro_index, 0, keepdims=False)
        placed = start_slot_matrix(route_now, expert_count, capacity)
        normed, scaled, inverse = start_normalize(hidden, gain_row)
        received = start_send_out(start_into_slots(placed, normed, TILE, dp_count))
        part_rows, kept_state = start_expert_forward(received, gate_weight, up_weight, down_weight)
        ffn_rows = start_from_slots(placed, start_send_back(part_rows, dp_count, TILE))
        new_hidden = (hidden.astype(jnp.float32) + ffn_rows.astype(jnp.float32)).astype(
            jnp.bfloat16
        )
        saved_ticks.append((placed, scaled, inverse, received, kept_state))
        if pass_index + 1 < PASSES:
            hidden = start_shifted(new_hidden, "pipe", 1)
        else:
            out_rows = new_hidden
    grad_rows = cotangent[0]
    grad_sums = (
        jnp.zeros(gate_weight.shape, jnp.float32),
        jnp.zeros(up_weight.shape, jnp.float32),
        jnp.zeros(down_weight.shape, jnp.float32),
    )
    gain_sum = jnp.zeros(gain_row.shape, jnp.float32)
    entry_grad = grad_rows
    for pass_index in reversed(range(PASSES)):
        placed, scaled, inverse, received, kept_state = saved_ticks[pass_index]
        grad_recv = start_send_out(start_into_slots(placed, grad_rows, TILE, dp_count))
        back_rows, grad_sums = start_expert_backward(
            received, grad_recv, kept_state, gate_weight, up_weight, down_weight, grad_sums
        )
        grad_normed = start_from_slots(placed, start_send_back(back_rows, dp_count, TILE)).astype(jnp.float32)
        gain_sum = gain_sum + jnp.sum(grad_normed * scaled, axis=0)
        grad_scaled = grad_normed * gain_row
        grad_wide = inverse * (
            grad_scaled - scaled * jnp.mean(grad_scaled * scaled, axis=-1, keepdims=True)
        )
        grad_in = (grad_rows.astype(jnp.float32) + grad_wide).astype(jnp.bfloat16)
        if pass_index > 0:
            grad_rows = start_shifted(grad_in, "pipe", -1)
        else:
            entry_grad = grad_in
    gain_total = lax.psum(gain_sum, ("dp", "expert"))
    return (
        out_rows[None],
        entry_grad[None],
        gain_total[None],
        grad_sums[0].astype(jnp.bfloat16)[None, None],
        grad_sums[1].astype(jnp.bfloat16)[None, None],
        grad_sums[2].astype(jnp.bfloat16)[None, None],
    )


def start_solution(mesh):
    placed = (
        P("pipe", ("dp", "expert"), None),
        P("pipe", ("dp", "expert"), None),
        P("pipe", None),
        P("pipe", "expert", "dp", None),
        P("pipe", "expert", "dp", None),
        P("pipe", "expert", None, "dp"),
        P("pipe", None, ("dp", "expert"), None),
    )
    return jax.shard_map(
        start_body,
        mesh=mesh,
        in_specs=placed,
        out_specs=(
            P("pipe", ("dp", "expert"), None),
            P("pipe", ("dp", "expert"), None),
            P("pipe", None),
            P("pipe", "expert", "dp", None),
            P("pipe", "expert", "dp", None),
            P("pipe", "expert", None, "dp"),
        ),
        check_vma=False,
    )


def solution(mesh):
    if mesh.shape["expert"] != PAIR:
        return start_solution(mesh)
    placed = (
        P("pipe", ("dp", "expert"), None),
        P("pipe", ("dp", "expert"), None),
        P("pipe", None),
        P("pipe", "expert", "dp", None),
        P("pipe", "expert", "dp", None),
        P("pipe", "expert", None, "dp"),
        P("pipe", None, ("dp", "expert"), None),
    )
    return jax.shard_map(
        body,
        mesh=mesh,
        in_specs=placed,
        out_specs=placed[:2] + (P("pipe", None),) + placed[3:6],
        check_vma=False,
    )
```

```python
import jax
import jax.numpy as jnp
from jax import lax
from jax.sharding import PartitionSpec as P

TILE = 8
PASSES = 2
PAIR = 2


epsilon = 1e-06
bf16 = jnp.bfloat16
f32 = jnp.float32


def dot(former, latter, contract):
    return lax.dot_general(
        former, latter, ((contract[:1], contract[1:]), ((), ())), preferred_element_type=f32
    )


def partner_route(size, step):
    return [(i, i ^ step) for i in range(size)]


def swap(block, axis, step):
    return lax.ppermute(block, axis, partner_route(lax.axis_size(axis), step))


def shifted(block, axis, distance):
    size = lax.axis_size(axis)
    return lax.ppermute(block, axis, [(i, (i + distance) % size) for i in range(size)])


def quarter_of(rows, index, width):
    return lax.dynamic_slice_in_dim(rows, index * width, width, axis=-1)


def to_quarters(rows, dp_count):
    width = rows.shape[-1] // dp_count
    here = lax.axis_index("dp")
    return jnp.concatenate(
        [quarter_of(rows, here, width)]
        + [swap(quarter_of(rows, here ^ step, width), "dp", step) for step in range(1, dp_count)]
    )


def from_quarters(parts, dp_count):
    here = lax.axis_index("dp")
    rows = parts.shape[0] // dp_count
    width = parts.shape[1]
    whole = jnp.zeros((rows, width * dp_count), parts.dtype)
    for step in range(dp_count):
        part = parts[step * rows : (step + 1) * rows]
        if step:
            part = swap(part, "dp", step)
        whole = lax.dynamic_update_slice_in_dim(whole, part, (here ^ step) * width, axis=1)
    return whole


def sum_parts(parts, dp_count):
    rows = parts.shape[0] // dp_count
    total = parts[:rows].astype(f32)
    for step in range(1, dp_count):
        total = total + swap(parts[step * rows : (step + 1) * rows], "dp", step).astype(f32)
    return total


def gather_rows(rows, dp_count):
    return jnp.concatenate([rows] + [swap(rows, "dp", step) for step in range(1, dp_count)])


def pick(mask, own, other):
    return jnp.where(mask, own, other)


def after(value, *earlier):
    return lax.optimization_barrier((value,) + earlier)[0]


def body(tokens, cotangent, gain, w_gate, w_up, w_down, route):
    pipe_count = lax.axis_size("pipe")
    dp_count = lax.axis_size("dp")
    section = lax.axis_index("pipe")
    expert = lax.axis_index("expert")
    here = lax.axis_index("dp")
    features = tokens.shape[-1]
    width = features // dp_count
    gain_part = lax.dynamic_slice_in_dim(gain[0], here * width, width)

    own_tokens = tokens[0]
    hidden = to_quarters(own_tokens, dp_count)
    w_both = jnp.concatenate([w_gate[0, 0], w_up[0, 0]], axis=1)
    both_own, both_other = w_both, swap(w_both, "expert", 1)
    down_own, down_other = w_down[0, 0], swap(w_down[0, 0], "expert", 1)
    micro = [(section - k + pipe_count) % pipe_count for k in range(PASSES)]
    route_rows = jnp.stack(
        [lax.dynamic_index_in_dim(route[0, :, :, 0], m, 0, keepdims=False) for m in micro], axis=1
    )
    route_all = gather_rows(route_rows, dp_count)
    masks = [
        jnp.repeat(route_all[:, k] == expert, TILE)[:, None] for k in range(PASSES)
    ]

    def scale_of(square_sum):
        return lax.rsqrt(square_sum / features + epsilon)

    def hidden_grad(grad, mask):
        return sum_parts(
            pick(mask, dot(grad, down_own, (1, 1)), dot(grad, down_other, (1, 1))).astype(bf16),
            dp_count,
        )

    def down(activated, mask):
        return pick(
            mask, dot(activated, down_own, (1, 0)), dot(activated, down_other, (1, 0))
        ).astype(bf16)

    def weight_grad(left, right, mask, wanted):
        return dot(left, jnp.where(mask == wanted, right, jnp.zeros_like(right)), (0, 0))

    def split(both):
        return jnp.split(both, 2, axis=1)

    wide = own_tokens.astype(f32)
    inverse = scale_of(jnp.sum(wide * wide, axis=-1, keepdims=True))
    kept = []
    for k in range(PASSES):
        mask = masks[k]
        wide = hidden.astype(f32)
        gained = (wide * gain_part).astype(bf16)
        parts = pick(mask, dot(gained, both_own, (1, 0)), dot(gained, both_other, (1, 0)))
        gate, up = split(sum_parts(parts.astype(bf16), dp_count) * inverse)
        sigmoid = jax.nn.sigmoid(gate)
        activated = (gate * sigmoid * up).astype(bf16)
        kept.append((hidden, gained, inverse, gate, up, sigmoid))
        if k + 1 < PASSES:
            first_activated = gather_rows(activated, dp_count)
            next_hidden = (wide + down(first_activated, mask).astype(f32)).astype(bf16)
            hidden = shifted(next_hidden, "pipe", 1)
            wide = next_hidden.astype(f32)
            squares = sum_parts(jnp.sum(wide * wide, axis=-1, keepdims=True), dp_count)
            inverse = shifted(scale_of(squares), "pipe", 1)
            grad = to_quarters(after(cotangent[0], next_hidden), dp_count)
            grad_act = hidden_grad(grad, masks[1])

    gain_sum = jnp.zeros((width,), f32)
    early = []
    for k in reversed(range(PASSES)):
        hidden, gained, inverse, gate, up, sigmoid = kept[k]
        mask = masks[k]
        gate_grad = grad_act * up * sigmoid * (1.0 + gate * (1.0 - sigmoid)) * inverse
        up_grad = grad_act * gate * sigmoid * inverse
        shrink = jnp.sum(gate_grad * gate + up_grad * up, axis=-1, keepdims=True) * (
            inverse / features
        )
        both_grad = gather_rows(
            jnp.concatenate([gate_grad.astype(bf16), up_grad.astype(bf16)], axis=1), dp_count
        )
        shrink = gather_rows(shrink, dp_count)
        back = pick(mask, dot(both_grad, both_own, (1, 1)), dot(both_grad, both_other, (1, 1)))
        wide = hidden.astype(f32)
        gain_sum = gain_sum + jnp.sum(back * wide, axis=0)
        grad_in = (grad.astype(f32) + back * gain_part - wide * shrink).astype(bf16)
        if k > 0:
            last_grad = grad
            grad = shifted(grad_in, "pipe", -1)
            last_activated = gather_rows(after(activated, grad_in), dp_count)
            out_parts = (wide + down(last_activated, mask).astype(f32)).astype(bf16)
            out_rows = from_quarters(out_parts, dp_count)
            for wanted in (False, True):
                for right in split(both_grad):
                    early.append(weight_grad(gained, right, mask, wanted).astype(bf16))
                early.append(weight_grad(last_activated, last_grad, mask, wanted).astype(bf16))
            grad = after(grad, out_rows, *early)
            grad_act = hidden_grad(grad, masks[0])
    gain_rows = gather_rows(gain_sum[None], dp_count)
    gain_rows = gain_rows + swap(gain_rows, "expert", 1)
    gain_all = jnp.zeros((features,), f32)
    for step in range(dp_count):
        gain_all = lax.dynamic_update_slice_in_dim(
            gain_all, gain_rows[step], (here ^ step) * width, axis=0
        )
    entry = from_quarters(grad_in, dp_count)
    late = [(gained, right) for right in split(both_grad)] + [(first_activated, grad)]
    received = [
        swap((weight_grad(*pair, mask, False) + early[i].astype(f32)).astype(bf16), "expert", 1)
        for i, pair in enumerate(late)
    ]
    grads = [
        (
            weight_grad(*pair, mask, True) + early[3 + i].astype(f32) + received[i].astype(f32)
        ).astype(bf16)
        for i, pair in enumerate(late)
    ]
    return (
        out_rows[None],
        entry[None],
        gain_all[None],
        grads[0][None, None],
        grads[1][None, None],
        grads[2][None, None],
    )


def start_shifted(block, axis, distance):
    devices = range(lax.axis_size(axis))
    route = [((i - distance) % len(devices), i) for i in devices]
    return lax.ppermute(block, axis, route)


def start_contract_last(former, latter):
    return lax.dot_general(
        former, latter, (((1,), (1,)), ((), ())), preferred_element_type=jnp.float32
    )


def start_contract_first(former, latter):
    return lax.dot_general(
        former, latter, (((0,), (0,)), ((), ())), preferred_element_type=jnp.float32
    )


def start_normalize(hidden, gain_row):
    widened = hidden.astype(jnp.float32)
    inverse = lax.rsqrt(jnp.mean(widened * widened, axis=-1, keepdims=True) + epsilon)
    scaled = widened * inverse
    return ((scaled * gain_row).astype(jnp.bfloat16), scaled, inverse)


def start_slot_matrix(route_now, expert_count, capacity):
    tile_count = route_now.shape[0]
    expert_ids = jnp.arange(expert_count, dtype=jnp.int32)
    member = (route_now[None, :] == expert_ids[:, None]).astype(jnp.int32)
    earlier = jnp.cumsum(member, axis=1) - member
    rank_ids = jnp.arange(capacity, dtype=jnp.int32)
    placed = member[:, None, :] * (earlier[:, None, :] == rank_ids[None, :, None]).astype(jnp.int32)
    return placed.reshape(expert_count * capacity, tile_count)


def start_into_slots(placed, rows, tile_rows, dp_count):
    width = rows.shape[-1]
    tile_blocks = rows.reshape(placed.shape[1], tile_rows, dp_count, width // dp_count)
    return jnp.einsum(
        "st,trqd->qsrd",
        placed.astype(jnp.bfloat16),
        tile_blocks,
        preferred_element_type=jnp.float32,
    ).astype(jnp.bfloat16)


def start_from_slots(placed, slot_rows):
    merged = jnp.einsum(
        "st,qsrd->trqd", placed.astype(jnp.bfloat16), slot_rows, preferred_element_type=jnp.float32
    ).astype(jnp.bfloat16)
    return merged.reshape(merged.shape[0] * merged.shape[1], -1)


def start_send_out(slot_rows):
    quarter = slot_rows.shape[-1]
    flat = slot_rows.reshape((-1,) + slot_rows.shape[2:])
    arrived = lax.all_to_all(flat, ("dp", "expert"), split_axis=0, concat_axis=0, tiled=True)
    return arrived.reshape(-1, quarter)


def start_send_back(part_rows, dp_count, tile_rows):
    quarter = part_rows.shape[-1]
    flat = part_rows.reshape(-1, tile_rows, quarter)
    returned = lax.all_to_all(flat, ("dp", "expert"), split_axis=0, concat_axis=0, tiled=True)
    return returned.reshape(dp_count, -1, tile_rows, quarter)


def start_widen_rounded(values):
    return lax.optimization_barrier(values.astype(jnp.bfloat16)).astype(jnp.float32)


def start_expert_forward(received, gate_weight, up_weight, down_weight):
    gate_terms = start_widen_rounded(jnp.dot(received, gate_weight, preferred_element_type=jnp.float32))
    up_terms = start_widen_rounded(jnp.dot(received, up_weight, preferred_element_type=jnp.float32))
    gate_pre, up_pre = (
        lax.psum(gate_terms.astype(jnp.bfloat16), "dp").astype(jnp.float32),
        lax.psum(up_terms.astype(jnp.bfloat16), "dp").astype(jnp.float32),
    )
    activated = (jax.nn.silu(gate_pre) * up_pre).astype(jnp.bfloat16)
    part_rows = jnp.dot(activated, down_weight, preferred_element_type=jnp.float32).astype(
        jnp.bfloat16
    )
    return (part_rows, (gate_pre, up_pre, activated))


def start_expert_backward(
    received, grad_recv, kept_state, gate_weight, up_weight, down_weight, grad_sums
):
    gate_pre, up_pre, activated = kept_state
    grad_terms = start_widen_rounded(start_contract_last(grad_recv, down_weight))
    grad_act = lax.psum(grad_terms.astype(jnp.bfloat16), "dp").astype(jnp.float32)
    sigmoid_gate = jax.nn.sigmoid(gate_pre)
    silu_gate = gate_pre * sigmoid_gate
    grad_gate_pre = (
        grad_act * up_pre * sigmoid_gate * (1.0 + gate_pre * (1.0 - sigmoid_gate))
    ).astype(jnp.bfloat16)
    grad_up_pre = (grad_act * silu_gate).astype(jnp.bfloat16)
    back_rows = (
        start_contract_last(grad_gate_pre, gate_weight) + start_contract_last(grad_up_pre, up_weight)
    ).astype(jnp.bfloat16)
    grad_gate = grad_sums[0] + start_contract_first(received, grad_gate_pre)
    grad_up = grad_sums[1] + start_contract_first(received, grad_up_pre)
    grad_down = grad_sums[2] + start_contract_first(activated, grad_recv)
    return (back_rows, (grad_gate, grad_up, grad_down))


def start_body(tokens, cotangent, gain, w_gate, w_up, w_down, route):
    pipe_count = lax.axis_size("pipe")
    dp_count = lax.axis_size("dp")
    expert_count = lax.axis_size("expert")
    section_index = lax.axis_index("pipe")
    gain_row = gain[0]
    gate_weight = w_gate[0, 0]
    up_weight = w_up[0, 0]
    down_weight = w_down[0, 0]
    route_table = route[0, :, :, 0]
    tile_count = route_table.shape[1]
    capacity = max(2, 3 * tile_count // (2 * expert_count))
    hidden = tokens[0]
    saved_ticks = []
    out_rows = hidden
    for pass_index in range(PASSES):
        micro_index = (section_index - pass_index + pipe_count) % pipe_count
        route_now = lax.dynamic_index_in_dim(route_table, micro_index, 0, keepdims=False)
        placed = start_slot_matrix(route_now, expert_count, capacity)
        normed, scaled, inverse = start_normalize(hidden, gain_row)
        received = start_send_out(start_into_slots(placed, normed, TILE, dp_count))
        part_rows, kept_state = start_expert_forward(received, gate_weight, up_weight, down_weight)
        ffn_rows = start_from_slots(placed, start_send_back(part_rows, dp_count, TILE))
        new_hidden = (hidden.astype(jnp.float32) + ffn_rows.astype(jnp.float32)).astype(
            jnp.bfloat16
        )
        saved_ticks.append((placed, scaled, inverse, received, kept_state))
        if pass_index + 1 < PASSES:
            hidden = start_shifted(new_hidden, "pipe", 1)
        else:
            out_rows = new_hidden
    grad_rows = cotangent[0]
    grad_sums = (
        jnp.zeros(gate_weight.shape, jnp.float32),
        jnp.zeros(up_weight.shape, jnp.float32),
        jnp.zeros(down_weight.shape, jnp.float32),
    )
    gain_sum = jnp.zeros(gain_row.shape, jnp.float32)
    entry_grad = grad_rows
    for pass_index in reversed(range(PASSES)):
        placed, scaled, inverse, received, kept_state = saved_ticks[pass_index]
        grad_recv = start_send_out(start_into_slots(placed, grad_rows, TILE, dp_count))
        back_rows, grad_sums = start_expert_backward(
            received, grad_recv, kept_state, gate_weight, up_weight, down_weight, grad_sums
        )
        grad_normed = start_from_slots(placed, start_send_back(back_rows, dp_count, TILE)).astype(jnp.float32)
        gain_sum = gain_sum + jnp.sum(grad_normed * scaled, axis=0)
        grad_scaled = grad_normed * gain_row
        grad_wide = inverse * (
            grad_scaled - scaled * jnp.mean(grad_scaled * scaled, axis=-1, keepdims=True)
        )
        grad_in = (grad_rows.astype(jnp.float32) + grad_wide).astype(jnp.bfloat16)
        if pass_index > 0:
            grad_rows = start_shifted(grad_in, "pipe", -1)
        else:
            entry_grad = grad_in
    gain_total = lax.psum(gain_sum, ("dp", "expert"))
    return (
        out_rows[None],
        entry_grad[None],
        gain_total[None],
        grad_sums[0].astype(jnp.bfloat16)[None, None],
        grad_sums[1].astype(jnp.bfloat16)[None, None],
        grad_sums[2].astype(jnp.bfloat16)[None, None],
    )


def start_solution(mesh):
    placed = (
        P("pipe", ("dp", "expert"), None),
        P("pipe", ("dp", "expert"), None),
        P("pipe", None),
        P("pipe", "expert", "dp", None),
        P("pipe", "expert", "dp", None),
        P("pipe", "expert", None, "dp"),
        P("pipe", None, ("dp", "expert"), None),
    )
    return jax.shard_map(
        start_body,
        mesh=mesh,
        in_specs=placed,
        out_specs=(
            P("pipe", ("dp", "expert"), None),
            P("pipe", ("dp", "expert"), None),
            P("pipe", None),
            P("pipe", "expert", "dp", None),
            P("pipe", "expert", "dp", None),
            P("pipe", "expert", None, "dp"),
        ),
        check_vma=False,
    )


def solution(mesh):
    if mesh.shape["expert"] != PAIR:
        return start_solution(mesh)
    placed = (
        P("pipe", ("dp", "expert"), None),
        P("pipe", ("dp", "expert"), None),
        P("pipe", None),
        P("pipe", "expert", "dp", None),
        P("pipe", "expert", "dp", None),
        P("pipe", "expert", None, "dp"),
        P("pipe", None, ("dp", "expert"), None),
    )
    return jax.shard_map(
        body,
        mesh=mesh,
        in_specs=placed,
        out_specs=placed[:2] + (P("pipe", None),) + placed[3:6],
        check_vma=False,
    )
```

```python
import jax
import jax.numpy as jnp
from jax import lax
from jax.experimental import pallas as pl
from jax.experimental.pallas import tpu as pltpu
from jax.sharding import PartitionSpec as P

TILE = 8
PASSES = 2
PAIR = 2
COLUMNS = 256
LANES = 128


epsilon = 1e-06
bf16 = jnp.bfloat16
f32 = jnp.float32


def dot(former, latter, contract):
    return lax.dot_general(
        former, latter, ((contract[:1], contract[1:]), ((), ())), preferred_element_type=f32
    )


def partner_route(size, step):
    return [(i, i ^ step) for i in range(size)]


def swap(block, axis, step):
    return lax.ppermute(block, axis, partner_route(lax.axis_size(axis), step))


def shifted(block, axis, distance):
    size = lax.axis_size(axis)
    return lax.ppermute(block, axis, [(i, (i + distance) % size) for i in range(size)])


def quarter_of(rows, index, width):
    return lax.dynamic_slice_in_dim(rows, index * width, width, axis=-1)


def to_quarters(rows, dp_count):
    width = rows.shape[-1] // dp_count
    here = lax.axis_index("dp")
    quarters = [quarter_of(rows, here ^ step, width) for step in range(dp_count)]
    return quarters[:1] + [swap(quarters[step], "dp", step) for step in range(1, dp_count)]


def from_quarters(parts):
    here = lax.axis_index("dp")
    rows, width = parts[0].shape
    whole = jnp.zeros((rows, width * len(parts)), parts[0].dtype)
    for step, part in enumerate(parts):
        if step:
            part = swap(part, "dp", step)
        whole = lax.dynamic_update_slice_in_dim(whole, part, (here ^ step) * width, axis=1)
    return whole


def sum_parts(parts):
    total = parts[0].astype(f32)
    for step in range(1, len(parts)):
        total = total + swap(parts[step], "dp", step).astype(f32)
    return total


def gather_rows(rows, dp_count):
    return [rows] + [swap(rows, "dp", step) for step in range(1, dp_count)]


def after(value, *earlier):
    return lax.optimization_barrier((value,) + earlier)[0]


def columns_of(extent):
    return COLUMNS if extent % COLUMNS == 0 else extent


def whole_spec(shape):
    return pl.BlockSpec(shape, lambda j: (0,) * len(shape))


def kernel_call(body, steps, in_specs, out_specs, out_shape, scratch, flops, arrays):
    moved = sum(a.size * a.dtype.itemsize for a in arrays)
    moved += sum(a.size * a.dtype.itemsize for a in out_shape)
    return pl.pallas_call(
        body,
        grid=(steps,),
        in_specs=in_specs,
        out_specs=out_specs,
        out_shape=out_shape,
        scratch_shapes=scratch,
        compiler_params=pltpu.CompilerParams(
            dimension_semantics=("arbitrary",), vmem_limit_bytes=40 * 1024 * 1024
        ),
        cost_estimate=pl.CostEstimate(flops=flops, bytes_accessed=moved, transcendentals=0),
    )(*arrays)


def hidden_parts(blocks, gain_part, mask, gate_pair, up_pair):
    count = len(blocks)
    rows = sum(block.shape[0] for block in blocks)
    parts_count = lax.axis_size("dp")
    part_rows = rows // parts_count
    width, units = gate_pair[0].shape
    tile = columns_of(units)
    half = units // tile

    def body(*refs):
        block_refs, refs = refs[:count], refs[count:]
        gain_ref, mask_ref, gate_own, gate_other, up_own, up_other = refs[:6]
        part_refs, gained_ref = refs[6:-1], refs[-1]
        step = pl.program_id(0)

        @pl.when(step == 0)
        def _():
            start = 0
            for ref in block_refs:
                size = ref.shape[0]
                gained_ref[start : start + size] = (ref[...].astype(f32) * gain_ref[...]).astype(
                    bf16
                )
                start += size

        def emit(own, other):
            part = jnp.where(
                mask_ref[...] > 0.5,
                dot(gained_ref[...], own[...], (1, 0)),
                dot(gained_ref[...], other[...], (1, 0)),
            ).astype(bf16)
            for index, ref in enumerate(part_refs):
                ref[...] = part[index * part_rows : (index + 1) * part_rows]

        @pl.when(step < half)
        def _():
            emit(gate_own, gate_other)

        @pl.when(step >= half)
        def _():
            emit(up_own, up_other)

    gate_spec = pl.BlockSpec((width, tile), lambda j: (0, jnp.minimum(j, half - 1)))
    up_spec = pl.BlockSpec((width, tile), lambda j: (0, jnp.maximum(j - half, 0)))
    outs = kernel_call(
        body,
        2 * half,
        [whole_spec(block.shape) for block in blocks]
        + [whole_spec((1, width)), whole_spec((rows, 1))]
        + [gate_spec] * 2
        + [up_spec] * 2,
        [pl.BlockSpec((part_rows, tile), lambda j: (0, j))] * parts_count
        + [whole_spec((rows, width))],
        [jax.ShapeDtypeStruct((part_rows, 2 * units), bf16)] * parts_count
        + [jax.ShapeDtypeStruct((rows, width), bf16)],
        [],
        8 * rows * width * units,
        (*blocks, gain_part, mask, *gate_pair, *up_pair),
    )
    return outs[:parts_count], outs[parts_count]


def add_down(blocks, mask, down_pair, hidden, in_parts):
    count = len(blocks)
    part_rows, units = blocks[0].shape
    rows = part_rows * count
    width = down_pair[0].shape[1]
    tile = columns_of(width)
    out_count = count if in_parts else 1

    def body(*refs):
        block_refs, refs = refs[:count], refs[count:]
        mask_ref, own, other, hidden_ref = refs[:4]
        out_refs, square_ref, joined = refs[4:-2], refs[-2], refs[-1]
        step = pl.program_id(0)

        @pl.when(step == 0)
        def _():
            for index, ref in enumerate(block_refs):
                joined[index * part_rows : (index + 1) * part_rows] = ref[...]
            square_ref[...] = jnp.zeros_like(square_ref)

        ffn = jnp.where(
            mask_ref[...] > 0.5,
            dot(joined[...], own[...], (1, 0)),
            dot(joined[...], other[...], (1, 0)),
        ).astype(bf16)
        out = (hidden_ref[...].astype(f32) + ffn.astype(f32)).astype(bf16)
        wide = out.astype(f32)
        square_ref[...] += jnp.sum(wide * wide, axis=-1, keepdims=True)
        size = rows // out_count
        for index, ref in enumerate(out_refs):
            ref[...] = out[index * size : (index + 1) * size]

    size = rows // out_count
    outs = kernel_call(
        body,
        width // tile,
        [whole_spec((part_rows, units))] * count
        + [whole_spec((rows, 1))]
        + [pl.BlockSpec((units, tile), lambda j: (0, j))] * 2
        + [pl.BlockSpec((rows, tile), lambda j: (0, j))],
        [pl.BlockSpec((size, tile), lambda j: (0, j))] * out_count + [whole_spec((rows, 1))],
        [jax.ShapeDtypeStruct((size, width), bf16)] * out_count
        + [jax.ShapeDtypeStruct((rows, 1), f32)],
        [pltpu.VMEM((rows, units), bf16)],
        4 * rows * width * units,
        (*blocks, mask, *down_pair, hidden),
    )
    return outs[:out_count], outs[out_count]


def act_grad_parts(grad, mask, down_pair):
    parts_count = lax.axis_size("dp")
    rows, width = grad.shape
    part_rows = rows // parts_count
    units = down_pair[0].shape[0]
    tile = columns_of(units)

    def body(grad_ref, mask_ref, own, other, *part_refs):
        part = jnp.where(
            mask_ref[...] > 0.5,
            dot(grad_ref[...], own[...], (1, 1)),
            dot(grad_ref[...], other[...], (1, 1)),
        ).astype(bf16)
        for index, ref in enumerate(part_refs):
            ref[...] = part[index * part_rows : (index + 1) * part_rows]

    return kernel_call(
        body,
        units // tile,
        [whole_spec((rows, width)), whole_spec((rows, 1))]
        + [pl.BlockSpec((tile, width), lambda j: (j, 0))] * 2,
        [pl.BlockSpec((part_rows, tile), lambda j: (0, j))] * parts_count,
        [jax.ShapeDtypeStruct((part_rows, units), bf16)] * parts_count,
        [],
        4 * rows * width * units,
        (grad, mask, *down_pair),
    )


def input_grad(blocks, mask, gate_pair, up_pair, grad, hidden, gain_part, in_parts):
    count = len(blocks)
    part_rows, sent = blocks[0].shape
    rows = part_rows * count
    width, units = gate_pair[0].shape
    tile = columns_of(width)
    out_count = count if in_parts else 1
    size = rows // out_count

    def body(*refs):
        block_refs, refs = refs[:count], refs[count:]
        mask_ref, gate_own, gate_other, up_own, up_other, grad_ref, hidden_ref, gain_ref = refs[:8]
        out_refs, sum_ref, joined, shrink = refs[8:-3], refs[-3], refs[-2], refs[-1]
        step = pl.program_id(0)

        @pl.when(step == 0)
        def _():
            for index, ref in enumerate(block_refs):
                place = slice(index * part_rows, (index + 1) * part_rows)
                joined[place] = ref[:, : 2 * units]
                tail = ref[:, 2 * units :].astype(f32)
                shrink[place] = jnp.sum(tail, axis=-1, keepdims=True)

        def back_of(gate, up):
            return dot(joined[:, :units], gate[...], (1, 1)) + dot(
                joined[:, units:], up[...], (1, 1)
            )

        back = jnp.where(
            mask_ref[...] > 0.5, back_of(gate_own, up_own), back_of(gate_other, up_other)
        )
        wide = hidden_ref[...].astype(f32)
        sum_ref[...] = jnp.sum(back * wide, axis=0, keepdims=True)
        out = (
            grad_ref[...].astype(f32) + back * gain_ref[...] - wide * shrink[...]
        ).astype(bf16)
        for index, ref in enumerate(out_refs):
            ref[...] = out[index * size : (index + 1) * size]

    outs = kernel_call(
        body,
        width // tile,
        [whole_spec((part_rows, sent))] * count
        + [whole_spec((rows, 1))]
        + [pl.BlockSpec((tile, units), lambda j: (j, 0))] * 4
        + [pl.BlockSpec((rows, tile), lambda j: (0, j))] * 2
        + [pl.BlockSpec((1, tile), lambda j: (0, j))],
        [pl.BlockSpec((size, tile), lambda j: (0, j))] * out_count
        + [pl.BlockSpec((1, tile), lambda j: (0, j))],
        [jax.ShapeDtypeStruct((size, width), bf16)] * out_count
        + [jax.ShapeDtypeStruct((1, width), f32)],
        [pltpu.VMEM((rows, 2 * units), bf16), pltpu.VMEM((rows, 1), f32)],
        8 * rows * width * units,
        (*blocks, mask, *gate_pair, *up_pair, grad, hidden, gain_part),
    )
    return outs[:out_count], outs[out_count]


def body(tokens, cotangent, gain, w_gate, w_up, w_down, route):
    pipe_count = lax.axis_size("pipe")
    dp_count = lax.axis_size("dp")
    section = lax.axis_index("pipe")
    expert = lax.axis_index("expert")
    here = lax.axis_index("dp")
    features = tokens.shape[-1]
    width = features // dp_count
    units = w_gate.shape[-1]
    gain_part = lax.dynamic_slice_in_dim(gain, here * width, width, axis=1)

    own_tokens = tokens[0]
    blocks = to_quarters(own_tokens, dp_count)
    gate_pair, up_pair, down_pair = (
        (weight[0, 0], swap(weight[0, 0], "expert", 1)) for weight in (w_gate, w_up, w_down)
    )
    micro = [(section - k + pipe_count) % pipe_count for k in range(PASSES)]
    route_rows = jnp.stack(
        [lax.dynamic_index_in_dim(route[0, :, :, 0], m, 0, keepdims=False) for m in micro], axis=1
    )
    route_all = jnp.concatenate(gather_rows(after(route_rows, blocks[0]), dp_count))
    masks = [
        jnp.repeat((route_all[:, k] == expert).astype(f32), TILE)[:, None] for k in range(PASSES)
    ]

    def scale_of(square_sum):
        return lax.rsqrt(square_sum / features + epsilon)

    def weight_grad(left, right, mask, wanted):
        return dot(left, jnp.where((mask > 0.5) == wanted, right, jnp.zeros_like(right)), (0, 0))

    wide = own_tokens.astype(f32)
    inverse = scale_of(jnp.sum(wide * wide, axis=-1, keepdims=True))
    kept = []
    for k in range(PASSES):
        mask = masks[k]
        parts, gained = hidden_parts(blocks, gain_part, mask, gate_pair, up_pair)
        total = sum_parts(parts) * inverse
        gate, up = total[:, :units], total[:, units:]
        sigmoid = jax.nn.sigmoid(gate)
        activated = (gate * sigmoid * up).astype(bf16)
        hidden = jnp.concatenate(blocks)
        kept.append((hidden, gained, inverse, gate, up, sigmoid))
        if k + 1 < PASSES:
            first_activated = gather_rows(activated, dp_count)
            (next_hidden,), squares = add_down(first_activated, mask, down_pair, hidden, False)
            blocks = [shifted(next_hidden, "pipe", 1)]
            squares = sum_parts(jnp.split(squares, dp_count))
            inverse = shifted(scale_of(squares), "pipe", 1)
            grad = jnp.concatenate(to_quarters(after(cotangent[0], squares), dp_count))
            grad_act = sum_parts(act_grad_parts(grad, masks[1], down_pair))

    gain_sum = jnp.zeros((1, width), f32)
    early = []
    for k in reversed(range(PASSES)):
        hidden, gained, inverse, gate, up, sigmoid = kept[k]
        mask = masks[k]
        gate_grad = grad_act * up * sigmoid * (1.0 + gate * (1.0 - sigmoid)) * inverse
        up_grad = grad_act * gate * sigmoid * inverse
        shrink = jnp.sum(gate_grad * gate + up_grad * up, axis=-1, keepdims=True) * (
            inverse / features
        )
        coarse = lax.reduce_precision(shrink, 8, 7)
        lane = lax.broadcasted_iota(jnp.int32, (shrink.shape[0], LANES), 1)
        tail = jnp.where(lane == 0, coarse, jnp.where(lane == 1, shrink - coarse, 0.0))
        sent = jnp.concatenate([gate_grad, up_grad, tail], axis=1).astype(bf16)
        both_grad = gather_rows(sent, dp_count)
        outs, gain_term = input_grad(
            both_grad, mask, gate_pair, up_pair, grad, hidden, gain_part, k == 0
        )
        gain_sum = gain_sum + gain_term
        joined = jnp.concatenate(both_grad)
        rights = (joined[:, :units], joined[:, units : 2 * units])
        if k > 0:
            last_grad = grad
            grad = shifted(outs[0], "pipe", -1)
            last_activated = gather_rows(after(activated, outs[0]), dp_count)
            out_parts, _ = add_down(last_activated, mask, down_pair, hidden, True)
            out_rows = from_quarters(out_parts)
            lefts = (gained, gained, jnp.concatenate(last_activated))
            for wanted in (False, True):
                for left, right in zip(lefts, rights + (last_grad,)):
                    early.append(weight_grad(left, right, mask, wanted).astype(bf16))
            grad = after(grad, out_rows, *early)
            grad_act = sum_parts(act_grad_parts(grad, masks[0], down_pair))
    entry = from_quarters(outs)
    gain_rows = jnp.concatenate(gather_rows(after(gain_sum, entry), dp_count))
    gain_rows = gain_rows + swap(gain_rows, "expert", 1)
    gain_all = jnp.zeros((features,), f32)
    for step in range(dp_count):
        gain_all = lax.dynamic_update_slice_in_dim(
            gain_all, gain_rows[step], (here ^ step) * width, axis=0
        )
    late = list(zip((gained, gained, jnp.concatenate(first_activated)), rights + (grad,)))
    received = [
        swap((weight_grad(*pair, mask, False) + early[i].astype(f32)).astype(bf16), "expert", 1)
        for i, pair in enumerate(late)
    ]
    grads = [
        (
            weight_grad(*pair, mask, True) + early[3 + i].astype(f32) + received[i].astype(f32)
        ).astype(bf16)
        for i, pair in enumerate(late)
    ]
    return (
        out_rows[None],
        entry[None],
        gain_all[None],
        grads[0][None, None],
        grads[1][None, None],
        grads[2][None, None],
    )


def start_shifted(block, axis, distance):
    devices = range(lax.axis_size(axis))
    route = [((i - distance) % len(devices), i) for i in devices]
    return lax.ppermute(block, axis, route)


def start_contract_last(former, latter):
    return lax.dot_general(
        former, latter, (((1,), (1,)), ((), ())), preferred_element_type=jnp.float32
    )


def start_contract_first(former, latter):
    return lax.dot_general(
        former, latter, (((0,), (0,)), ((), ())), preferred_element_type=jnp.float32
    )


def start_normalize(hidden, gain_row):
    widened = hidden.astype(jnp.float32)
    inverse = lax.rsqrt(jnp.mean(widened * widened, axis=-1, keepdims=True) + epsilon)
    scaled = widened * inverse
    return ((scaled * gain_row).astype(jnp.bfloat16), scaled, inverse)


def start_slot_matrix(route_now, expert_count, capacity):
    tile_count = route_now.shape[0]
    expert_ids = jnp.arange(expert_count, dtype=jnp.int32)
    member = (route_now[None, :] == expert_ids[:, None]).astype(jnp.int32)
    earlier = jnp.cumsum(member, axis=1) - member
    rank_ids = jnp.arange(capacity, dtype=jnp.int32)
    placed = member[:, None, :] * (earlier[:, None, :] == rank_ids[None, :, None]).astype(jnp.int32)
    return placed.reshape(expert_count * capacity, tile_count)


def start_into_slots(placed, rows, tile_rows, dp_count):
    width = rows.shape[-1]
    tile_blocks = rows.reshape(placed.shape[1], tile_rows, dp_count, width // dp_count)
    return jnp.einsum(
        "st,trqd->qsrd",
        placed.astype(jnp.bfloat16),
        tile_blocks,
        preferred_element_type=jnp.float32,
    ).astype(jnp.bfloat16)


def start_from_slots(placed, slot_rows):
    merged = jnp.einsum(
        "st,qsrd->trqd", placed.astype(jnp.bfloat16), slot_rows, preferred_element_type=jnp.float32
    ).astype(jnp.bfloat16)
    return merged.reshape(merged.shape[0] * merged.shape[1], -1)


def start_send_out(slot_rows):
    quarter = slot_rows.shape[-1]
    flat = slot_rows.reshape((-1,) + slot_rows.shape[2:])
    arrived = lax.all_to_all(flat, ("dp", "expert"), split_axis=0, concat_axis=0, tiled=True)
    return arrived.reshape(-1, quarter)


def start_send_back(part_rows, dp_count, tile_rows):
    quarter = part_rows.shape[-1]
    flat = part_rows.reshape(-1, tile_rows, quarter)
    returned = lax.all_to_all(flat, ("dp", "expert"), split_axis=0, concat_axis=0, tiled=True)
    return returned.reshape(dp_count, -1, tile_rows, quarter)


def start_widen_rounded(values):
    return lax.optimization_barrier(values.astype(jnp.bfloat16)).astype(jnp.float32)


def start_expert_forward(received, gate_weight, up_weight, down_weight):
    gate_terms = start_widen_rounded(jnp.dot(received, gate_weight, preferred_element_type=jnp.float32))
    up_terms = start_widen_rounded(jnp.dot(received, up_weight, preferred_element_type=jnp.float32))
    gate_pre, up_pre = (
        lax.psum(gate_terms.astype(jnp.bfloat16), "dp").astype(jnp.float32),
        lax.psum(up_terms.astype(jnp.bfloat16), "dp").astype(jnp.float32),
    )
    activated = (jax.nn.silu(gate_pre) * up_pre).astype(jnp.bfloat16)
    part_rows = jnp.dot(activated, down_weight, preferred_element_type=jnp.float32).astype(
        jnp.bfloat16
    )
    return (part_rows, (gate_pre, up_pre, activated))


def start_expert_backward(
    received, grad_recv, kept_state, gate_weight, up_weight, down_weight, grad_sums
):
    gate_pre, up_pre, activated = kept_state
    grad_terms = start_widen_rounded(start_contract_last(grad_recv, down_weight))
    grad_act = lax.psum(grad_terms.astype(jnp.bfloat16), "dp").astype(jnp.float32)
    sigmoid_gate = jax.nn.sigmoid(gate_pre)
    silu_gate = gate_pre * sigmoid_gate
    grad_gate_pre = (
        grad_act * up_pre * sigmoid_gate * (1.0 + gate_pre * (1.0 - sigmoid_gate))
    ).astype(jnp.bfloat16)
    grad_up_pre = (grad_act * silu_gate).astype(jnp.bfloat16)
    back_rows = (
        start_contract_last(grad_gate_pre, gate_weight) + start_contract_last(grad_up_pre, up_weight)
    ).astype(jnp.bfloat16)
    grad_gate = grad_sums[0] + start_contract_first(received, grad_gate_pre)
    grad_up = grad_sums[1] + start_contract_first(received, grad_up_pre)
    grad_down = grad_sums[2] + start_contract_first(activated, grad_recv)
    return (back_rows, (grad_gate, grad_up, grad_down))


def start_body(tokens, cotangent, gain, w_gate, w_up, w_down, route):
    pipe_count = lax.axis_size("pipe")
    dp_count = lax.axis_size("dp")
    expert_count = lax.axis_size("expert")
    section_index = lax.axis_index("pipe")
    gain_row = gain[0]
    gate_weight = w_gate[0, 0]
    up_weight = w_up[0, 0]
    down_weight = w_down[0, 0]
    route_table = route[0, :, :, 0]
    tile_count = route_table.shape[1]
    capacity = max(2, 3 * tile_count // (2 * expert_count))
    hidden = tokens[0]
    saved_ticks = []
    out_rows = hidden
    for pass_index in range(PASSES):
        micro_index = (section_index - pass_index + pipe_count) % pipe_count
        route_now = lax.dynamic_index_in_dim(route_table, micro_index, 0, keepdims=False)
        placed = start_slot_matrix(route_now, expert_count, capacity)
        normed, scaled, inverse = start_normalize(hidden, gain_row)
        received = start_send_out(start_into_slots(placed, normed, TILE, dp_count))
        part_rows, kept_state = start_expert_forward(received, gate_weight, up_weight, down_weight)
        ffn_rows = start_from_slots(placed, start_send_back(part_rows, dp_count, TILE))
        new_hidden = (hidden.astype(jnp.float32) + ffn_rows.astype(jnp.float32)).astype(
            jnp.bfloat16
        )
        saved_ticks.append((placed, scaled, inverse, received, kept_state))
        if pass_index + 1 < PASSES:
            hidden = start_shifted(new_hidden, "pipe", 1)
        else:
            out_rows = new_hidden
    grad_rows = cotangent[0]
    grad_sums = (
        jnp.zeros(gate_weight.shape, jnp.float32),
        jnp.zeros(up_weight.shape, jnp.float32),
        jnp.zeros(down_weight.shape, jnp.float32),
    )
    gain_sum = jnp.zeros(gain_row.shape, jnp.float32)
    entry_grad = grad_rows
    for pass_index in reversed(range(PASSES)):
        placed, scaled, inverse, received, kept_state = saved_ticks[pass_index]
        grad_recv = start_send_out(start_into_slots(placed, grad_rows, TILE, dp_count))
        back_rows, grad_sums = start_expert_backward(
            received, grad_recv, kept_state, gate_weight, up_weight, down_weight, grad_sums
        )
        grad_normed = start_from_slots(placed, start_send_back(back_rows, dp_count, TILE)).astype(jnp.float32)
        gain_sum = gain_sum + jnp.sum(grad_normed * scaled, axis=0)
        grad_scaled = grad_normed * gain_row
        grad_wide = inverse * (
            grad_scaled - scaled * jnp.mean(grad_scaled * scaled, axis=-1, keepdims=True)
        )
        grad_in = (grad_rows.astype(jnp.float32) + grad_wide).astype(jnp.bfloat16)
        if pass_index > 0:
            grad_rows = start_shifted(grad_in, "pipe", -1)
        else:
            entry_grad = grad_in
    gain_total = lax.psum(gain_sum, ("dp", "expert"))
    return (
        out_rows[None],
        entry_grad[None],
        gain_total[None],
        grad_sums[0].astype(jnp.bfloat16)[None, None],
        grad_sums[1].astype(jnp.bfloat16)[None, None],
        grad_sums[2].astype(jnp.bfloat16)[None, None],
    )


def start_solution(mesh):
    placed = (
        P("pipe", ("dp", "expert"), None),
        P("pipe", ("dp", "expert"), None),
        P("pipe", None),
        P("pipe", "expert", "dp", None),
        P("pipe", "expert", "dp", None),
        P("pipe", "expert", None, "dp"),
        P("pipe", None, ("dp", "expert"), None),
    )
    return jax.shard_map(
        start_body,
        mesh=mesh,
        in_specs=placed,
        out_specs=(
            P("pipe", ("dp", "expert"), None),
            P("pipe", ("dp", "expert"), None),
            P("pipe", None),
            P("pipe", "expert", "dp", None),
            P("pipe", "expert", "dp", None),
            P("pipe", "expert", None, "dp"),
        ),
        check_vma=False,
    )


def solution(mesh):
    if mesh.shape["expert"] != PAIR:
        return start_solution(mesh)
    placed = (
        P("pipe", ("dp", "expert"), None),
        P("pipe", ("dp", "expert"), None),
        P("pipe", None),
        P("pipe", "expert", "dp", None),
        P("pipe", "expert", "dp", None),
        P("pipe", "expert", None, "dp"),
        P("pipe", None, ("dp", "expert"), None),
    )
    return jax.shard_map(
        body,
        mesh=mesh,
        in_specs=placed,
        out_specs=placed[:2] + (P("pipe", None),) + placed[3:6],
        check_vma=False,
    )
```

```python
import jax
import jax.numpy as jnp
from jax import lax
from jax.experimental import pallas as pl
from jax.experimental.pallas import tpu as pltpu
from jax.sharding import PartitionSpec as P

TILE = 8
PASSES = 2
PAIR = 2
COLUMNS = 256
LANES = 128


epsilon = 1e-06
bf16 = jnp.bfloat16
f32 = jnp.float32


def dot(former, latter, contract):
    return lax.dot_general(
        former, latter, ((contract[:1], contract[1:]), ((), ())), preferred_element_type=f32
    )


def partner_route(size, step):
    return [(i, i ^ step) for i in range(size)]


def swap(block, axis, step):
    return lax.ppermute(block, axis, partner_route(lax.axis_size(axis), step))


def shifted(block, axis, distance):
    size = lax.axis_size(axis)
    return lax.ppermute(block, axis, [(i, (i + distance) % size) for i in range(size)])


def quarter_of(rows, index, width):
    return lax.dynamic_slice_in_dim(rows, index * width, width, axis=-1)


def to_quarters(rows, dp_count):
    width = rows.shape[-1] // dp_count
    here = lax.axis_index("dp")
    quarters = [quarter_of(rows, here ^ step, width) for step in range(dp_count)]
    return quarters[:1] + [swap(quarters[step], "dp", step) for step in range(1, dp_count)]


def assemble(parts):
    here = lax.axis_index("dp")
    rows, width = parts[0].shape
    whole = jnp.zeros((rows, width * len(parts)), parts[0].dtype)
    for step, part in enumerate(parts):
        whole = lax.dynamic_update_slice_in_dim(whole, part, (here ^ step) * width, axis=1)
    return whole


def from_quarters(parts):
    return assemble(
        [swap(part, "dp", step) if step else part for step, part in enumerate(parts)]
    )


def sum_parts(parts):
    total = parts[0].astype(f32)
    for step in range(1, len(parts)):
        total = total + swap(parts[step], "dp", step).astype(f32)
    return total


def gather_rows(rows, dp_count):
    return [rows] + [swap(rows, "dp", step) for step in range(1, dp_count)]


def after(value, *earlier):
    return lax.optimization_barrier((value,) + earlier)[0]


def columns_of(extent):
    return COLUMNS if extent % COLUMNS == 0 else extent


def kernel_call(body, operands, weights, out_shape, scratch, flops):
    arrays = [array for array, _ in weights]
    count, fetched, made = len(operands), len(weights), len(out_shape)
    tiles = [columns_of(array.shape[axis]) for array, axis in weights]
    counts = [array.shape[axis] // tile for (array, axis), tile in zip(weights, tiles)]

    def call(*refs):
        operand_refs, refs = refs[:count], refs[count:]
        weight_refs, refs = refs[:fetched], refs[fetched:]
        out_refs, refs = refs[:made], refs[made:]
        landed, arrivals, refs = refs[:fetched], refs[fetched], refs[fetched + 1 :]

        def place(index, tile):
            span = pl.ds(tile * tiles[index], tiles[index])
            return (span, slice(None)) if weights[index][1] == 0 else (slice(None), span)

        def copy(index, tile):
            where = place(index, tile)
            return pltpu.make_async_copy(
                weight_refs[index].at[where], landed[index].at[where], arrivals.at[index, tile]
            )

        for tile in range(max(counts, default=0)):
            for index in range(fetched):
                if tile < counts[index]:
                    copy(index, tile).start()

        def fetch(index, tile):
            copy(index, tile).wait()
            return landed[index][place(index, tile)]

        body(operand_refs, fetch, out_refs, refs)

    moved = sum(a.size * a.dtype.itemsize for a in (*operands, *arrays, *out_shape))
    return pl.pallas_call(
        call,
        in_specs=[pl.BlockSpec(memory_space=pltpu.VMEM)] * count
        + [pl.BlockSpec(memory_space=pltpu.HBM)] * fetched,
        out_specs=[pl.BlockSpec(memory_space=pltpu.VMEM)] * made,
        out_shape=out_shape,
        scratch_shapes=[pltpu.VMEM(a.shape, a.dtype) for a in arrays]
        + [pltpu.SemaphoreType.DMA((fetched, max(counts, default=1)))]
        + scratch,
        compiler_params=pltpu.CompilerParams(vmem_limit_bytes=40 * 1024 * 1024),
        cost_estimate=pl.CostEstimate(flops=flops, bytes_accessed=moved, transcendentals=0),
    )(*operands, *arrays)


def store_parts(refs, columns, value):
    size = value.shape[0] // len(refs)
    for index, ref in enumerate(refs):
        ref[:, columns] = value[index * size : (index + 1) * size]


def hidden_parts(blocks, gain_part, mask, gate_pair, up_pair):
    rows = sum(block.shape[0] for block in blocks)
    parts_count = lax.axis_size("dp")
    width, units = gate_pair[0].shape
    tile = columns_of(units)

    def body(operand_refs, fetch, out_refs, _):
        *block_refs, gain_ref, mask_ref = operand_refs
        *part_refs, gained_ref = out_refs
        start = 0
        for ref in block_refs:
            size = ref.shape[0]
            gained_ref[start : start + size] = (ref[...].astype(f32) * gain_ref[...]).astype(bf16)
            start += size
        for pair in range(2):
            for j in range(units // tile):
                part = jnp.where(
                    mask_ref[...] > 0.5,
                    dot(gained_ref[...], fetch(2 * pair, j), (1, 0)),
                    dot(gained_ref[...], fetch(2 * pair + 1, j), (1, 0)),
                ).astype(bf16)
                store_parts(part_refs, pl.ds(pair * units + j * tile, tile), part)

    outs = kernel_call(
        body,
        (*blocks, gain_part, mask),
        [(weight, 1) for weight in (*gate_pair, *up_pair)],
        [jax.ShapeDtypeStruct((rows // parts_count, 2 * units), bf16)] * parts_count
        + [jax.ShapeDtypeStruct((rows, width), bf16)],
        [],
        8 * rows * width * units,
    )
    return outs[:parts_count], outs[parts_count]


def join(joined, refs, columns):
    size = refs[0].shape[0]
    for index, ref in enumerate(refs):
        joined[index * size : (index + 1) * size] = ref[:, columns]


def add_down(blocks, mask, down_pair, hidden, in_parts):
    count = len(blocks)
    part_rows, units = blocks[0].shape
    rows = part_rows * count
    width = down_pair[0].shape[1]
    tile = columns_of(width)
    out_count = count if in_parts else 1

    def body(operand_refs, fetch, out_refs, scratch):
        *block_refs, mask_ref, hidden_ref = operand_refs
        *row_refs, square_ref = out_refs
        (joined,) = scratch
        join(joined, block_refs, slice(None))
        squares = jnp.zeros((rows, 1), f32)
        for j in range(width // tile):
            columns = pl.ds(j * tile, tile)
            ffn = jnp.where(
                mask_ref[...] > 0.5,
                dot(joined[...], fetch(0, j), (1, 0)),
                dot(joined[...], fetch(1, j), (1, 0)),
            ).astype(bf16)
            out = (hidden_ref[:, columns].astype(f32) + ffn.astype(f32)).astype(bf16)
            wide = out.astype(f32)
            squares = squares + jnp.sum(wide * wide, axis=-1, keepdims=True)
            store_parts(row_refs, columns, out)
        square_ref[...] = squares

    outs = kernel_call(
        body,
        (*blocks, mask, hidden),
        [(weight, 1) for weight in down_pair],
        [jax.ShapeDtypeStruct((rows // out_count, width), bf16)] * out_count
        + [jax.ShapeDtypeStruct((rows, 1), f32)],
        [pltpu.VMEM((rows, units), bf16)],
        4 * rows * width * units,
    )
    return outs[:out_count], outs[out_count]


def act_grad_parts(grad, mask, down_pair):
    parts_count = lax.axis_size("dp")
    rows, width = grad.shape
    units = down_pair[0].shape[0]
    tile = columns_of(units)

    def body(operand_refs, fetch, out_refs, _):
        grad_ref, mask_ref = operand_refs
        for j in range(units // tile):
            part = jnp.where(
                mask_ref[...] > 0.5,
                dot(grad_ref[...], fetch(0, j), (1, 1)),
                dot(grad_ref[...], fetch(1, j), (1, 1)),
            ).astype(bf16)
            store_parts(out_refs, pl.ds(j * tile, tile), part)

    return kernel_call(
        body,
        (grad, mask),
        [(weight, 0) for weight in down_pair],
        [jax.ShapeDtypeStruct((rows // parts_count, units), bf16)] * parts_count,
        [],
        4 * rows * width * units,
    )


def hidden_grads(parts, gate, up, inverse, features):
    rows, units = gate.shape

    def body(operand_refs, fetch, out_refs, _):
        *part_refs, gate_ref, up_ref, inverse_ref = operand_refs
        (out_ref,) = out_refs
        grad_act = part_refs[0][...].astype(f32)
        for ref in part_refs[1:]:
            grad_act = grad_act + ref[...].astype(f32)
        gate_now, up_now, scale = gate_ref[...], up_ref[...], inverse_ref[...]
        sigmoid = 1.0 / (1.0 + jnp.exp(-gate_now))
        scaled = grad_act * scale
        gate_grad = scaled * up_now * sigmoid * (1.0 + gate_now * (1.0 - sigmoid))
        up_grad = scaled * (gate_now * sigmoid)
        shrink = jnp.sum(gate_grad * gate_now + up_grad * up_now, axis=-1, keepdims=True) * (
            scale / features
        )
        out_ref[:, :units] = gate_grad.astype(bf16)
        out_ref[:, units : 2 * units] = up_grad.astype(bf16)
        coarse = shrink.astype(bf16).astype(f32)
        lane = lax.broadcasted_iota(jnp.int32, (rows, LANES), 1)
        out_ref[:, 2 * units :] = jnp.where(
            lane == 0, coarse, jnp.where(lane == 1, shrink - coarse, 0.0)
        ).astype(bf16)

    (sent,) = kernel_call(
        body,
        (*parts, gate, up, inverse),
        [],
        [jax.ShapeDtypeStruct((rows, 2 * units + LANES), bf16)],
        [],
        20 * rows * units,
    )
    return sent


def input_grad(blocks, mask, gate_pair, up_pair, grad, hidden, gain_part, in_parts):
    count = len(blocks)
    part_rows = blocks[0].shape[0]
    rows = part_rows * count
    width, units = gate_pair[0].shape
    tile = columns_of(width)
    out_count = count if in_parts else 1

    def body(operand_refs, fetch, out_refs, scratch):
        *block_refs, mask_ref, grad_ref, hidden_ref, gain_ref = operand_refs
        *row_refs, sum_ref = out_refs
        joined, shrink = scratch
        join(joined, block_refs, slice(0, 2 * units))
        for index, ref in enumerate(block_refs):
            tail = ref[:, 2 * units :].astype(f32)
            shrink[index * part_rows : (index + 1) * part_rows] = jnp.sum(
                tail, axis=-1, keepdims=True
            )
        for j in range(width // tile):
            columns = pl.ds(j * tile, tile)

            def back_of(kind):
                return dot(joined[:, :units], fetch(kind, j), (1, 1)) + dot(
                    joined[:, units:], fetch(2 + kind, j), (1, 1)
                )

            back = jnp.where(mask_ref[...] > 0.5, back_of(0), back_of(1))
            wide = hidden_ref[:, columns].astype(f32)
            sum_ref[:, columns] = jnp.sum(back * wide, axis=0, keepdims=True)
            out = (
                grad_ref[:, columns].astype(f32)
                + back * gain_ref[:, columns]
                - wide * shrink[...]
            ).astype(bf16)
            store_parts(row_refs, columns, out)

    outs = kernel_call(
        body,
        (*blocks, mask, grad, hidden, gain_part),
        [(weight, 0) for weight in (*gate_pair, *up_pair)],
        [jax.ShapeDtypeStruct((rows // out_count, width), bf16)] * out_count
        + [jax.ShapeDtypeStruct((1, width), f32)],
        [pltpu.VMEM((rows, 2 * units), bf16), pltpu.VMEM((rows, 1), f32)],
        8 * rows * width * units,
    )
    return outs[:out_count], outs[out_count]


def body(tokens, cotangent, gain, w_gate, w_up, w_down, route):
    pipe_count = lax.axis_size("pipe")
    dp_count = lax.axis_size("dp")
    section = lax.axis_index("pipe")
    expert = lax.axis_index("expert")
    here = lax.axis_index("dp")
    features = tokens.shape[-1]
    width = features // dp_count
    units = w_gate.shape[-1]
    gain_part = lax.dynamic_slice_in_dim(gain, here * width, width, axis=1)

    own_tokens = tokens[0]
    blocks = to_quarters(own_tokens, dp_count)
    gate_pair, up_pair, down_pair = (
        (weight[0, 0], swap(weight[0, 0], "expert", 1)) for weight in (w_gate, w_up, w_down)
    )
    micro = [(section - k + pipe_count) % pipe_count for k in range(PASSES)]
    route_rows = jnp.stack(
        [lax.dynamic_index_in_dim(route[0, :, :, 0], m, 0, keepdims=False) for m in micro], axis=1
    )
    route_all = jnp.concatenate(gather_rows(after(route_rows, blocks[1]), dp_count))
    masks = [
        jnp.repeat((route_all[:, k] == expert).astype(f32), TILE)[:, None] for k in range(PASSES)
    ]

    def scale_of(square_sum):
        return lax.rsqrt(square_sum / features + epsilon)

    def weight_grad(left, right, mask, wanted):
        return dot(left, jnp.where((mask > 0.5) == wanted, right, jnp.zeros_like(right)), (0, 0))

    wide = own_tokens.astype(f32)
    inverse = scale_of(jnp.sum(wide * wide, axis=-1, keepdims=True))
    kept = []
    for k in range(PASSES):
        mask = masks[k]
        parts, gained = hidden_parts(blocks, gain_part, mask, gate_pair, up_pair)
        total = sum_parts(parts) * inverse
        gate, up = total[:, :units], total[:, units:]
        activated = (gate * jax.nn.sigmoid(gate) * up).astype(bf16)
        hidden = jnp.concatenate(blocks)
        kept.append((hidden, gained, inverse, gate, up))
        if k + 1 < PASSES:
            first_activated = gather_rows(activated, dp_count)
            (next_hidden,), squares = add_down(first_activated, mask, down_pair, hidden, False)
            blocks = [shifted(next_hidden, "pipe", 1)]
            grad_blocks = to_quarters(after(cotangent[0], squares), dp_count)
            grad = jnp.concatenate(grad_blocks)
            squares = sum_parts(jnp.split(after(squares, grad_blocks[1]), dp_count))
            inverse = shifted(scale_of(squares), "pipe", 1)
            act_parts = act_grad_parts(grad, masks[1], down_pair)
            act_parts = [act_parts[0]] + [
                swap(act_parts[step], "dp", step) for step in range(1, dp_count)
            ]
            blocks[0] = after(blocks[0], act_parts[1])

    gain_sum = jnp.zeros((1, width), f32)
    for k in reversed(range(PASSES)):
        hidden, gained, inverse, gate, up = kept[k]
        mask = masks[k]
        sent = hidden_grads(act_parts, gate, up, inverse, features)
        both_grad = gather_rows(sent, dp_count)
        if k == 0:
            late_down = jnp.concatenate(first_activated)
            other_down = swap(
                (weight_grad(late_down, grad, mask, False) + early[False][2].astype(f32)).astype(
                    bf16
                ),
                "expert",
                1,
            )
            down_grad = (
                weight_grad(late_down, grad, mask, True)
                + early[True][2].astype(f32)
                + other_down.astype(f32)
            ).astype(bf16)
            both_grad[1] = after(both_grad[1], down_grad)
        outs, gain_term = input_grad(
            both_grad, mask, gate_pair, up_pair, grad, hidden, gain_part, k == 0
        )
        gain_sum = gain_sum + gain_term
        joined = jnp.concatenate(both_grad)
        rights = [joined[:, :units], joined[:, units : 2 * units]]
        if k > 0:
            last_grad = grad
            grad = shifted(outs[0], "pipe", -1)
            rights[0] = after(rights[0], outs[0])
            first = weight_grad(gained, rights[0], mask, False).astype(bf16)
            last_activated = gather_rows(after(activated, first), dp_count)
            early = {
                False: [first, weight_grad(gained, rights[1], mask, False).astype(bf16)],
                True: [weight_grad(gained, right, mask, True).astype(bf16) for right in rights],
            }
            out_parts, _ = add_down(last_activated, mask, down_pair, hidden, True)
            out_rows = from_quarters(out_parts)
            grad = after(grad, out_rows, *early[False], *early[True])
            act_parts = act_grad_parts(grad, masks[0], down_pair)
            last_activated = jnp.concatenate(last_activated)
            for wanted in (False, True):
                early[wanted].append(
                    weight_grad(last_activated, last_grad, mask, wanted).astype(bf16)
                )
            act_parts = [act_parts[0]] + [
                swap(act_parts[step], "dp", step) for step in range(1, dp_count)
            ]
            act_parts[1] = after(act_parts[1], early[False][2], early[True][2])

    returned = [outs[0]] + [swap(outs[step], "dp", step) for step in range(1, dp_count)]
    rights = [after(right, outs[0]) for right in rights]
    received = [
        swap((weight_grad(gained, right, mask, False) + soon.astype(f32)).astype(bf16), "expert", 1)
        for right, soon in zip(rights, early[False])
    ]
    gain_rows = jnp.concatenate(gather_rows(after(gain_sum, received[0]), dp_count))
    gain_rows = gain_rows + swap(gain_rows, "expert", 1)
    gain_all = jnp.zeros((features,), f32)
    for step in range(dp_count):
        gain_all = lax.dynamic_update_slice_in_dim(
            gain_all, gain_rows[step], (here ^ step) * width, axis=0
        )
    grads = [
        (
            weight_grad(gained, right, mask, True) + soon.astype(f32) + other.astype(f32)
        ).astype(bf16)
        for right, soon, other in zip(rights, early[True], received)
    ] + [down_grad]
    returned = list(lax.optimization_barrier((*returned, *grads)))[:dp_count]
    entry = assemble(returned)
    return (
        out_rows[None],
        entry[None],
        gain_all[None],
        grads[0][None, None],
        grads[1][None, None],
        grads[2][None, None],
    )


def start_shifted(block, axis, distance):
    devices = range(lax.axis_size(axis))
    route = [((i - distance) % len(devices), i) for i in devices]
    return lax.ppermute(block, axis, route)


def start_contract_last(former, latter):
    return lax.dot_general(
        former, latter, (((1,), (1,)), ((), ())), preferred_element_type=jnp.float32
    )


def start_contract_first(former, latter):
    return lax.dot_general(
        former, latter, (((0,), (0,)), ((), ())), preferred_element_type=jnp.float32
    )


def start_normalize(hidden, gain_row):
    widened = hidden.astype(jnp.float32)
    inverse = lax.rsqrt(jnp.mean(widened * widened, axis=-1, keepdims=True) + epsilon)
    scaled = widened * inverse
    return ((scaled * gain_row).astype(jnp.bfloat16), scaled, inverse)


def start_slot_matrix(route_now, expert_count, capacity):
    tile_count = route_now.shape[0]
    expert_ids = jnp.arange(expert_count, dtype=jnp.int32)
    member = (route_now[None, :] == expert_ids[:, None]).astype(jnp.int32)
    earlier = jnp.cumsum(member, axis=1) - member
    rank_ids = jnp.arange(capacity, dtype=jnp.int32)
    placed = member[:, None, :] * (earlier[:, None, :] == rank_ids[None, :, None]).astype(jnp.int32)
    return placed.reshape(expert_count * capacity, tile_count)


def start_into_slots(placed, rows, tile_rows, dp_count):
    width = rows.shape[-1]
    tile_blocks = rows.reshape(placed.shape[1], tile_rows, dp_count, width // dp_count)
    return jnp.einsum(
        "st,trqd->qsrd",
        placed.astype(jnp.bfloat16),
        tile_blocks,
        preferred_element_type=jnp.float32,
    ).astype(jnp.bfloat16)


def start_from_slots(placed, slot_rows):
    merged = jnp.einsum(
        "st,qsrd->trqd", placed.astype(jnp.bfloat16), slot_rows, preferred_element_type=jnp.float32
    ).astype(jnp.bfloat16)
    return merged.reshape(merged.shape[0] * merged.shape[1], -1)


def start_send_out(slot_rows):
    quarter = slot_rows.shape[-1]
    flat = slot_rows.reshape((-1,) + slot_rows.shape[2:])
    arrived = lax.all_to_all(flat, ("dp", "expert"), split_axis=0, concat_axis=0, tiled=True)
    return arrived.reshape(-1, quarter)


def start_send_back(part_rows, dp_count, tile_rows):
    quarter = part_rows.shape[-1]
    flat = part_rows.reshape(-1, tile_rows, quarter)
    returned = lax.all_to_all(flat, ("dp", "expert"), split_axis=0, concat_axis=0, tiled=True)
    return returned.reshape(dp_count, -1, tile_rows, quarter)


def start_widen_rounded(values):
    return lax.optimization_barrier(values.astype(jnp.bfloat16)).astype(jnp.float32)


def start_expert_forward(received, gate_weight, up_weight, down_weight):
    gate_terms = start_widen_rounded(jnp.dot(received, gate_weight, preferred_element_type=jnp.float32))
    up_terms = start_widen_rounded(jnp.dot(received, up_weight, preferred_element_type=jnp.float32))
    gate_pre, up_pre = (
        lax.psum(gate_terms.astype(jnp.bfloat16), "dp").astype(jnp.float32),
        lax.psum(up_terms.astype(jnp.bfloat16), "dp").astype(jnp.float32),
    )
    activated = (jax.nn.silu(gate_pre) * up_pre).astype(jnp.bfloat16)
    part_rows = jnp.dot(activated, down_weight, preferred_element_type=jnp.float32).astype(
        jnp.bfloat16
    )
    return (part_rows, (gate_pre, up_pre, activated))


def start_expert_backward(
    received, grad_recv, kept_state, gate_weight, up_weight, down_weight, grad_sums
):
    gate_pre, up_pre, activated = kept_state
    grad_terms = start_widen_rounded(start_contract_last(grad_recv, down_weight))
    grad_act = lax.psum(grad_terms.astype(jnp.bfloat16), "dp").astype(jnp.float32)
    sigmoid_gate = jax.nn.sigmoid(gate_pre)
    silu_gate = gate_pre * sigmoid_gate
    grad_gate_pre = (
        grad_act * up_pre * sigmoid_gate * (1.0 + gate_pre * (1.0 - sigmoid_gate))
    ).astype(jnp.bfloat16)
    grad_up_pre = (grad_act * silu_gate).astype(jnp.bfloat16)
    back_rows = (
        start_contract_last(grad_gate_pre, gate_weight) + start_contract_last(grad_up_pre, up_weight)
    ).astype(jnp.bfloat16)
    grad_gate = grad_sums[0] + start_contract_first(received, grad_gate_pre)
    grad_up = grad_sums[1] + start_contract_first(received, grad_up_pre)
    grad_down = grad_sums[2] + start_contract_first(activated, grad_recv)
    return (back_rows, (grad_gate, grad_up, grad_down))


def start_body(tokens, cotangent, gain, w_gate, w_up, w_down, route):
    pipe_count = lax.axis_size("pipe")
    dp_count = lax.axis_size("dp")
    expert_count = lax.axis_size("expert")
    section_index = lax.axis_index("pipe")
    gain_row = gain[0]
    gate_weight = w_gate[0, 0]
    up_weight = w_up[0, 0]
    down_weight = w_down[0, 0]
    route_table = route[0, :, :, 0]
    tile_count = route_table.shape[1]
    capacity = max(2, 3 * tile_count // (2 * expert_count))
    hidden = tokens[0]
    saved_ticks = []
    out_rows = hidden
    for pass_index in range(PASSES):
        micro_index = (section_index - pass_index + pipe_count) % pipe_count
        route_now = lax.dynamic_index_in_dim(route_table, micro_index, 0, keepdims=False)
        placed = start_slot_matrix(route_now, expert_count, capacity)
        normed, scaled, inverse = start_normalize(hidden, gain_row)
        received = start_send_out(start_into_slots(placed, normed, TILE, dp_count))
        part_rows, kept_state = start_expert_forward(received, gate_weight, up_weight, down_weight)
        ffn_rows = start_from_slots(placed, start_send_back(part_rows, dp_count, TILE))
        new_hidden = (hidden.astype(jnp.float32) + ffn_rows.astype(jnp.float32)).astype(
            jnp.bfloat16
        )
        saved_ticks.append((placed, scaled, inverse, received, kept_state))
        if pass_index + 1 < PASSES:
            hidden = start_shifted(new_hidden, "pipe", 1)
        else:
            out_rows = new_hidden
    grad_rows = cotangent[0]
    grad_sums = (
        jnp.zeros(gate_weight.shape, jnp.float32),
        jnp.zeros(up_weight.shape, jnp.float32),
        jnp.zeros(down_weight.shape, jnp.float32),
    )
    gain_sum = jnp.zeros(gain_row.shape, jnp.float32)
    entry_grad = grad_rows
    for pass_index in reversed(range(PASSES)):
        placed, scaled, inverse, received, kept_state = saved_ticks[pass_index]
        grad_recv = start_send_out(start_into_slots(placed, grad_rows, TILE, dp_count))
        back_rows, grad_sums = start_expert_backward(
            received, grad_recv, kept_state, gate_weight, up_weight, down_weight, grad_sums
        )
        grad_normed = start_from_slots(placed, start_send_back(back_rows, dp_count, TILE)).astype(jnp.float32)
        gain_sum = gain_sum + jnp.sum(grad_normed * scaled, axis=0)
        grad_scaled = grad_normed * gain_row
        grad_wide = inverse * (
            grad_scaled - scaled * jnp.mean(grad_scaled * scaled, axis=-1, keepdims=True)
        )
        grad_in = (grad_rows.astype(jnp.float32) + grad_wide).astype(jnp.bfloat16)
        if pass_index > 0:
            grad_rows = start_shifted(grad_in, "pipe", -1)
        else:
            entry_grad = grad_in
    gain_total = lax.psum(gain_sum, ("dp", "expert"))
    return (
        out_rows[None],
        entry_grad[None],
        gain_total[None],
        grad_sums[0].astype(jnp.bfloat16)[None, None],
        grad_sums[1].astype(jnp.bfloat16)[None, None],
        grad_sums[2].astype(jnp.bfloat16)[None, None],
    )


def start_solution(mesh):
    placed = (
        P("pipe", ("dp", "expert"), None),
        P("pipe", ("dp", "expert"), None),
        P("pipe", None),
        P("pipe", "expert", "dp", None),
        P("pipe", "expert", "dp", None),
        P("pipe", "expert", None, "dp"),
        P("pipe", None, ("dp", "expert"), None),
    )
    return jax.shard_map(
        start_body,
        mesh=mesh,
        in_specs=placed,
        out_specs=(
            P("pipe", ("dp", "expert"), None),
            P("pipe", ("dp", "expert"), None),
            P("pipe", None),
            P("pipe", "expert", "dp", None),
            P("pipe", "expert", "dp", None),
            P("pipe", "expert", None, "dp"),
        ),
        check_vma=False,
    )


def solution(mesh):
    if mesh.shape["expert"] != PAIR:
        return start_solution(mesh)
    placed = (
        P("pipe", ("dp", "expert"), None),
        P("pipe", ("dp", "expert"), None),
        P("pipe", None),
        P("pipe", "expert", "dp", None),
        P("pipe", "expert", "dp", None),
        P("pipe", "expert", None, "dp"),
        P("pipe", None, ("dp", "expert"), None),
    )
    return jax.shard_map(
        body,
        mesh=mesh,
        in_specs=placed,
        out_specs=placed[:2] + (P("pipe", None),) + placed[3:6],
        check_vma=False,
    )
```

```python
import jax
import jax.numpy as jnp
from jax import lax
from jax.experimental import pallas as pl
from jax.experimental.pallas import tpu as pltpu
from jax.sharding import PartitionSpec as P

TILE = 8
PASSES = 2
PAIR = 2
COLUMNS = 256
LANES = 128
VMEM_BYTES = 56 * 1024 * 1024


epsilon = 1e-06
bf16 = jnp.bfloat16
f32 = jnp.float32


def dot(former, latter, contract):
    return lax.dot_general(
        former, latter, ((contract[:1], contract[1:]), ((), ())), preferred_element_type=f32
    )


def partner_route(size, step):
    return [(i, i ^ step) for i in range(size)]


def swap(block, axis, step):
    return lax.ppermute(block, axis, partner_route(lax.axis_size(axis), step))


def shifted(block, axis, distance):
    size = lax.axis_size(axis)
    return lax.ppermute(block, axis, [(i, (i + distance) % size) for i in range(size)])


def quarter_of(rows, index, width):
    return lax.dynamic_slice_in_dim(rows, index * width, width, axis=-1)


def to_quarters(rows, dp_count):
    width = rows.shape[-1] // dp_count
    here = lax.axis_index("dp")
    quarters = [quarter_of(rows, here ^ step, width) for step in range(dp_count)]
    return quarters[:1] + [swap(quarters[step], "dp", step) for step in range(1, dp_count)]


def assemble(parts):
    here = lax.axis_index("dp")
    rows, width = parts[0].shape
    whole = jnp.zeros((rows, width * len(parts)), parts[0].dtype)
    for step, part in enumerate(parts):
        whole = lax.dynamic_update_slice_in_dim(whole, part, (here ^ step) * width, axis=1)
    return whole


def from_quarters(parts):
    return assemble(
        [swap(part, "dp", step) if step else part for step, part in enumerate(parts)]
    )


def sum_parts(parts):
    total = parts[0].astype(f32)
    for step in range(1, len(parts)):
        total = total + swap(parts[step], "dp", step).astype(f32)
    return total


def gather_rows(rows, dp_count):
    return [rows] + [swap(rows, "dp", step) for step in range(1, dp_count)]


def after(value, *earlier):
    return lax.optimization_barrier((value,) + earlier)[0]


def columns_of(extent):
    return COLUMNS if extent % COLUMNS == 0 else extent


def kernel_call(body, operands, pieces, landed, out_shape, scratch):
    arrays = []
    for piece in pieces:
        for array, _, _ in piece:
            if not any(array is other for other in arrays):
                arrays.append(array)
    count, fetched, made = len(operands), len(arrays), len(out_shape)

    def call(*refs):
        operand_refs, refs = refs[:count], refs[count:]
        array_refs, refs = refs[:fetched], refs[fetched:]
        out_refs, refs = refs[:made], refs[made:]
        if pieces:
            tiles, arrivals, *refs = refs
        for step, piece in enumerate(pieces):
            for array, source, target in piece:
                (index,) = [i for i, other in enumerate(arrays) if other is array]
                pltpu.make_async_copy(
                    array_refs[index].at[source], tiles.at[(step, *target)], arrivals.at[step]
                ).start()

        def fetch(step):
            pltpu.make_async_copy(tiles.at[step], tiles.at[step], arrivals.at[step]).wait()
            return tiles[step]

        body(operand_refs, fetch, out_refs, refs)

    own_scratch = []
    if pieces:
        own_scratch = [
            pltpu.VMEM((len(pieces), *landed), arrays[0].dtype),
            pltpu.SemaphoreType.DMA((len(pieces),)),
        ]
    return pl.pallas_call(
        call,
        in_specs=[pl.BlockSpec(memory_space=pltpu.VMEM)] * count
        + [pl.BlockSpec(memory_space=pltpu.HBM)] * fetched,
        out_specs=[pl.BlockSpec(memory_space=pltpu.VMEM)] * made,
        out_shape=out_shape,
        scratch_shapes=own_scratch + scratch,
        compiler_params=pltpu.CompilerParams(vmem_limit_bytes=VMEM_BYTES),
        cost_estimate=pl.CostEstimate(flops=0, bytes_accessed=0, transcendentals=0),
    )(*operands, *arrays)


def store_parts(refs, columns, value):
    size = value.shape[0] // len(refs)
    for index, ref in enumerate(refs):
        ref[:, columns] = value[index * size : (index + 1) * size]


def each_tile(fetch, count, product, finish, held):
    def visit(step, carry):
        result = product(fetch(step))

        @pl.when(step % 2 == 0)
        def _():
            held[...] = result

        @pl.when(step % 2 == 1)
        def _():
            finish(step // 2, held[...], result)

        return carry

    lax.fori_loop(0, 2 * count, visit, 0)


def span(tile, size):
    return pl.ds(pl.multiple_of(tile * size, size), size)


def hidden_parts(blocks, gain_part, mask, gate_pair, up_pair):
    rows = sum(block.shape[0] for block in blocks)
    parts_count = lax.axis_size("dp")
    width, units = gate_pair[0].shape
    tile = columns_of(units)

    def body(operand_refs, fetch, out_refs, scratch):
        *block_refs, gain_ref, mask_ref = operand_refs
        *part_refs, gained_ref = out_refs
        start = 0
        for ref in block_refs:
            size = ref.shape[0]
            gained_ref[start : start + size] = (ref[...].astype(f32) * gain_ref[...]).astype(bf16)
            start += size

        def finish(j, own, other):
            part = jnp.where(mask_ref[...] > 0.5, own, other).astype(bf16)
            store_parts(part_refs, span(j, tile), part)

        each_tile(
            fetch,
            2 * units // tile,
            lambda weight: dot(gained_ref[...], weight, (1, 0)),
            finish,
            scratch[0],
        )

    everything = (slice(None), slice(None))
    outs = kernel_call(
        body,
        (*blocks, gain_part, mask),
        [
            [(weight, (slice(None), pl.ds(j * tile, tile)), everything)]
            for pair in (gate_pair, up_pair)
            for j in range(units // tile)
            for weight in pair
        ],
        (width, tile),
        [jax.ShapeDtypeStruct((rows // parts_count, 2 * units), bf16)] * parts_count
        + [jax.ShapeDtypeStruct((rows, width), bf16)],
        [pltpu.VMEM((rows, tile), f32)],
    )
    return outs[:parts_count], outs[parts_count]


def join(joined, refs, columns):
    size = refs[0].shape[0]
    for index, ref in enumerate(refs):
        joined[index * size : (index + 1) * size] = ref[:, columns]


def add_down(blocks, mask, down_pair, hidden, in_parts):
    count = len(blocks)
    part_rows, units = blocks[0].shape
    rows = part_rows * count
    width = down_pair[0].shape[1]
    tile = columns_of(width)
    out_count = count if in_parts else 1

    def body(operand_refs, fetch, out_refs, scratch):
        *block_refs, mask_ref, hidden_ref = operand_refs
        *row_refs, square_ref = out_refs
        joined, held = scratch
        join(joined, block_refs, slice(None))
        square_ref[...] = jnp.zeros_like(square_ref)

        def finish(j, own, other):
            ffn = jnp.where(mask_ref[...] > 0.5, own, other).astype(bf16)
            columns = span(j, tile)
            out = (hidden_ref[:, columns].astype(f32) + ffn.astype(f32)).astype(bf16)
            wide = out.astype(f32)
            square_ref[...] += jnp.sum(wide * wide, axis=-1, keepdims=True)
            store_parts(row_refs, columns, out)

        each_tile(
            fetch, width // tile, lambda weight: dot(joined[...], weight, (1, 0)), finish, held
        )

    everything = (slice(None), slice(None))
    outs = kernel_call(
        body,
        (*blocks, mask, hidden),
        [
            [(weight, (slice(None), pl.ds(j * tile, tile)), everything)]
            for j in range(width // tile)
            for weight in down_pair
        ],
        (units, tile),
        [jax.ShapeDtypeStruct((rows // out_count, width), bf16)] * out_count
        + [jax.ShapeDtypeStruct((rows, 1), f32)],
        [pltpu.VMEM((rows, units), bf16), pltpu.VMEM((rows, tile), f32)],
    )
    return outs[:out_count], outs[out_count]


def act_grad_parts(grad, mask, down_pair):
    parts_count = lax.axis_size("dp")
    rows, width = grad.shape
    units = down_pair[0].shape[0]
    tile = columns_of(units)

    def body(operand_refs, fetch, out_refs, scratch):
        grad_ref, mask_ref = operand_refs

        def finish(j, own, other):
            part = jnp.where(mask_ref[...] > 0.5, own, other).astype(bf16)
            store_parts(out_refs, span(j, tile), part)

        each_tile(
            fetch,
            units // tile,
            lambda weight: dot(grad_ref[...], weight, (1, 1)),
            finish,
            scratch[0],
        )

    everything = (slice(None), slice(None))
    return kernel_call(
        body,
        (grad, mask),
        [
            [(weight, (pl.ds(j * tile, tile), slice(None)), everything)]
            for j in range(units // tile)
            for weight in down_pair
        ],
        (tile, width),
        [jax.ShapeDtypeStruct((rows // parts_count, units), bf16)] * parts_count,
        [pltpu.VMEM((rows, tile), f32)],
    )


def hidden_grads(parts, gate, up, inverse, features):
    rows, units = gate.shape

    def body(operand_refs, fetch, out_refs, _):
        *part_refs, gate_ref, up_ref, inverse_ref = operand_refs
        (out_ref,) = out_refs
        grad_act = part_refs[0][...].astype(f32)
        for ref in part_refs[1:]:
            grad_act = grad_act + ref[...].astype(f32)
        gate_now, up_now, scale = gate_ref[...], up_ref[...], inverse_ref[...]
        sigmoid = 1.0 / (1.0 + jnp.exp(-gate_now))
        scaled = grad_act * scale
        gate_grad = scaled * up_now * sigmoid * (1.0 + gate_now * (1.0 - sigmoid))
        up_grad = scaled * (gate_now * sigmoid)
        shrink = jnp.sum(gate_grad * gate_now + up_grad * up_now, axis=-1, keepdims=True) * (
            scale / features
        )
        out_ref[:, :units] = gate_grad.astype(bf16)
        out_ref[:, units : 2 * units] = up_grad.astype(bf16)
        coarse = shrink.astype(bf16).astype(f32)
        lane = lax.broadcasted_iota(jnp.int32, (rows, LANES), 1)
        out_ref[:, 2 * units :] = jnp.where(
            lane == 0, coarse, jnp.where(lane == 1, shrink - coarse, 0.0)
        ).astype(bf16)

    (sent,) = kernel_call(
        body,
        (*parts, gate, up, inverse),
        [],
        None,
        [jax.ShapeDtypeStruct((rows, 2 * units + LANES), bf16)],
        [],
    )
    return sent


def input_grad(blocks, mask, gate_pair, up_pair, grad, hidden, gain_part, in_parts):
    count = len(blocks)
    part_rows = blocks[0].shape[0]
    rows = part_rows * count
    width, units = gate_pair[0].shape
    tile = columns_of(width)
    out_count = count if in_parts else 1

    def body(operand_refs, fetch, out_refs, scratch):
        *block_refs, mask_ref, grad_ref, hidden_ref, gain_ref = operand_refs
        *row_refs, sum_ref = out_refs
        joined, shrink, held = scratch
        join(joined, block_refs, slice(0, 2 * units))
        for index, ref in enumerate(block_refs):
            tail = ref[:, 2 * units :].astype(f32)
            shrink[index * part_rows : (index + 1) * part_rows] = jnp.sum(
                tail, axis=-1, keepdims=True
            )

        def finish(j, own, other):
            columns = span(j, tile)
            back = jnp.where(mask_ref[...] > 0.5, own, other)
            wide = hidden_ref[:, columns].astype(f32)
            sum_ref[:, columns] = jnp.sum(back * wide, axis=0, keepdims=True)
            out = (
                grad_ref[:, columns].astype(f32)
                + back * gain_ref[:, columns]
                - wide * shrink[...]
            ).astype(bf16)
            store_parts(row_refs, columns, out)

        each_tile(
            fetch, width // tile, lambda weight: dot(joined[...], weight, (1, 1)), finish, held
        )

    outs = kernel_call(
        body,
        (*blocks, mask, grad, hidden, gain_part),
        [
            [
                (pair[which], (pl.ds(j * tile, tile), slice(None)), (slice(None), pl.ds(at, units)))
                for pair, at in ((gate_pair, 0), (up_pair, units))
            ]
            for j in range(width // tile)
            for which in range(2)
        ],
        (tile, 2 * units),
        [jax.ShapeDtypeStruct((rows // out_count, width), bf16)] * out_count
        + [jax.ShapeDtypeStruct((1, width), f32)],
        [
            pltpu.VMEM((rows, 2 * units), bf16),
            pltpu.VMEM((rows, 1), f32),
            pltpu.VMEM((rows, tile), f32),
        ],
    )
    return outs[:out_count], outs[out_count]


def body(tokens, cotangent, gain, w_gate, w_up, w_down, route):
    pipe_count = lax.axis_size("pipe")
    dp_count = lax.axis_size("dp")
    section = lax.axis_index("pipe")
    expert = lax.axis_index("expert")
    here = lax.axis_index("dp")
    features = tokens.shape[-1]
    width = features // dp_count
    units = w_gate.shape[-1]
    gain_part = lax.dynamic_slice_in_dim(gain, here * width, width, axis=1)

    own_tokens = tokens[0]
    blocks = to_quarters(own_tokens, dp_count)
    gate_pair, up_pair, down_pair = (
        (weight[0, 0], swap(weight[0, 0], "expert", 1)) for weight in (w_gate, w_up, w_down)
    )
    micro = [(section - k + pipe_count) % pipe_count for k in range(PASSES)]
    route_rows = jnp.stack(
        [lax.dynamic_index_in_dim(route[0, :, :, 0], m, 0, keepdims=False) for m in micro], axis=1
    )
    route_all = jnp.concatenate(gather_rows(after(route_rows, blocks[1]), dp_count))
    masks = [
        jnp.repeat((route_all[:, k] == expert).astype(f32), TILE)[:, None] for k in range(PASSES)
    ]

    def scale_of(square_sum):
        return lax.rsqrt(square_sum / features + epsilon)

    def weight_grad(left, right, mask, wanted):
        return dot(left, jnp.where((mask > 0.5) == wanted, right, jnp.zeros_like(right)), (0, 0))

    wide = own_tokens.astype(f32)
    inverse = scale_of(jnp.sum(wide * wide, axis=-1, keepdims=True))
    kept = []

    def cotangent_quarter(step):
        return quarter_of(after(cotangent[0], *blocks), here ^ step, width)

    for k in range(PASSES):
        mask = masks[k]
        parts, gained = hidden_parts(blocks, gain_part, mask, gate_pair, up_pair)
        if k == 0:
            grad_blocks = [cotangent_quarter(0)] + [
                swap(cotangent_quarter(step), "dp", step) for step in range(1, dp_count - 1)
            ]
            parts = lax.optimization_barrier((*parts, *grad_blocks))[:dp_count]
        total = sum_parts(parts) * inverse
        gate, up = total[:, :units], total[:, units:]
        activated = (gate * jax.nn.sigmoid(gate) * up).astype(bf16)
        hidden = jnp.concatenate(blocks)
        kept.append((hidden, gained, inverse, gate, up))
        if k + 1 < PASSES:
            first_activated = gather_rows(activated, dp_count)
            (next_hidden,), squares = add_down(first_activated, mask, down_pair, hidden, False)
            blocks = [shifted(next_hidden, "pipe", 1)]
            last = quarter_of(after(cotangent[0], squares), here ^ (dp_count - 1), width)
            grad = jnp.concatenate(grad_blocks + [swap(last, "dp", dp_count - 1)])
            squares = sum_parts(jnp.split(squares, dp_count))
            inverse = shifted(scale_of(squares), "pipe", 1)
            act_parts = act_grad_parts(grad, masks[1], down_pair)
            act_parts = [act_parts[0]] + [
                swap(act_parts[step], "dp", step) for step in range(1, dp_count)
            ]
            blocks[0] = after(blocks[0], *act_parts[1:])

    gain_sum = jnp.zeros((1, width), f32)
    for k in reversed(range(PASSES)):
        hidden, gained, inverse, gate, up = kept[k]
        mask = masks[k]
        sent = hidden_grads(act_parts, gate, up, inverse, features)
        both_grad = gather_rows(sent, dp_count)
        if k == 0:
            late_down = jnp.concatenate(first_activated)
            other_down = swap(
                (weight_grad(late_down, grad, mask, False) + early[False][2].astype(f32)).astype(
                    bf16
                ),
                "expert",
                1,
            )
            down_grad = (
                weight_grad(late_down, grad, mask, True)
                + early[True][2].astype(f32)
                + other_down.astype(f32)
            ).astype(bf16)
            both_grad[1] = after(both_grad[1], down_grad)
        outs, gain_term = input_grad(
            both_grad, mask, gate_pair, up_pair, grad, hidden, gain_part, k == 0
        )
        gain_sum = gain_sum + gain_term
        joined = jnp.concatenate(both_grad)
        rights = [joined[:, :units], joined[:, units : 2 * units]]
        if k > 0:
            last_grad = grad
            grad = shifted(outs[0], "pipe", -1)
            rights[0] = after(rights[0], outs[0])
            first = weight_grad(gained, rights[0], mask, False).astype(bf16)
            last_activated = gather_rows(after(activated, first), dp_count)
            early = {
                False: [first, weight_grad(gained, rights[1], mask, False).astype(bf16)],
                True: [weight_grad(gained, right, mask, True).astype(bf16) for right in rights],
            }
            out_parts, _ = add_down(last_activated, mask, down_pair, hidden, True)
            out_rows = from_quarters(out_parts)
            grad = after(grad, out_rows, *early[False], *early[True])
            act_parts = act_grad_parts(grad, masks[0], down_pair)
            last_activated = jnp.concatenate(last_activated)
            for wanted in (False, True):
                early[wanted].append(
                    weight_grad(last_activated, last_grad, mask, wanted).astype(bf16)
                )
            act_parts = [act_parts[0]] + [
                swap(act_parts[step], "dp", step) for step in range(1, dp_count)
            ]
            act_parts[1] = after(act_parts[1], early[False][2], early[True][2])

    returned = [outs[0]] + [swap(outs[step], "dp", step) for step in range(1, dp_count)]
    rights = [after(right, outs[0]) for right in rights]
    received = [
        swap((weight_grad(gained, right, mask, False) + soon.astype(f32)).astype(bf16), "expert", 1)
        for right, soon in zip(rights, early[False])
    ]
    gain_rows = jnp.concatenate(gather_rows(after(gain_sum, received[0]), dp_count))
    gain_rows = gain_rows + swap(gain_rows, "expert", 1)
    gain_all = jnp.zeros((features,), f32)
    for step in range(dp_count):
        gain_all = lax.dynamic_update_slice_in_dim(
            gain_all, gain_rows[step], (here ^ step) * width, axis=0
        )
    grads = [
        (
            weight_grad(gained, right, mask, True) + soon.astype(f32) + other.astype(f32)
        ).astype(bf16)
        for right, soon, other in zip(rights, early[True], received)
    ] + [down_grad]
    returned = list(lax.optimization_barrier((*returned, *grads)))[:dp_count]
    entry = assemble(returned)
    return (
        out_rows[None],
        entry[None],
        gain_all[None],
        grads[0][None, None],
        grads[1][None, None],
        grads[2][None, None],
    )


def start_shifted(block, axis, distance):
    devices = range(lax.axis_size(axis))
    route = [((i - distance) % len(devices), i) for i in devices]
    return lax.ppermute(block, axis, route)


def start_contract_last(former, latter):
    return lax.dot_general(
        former, latter, (((1,), (1,)), ((), ())), preferred_element_type=jnp.float32
    )


def start_contract_first(former, latter):
    return lax.dot_general(
        former, latter, (((0,), (0,)), ((), ())), preferred_element_type=jnp.float32
    )


def start_normalize(hidden, gain_row):
    widened = hidden.astype(jnp.float32)
    inverse = lax.rsqrt(jnp.mean(widened * widened, axis=-1, keepdims=True) + epsilon)
    scaled = widened * inverse
    return ((scaled * gain_row).astype(jnp.bfloat16), scaled, inverse)


def start_slot_matrix(route_now, expert_count, capacity):
    tile_count = route_now.shape[0]
    expert_ids = jnp.arange(expert_count, dtype=jnp.int32)
    member = (route_now[None, :] == expert_ids[:, None]).astype(jnp.int32)
    earlier = jnp.cumsum(member, axis=1) - member
    rank_ids = jnp.arange(capacity, dtype=jnp.int32)
    placed = member[:, None, :] * (earlier[:, None, :] == rank_ids[None, :, None]).astype(jnp.int32)
    return placed.reshape(expert_count * capacity, tile_count)


def start_into_slots(placed, rows, tile_rows, dp_count):
    width = rows.shape[-1]
    tile_blocks = rows.reshape(placed.shape[1], tile_rows, dp_count, width // dp_count)
    return jnp.einsum(
        "st,trqd->qsrd",
        placed.astype(jnp.bfloat16),
        tile_blocks,
        preferred_element_type=jnp.float32,
    ).astype(jnp.bfloat16)


def start_from_slots(placed, slot_rows):
    merged = jnp.einsum(
        "st,qsrd->trqd", placed.astype(jnp.bfloat16), slot_rows, preferred_element_type=jnp.float32
    ).astype(jnp.bfloat16)
    return merged.reshape(merged.shape[0] * merged.shape[1], -1)


def start_send_out(slot_rows):
    quarter = slot_rows.shape[-1]
    flat = slot_rows.reshape((-1,) + slot_rows.shape[2:])
    arrived = lax.all_to_all(flat, ("dp", "expert"), split_axis=0, concat_axis=0, tiled=True)
    return arrived.reshape(-1, quarter)


def start_send_back(part_rows, dp_count, tile_rows):
    quarter = part_rows.shape[-1]
    flat = part_rows.reshape(-1, tile_rows, quarter)
    returned = lax.all_to_all(flat, ("dp", "expert"), split_axis=0, concat_axis=0, tiled=True)
    return returned.reshape(dp_count, -1, tile_rows, quarter)


def start_widen_rounded(values):
    return lax.optimization_barrier(values.astype(jnp.bfloat16)).astype(jnp.float32)


def start_expert_forward(received, gate_weight, up_weight, down_weight):
    gate_terms = start_widen_rounded(jnp.dot(received, gate_weight, preferred_element_type=jnp.float32))
    up_terms = start_widen_rounded(jnp.dot(received, up_weight, preferred_element_type=jnp.float32))
    gate_pre, up_pre = (
        lax.psum(gate_terms.astype(jnp.bfloat16), "dp").astype(jnp.float32),
        lax.psum(up_terms.astype(jnp.bfloat16), "dp").astype(jnp.float32),
    )
    activated = (jax.nn.silu(gate_pre) * up_pre).astype(jnp.bfloat16)
    part_rows = jnp.dot(activated, down_weight, preferred_element_type=jnp.float32).astype(
        jnp.bfloat16
    )
    return (part_rows, (gate_pre, up_pre, activated))


def start_expert_backward(
    received, grad_recv, kept_state, gate_weight, up_weight, down_weight, grad_sums
):
    gate_pre, up_pre, activated = kept_state
    grad_terms = start_widen_rounded(start_contract_last(grad_recv, down_weight))
    grad_act = lax.psum(grad_terms.astype(jnp.bfloat16), "dp").astype(jnp.float32)
    sigmoid_gate = jax.nn.sigmoid(gate_pre)
    silu_gate = gate_pre * sigmoid_gate
    grad_gate_pre = (
        grad_act * up_pre * sigmoid_gate * (1.0 + gate_pre * (1.0 - sigmoid_gate))
    ).astype(jnp.bfloat16)
    grad_up_pre = (grad_act * silu_gate).astype(jnp.bfloat16)
    back_rows = (
        start_contract_last(grad_gate_pre, gate_weight) + start_contract_last(grad_up_pre, up_weight)
    ).astype(jnp.bfloat16)
    grad_gate = grad_sums[0] + start_contract_first(received, grad_gate_pre)
    grad_up = grad_sums[1] + start_contract_first(received, grad_up_pre)
    grad_down = grad_sums[2] + start_contract_first(activated, grad_recv)
    return (back_rows, (grad_gate, grad_up, grad_down))


def start_body(tokens, cotangent, gain, w_gate, w_up, w_down, route):
    pipe_count = lax.axis_size("pipe")
    dp_count = lax.axis_size("dp")
    expert_count = lax.axis_size("expert")
    section_index = lax.axis_index("pipe")
    gain_row = gain[0]
    gate_weight = w_gate[0, 0]
    up_weight = w_up[0, 0]
    down_weight = w_down[0, 0]
    route_table = route[0, :, :, 0]
    tile_count = route_table.shape[1]
    capacity = max(2, 3 * tile_count // (2 * expert_count))
    hidden = tokens[0]
    saved_ticks = []
    out_rows = hidden
    for pass_index in range(PASSES):
        micro_index = (section_index - pass_index + pipe_count) % pipe_count
        route_now = lax.dynamic_index_in_dim(route_table, micro_index, 0, keepdims=False)
        placed = start_slot_matrix(route_now, expert_count, capacity)
        normed, scaled, inverse = start_normalize(hidden, gain_row)
        received = start_send_out(start_into_slots(placed, normed, TILE, dp_count))
        part_rows, kept_state = start_expert_forward(received, gate_weight, up_weight, down_weight)
        ffn_rows = start_from_slots(placed, start_send_back(part_rows, dp_count, TILE))
        new_hidden = (hidden.astype(jnp.float32) + ffn_rows.astype(jnp.float32)).astype(
            jnp.bfloat16
        )
        saved_ticks.append((placed, scaled, inverse, received, kept_state))
        if pass_index + 1 < PASSES:
            hidden = start_shifted(new_hidden, "pipe", 1)
        else:
            out_rows = new_hidden
    grad_rows = cotangent[0]
    grad_sums = (
        jnp.zeros(gate_weight.shape, jnp.float32),
        jnp.zeros(up_weight.shape, jnp.float32),
        jnp.zeros(down_weight.shape, jnp.float32),
    )
    gain_sum = jnp.zeros(gain_row.shape, jnp.float32)
    entry_grad = grad_rows
    for pass_index in reversed(range(PASSES)):
        placed, scaled, inverse, received, kept_state = saved_ticks[pass_index]
        grad_recv = start_send_out(start_into_slots(placed, grad_rows, TILE, dp_count))
        back_rows, grad_sums = start_expert_backward(
            received, grad_recv, kept_state, gate_weight, up_weight, down_weight, grad_sums
        )
        grad_normed = start_from_slots(placed, start_send_back(back_rows, dp_count, TILE)).astype(jnp.float32)
        gain_sum = gain_sum + jnp.sum(grad_normed * scaled, axis=0)
        grad_scaled = grad_normed * gain_row
        grad_wide = inverse * (
            grad_scaled - scaled * jnp.mean(grad_scaled * scaled, axis=-1, keepdims=True)
        )
        grad_in = (grad_rows.astype(jnp.float32) + grad_wide).astype(jnp.bfloat16)
        if pass_index > 0:
            grad_rows = start_shifted(grad_in, "pipe", -1)
        else:
            entry_grad = grad_in
    gain_total = lax.psum(gain_sum, ("dp", "expert"))
    return (
        out_rows[None],
        entry_grad[None],
        gain_total[None],
        grad_sums[0].astype(jnp.bfloat16)[None, None],
        grad_sums[1].astype(jnp.bfloat16)[None, None],
        grad_sums[2].astype(jnp.bfloat16)[None, None],
    )


def start_solution(mesh):
    placed = (
        P("pipe", ("dp", "expert"), None),
        P("pipe", ("dp", "expert"), None),
        P("pipe", None),
        P("pipe", "expert", "dp", None),
        P("pipe", "expert", "dp", None),
        P("pipe", "expert", None, "dp"),
        P("pipe", None, ("dp", "expert"), None),
    )
    return jax.shard_map(
        start_body,
        mesh=mesh,
        in_specs=placed,
        out_specs=(
            P("pipe", ("dp", "expert"), None),
            P("pipe", ("dp", "expert"), None),
            P("pipe", None),
            P("pipe", "expert", "dp", None),
            P("pipe", "expert", "dp", None),
            P("pipe", "expert", None, "dp"),
        ),
        check_vma=False,
    )


def solution(mesh):
    if mesh.shape["expert"] != PAIR:
        return start_solution(mesh)
    placed = (
        P("pipe", ("dp", "expert"), None),
        P("pipe", ("dp", "expert"), None),
        P("pipe", None),
        P("pipe", "expert", "dp", None),
        P("pipe", "expert", "dp", None),
        P("pipe", "expert", None, "dp"),
        P("pipe", None, ("dp", "expert"), None),
    )
    return jax.shard_map(
        body,
        mesh=mesh,
        in_specs=placed,
        out_specs=placed[:2] + (P("pipe", None),) + placed[3:6],
        check_vma=False,
    )
```

```python
import jax
import jax.numpy as jnp
from jax import lax
from jax.experimental import pallas as pl
from jax.experimental.pallas import tpu as pltpu
from jax.sharding import PartitionSpec as P

TILE = 8
PASSES = 2
PAIR = 2
COLUMNS = 256
LANES = 128
VMEM_BYTES = 24 * 1024 * 1024


epsilon = 1e-06
bf16 = jnp.bfloat16
f32 = jnp.float32


def dot(former, latter, contract):
    return lax.dot_general(
        former, latter, ((contract[:1], contract[1:]), ((), ())), preferred_element_type=f32
    )


def partner_route(size, step):
    return [(i, i ^ step) for i in range(size)]


def swap(block, axis, step):
    return lax.ppermute(block, axis, partner_route(lax.axis_size(axis), step))


def shifted(block, axis, distance):
    size = lax.axis_size(axis)
    return lax.ppermute(block, axis, [(i, (i + distance) % size) for i in range(size)])


def quarter_of(rows, index, width):
    return lax.dynamic_slice_in_dim(rows, index * width, width, axis=-1)


def to_quarters(rows, dp_count):
    width = rows.shape[-1] // dp_count
    here = lax.axis_index("dp")
    quarters = [quarter_of(rows, here ^ step, width) for step in range(dp_count)]
    return quarters[:1] + [swap(quarters[step], "dp", step) for step in range(1, dp_count)]


def assemble(parts):
    here = lax.axis_index("dp")
    rows, width = parts[0].shape
    whole = jnp.zeros((rows, width * len(parts)), parts[0].dtype)
    for step, part in enumerate(parts):
        whole = lax.dynamic_update_slice_in_dim(whole, part, (here ^ step) * width, axis=1)
    return whole


def from_quarters(parts):
    return assemble(
        [swap(part, "dp", step) if step else part for step, part in enumerate(parts)]
    )


def sum_parts(parts):
    total = parts[0].astype(f32)
    for step in range(1, len(parts)):
        total = total + swap(parts[step], "dp", step).astype(f32)
    return total


def gather_rows(rows, dp_count):
    return [rows] + [swap(rows, "dp", step) for step in range(1, dp_count)]


def after(value, *earlier):
    return lax.optimization_barrier((value,) + earlier)[0]


def columns_of(extent):
    return COLUMNS if extent % COLUMNS == 0 else extent


def kernel_call(body, operands, weights, out_shape, scratch):
    count, kept, made = len(operands), len(weights), len(out_shape)

    def call(*refs):
        operand_refs, refs = refs[:count], refs[count:]
        weight_refs, refs = refs[:kept], refs[kept:]
        body(operand_refs, weight_refs, refs[:made], refs[made:])

    in_vmem = pl.BlockSpec(memory_space=pltpu.VMEM)
    return pl.pallas_call(
        call,
        in_specs=[in_vmem] * (count + kept),
        out_specs=[in_vmem] * made,
        out_shape=out_shape,
        scratch_shapes=scratch,
        compiler_params=pltpu.CompilerParams(vmem_limit_bytes=VMEM_BYTES),
        cost_estimate=pl.CostEstimate(flops=0, bytes_accessed=0, transcendentals=0),
    )(*operands, *weights)


def resident(arrays):
    count = len(arrays)

    def call(*refs):
        arrivals = refs[-1]
        copies = [
            pltpu.make_async_copy(refs[i], refs[count + i], arrivals.at[i]) for i in range(count)
        ]
        for copy in copies:
            copy.start()
        for copy in copies:
            copy.wait()

    return pl.pallas_call(
        call,
        in_specs=[pl.BlockSpec(memory_space=pltpu.HBM)] * count,
        out_specs=[pl.BlockSpec(memory_space=pltpu.VMEM)] * count,
        out_shape=[pltpu.VMEM(a.shape, a.dtype) for a in arrays],
        scratch_shapes=[pltpu.SemaphoreType.DMA((count,))],
        compiler_params=pltpu.CompilerParams(vmem_limit_bytes=VMEM_BYTES),
        cost_estimate=pl.CostEstimate(flops=0, bytes_accessed=0, transcendentals=0),
    )(*arrays)


def store_parts(refs, columns, value):
    size = value.shape[0] // len(refs)
    for index, ref in enumerate(refs):
        ref[:, columns] = value[index * size : (index + 1) * size]


def each_tile(extent, visit):
    tile = columns_of(extent)

    def step(j, carry):
        visit(span(j, tile))
        return carry

    lax.fori_loop(0, extent // tile, step, 0)


def span(tile, size):
    return pl.ds(pl.multiple_of(tile * size, size), size)


def hidden_parts(blocks, gain_part, mask, gate_pair, up_pair):
    rows = sum(block.shape[0] for block in blocks)
    parts_count = lax.axis_size("dp")
    width, units = gate_pair[0].shape

    def body(operand_refs, weight_refs, out_refs, scratch):
        *block_refs, gain_ref, mask_ref = operand_refs
        *part_refs, gained_ref = out_refs
        start = 0
        for ref in block_refs:
            size = ref.shape[0]
            gained_ref[start : start + size] = (ref[...].astype(f32) * gain_ref[...]).astype(bf16)
            start += size

        for pair in range(2):

            def visit(columns, pair=pair):
                own, other = weight_refs[2 * pair : 2 * pair + 2]
                part = jnp.where(
                    mask_ref[...] > 0.5,
                    dot(gained_ref[...], own[:, columns], (1, 0)),
                    dot(gained_ref[...], other[:, columns], (1, 0)),
                ).astype(bf16)
                store_parts([ref.at[:, pair * units :] for ref in part_refs], columns, part)

            each_tile(units, visit)

    outs = kernel_call(
        body,
        (*blocks, gain_part, mask),
        (*gate_pair, *up_pair),
        [jax.ShapeDtypeStruct((rows // parts_count, 2 * units), bf16)] * parts_count
        + [jax.ShapeDtypeStruct((rows, width), bf16)],
        [],
    )
    return outs[:parts_count], outs[parts_count]


def join(joined, refs, columns):
    size = refs[0].shape[0]
    for index, ref in enumerate(refs):
        joined[index * size : (index + 1) * size] = ref[:, columns]


def add_down(blocks, mask, down_pair, hidden, in_parts):
    count = len(blocks)
    part_rows, units = blocks[0].shape
    rows = part_rows * count
    width = down_pair[0].shape[1]
    out_count = count if in_parts else 1

    def body(operand_refs, weight_refs, out_refs, scratch):
        *block_refs, mask_ref, hidden_ref = operand_refs
        *row_refs, square_ref = out_refs
        (joined,) = scratch
        join(joined, block_refs, slice(None))
        square_ref[...] = jnp.zeros_like(square_ref)

        own, other = weight_refs

        def visit(columns):
            ffn = jnp.where(
                mask_ref[...] > 0.5,
                dot(joined[...], own[:, columns], (1, 0)),
                dot(joined[...], other[:, columns], (1, 0)),
            ).astype(bf16)
            out = (hidden_ref[:, columns].astype(f32) + ffn.astype(f32)).astype(bf16)
            wide = out.astype(f32)
            square_ref[...] += jnp.sum(wide * wide, axis=-1, keepdims=True)
            store_parts(row_refs, columns, out)

        each_tile(width, visit)

    outs = kernel_call(
        body,
        (*blocks, mask, hidden),
        down_pair,
        [jax.ShapeDtypeStruct((rows // out_count, width), bf16)] * out_count
        + [jax.ShapeDtypeStruct((rows, 1), f32)],
        [pltpu.VMEM((rows, units), bf16)],
    )
    return outs[:out_count], outs[out_count]


def act_grad_parts(grad, mask, down_pair):
    parts_count = lax.axis_size("dp")
    rows, width = grad.shape
    units = down_pair[0].shape[0]

    def body(operand_refs, weight_refs, out_refs, scratch):
        grad_ref, mask_ref = operand_refs

        own, other = weight_refs

        def visit(columns):
            part = jnp.where(
                mask_ref[...] > 0.5,
                dot(grad_ref[...], own[columns], (1, 1)),
                dot(grad_ref[...], other[columns], (1, 1)),
            ).astype(bf16)
            store_parts(out_refs, columns, part)

        each_tile(units, visit)

    return kernel_call(
        body,
        (grad, mask),
        down_pair,
        [jax.ShapeDtypeStruct((rows // parts_count, units), bf16)] * parts_count,
        [],
    )


def hidden_grads(parts, gate, up, inverse, features):
    rows, units = gate.shape

    def body(operand_refs, weight_refs, out_refs, scratch):
        *part_refs, gate_ref, up_ref, inverse_ref = operand_refs
        (out_ref,) = out_refs
        grad_act = part_refs[0][...].astype(f32)
        for ref in part_refs[1:]:
            grad_act = grad_act + ref[...].astype(f32)
        gate_now, up_now, scale = gate_ref[...], up_ref[...], inverse_ref[...]
        sigmoid = 1.0 / (1.0 + jnp.exp(-gate_now))
        scaled = grad_act * scale
        gate_grad = scaled * up_now * sigmoid * (1.0 + gate_now * (1.0 - sigmoid))
        up_grad = scaled * (gate_now * sigmoid)
        shrink = jnp.sum(gate_grad * gate_now + up_grad * up_now, axis=-1, keepdims=True) * (
            scale / features
        )
        out_ref[:, :units] = gate_grad.astype(bf16)
        out_ref[:, units : 2 * units] = up_grad.astype(bf16)
        coarse = shrink.astype(bf16).astype(f32)
        lane = lax.broadcasted_iota(jnp.int32, (rows, LANES), 1)
        out_ref[:, 2 * units :] = jnp.where(
            lane == 0, coarse, jnp.where(lane == 1, shrink - coarse, 0.0)
        ).astype(bf16)

    (sent,) = kernel_call(
        body,
        (*parts, gate, up, inverse),
        [],
        [jax.ShapeDtypeStruct((rows, 2 * units + LANES), bf16)],
        [],
    )
    return sent


def input_grad(blocks, mask, gate_pair, up_pair, grad, hidden, gain_part, in_parts):
    count = len(blocks)
    part_rows = blocks[0].shape[0]
    rows = part_rows * count
    width, units = gate_pair[0].shape
    out_count = count if in_parts else 1

    def body(operand_refs, weight_refs, out_refs, scratch):
        *block_refs, mask_ref, grad_ref, hidden_ref, gain_ref = operand_refs
        *row_refs, sum_ref = out_refs
        joined, shrink = scratch
        join(joined, block_refs, slice(0, 2 * units))
        for index, ref in enumerate(block_refs):
            tail = ref[:, 2 * units :].astype(f32)
            shrink[index * part_rows : (index + 1) * part_rows] = jnp.sum(
                tail, axis=-1, keepdims=True
            )

        gate_own, gate_other, up_own, up_other = weight_refs

        def visit(columns):
            def back_of(gate, up):
                return dot(joined[:, :units], gate[columns], (1, 1)) + dot(
                    joined[:, units:], up[columns], (1, 1)
                )

            back = jnp.where(
                mask_ref[...] > 0.5, back_of(gate_own, up_own), back_of(gate_other, up_other)
            )
            wide = hidden_ref[:, columns].astype(f32)
            sum_ref[:, columns] = jnp.sum(back * wide, axis=0, keepdims=True)
            out = (
                grad_ref[:, columns].astype(f32)
                + back * gain_ref[:, columns]
                - wide * shrink[...]
            ).astype(bf16)
            store_parts(row_refs, columns, out)

        each_tile(width, visit)

    outs = kernel_call(
        body,
        (*blocks, mask, grad, hidden, gain_part),
        (*gate_pair, *up_pair),
        [jax.ShapeDtypeStruct((rows // out_count, width), bf16)] * out_count
        + [jax.ShapeDtypeStruct((1, width), f32)],
        [
            pltpu.VMEM((rows, 2 * units), bf16),
            pltpu.VMEM((rows, 1), f32),
        ],
    )
    return outs[:out_count], outs[out_count]


def body(tokens, cotangent, gain, w_gate, w_up, w_down, route):
    pipe_count = lax.axis_size("pipe")
    dp_count = lax.axis_size("dp")
    section = lax.axis_index("pipe")
    expert = lax.axis_index("expert")
    here = lax.axis_index("dp")
    features = tokens.shape[-1]
    width = features // dp_count
    units = w_gate.shape[-1]
    gain_part = lax.dynamic_slice_in_dim(gain, here * width, width, axis=1)

    own_tokens = tokens[0]
    blocks = to_quarters(own_tokens, dp_count)
    gate_pair, up_pair, down_pair = (
        (weight[0, 0], swap(weight[0, 0], "expert", 1)) for weight in (w_gate, w_up, w_down)
    )
    weights = resident([*gate_pair, *up_pair, *down_pair])
    gate_pair, up_pair, down_pair = weights[:2], weights[2:4], weights[4:]
    micro = [(section - k + pipe_count) % pipe_count for k in range(PASSES)]
    route_rows = jnp.stack(
        [lax.dynamic_index_in_dim(route[0, :, :, 0], m, 0, keepdims=False) for m in micro], axis=1
    )
    route_all = jnp.concatenate(gather_rows(after(route_rows, blocks[1]), dp_count))
    masks = [
        jnp.repeat((route_all[:, k] == expert).astype(f32), TILE)[:, None] for k in range(PASSES)
    ]

    def scale_of(square_sum):
        return lax.rsqrt(square_sum / features + epsilon)

    def weight_grad(left, right, mask, wanted):
        return dot(left, jnp.where((mask > 0.5) == wanted, right, jnp.zeros_like(right)), (0, 0))

    wide = own_tokens.astype(f32)
    inverse = scale_of(jnp.sum(wide * wide, axis=-1, keepdims=True))
    kept = []

    def cotangent_quarter(step):
        return quarter_of(after(cotangent[0], *blocks), here ^ step, width)

    for k in range(PASSES):
        mask = masks[k]
        parts, gained = hidden_parts(blocks, gain_part, mask, gate_pair, up_pair)
        if k == 0:
            grad_blocks = [cotangent_quarter(0)] + [
                swap(cotangent_quarter(step), "dp", step) for step in range(1, dp_count - 1)
            ]
            parts = lax.optimization_barrier((*parts, *grad_blocks))[:dp_count]
        total = sum_parts(parts) * inverse
        gate, up = total[:, :units], total[:, units:]
        activated = (gate * jax.nn.sigmoid(gate) * up).astype(bf16)
        hidden = jnp.concatenate(blocks)
        kept.append((hidden, gained, inverse, gate, up))
        if k + 1 < PASSES:
            first_activated = gather_rows(activated, dp_count)
            (next_hidden,), squares = add_down(first_activated, mask, down_pair, hidden, False)
            blocks = [shifted(next_hidden, "pipe", 1)]
            last = quarter_of(after(cotangent[0], squares), here ^ (dp_count - 1), width)
            grad = jnp.concatenate(grad_blocks + [swap(last, "dp", dp_count - 1)])
            squares = sum_parts(jnp.split(squares, dp_count))
            inverse = shifted(scale_of(squares), "pipe", 1)
            act_parts = act_grad_parts(grad, masks[1], down_pair)
            act_parts = [act_parts[0]] + [
                swap(act_parts[step], "dp", step) for step in range(1, dp_count)
            ]
            blocks[0] = after(blocks[0], *act_parts[1:])

    gain_sum = jnp.zeros((1, width), f32)
    for k in reversed(range(PASSES)):
        hidden, gained, inverse, gate, up = kept[k]
        mask = masks[k]
        sent = hidden_grads(act_parts, gate, up, inverse, features)
        both_grad = gather_rows(sent, dp_count)
        if k == 0:
            late_down = jnp.concatenate(first_activated)
            other_down = swap(
                (weight_grad(late_down, grad, mask, False) + early[False][2].astype(f32)).astype(
                    bf16
                ),
                "expert",
                1,
            )
            down_grad = (
                weight_grad(late_down, grad, mask, True)
                + early[True][2].astype(f32)
                + other_down.astype(f32)
            ).astype(bf16)
            both_grad[1] = after(both_grad[1], down_grad)
        outs, gain_term = input_grad(
            both_grad, mask, gate_pair, up_pair, grad, hidden, gain_part, k == 0
        )
        gain_sum = gain_sum + gain_term
        joined = jnp.concatenate(both_grad)
        rights = [joined[:, :units], joined[:, units : 2 * units]]
        if k > 0:
            last_grad = grad
            grad = shifted(outs[0], "pipe", -1)
            rights[0] = after(rights[0], outs[0])
            first = weight_grad(gained, rights[0], mask, False).astype(bf16)
            last_activated = gather_rows(after(activated, first), dp_count)
            early = {
                False: [first, weight_grad(gained, rights[1], mask, False).astype(bf16)],
                True: [weight_grad(gained, right, mask, True).astype(bf16) for right in rights],
            }
            out_parts, _ = add_down(last_activated, mask, down_pair, hidden, True)
            out_rows = from_quarters(out_parts)
            grad = after(grad, out_rows, *early[False], *early[True])
            act_parts = act_grad_parts(grad, masks[0], down_pair)
            last_activated = jnp.concatenate(last_activated)
            for wanted in (False, True):
                early[wanted].append(
                    weight_grad(last_activated, last_grad, mask, wanted).astype(bf16)
                )
            act_parts = [act_parts[0]] + [
                swap(act_parts[step], "dp", step) for step in range(1, dp_count)
            ]
            act_parts[1] = after(act_parts[1], early[False][2], early[True][2])

    returned = [outs[0]] + [swap(outs[step], "dp", step) for step in range(1, dp_count)]
    rights = [after(right, outs[0]) for right in rights]
    received = [
        swap((weight_grad(gained, right, mask, False) + soon.astype(f32)).astype(bf16), "expert", 1)
        for right, soon in zip(rights, early[False])
    ]
    gain_rows = jnp.concatenate(gather_rows(after(gain_sum, received[0]), dp_count))
    gain_rows = gain_rows + swap(gain_rows, "expert", 1)
    gain_all = jnp.zeros((features,), f32)
    for step in range(dp_count):
        gain_all = lax.dynamic_update_slice_in_dim(
            gain_all, gain_rows[step], (here ^ step) * width, axis=0
        )
    grads = [
        (
            weight_grad(gained, right, mask, True) + soon.astype(f32) + other.astype(f32)
        ).astype(bf16)
        for right, soon, other in zip(rights, early[True], received)
    ] + [down_grad]
    returned = list(lax.optimization_barrier((*returned, *grads)))[:dp_count]
    entry = assemble(returned)
    return (
        out_rows[None],
        entry[None],
        gain_all[None],
        grads[0][None, None],
        grads[1][None, None],
        grads[2][None, None],
    )


def start_shifted(block, axis, distance):
    devices = range(lax.axis_size(axis))
    route = [((i - distance) % len(devices), i) for i in devices]
    return lax.ppermute(block, axis, route)


def start_contract_last(former, latter):
    return lax.dot_general(
        former, latter, (((1,), (1,)), ((), ())), preferred_element_type=jnp.float32
    )


def start_contract_first(former, latter):
    return lax.dot_general(
        former, latter, (((0,), (0,)), ((), ())), preferred_element_type=jnp.float32
    )


def start_normalize(hidden, gain_row):
    widened = hidden.astype(jnp.float32)
    inverse = lax.rsqrt(jnp.mean(widened * widened, axis=-1, keepdims=True) + epsilon)
    scaled = widened * inverse
    return ((scaled * gain_row).astype(jnp.bfloat16), scaled, inverse)


def start_slot_matrix(route_now, expert_count, capacity):
    tile_count = route_now.shape[0]
    expert_ids = jnp.arange(expert_count, dtype=jnp.int32)
    member = (route_now[None, :] == expert_ids[:, None]).astype(jnp.int32)
    earlier = jnp.cumsum(member, axis=1) - member
    rank_ids = jnp.arange(capacity, dtype=jnp.int32)
    placed = member[:, None, :] * (earlier[:, None, :] == rank_ids[None, :, None]).astype(jnp.int32)
    return placed.reshape(expert_count * capacity, tile_count)


def start_into_slots(placed, rows, tile_rows, dp_count):
    width = rows.shape[-1]
    tile_blocks = rows.reshape(placed.shape[1], tile_rows, dp_count, width // dp_count)
    return jnp.einsum(
        "st,trqd->qsrd",
        placed.astype(jnp.bfloat16),
        tile_blocks,
        preferred_element_type=jnp.float32,
    ).astype(jnp.bfloat16)


def start_from_slots(placed, slot_rows):
    merged = jnp.einsum(
        "st,qsrd->trqd", placed.astype(jnp.bfloat16), slot_rows, preferred_element_type=jnp.float32
    ).astype(jnp.bfloat16)
    return merged.reshape(merged.shape[0] * merged.shape[1], -1)


def start_send_out(slot_rows):
    quarter = slot_rows.shape[-1]
    flat = slot_rows.reshape((-1,) + slot_rows.shape[2:])
    arrived = lax.all_to_all(flat, ("dp", "expert"), split_axis=0, concat_axis=0, tiled=True)
    return arrived.reshape(-1, quarter)


def start_send_back(part_rows, dp_count, tile_rows):
    quarter = part_rows.shape[-1]
    flat = part_rows.reshape(-1, tile_rows, quarter)
    returned = lax.all_to_all(flat, ("dp", "expert"), split_axis=0, concat_axis=0, tiled=True)
    return returned.reshape(dp_count, -1, tile_rows, quarter)


def start_widen_rounded(values):
    return lax.optimization_barrier(values.astype(jnp.bfloat16)).astype(jnp.float32)


def start_expert_forward(received, gate_weight, up_weight, down_weight):
    gate_terms = start_widen_rounded(jnp.dot(received, gate_weight, preferred_element_type=jnp.float32))
    up_terms = start_widen_rounded(jnp.dot(received, up_weight, preferred_element_type=jnp.float32))
    gate_pre, up_pre = (
        lax.psum(gate_terms.astype(jnp.bfloat16), "dp").astype(jnp.float32),
        lax.psum(up_terms.astype(jnp.bfloat16), "dp").astype(jnp.float32),
    )
    activated = (jax.nn.silu(gate_pre) * up_pre).astype(jnp.bfloat16)
    part_rows = jnp.dot(activated, down_weight, preferred_element_type=jnp.float32).astype(
        jnp.bfloat16
    )
    return (part_rows, (gate_pre, up_pre, activated))


def start_expert_backward(
    received, grad_recv, kept_state, gate_weight, up_weight, down_weight, grad_sums
):
    gate_pre, up_pre, activated = kept_state
    grad_terms = start_widen_rounded(start_contract_last(grad_recv, down_weight))
    grad_act = lax.psum(grad_terms.astype(jnp.bfloat16), "dp").astype(jnp.float32)
    sigmoid_gate = jax.nn.sigmoid(gate_pre)
    silu_gate = gate_pre * sigmoid_gate
    grad_gate_pre = (
        grad_act * up_pre * sigmoid_gate * (1.0 + gate_pre * (1.0 - sigmoid_gate))
    ).astype(jnp.bfloat16)
    grad_up_pre = (grad_act * silu_gate).astype(jnp.bfloat16)
    back_rows = (
        start_contract_last(grad_gate_pre, gate_weight) + start_contract_last(grad_up_pre, up_weight)
    ).astype(jnp.bfloat16)
    grad_gate = grad_sums[0] + start_contract_first(received, grad_gate_pre)
    grad_up = grad_sums[1] + start_contract_first(received, grad_up_pre)
    grad_down = grad_sums[2] + start_contract_first(activated, grad_recv)
    return (back_rows, (grad_gate, grad_up, grad_down))


def start_body(tokens, cotangent, gain, w_gate, w_up, w_down, route):
    pipe_count = lax.axis_size("pipe")
    dp_count = lax.axis_size("dp")
    expert_count = lax.axis_size("expert")
    section_index = lax.axis_index("pipe")
    gain_row = gain[0]
    gate_weight = w_gate[0, 0]
    up_weight = w_up[0, 0]
    down_weight = w_down[0, 0]
    route_table = route[0, :, :, 0]
    tile_count = route_table.shape[1]
    capacity = max(2, 3 * tile_count // (2 * expert_count))
    hidden = tokens[0]
    saved_ticks = []
    out_rows = hidden
    for pass_index in range(PASSES):
        micro_index = (section_index - pass_index + pipe_count) % pipe_count
        route_now = lax.dynamic_index_in_dim(route_table, micro_index, 0, keepdims=False)
        placed = start_slot_matrix(route_now, expert_count, capacity)
        normed, scaled, inverse = start_normalize(hidden, gain_row)
        received = start_send_out(start_into_slots(placed, normed, TILE, dp_count))
        part_rows, kept_state = start_expert_forward(received, gate_weight, up_weight, down_weight)
        ffn_rows = start_from_slots(placed, start_send_back(part_rows, dp_count, TILE))
        new_hidden = (hidden.astype(jnp.float32) + ffn_rows.astype(jnp.float32)).astype(
            jnp.bfloat16
        )
        saved_ticks.append((placed, scaled, inverse, received, kept_state))
        if pass_index + 1 < PASSES:
            hidden = start_shifted(new_hidden, "pipe", 1)
        else:
            out_rows = new_hidden
    grad_rows = cotangent[0]
    grad_sums = (
        jnp.zeros(gate_weight.shape, jnp.float32),
        jnp.zeros(up_weight.shape, jnp.float32),
        jnp.zeros(down_weight.shape, jnp.float32),
    )
    gain_sum = jnp.zeros(gain_row.shape, jnp.float32)
    entry_grad = grad_rows
    for pass_index in reversed(range(PASSES)):
        placed, scaled, inverse, received, kept_state = saved_ticks[pass_index]
        grad_recv = start_send_out(start_into_slots(placed, grad_rows, TILE, dp_count))
        back_rows, grad_sums = start_expert_backward(
            received, grad_recv, kept_state, gate_weight, up_weight, down_weight, grad_sums
        )
        grad_normed = start_from_slots(placed, start_send_back(back_rows, dp_count, TILE)).astype(jnp.float32)
        gain_sum = gain_sum + jnp.sum(grad_normed * scaled, axis=0)
        grad_scaled = grad_normed * gain_row
        grad_wide = inverse * (
            grad_scaled - scaled * jnp.mean(grad_scaled * scaled, axis=-1, keepdims=True)
        )
        grad_in = (grad_rows.astype(jnp.float32) + grad_wide).astype(jnp.bfloat16)
        if pass_index > 0:
            grad_rows = start_shifted(grad_in, "pipe", -1)
        else:
            entry_grad = grad_in
    gain_total = lax.psum(gain_sum, ("dp", "expert"))
    return (
        out_rows[None],
        entry_grad[None],
        gain_total[None],
        grad_sums[0].astype(jnp.bfloat16)[None, None],
        grad_sums[1].astype(jnp.bfloat16)[None, None],
        grad_sums[2].astype(jnp.bfloat16)[None, None],
    )


def start_solution(mesh):
    placed = (
        P("pipe", ("dp", "expert"), None),
        P("pipe", ("dp", "expert"), None),
        P("pipe", None),
        P("pipe", "expert", "dp", None),
        P("pipe", "expert", "dp", None),
        P("pipe", "expert", None, "dp"),
        P("pipe", None, ("dp", "expert"), None),
    )
    return jax.shard_map(
        start_body,
        mesh=mesh,
        in_specs=placed,
        out_specs=(
            P("pipe", ("dp", "expert"), None),
            P("pipe", ("dp", "expert"), None),
            P("pipe", None),
            P("pipe", "expert", "dp", None),
            P("pipe", "expert", "dp", None),
            P("pipe", "expert", None, "dp"),
        ),
        check_vma=False,
    )


def solution(mesh):
    if mesh.shape["expert"] != PAIR:
        return start_solution(mesh)
    placed = (
        P("pipe", ("dp", "expert"), None),
        P("pipe", ("dp", "expert"), None),
        P("pipe", None),
        P("pipe", "expert", "dp", None),
        P("pipe", "expert", "dp", None),
        P("pipe", "expert", None, "dp"),
        P("pipe", None, ("dp", "expert"), None),
    )
    return jax.shard_map(
        body,
        mesh=mesh,
        in_specs=placed,
        out_specs=placed[:2] + (P("pipe", None),) + placed[3:6],
        check_vma=False,
    )
```

```python
import jax
import jax.numpy as jnp
from jax import lax
from jax.experimental import pallas as pl
from jax.experimental.pallas import tpu as pltpu
from jax.sharding import PartitionSpec as P

TILE = 8
PASSES = 2
PAIR = 2
COLUMNS = 256
LANES = 128
VMEM_BYTES = 24 * 1024 * 1024


epsilon = 1e-06
bf16 = jnp.bfloat16
f32 = jnp.float32


def dot(former, latter, contract):
    return lax.dot_general(
        former, latter, ((contract[:1], contract[1:]), ((), ())), preferred_element_type=f32
    )


def partner_route(size, step):
    return [(i, i ^ step) for i in range(size)]


def swap(block, axis, step):
    return lax.ppermute(block, axis, partner_route(lax.axis_size(axis), step))


def shifted(block, axis, distance):
    size = lax.axis_size(axis)
    return lax.ppermute(block, axis, [(i, (i + distance) % size) for i in range(size)])


def quarter_of(rows, index, width):
    return lax.dynamic_slice_in_dim(rows, index * width, width, axis=-1)


def to_quarters(rows, dp_count):
    width = rows.shape[-1] // dp_count
    here = lax.axis_index("dp")
    quarters = [quarter_of(rows, here ^ step, width) for step in range(dp_count)]
    return quarters[:1] + [swap(quarters[step], "dp", step) for step in range(1, dp_count)]


def assemble(parts):
    here = lax.axis_index("dp")
    rows, width = parts[0].shape
    whole = jnp.zeros((rows, width * len(parts)), parts[0].dtype)
    for step, part in enumerate(parts):
        whole = lax.dynamic_update_slice_in_dim(whole, part, (here ^ step) * width, axis=1)
    return whole


def from_quarters(parts):
    return assemble(
        [swap(part, "dp", step) if step else part for step, part in enumerate(parts)]
    )


def sum_parts(parts):
    total = parts[0].astype(f32)
    for step in range(1, len(parts)):
        total = total + swap(parts[step], "dp", step).astype(f32)
    return total


def gather_rows(rows, dp_count):
    return [rows] + [swap(rows, "dp", step) for step in range(1, dp_count)]


def after(value, *earlier):
    return lax.optimization_barrier((value,) + earlier)[0]


def columns_of(extent):
    return COLUMNS if extent % COLUMNS == 0 else extent


def kernel_call(body, operands, weights, out_shape, scratch):
    count, kept, made = len(operands), len(weights), len(out_shape)

    def call(*refs):
        operand_refs, refs = refs[:count], refs[count:]
        weight_refs, refs = refs[:kept], refs[kept:]
        body(operand_refs, weight_refs, refs[:made], refs[made:])

    in_vmem = pl.BlockSpec(memory_space=pltpu.VMEM)
    return pl.pallas_call(
        call,
        in_specs=[in_vmem] * (count + kept),
        out_specs=[in_vmem] * made,
        out_shape=out_shape,
        scratch_shapes=scratch,
        compiler_params=pltpu.CompilerParams(vmem_limit_bytes=VMEM_BYTES),
        cost_estimate=pl.CostEstimate(flops=0, bytes_accessed=0, transcendentals=0),
    )(*operands, *weights)


def resident(arrays):
    count = len(arrays)

    def call(*refs):
        arrivals = refs[-1]
        copies = [
            pltpu.make_async_copy(refs[i], refs[count + i], arrivals.at[i]) for i in range(count)
        ]
        for copy in copies:
            copy.start()
        for copy in copies:
            copy.wait()

    return pl.pallas_call(
        call,
        in_specs=[pl.BlockSpec(memory_space=pltpu.HBM)] * count,
        out_specs=[pl.BlockSpec(memory_space=pltpu.VMEM)] * count,
        out_shape=[pltpu.VMEM(a.shape, a.dtype) for a in arrays],
        scratch_shapes=[pltpu.SemaphoreType.DMA((count,))],
        compiler_params=pltpu.CompilerParams(vmem_limit_bytes=VMEM_BYTES),
        cost_estimate=pl.CostEstimate(
            flops=0,
            bytes_accessed=2 * sum(a.size * a.dtype.itemsize for a in arrays),
            transcendentals=0,
        ),
    )(*(pltpu.with_memory_space_constraint(a, pltpu.HBM) for a in arrays))


def store_parts(refs, columns, value):
    size = value.shape[0] // len(refs)
    for index, ref in enumerate(refs):
        ref[:, columns] = value[index * size : (index + 1) * size]


def each_tile(extent, visit):
    tile = columns_of(extent)

    def step(j, carry):
        visit(span(j, tile))
        return carry

    lax.fori_loop(0, extent // tile, step, 0)


def span(tile, size):
    return pl.ds(pl.multiple_of(tile * size, size), size)


def hidden_parts(blocks, gain_part, mask, gate_pair, up_pair, expert=None):
    parts_count = lax.axis_size("dp")
    width, units = gate_pair[0].shape
    routed = expert is not None
    block_rows = blocks[0].shape[0]
    if routed:
        block_rows = block_rows * TILE // (TILE + 1)
    rows = block_rows * len(blocks)
    passes = PASSES if routed else 0

    def body(operand_refs, weight_refs, out_refs, scratch):
        *block_refs, gain_ref, choice_ref = operand_refs
        part_refs, gained_ref = out_refs[:parts_count], out_refs[parts_count]
        mask_ref = out_refs[parts_count + 1] if routed else choice_ref
        for index, ref in enumerate(block_refs):
            place = slice(index * block_rows, (index + 1) * block_rows)
            block = ref[:block_rows]
            gained_ref[place] = (block.astype(f32) * gain_ref[...]).astype(bf16)
            if routed:
                out_refs[-1][place] = block
                tiles = block_rows // TILE
                row = lax.broadcasted_iota(jnp.int32, (block_rows, tiles), 0)
                first = TILE * lax.broadcasted_iota(jnp.int32, (block_rows, tiles), 1)
                chosen = ((row >= first) & (row < first + TILE)).astype(bf16)
                experts = dot(chosen, ref[block_rows:, :LANES], (1, 0)) - choice_ref[...]
                for k in range(passes):
                    near = jnp.abs(experts[:, k : k + 1]) < 0.5
                    out_refs[parts_count + 1 + k][place] = jnp.where(near, 1.0, 0.0)

        for pair in range(2):

            def visit(columns, pair=pair):
                own, other = weight_refs[2 * pair : 2 * pair + 2]
                part = jnp.where(
                    mask_ref[...] > 0.5,
                    dot(gained_ref[...], own[:, columns], (1, 0)),
                    dot(gained_ref[...], other[:, columns], (1, 0)),
                ).astype(bf16)
                store_parts([ref.at[:, pair * units :] for ref in part_refs], columns, part)

            each_tile(units, visit)

    outs = kernel_call(
        body,
        (*blocks, gain_part, expert if routed else mask),
        (*gate_pair, *up_pair),
        [jax.ShapeDtypeStruct((rows // parts_count, 2 * units), bf16)] * parts_count
        + [jax.ShapeDtypeStruct((rows, width), bf16)]
        + [jax.ShapeDtypeStruct((rows, 1), f32)] * passes
        + [jax.ShapeDtypeStruct((rows, width), bf16)] * int(routed),
        [],
    )
    return outs[:parts_count], outs[parts_count], outs[parts_count + 1 :]


def activate(parts, inverse):
    rows, both = parts[0].shape
    units = both // 2

    def body(operand_refs, weight_refs, out_refs, scratch):
        *part_refs, inverse_ref = operand_refs
        total = part_refs[0][...].astype(f32)
        for ref in part_refs[1:]:
            total = total + ref[...].astype(f32)
        total = total * inverse_ref[...]
        gate, up = total[:, :units], total[:, units:]
        out_refs[0][...] = gate
        out_refs[1][...] = up
        out_refs[2][...] = (gate / (1.0 + jnp.exp(-gate)) * up).astype(bf16)

    return kernel_call(
        body,
        (*parts, inverse),
        (),
        [jax.ShapeDtypeStruct((rows, units), f32)] * 2
        + [jax.ShapeDtypeStruct((rows, units), bf16)],
        [],
    )


def join(joined, refs, columns):
    size = refs[0].shape[0]
    for index, ref in enumerate(refs):
        joined[index * size : (index + 1) * size] = ref[:, columns]


def add_down(blocks, mask, down_pair, hidden, in_parts):
    count = len(blocks)
    part_rows, units = blocks[0].shape
    rows = part_rows * count
    width = down_pair[0].shape[1]
    out_count = count if in_parts else 1

    def body(operand_refs, weight_refs, out_refs, scratch):
        *block_refs, mask_ref, hidden_ref = operand_refs
        *row_refs, square_ref = out_refs
        (joined,) = scratch
        join(joined, block_refs, slice(None))
        square_ref[...] = jnp.zeros_like(square_ref)

        own, other = weight_refs

        def visit(columns):
            ffn = jnp.where(
                mask_ref[...] > 0.5,
                dot(joined[...], own[:, columns], (1, 0)),
                dot(joined[...], other[:, columns], (1, 0)),
            ).astype(bf16)
            out = (hidden_ref[:, columns].astype(f32) + ffn.astype(f32)).astype(bf16)
            wide = out.astype(f32)
            square_ref[...] += jnp.sum(wide * wide, axis=-1, keepdims=True)
            store_parts(row_refs, columns, out)

        each_tile(width, visit)

    outs = kernel_call(
        body,
        (*blocks, mask, hidden),
        down_pair,
        [jax.ShapeDtypeStruct((rows // out_count, width), bf16)] * out_count
        + [jax.ShapeDtypeStruct((rows, 1), f32)],
        [pltpu.VMEM((rows, units), bf16)],
    )
    return outs[:out_count], outs[out_count]


def act_grad_parts(blocks, mask, down_pair):
    parts_count = lax.axis_size("dp")
    rows = sum(block.shape[0] for block in blocks)
    units, width = down_pair[0].shape

    def body(operand_refs, weight_refs, out_refs, scratch):
        *block_refs, mask_ref = operand_refs
        *part_refs, grad_ref = out_refs
        own, other = weight_refs
        join(grad_ref, block_refs, slice(None))

        def visit(columns):
            part = jnp.where(
                mask_ref[...] > 0.5,
                dot(grad_ref[...], own[columns], (1, 1)),
                dot(grad_ref[...], other[columns], (1, 1)),
            ).astype(bf16)
            store_parts(part_refs, columns, part)

        each_tile(units, visit)

    outs = kernel_call(
        body,
        (*blocks, mask),
        down_pair,
        [jax.ShapeDtypeStruct((rows // parts_count, units), bf16)] * parts_count
        + [jax.ShapeDtypeStruct((rows, width), bf16)],
        [],
    )
    return outs[:parts_count], outs[parts_count]


def hidden_grads(parts, gate, up, inverse, features):
    rows, units = gate.shape

    def body(operand_refs, weight_refs, out_refs, scratch):
        *part_refs, gate_ref, up_ref, inverse_ref = operand_refs
        (out_ref,) = out_refs
        grad_act = part_refs[0][...].astype(f32)
        for ref in part_refs[1:]:
            grad_act = grad_act + ref[...].astype(f32)
        gate_now, up_now, scale = gate_ref[...], up_ref[...], inverse_ref[...]
        sigmoid = 1.0 / (1.0 + jnp.exp(-gate_now))
        scaled = grad_act * scale
        gate_grad = scaled * up_now * sigmoid * (1.0 + gate_now * (1.0 - sigmoid))
        up_grad = scaled * (gate_now * sigmoid)
        shrink = jnp.sum(gate_grad * gate_now + up_grad * up_now, axis=-1, keepdims=True) * (
            scale / features
        )
        out_ref[:, :units] = gate_grad.astype(bf16)
        out_ref[:, units : 2 * units] = up_grad.astype(bf16)
        coarse = shrink.astype(bf16).astype(f32)
        lane = lax.broadcasted_iota(jnp.int32, (rows, LANES), 1)
        out_ref[:, 2 * units :] = jnp.where(
            lane == 0, coarse, jnp.where(lane == 1, shrink - coarse, 0.0)
        ).astype(bf16)

    (sent,) = kernel_call(
        body,
        (*parts, gate, up, inverse),
        [],
        [jax.ShapeDtypeStruct((rows, 2 * units + LANES), bf16)],
        [],
    )
    return sent


def input_grad(blocks, mask, gate_pair, up_pair, grad, hidden, gain_part, in_parts):
    count = len(blocks)
    part_rows = blocks[0].shape[0]
    rows = part_rows * count
    width, units = gate_pair[0].shape
    out_count = count if in_parts else 1

    def body(operand_refs, weight_refs, out_refs, scratch):
        *block_refs, mask_ref, grad_ref, hidden_ref, gain_ref = operand_refs
        *row_refs, sum_ref = out_refs
        joined, shrink = scratch
        join(joined, block_refs, slice(0, 2 * units))
        for index, ref in enumerate(block_refs):
            tail = ref[:, 2 * units :].astype(f32)
            shrink[index * part_rows : (index + 1) * part_rows] = jnp.sum(
                tail, axis=-1, keepdims=True
            )

        gate_own, gate_other, up_own, up_other = weight_refs

        def visit(columns):
            def back_of(gate, up):
                return dot(joined[:, :units], gate[columns], (1, 1)) + dot(
                    joined[:, units:], up[columns], (1, 1)
                )

            back = jnp.where(
                mask_ref[...] > 0.5, back_of(gate_own, up_own), back_of(gate_other, up_other)
            )
            wide = hidden_ref[:, columns].astype(f32)
            sum_ref[:, columns] = jnp.sum(back * wide, axis=0, keepdims=True)
            out = (
                grad_ref[:, columns].astype(f32)
                + back * gain_ref[:, columns]
                - wide * shrink[...]
            ).astype(bf16)
            store_parts(row_refs, columns, out)

        each_tile(width, visit)

    outs = kernel_call(
        body,
        (*blocks, mask, grad, hidden, gain_part),
        (*gate_pair, *up_pair),
        [jax.ShapeDtypeStruct((rows // out_count, width), bf16)] * out_count
        + [jax.ShapeDtypeStruct((1, width), f32)],
        [
            pltpu.VMEM((rows, 2 * units), bf16),
            pltpu.VMEM((rows, 1), f32),
        ],
    )
    return outs[:out_count], outs[out_count]


def body(tokens, cotangent, gain, w_gate, w_up, w_down, route):
    pipe_count = lax.axis_size("pipe")
    dp_count = lax.axis_size("dp")
    section = lax.axis_index("pipe")
    expert = lax.axis_index("expert")
    here = lax.axis_index("dp")
    features = tokens.shape[-1]
    width = features // dp_count
    units = w_gate.shape[-1]
    gain_part = lax.dynamic_slice_in_dim(gain, here * width, width, axis=1)

    own_tokens = tokens[0]
    micro = [(section - k + pipe_count) % pipe_count for k in range(PASSES)]
    route_rows = jnp.stack(
        [lax.dynamic_index_in_dim(route[0, :, :, 0], m, 0, keepdims=False) for m in micro], axis=1
    ).astype(bf16)
    route_rows = jnp.pad(route_rows, ((0, 0), (0, width - PASSES)))

    def tokens_quarter(step):
        return jnp.concatenate([quarter_of(own_tokens, here ^ step, width), route_rows])

    blocks = [tokens_quarter(0)] + [
        swap(tokens_quarter(step), "dp", step) for step in range(1, dp_count)
    ]
    weights = [
        weight
        for own in (w_gate, w_up, w_down)
        for weight in (own[0, 0], swap(own[0, 0], "expert", 1))
    ]
    weights = resident(weights)
    gate_pair, up_pair, down_pair = weights[:2], weights[2:4], weights[4:]
    expert_id = jnp.full((1, LANES), expert, f32)

    def scale_of(square_sum):
        return lax.rsqrt(square_sum / features + epsilon)

    def weight_grad(left, right, mask, wanted):
        return dot(left, jnp.where((mask > 0.5) == wanted, right, jnp.zeros_like(right)), (0, 0))

    wide = own_tokens.astype(f32)
    inverse = scale_of(jnp.sum(wide * wide, axis=-1, keepdims=True))
    def cotangent_quarter(step, *earlier):
        return quarter_of(after(cotangent[0], *earlier), here ^ step, width)

    def sent_parts(parts):
        return [parts[0]] + [swap(parts[step], "dp", step) for step in range(1, dp_count)]

    parts, gained, (*masks, hidden) = hidden_parts(
        blocks, gain_part, None, gate_pair, up_pair, expert_id
    )
    grad_blocks = [cotangent_quarter(0, *blocks)] + [
        swap(cotangent_quarter(step, *blocks), "dp", step) for step in range(1, dp_count - 1)
    ]
    parts = list(lax.optimization_barrier((*parts, *grad_blocks)))[:dp_count]
    gate, up, activated = activate(sent_parts(parts), inverse)
    kept = [(hidden, gained, inverse, gate, up)]
    first_activated = gather_rows(activated, dp_count)
    (next_hidden,), squares = add_down(first_activated, masks[0], down_pair, hidden, False)
    hidden = shifted(next_hidden, "pipe", 1)
    grad_blocks.append(
        swap(cotangent_quarter(dp_count - 1, next_hidden), "dp", dp_count - 1)
    )
    inverse = shifted(scale_of(sum_parts(jnp.split(squares, dp_count))), "pipe", 1)
    act_parts, grad = act_grad_parts(grad_blocks, masks[1], down_pair)
    act_parts = sent_parts(act_parts)
    hidden = after(hidden, inverse, *act_parts[1:])

    parts, gained, _ = hidden_parts([hidden], gain_part, masks[1], gate_pair, up_pair)
    gate, up, activated = activate(sent_parts(parts), inverse)
    kept.append((hidden, gained, inverse, gate, up))

    gain_sum = jnp.zeros((1, width), f32)
    for k in reversed(range(PASSES)):
        hidden, gained, inverse, gate, up = kept[k]
        mask = masks[k]
        sent = hidden_grads(act_parts, gate, up, inverse, features)
        both_grad = gather_rows(sent, dp_count)
        if k == 0:
            late_down = jnp.concatenate(first_activated)
            other_down = swap(
                (weight_grad(late_down, grad, mask, False) + early[False][2].astype(f32)).astype(
                    bf16
                ),
                "expert",
                1,
            )
            down_grad = (
                weight_grad(late_down, grad, mask, True)
                + early[True][2].astype(f32)
                + other_down.astype(f32)
            ).astype(bf16)
            both_grad[1] = after(both_grad[1], down_grad)
        else:
            last_activated = gather_rows(after(activated, *both_grad[1:]), dp_count)
        outs, gain_term = input_grad(
            both_grad, mask, gate_pair, up_pair, grad, hidden, gain_part, k == 0
        )
        gain_sum = gain_sum + gain_term
        joined = jnp.concatenate(both_grad)
        rights = [joined[:, :units], joined[:, units : 2 * units]]
        if k > 0:
            last_grad = grad
            grad = shifted(outs[0], "pipe", -1)
            rights = [after(right, outs[0]) for right in rights]
            early = {
                wanted: [weight_grad(gained, right, mask, wanted).astype(bf16) for right in rights]
                for wanted in (False, True)
            }
            out_parts, _ = add_down(last_activated, mask, down_pair, hidden, True)
            out_rows = from_quarters(out_parts)
            grad = after(grad, out_rows, *early[False], *early[True])
            act_parts, grad = act_grad_parts([grad], masks[0], down_pair)
            last_activated = jnp.concatenate(last_activated)
            for wanted in (False, True):
                early[wanted].append(
                    weight_grad(last_activated, last_grad, mask, wanted).astype(bf16)
                )
            act_parts = sent_parts(act_parts)
            act_parts[1] = after(act_parts[1], early[False][2], early[True][2])

    returned = sent_parts(outs)
    rights = [after(right, returned[1]) for right in rights]
    received = [
        swap((weight_grad(gained, right, mask, False) + soon.astype(f32)).astype(bf16), "expert", 1)
        for right, soon in zip(rights, early[False])
    ]
    gain_rows = jnp.concatenate(gather_rows(after(gain_sum, received[0]), dp_count))
    gain_rows = gain_rows + swap(gain_rows, "expert", 1)
    gain_all = jnp.zeros((features,), f32)
    for step in range(dp_count):
        gain_all = lax.dynamic_update_slice_in_dim(
            gain_all, gain_rows[step], (here ^ step) * width, axis=0
        )
    grads = [
        (
            weight_grad(gained, right, mask, True) + soon.astype(f32) + other.astype(f32)
        ).astype(bf16)
        for right, soon, other in zip(rights, early[True], received)
    ] + [down_grad]
    returned = list(lax.optimization_barrier((*returned, *grads)))[:dp_count]
    entry = assemble(returned)
    return (
        out_rows[None],
        entry[None],
        gain_all[None],
        grads[0][None, None],
        grads[1][None, None],
        grads[2][None, None],
    )


def start_shifted(block, axis, distance):
    devices = range(lax.axis_size(axis))
    route = [((i - distance) % len(devices), i) for i in devices]
    return lax.ppermute(block, axis, route)


def start_contract_last(former, latter):
    return lax.dot_general(
        former, latter, (((1,), (1,)), ((), ())), preferred_element_type=jnp.float32
    )


def start_contract_first(former, latter):
    return lax.dot_general(
        former, latter, (((0,), (0,)), ((), ())), preferred_element_type=jnp.float32
    )


def start_normalize(hidden, gain_row):
    widened = hidden.astype(jnp.float32)
    inverse = lax.rsqrt(jnp.mean(widened * widened, axis=-1, keepdims=True) + epsilon)
    scaled = widened * inverse
    return ((scaled * gain_row).astype(jnp.bfloat16), scaled, inverse)


def start_slot_matrix(route_now, expert_count, capacity):
    tile_count = route_now.shape[0]
    expert_ids = jnp.arange(expert_count, dtype=jnp.int32)
    member = (route_now[None, :] == expert_ids[:, None]).astype(jnp.int32)
    earlier = jnp.cumsum(member, axis=1) - member
    rank_ids = jnp.arange(capacity, dtype=jnp.int32)
    placed = member[:, None, :] * (earlier[:, None, :] == rank_ids[None, :, None]).astype(jnp.int32)
    return placed.reshape(expert_count * capacity, tile_count)


def start_into_slots(placed, rows, tile_rows, dp_count):
    width = rows.shape[-1]
    tile_blocks = rows.reshape(placed.shape[1], tile_rows, dp_count, width // dp_count)
    return jnp.einsum(
        "st,trqd->qsrd",
        placed.astype(jnp.bfloat16),
        tile_blocks,
        preferred_element_type=jnp.float32,
    ).astype(jnp.bfloat16)


def start_from_slots(placed, slot_rows):
    merged = jnp.einsum(
        "st,qsrd->trqd", placed.astype(jnp.bfloat16), slot_rows, preferred_element_type=jnp.float32
    ).astype(jnp.bfloat16)
    return merged.reshape(merged.shape[0] * merged.shape[1], -1)


def start_send_out(slot_rows):
    quarter = slot_rows.shape[-1]
    flat = slot_rows.reshape((-1,) + slot_rows.shape[2:])
    arrived = lax.all_to_all(flat, ("dp", "expert"), split_axis=0, concat_axis=0, tiled=True)
    return arrived.reshape(-1, quarter)


def start_send_back(part_rows, dp_count, tile_rows):
    quarter = part_rows.shape[-1]
    flat = part_rows.reshape(-1, tile_rows, quarter)
    returned = lax.all_to_all(flat, ("dp", "expert"), split_axis=0, concat_axis=0, tiled=True)
    return returned.reshape(dp_count, -1, tile_rows, quarter)


def start_widen_rounded(values):
    return lax.optimization_barrier(values.astype(jnp.bfloat16)).astype(jnp.float32)


def start_expert_forward(received, gate_weight, up_weight, down_weight):
    gate_terms = start_widen_rounded(jnp.dot(received, gate_weight, preferred_element_type=jnp.float32))
    up_terms = start_widen_rounded(jnp.dot(received, up_weight, preferred_element_type=jnp.float32))
    gate_pre, up_pre = (
        lax.psum(gate_terms.astype(jnp.bfloat16), "dp").astype(jnp.float32),
        lax.psum(up_terms.astype(jnp.bfloat16), "dp").astype(jnp.float32),
    )
    activated = (jax.nn.silu(gate_pre) * up_pre).astype(jnp.bfloat16)
    part_rows = jnp.dot(activated, down_weight, preferred_element_type=jnp.float32).astype(
        jnp.bfloat16
    )
    return (part_rows, (gate_pre, up_pre, activated))


def start_expert_backward(
    received, grad_recv, kept_state, gate_weight, up_weight, down_weight, grad_sums
):
    gate_pre, up_pre, activated = kept_state
    grad_terms = start_widen_rounded(start_contract_last(grad_recv, down_weight))
    grad_act = lax.psum(grad_terms.astype(jnp.bfloat16), "dp").astype(jnp.float32)
    sigmoid_gate = jax.nn.sigmoid(gate_pre)
    silu_gate = gate_pre * sigmoid_gate
    grad_gate_pre = (
        grad_act * up_pre * sigmoid_gate * (1.0 + gate_pre * (1.0 - sigmoid_gate))
    ).astype(jnp.bfloat16)
    grad_up_pre = (grad_act * silu_gate).astype(jnp.bfloat16)
    back_rows = (
        start_contract_last(grad_gate_pre, gate_weight) + start_contract_last(grad_up_pre, up_weight)
    ).astype(jnp.bfloat16)
    grad_gate = grad_sums[0] + start_contract_first(received, grad_gate_pre)
    grad_up = grad_sums[1] + start_contract_first(received, grad_up_pre)
    grad_down = grad_sums[2] + start_contract_first(activated, grad_recv)
    return (back_rows, (grad_gate, grad_up, grad_down))


def start_body(tokens, cotangent, gain, w_gate, w_up, w_down, route):
    pipe_count = lax.axis_size("pipe")
    dp_count = lax.axis_size("dp")
    expert_count = lax.axis_size("expert")
    section_index = lax.axis_index("pipe")
    gain_row = gain[0]
    gate_weight = w_gate[0, 0]
    up_weight = w_up[0, 0]
    down_weight = w_down[0, 0]
    route_table = route[0, :, :, 0]
    tile_count = route_table.shape[1]
    capacity = max(2, 3 * tile_count // (2 * expert_count))
    hidden = tokens[0]
    saved_ticks = []
    out_rows = hidden
    for pass_index in range(PASSES):
        micro_index = (section_index - pass_index + pipe_count) % pipe_count
        route_now = lax.dynamic_index_in_dim(route_table, micro_index, 0, keepdims=False)
        placed = start_slot_matrix(route_now, expert_count, capacity)
        normed, scaled, inverse = start_normalize(hidden, gain_row)
        received = start_send_out(start_into_slots(placed, normed, TILE, dp_count))
        part_rows, kept_state = start_expert_forward(received, gate_weight, up_weight, down_weight)
        ffn_rows = start_from_slots(placed, start_send_back(part_rows, dp_count, TILE))
        new_hidden = (hidden.astype(jnp.float32) + ffn_rows.astype(jnp.float32)).astype(
            jnp.bfloat16
        )
        saved_ticks.append((placed, scaled, inverse, received, kept_state))
        if pass_index + 1 < PASSES:
            hidden = start_shifted(new_hidden, "pipe", 1)
        else:
            out_rows = new_hidden
    grad_rows = cotangent[0]
    grad_sums = (
        jnp.zeros(gate_weight.shape, jnp.float32),
        jnp.zeros(up_weight.shape, jnp.float32),
        jnp.zeros(down_weight.shape, jnp.float32),
    )
    gain_sum = jnp.zeros(gain_row.shape, jnp.float32)
    entry_grad = grad_rows
    for pass_index in reversed(range(PASSES)):
        placed, scaled, inverse, received, kept_state = saved_ticks[pass_index]
        grad_recv = start_send_out(start_into_slots(placed, grad_rows, TILE, dp_count))
        back_rows, grad_sums = start_expert_backward(
            received, grad_recv, kept_state, gate_weight, up_weight, down_weight, grad_sums
        )
        grad_normed = start_from_slots(placed, start_send_back(back_rows, dp_count, TILE)).astype(jnp.float32)
        gain_sum = gain_sum + jnp.sum(grad_normed * scaled, axis=0)
        grad_scaled = grad_normed * gain_row
        grad_wide = inverse * (
            grad_scaled - scaled * jnp.mean(grad_scaled * scaled, axis=-1, keepdims=True)
        )
        grad_in = (grad_rows.astype(jnp.float32) + grad_wide).astype(jnp.bfloat16)
        if pass_index > 0:
            grad_rows = start_shifted(grad_in, "pipe", -1)
        else:
            entry_grad = grad_in
    gain_total = lax.psum(gain_sum, ("dp", "expert"))
    return (
        out_rows[None],
        entry_grad[None],
        gain_total[None],
        grad_sums[0].astype(jnp.bfloat16)[None, None],
        grad_sums[1].astype(jnp.bfloat16)[None, None],
        grad_sums[2].astype(jnp.bfloat16)[None, None],
    )


def start_solution(mesh):
    placed = (
        P("pipe", ("dp", "expert"), None),
        P("pipe", ("dp", "expert"), None),
        P("pipe", None),
        P("pipe", "expert", "dp", None),
        P("pipe", "expert", "dp", None),
        P("pipe", "expert", None, "dp"),
        P("pipe", None, ("dp", "expert"), None),
    )
    return jax.shard_map(
        start_body,
        mesh=mesh,
        in_specs=placed,
        out_specs=(
            P("pipe", ("dp", "expert"), None),
            P("pipe", ("dp", "expert"), None),
            P("pipe", None),
            P("pipe", "expert", "dp", None),
            P("pipe", "expert", "dp", None),
            P("pipe", "expert", None, "dp"),
        ),
        check_vma=False,
    )


def solution(mesh):
    if mesh.shape["expert"] != PAIR:
        return start_solution(mesh)
    placed = (
        P("pipe", ("dp", "expert"), None),
        P("pipe", ("dp", "expert"), None),
        P("pipe", None),
        P("pipe", "expert", "dp", None),
        P("pipe", "expert", "dp", None),
        P("pipe", "expert", None, "dp"),
        P("pipe", None, ("dp", "expert"), None),
    )
    return jax.shard_map(
        body,
        mesh=mesh,
        in_specs=placed,
        out_specs=placed[:2] + (P("pipe", None),) + placed[3:6],
        check_vma=False,
    )
```

```python
import jax
import jax.numpy as jnp
from jax import lax
from jax.experimental import pallas as pl
from jax.experimental.pallas import tpu as pltpu
from jax.sharding import PartitionSpec as P

TILE = 8
PASSES = 2
PAIR = 2
COLUMNS = 256
LANES = 128
VMEM_BYTES = 12 * 1024 * 1024


epsilon = 1e-06
bf16 = jnp.bfloat16
f32 = jnp.float32


def dot(former, latter, contract):
    return lax.dot_general(
        former, latter, ((contract[:1], contract[1:]), ((), ())), preferred_element_type=f32
    )


def partner_route(size, step):
    return [(i, i ^ step) for i in range(size)]


def swap(block, axis, step):
    return lax.ppermute(block, axis, partner_route(lax.axis_size(axis), step))


def shifted(block, axis, distance):
    size = lax.axis_size(axis)
    return lax.ppermute(block, axis, [(i, (i + distance) % size) for i in range(size)])


def quarter_of(rows, index, width):
    return lax.dynamic_slice_in_dim(rows, index * width, width, axis=-1)


def to_quarters(rows, dp_count):
    width = rows.shape[-1] // dp_count
    here = lax.axis_index("dp")
    quarters = [quarter_of(rows, here ^ step, width) for step in range(dp_count)]
    return quarters[:1] + [swap(quarters[step], "dp", step) for step in range(1, dp_count)]


def assemble(parts):
    here = lax.axis_index("dp")
    rows, width = parts[0].shape
    whole = jnp.zeros((rows, width * len(parts)), parts[0].dtype)
    for step, part in enumerate(parts):
        whole = lax.dynamic_update_slice_in_dim(whole, part, (here ^ step) * width, axis=1)
    return whole


def from_quarters(parts):
    return assemble(
        [swap(part, "dp", step) if step else part for step, part in enumerate(parts)]
    )


def sum_parts(parts):
    total = parts[0].astype(f32)
    for step in range(1, len(parts)):
        total = total + swap(parts[step], "dp", step).astype(f32)
    return total


def gather_rows(rows, dp_count):
    return [rows] + [swap(rows, "dp", step) for step in range(1, dp_count)]


def after(value, *earlier):
    return lax.optimization_barrier((value,) + earlier)[0]


def columns_of(extent):
    return COLUMNS if extent % COLUMNS == 0 else extent


def kernel_call(body, operands, weights, out_shape, scratch):
    count, kept, made = len(operands), len(weights), len(out_shape)

    def call(*refs):
        operand_refs, refs = refs[:count], refs[count:]
        weight_refs, refs = refs[:kept], refs[kept:]
        body(operand_refs, weight_refs, refs[:made], refs[made:])

    in_vmem = pl.BlockSpec(memory_space=pltpu.VMEM)
    return pl.pallas_call(
        call,
        in_specs=[in_vmem] * (count + kept),
        out_specs=[in_vmem] * made,
        out_shape=out_shape,
        scratch_shapes=scratch,
        compiler_params=pltpu.CompilerParams(vmem_limit_bytes=VMEM_BYTES),
        cost_estimate=pl.CostEstimate(flops=0, bytes_accessed=0, transcendentals=0),
    )(*operands, *weights)


def resident(arrays):
    count = len(arrays)

    def call(*refs):
        arrivals = refs[-1]
        copies = [
            pltpu.make_async_copy(refs[i], refs[count + i], arrivals.at[i]) for i in range(count)
        ]
        for copy in copies:
            copy.start()
        for copy in copies:
            copy.wait()

    return pl.pallas_call(
        call,
        in_specs=[pl.BlockSpec(memory_space=pltpu.HBM)] * count,
        out_specs=[pl.BlockSpec(memory_space=pltpu.VMEM)] * count,
        out_shape=[pltpu.VMEM(a.shape, a.dtype) for a in arrays],
        scratch_shapes=[pltpu.SemaphoreType.DMA((count,))],
        compiler_params=pltpu.CompilerParams(vmem_limit_bytes=VMEM_BYTES),
        cost_estimate=pl.CostEstimate(
            flops=0,
            bytes_accessed=2 * sum(a.size * a.dtype.itemsize for a in arrays),
            transcendentals=0,
        ),
    )(*(pltpu.with_memory_space_constraint(a, pltpu.HBM) for a in arrays))


def store_parts(refs, columns, value):
    size = value.shape[0] // len(refs)
    for index, ref in enumerate(refs):
        ref[:, columns] = value[index * size : (index + 1) * size]


def each_tile(extent, visit):
    tile = columns_of(extent)

    def step(j, carry):
        visit(span(j, tile))
        return carry

    lax.fori_loop(0, extent // tile, step, 0)


def span(tile, size):
    return pl.ds(pl.multiple_of(tile * size, size), size)


def hidden_parts(blocks, part_rows, gain_part, mask, gate_pair, up_pair, expert=None):
    width, units = gate_pair[0].shape
    routed = expert is not None
    block_rows = part_rows if routed else blocks[0].shape[0]
    rows = block_rows * len(blocks)
    parts_count = rows // part_rows
    passes = PASSES if routed else 0

    def body(operand_refs, weight_refs, out_refs, scratch):
        *block_refs, gain_ref, choice_ref = operand_refs
        part_refs, gained_ref = out_refs[:parts_count], out_refs[parts_count]
        mask_ref = out_refs[parts_count + 1] if routed else choice_ref
        for index, ref in enumerate(block_refs):
            place = slice(index * block_rows, (index + 1) * block_rows)
            block = ref[:block_rows]
            gained_ref[place] = (block.astype(f32) * gain_ref[...]).astype(bf16)
            if routed:
                out_refs[-1][place] = block
                tiles = block_rows // TILE
                row = lax.broadcasted_iota(jnp.int32, (block_rows, tiles), 0)
                first = TILE * lax.broadcasted_iota(jnp.int32, (block_rows, tiles), 1)
                chosen = ((row >= first) & (row < first + TILE)).astype(bf16)
                experts = dot(chosen, ref[block_rows:, :LANES], (1, 0)) - choice_ref[...]
                for k in range(passes):
                    near = jnp.abs(experts[:, k : k + 1]) < 0.5
                    out_refs[parts_count + 1 + k][place] = jnp.where(near, 1.0, 0.0)

        for pair in range(2):

            def visit(columns, pair=pair):
                own, other = weight_refs[2 * pair : 2 * pair + 2]
                part = jnp.where(
                    mask_ref[...] > 0.5,
                    dot(gained_ref[...], own[:, columns], (1, 0)),
                    dot(gained_ref[...], other[:, columns], (1, 0)),
                ).astype(bf16)
                store_parts([ref.at[:, pair * units :] for ref in part_refs], columns, part)

            each_tile(units, visit)

    outs = kernel_call(
        body,
        (*blocks, gain_part, expert if routed else mask),
        (*gate_pair, *up_pair),
        [jax.ShapeDtypeStruct((part_rows, 2 * units), bf16)] * parts_count
        + [jax.ShapeDtypeStruct((rows, width), bf16)]
        + [jax.ShapeDtypeStruct((rows, 1), f32)] * passes
        + [jax.ShapeDtypeStruct((rows, width), bf16)] * int(routed),
        [],
    )
    return outs[:parts_count], outs[parts_count], outs[parts_count + 1 :]


def activate(parts, inverse):
    rows, both = parts[0].shape
    units = both // 2

    def body(operand_refs, weight_refs, out_refs, scratch):
        *part_refs, inverse_ref = operand_refs
        total = part_refs[0][...].astype(f32)
        for ref in part_refs[1:]:
            total = total + ref[...].astype(f32)
        total = total * inverse_ref[...]
        gate, up = total[:, :units], total[:, units:]
        out_refs[0][...] = gate
        out_refs[1][...] = up
        out_refs[2][...] = (gate / (1.0 + jnp.exp(-gate)) * up).astype(bf16)

    return kernel_call(
        body,
        (*parts, inverse),
        (),
        [jax.ShapeDtypeStruct((rows, units), f32)] * 2
        + [jax.ShapeDtypeStruct((rows, units), bf16)],
        [],
    )


def join(joined, refs, columns):
    size = refs[0].shape[0]
    for index, ref in enumerate(refs):
        joined[index * size : (index + 1) * size] = ref[:, columns]


def add_down(blocks, mask, down_pair, hidden, in_parts):
    count = len(blocks)
    part_rows, units = blocks[0].shape
    rows = part_rows * count
    width = down_pair[0].shape[1]
    out_count = count if in_parts else 1

    def body(operand_refs, weight_refs, out_refs, scratch):
        *block_refs, mask_ref, hidden_ref = operand_refs
        *row_refs, square_ref = out_refs
        (joined,) = scratch
        join(joined, block_refs, slice(None))
        square_ref[...] = jnp.zeros_like(square_ref)

        own, other = weight_refs

        def visit(columns):
            ffn = jnp.where(
                mask_ref[...] > 0.5,
                dot(joined[...], own[:, columns], (1, 0)),
                dot(joined[...], other[:, columns], (1, 0)),
            ).astype(bf16)
            out = (hidden_ref[:, columns].astype(f32) + ffn.astype(f32)).astype(bf16)
            wide = out.astype(f32)
            square_ref[...] += jnp.sum(wide * wide, axis=-1, keepdims=True)
            store_parts(row_refs, columns, out)

        each_tile(width, visit)

    outs = kernel_call(
        body,
        (*blocks, mask, hidden),
        down_pair,
        [jax.ShapeDtypeStruct((rows // out_count, width), bf16)] * out_count
        + [jax.ShapeDtypeStruct((rows, 1), f32)],
        [pltpu.VMEM((rows, units), bf16)],
    )
    return outs[:out_count], outs[out_count]


def act_grad_parts(blocks, part_rows, mask, down_pair):
    rows = sum(block.shape[0] for block in blocks)
    parts_count = rows // part_rows
    units, width = down_pair[0].shape

    def body(operand_refs, weight_refs, out_refs, scratch):
        *block_refs, mask_ref = operand_refs
        *part_refs, grad_ref = out_refs
        own, other = weight_refs
        join(grad_ref, block_refs, slice(None))

        def visit(columns):
            part = jnp.where(
                mask_ref[...] > 0.5,
                dot(grad_ref[...], own[columns], (1, 1)),
                dot(grad_ref[...], other[columns], (1, 1)),
            ).astype(bf16)
            store_parts(part_refs, columns, part)

        each_tile(units, visit)

    outs = kernel_call(
        body,
        (*blocks, mask),
        down_pair,
        [jax.ShapeDtypeStruct((part_rows, units), bf16)] * parts_count
        + [jax.ShapeDtypeStruct((rows, width), bf16)],
        [],
    )
    return outs[:parts_count], outs[parts_count]


def hidden_grads(parts, gate, up, inverse, features):
    rows, units = gate.shape

    def body(operand_refs, weight_refs, out_refs, scratch):
        *part_refs, gate_ref, up_ref, inverse_ref = operand_refs
        (out_ref,) = out_refs
        grad_act = part_refs[0][...].astype(f32)
        for ref in part_refs[1:]:
            grad_act = grad_act + ref[...].astype(f32)
        gate_now, up_now, scale = gate_ref[...], up_ref[...], inverse_ref[...]
        sigmoid = 1.0 / (1.0 + jnp.exp(-gate_now))
        scaled = grad_act * scale
        gate_grad = scaled * up_now * sigmoid * (1.0 + gate_now * (1.0 - sigmoid))
        up_grad = scaled * (gate_now * sigmoid)
        shrink = jnp.sum(gate_grad * gate_now + up_grad * up_now, axis=-1, keepdims=True) * (
            scale / features
        )
        out_ref[:, :units] = gate_grad.astype(bf16)
        out_ref[:, units : 2 * units] = up_grad.astype(bf16)
        coarse = shrink.astype(bf16).astype(f32)
        lane = lax.broadcasted_iota(jnp.int32, (rows, LANES), 1)
        out_ref[:, 2 * units :] = jnp.where(
            lane == 0, coarse, jnp.where(lane == 1, shrink - coarse, 0.0)
        ).astype(bf16)

    (sent,) = kernel_call(
        body,
        (*parts, gate, up, inverse),
        [],
        [jax.ShapeDtypeStruct((rows, 2 * units + LANES), bf16)],
        [],
    )
    return sent


def input_grad(blocks, mask, gate_pair, up_pair, grad, hidden, gain_part, in_parts):
    count = len(blocks)
    part_rows = blocks[0].shape[0]
    rows = part_rows * count
    width, units = gate_pair[0].shape
    out_count = count if in_parts else 1

    def body(operand_refs, weight_refs, out_refs, scratch):
        *block_refs, mask_ref, grad_ref, hidden_ref, gain_ref = operand_refs
        *row_refs, sum_ref = out_refs
        joined, shrink = scratch
        join(joined, block_refs, slice(0, 2 * units))
        for index, ref in enumerate(block_refs):
            tail = ref[:, 2 * units :].astype(f32)
            shrink[index * part_rows : (index + 1) * part_rows] = jnp.sum(
                tail, axis=-1, keepdims=True
            )

        gate_own, gate_other, up_own, up_other = weight_refs

        def visit(columns):
            def back_of(gate, up):
                return dot(joined[:, :units], gate[columns], (1, 1)) + dot(
                    joined[:, units:], up[columns], (1, 1)
                )

            back = jnp.where(
                mask_ref[...] > 0.5, back_of(gate_own, up_own), back_of(gate_other, up_other)
            )
            wide = hidden_ref[:, columns].astype(f32)
            sum_ref[:, columns] = jnp.sum(back * wide, axis=0, keepdims=True)
            out = (
                grad_ref[:, columns].astype(f32)
                + back * gain_ref[:, columns]
                - wide * shrink[...]
            ).astype(bf16)
            store_parts(row_refs, columns, out)

        each_tile(width, visit)

    outs = kernel_call(
        body,
        (*blocks, mask, grad, hidden, gain_part),
        (*gate_pair, *up_pair),
        [jax.ShapeDtypeStruct((rows // out_count, width), bf16)] * out_count
        + [jax.ShapeDtypeStruct((1, width), f32)],
        [
            pltpu.VMEM((rows, 2 * units), bf16),
            pltpu.VMEM((rows, 1), f32),
        ],
    )
    return outs[:out_count], outs[out_count]


def body(tokens, cotangent, gain, w_gate, w_up, w_down, route):
    pipe_count = lax.axis_size("pipe")
    dp_count = lax.axis_size("dp")
    section = lax.axis_index("pipe")
    expert = lax.axis_index("expert")
    here = lax.axis_index("dp")
    features = tokens.shape[-1]
    width = features // dp_count
    units = w_gate.shape[-1]
    gain_part = lax.dynamic_slice_in_dim(gain, here * width, width, axis=1)

    groups = (slice(0, dp_count - 1), slice(dp_count - 1, dp_count))
    own_tokens = tokens[0]
    rows = own_tokens.shape[0]
    micro = [(section - k + pipe_count) % pipe_count for k in range(PASSES)]
    route_rows = jnp.stack(
        [lax.dynamic_index_in_dim(route[0, :, :, 0], m, 0, keepdims=False) for m in micro], axis=1
    ).astype(bf16)
    route_rows = jnp.pad(route_rows, ((0, 0), (0, width - PASSES)))

    def tokens_quarter(step):
        return jnp.concatenate([quarter_of(own_tokens, here ^ step, width), route_rows])

    def cotangent_quarter(step, *earlier):
        return quarter_of(after(cotangent[0], *earlier), here ^ step, width)

    def sent(parts):
        return [swap(part, "dp", step) if step else part for step, part in enumerate(parts)]

    def moved(pieces, distance):
        return [shifted(piece, "pipe", distance) for piece in pieces]

    def scale_of(square_sum):
        return lax.rsqrt(square_sum / features + epsilon)

    def weight_grad(left, right, mask, wanted):
        return dot(left, jnp.where((mask > 0.5) == wanted, right, jnp.zeros_like(right)), (0, 0))

    quarters = [tokens_quarter(step) for step in range(dp_count)]
    weights = [
        weight
        for own in (w_gate, w_up, w_down)
        for weight in (own[0, 0], swap(own[0, 0], "expert", 1))
    ]
    weights = resident(weights)
    gate_pair, up_pair, down_pair = weights[:2], weights[2:4], weights[4:]
    quarters[-1] = after(quarters[-1], *weights)
    blocks = sent(quarters)
    expert_id = jnp.full((1, LANES), expert, f32)
    wide = own_tokens.astype(f32)
    inverse = scale_of(jnp.sum(wide * wide, axis=-1, keepdims=True))

    parts, gained, masks, hidden = [], [], [], []
    for group in groups:
        made, scaled, (*choices, joined) = hidden_parts(
            blocks[group], rows, gain_part, None, gate_pair, up_pair, expert_id
        )
        parts += made
        gained.append(scaled)
        masks.append(choices)
        hidden.append(joined)
    masks = list(zip(*masks))
    gate, up, activated = activate(sent(parts), inverse)
    kept = [(hidden, gained, inverse, gate, up)]
    first_activated = gather_rows(activated, dp_count)
    next_hidden, squares = [], []
    for group, mask, rows_in in zip(groups, masks[0], hidden):
        (out,), square = add_down(first_activated[group], mask, down_pair, rows_in, False)
        next_hidden.append(out)
        squares += jnp.split(square, square.shape[0] // rows)
    hidden = moved(next_hidden, 1)
    grad_blocks = sent([cotangent_quarter(step, *next_hidden) for step in range(dp_count)])
    inverse = shifted(scale_of(sum_parts(squares)), "pipe", 1)
    act_parts, grad = [], []
    for group, mask in zip(groups, masks[1]):
        made, joined = act_grad_parts(grad_blocks[group], rows, mask, down_pair)
        act_parts += made
        grad.append(joined)
    act_parts = sent(act_parts)
    hidden[0] = after(hidden[0], inverse, *act_parts[1:-1])

    parts, gained = [], []
    for rows_in, mask in zip(hidden, masks[1]):
        made, scaled, _ = hidden_parts([rows_in], rows, gain_part, mask, gate_pair, up_pair)
        parts += made
        gained.append(scaled)
    gate, up, activated = activate(sent(parts), inverse)
    kept.append((hidden, gained, inverse, gate, up))

    gain_sum = jnp.zeros((1, width), f32)
    for k in reversed(range(PASSES)):
        hidden, gained, inverse, gate, up = kept[k]
        gained = jnp.concatenate(gained)
        mask = jnp.concatenate(masks[k])
        payload = hidden_grads(act_parts, gate, up, inverse, features)
        both_grad = gather_rows(payload, dp_count)
        joined = jnp.concatenate(both_grad)
        rights = [joined[:, :units], joined[:, units : 2 * units]]
        if k == 0:
            late_down = jnp.concatenate(first_activated)
            grad_now = jnp.concatenate(grad)
            other_down = swap(
                (
                    weight_grad(late_down, grad_now, mask, False) + early[False][2].astype(f32)
                ).astype(bf16),
                "expert",
                1,
            )
            down_grad = (
                weight_grad(late_down, grad_now, mask, True)
                + early[True][2].astype(f32)
                + other_down.astype(f32)
            ).astype(bf16)
            both_grad[1] = after(both_grad[1], down_grad)
            received = [
                swap(
                    (weight_grad(gained, right, mask, False) + soon.astype(f32)).astype(bf16),
                    "expert",
                    1,
                )
                for right, soon in zip(rights, early[False])
            ]
        else:
            last_activated = gather_rows(after(activated, *both_grad[1:]), dp_count)
        outs = []
        for group, choice, rows_in, grad_in in zip(groups, masks[k], hidden, grad):
            made, gain_term = input_grad(
                both_grad[group], choice, gate_pair, up_pair, grad_in, rows_in, gain_part, k == 0
            )
            outs += made
            gain_sum = gain_sum + gain_term
        if k > 0:
            last_grad = jnp.concatenate(grad)
            grad = moved(outs, -1)
            rights = [after(right, *outs) for right in rights]
            early = {
                wanted: [weight_grad(gained, right, mask, wanted).astype(bf16) for right in rights]
                for wanted in (False, True)
            }
            out_parts = []
            for group, choice, rows_in in zip(groups, masks[1], hidden):
                made, _ = add_down(last_activated[group], choice, down_pair, rows_in, True)
                out_parts += made
            out_rows = from_quarters(out_parts)
            grad[0] = after(grad[0], out_rows, *early[False], *early[True])
            act_parts, joined = [], []
            for rows_in, choice in zip(grad, masks[0]):
                made, copied = act_grad_parts([rows_in], rows, choice, down_pair)
                act_parts += made
                joined.append(copied)
            grad = joined
            last_activated = jnp.concatenate(last_activated)
            for wanted in (False, True):
                early[wanted].append(
                    weight_grad(last_activated, last_grad, mask, wanted).astype(bf16)
                )
            act_parts = sent(act_parts)
            act_parts[1] = after(act_parts[1], early[False][2], early[True][2])

    returned = sent(outs)
    rights = [after(right, *outs) for right in rights]
    gain_rows = jnp.concatenate(gather_rows(after(gain_sum, *received), dp_count))
    gain_rows = gain_rows + swap(gain_rows, "expert", 1)
    gain_all = jnp.zeros((features,), f32)
    for step in range(dp_count):
        gain_all = lax.dynamic_update_slice_in_dim(
            gain_all, gain_rows[step], (here ^ step) * width, axis=0
        )
    grads = [
        (
            weight_grad(gained, right, mask, True) + soon.astype(f32) + other.astype(f32)
        ).astype(bf16)
        for right, soon, other in zip(rights, early[True], received)
    ] + [down_grad]
    returned = list(lax.optimization_barrier((*returned, *grads)))[:dp_count]
    entry = assemble(returned)
    return (
        out_rows[None],
        entry[None],
        gain_all[None],
        grads[0][None, None],
        grads[1][None, None],
        grads[2][None, None],
    )


def start_shifted(block, axis, distance):
    devices = range(lax.axis_size(axis))
    route = [((i - distance) % len(devices), i) for i in devices]
    return lax.ppermute(block, axis, route)


def start_contract_last(former, latter):
    return lax.dot_general(
        former, latter, (((1,), (1,)), ((), ())), preferred_element_type=jnp.float32
    )


def start_contract_first(former, latter):
    return lax.dot_general(
        former, latter, (((0,), (0,)), ((), ())), preferred_element_type=jnp.float32
    )


def start_normalize(hidden, gain_row):
    widened = hidden.astype(jnp.float32)
    inverse = lax.rsqrt(jnp.mean(widened * widened, axis=-1, keepdims=True) + epsilon)
    scaled = widened * inverse
    return ((scaled * gain_row).astype(jnp.bfloat16), scaled, inverse)


def start_slot_matrix(route_now, expert_count, capacity):
    tile_count = route_now.shape[0]
    expert_ids = jnp.arange(expert_count, dtype=jnp.int32)
    member = (route_now[None, :] == expert_ids[:, None]).astype(jnp.int32)
    earlier = jnp.cumsum(member, axis=1) - member
    rank_ids = jnp.arange(capacity, dtype=jnp.int32)
    placed = member[:, None, :] * (earlier[:, None, :] == rank_ids[None, :, None]).astype(jnp.int32)
    return placed.reshape(expert_count * capacity, tile_count)


def start_into_slots(placed, rows, tile_rows, dp_count):
    width = rows.shape[-1]
    tile_blocks = rows.reshape(placed.shape[1], tile_rows, dp_count, width // dp_count)
    return jnp.einsum(
        "st,trqd->qsrd",
        placed.astype(jnp.bfloat16),
        tile_blocks,
        preferred_element_type=jnp.float32,
    ).astype(jnp.bfloat16)


def start_from_slots(placed, slot_rows):
    merged = jnp.einsum(
        "st,qsrd->trqd", placed.astype(jnp.bfloat16), slot_rows, preferred_element_type=jnp.float32
    ).astype(jnp.bfloat16)
    return merged.reshape(merged.shape[0] * merged.shape[1], -1)


def start_send_out(slot_rows):
    quarter = slot_rows.shape[-1]
    flat = slot_rows.reshape((-1,) + slot_rows.shape[2:])
    arrived = lax.all_to_all(flat, ("dp", "expert"), split_axis=0, concat_axis=0, tiled=True)
    return arrived.reshape(-1, quarter)


def start_send_back(part_rows, dp_count, tile_rows):
    quarter = part_rows.shape[-1]
    flat = part_rows.reshape(-1, tile_rows, quarter)
    returned = lax.all_to_all(flat, ("dp", "expert"), split_axis=0, concat_axis=0, tiled=True)
    return returned.reshape(dp_count, -1, tile_rows, quarter)


def start_widen_rounded(values):
    return lax.optimization_barrier(values.astype(jnp.bfloat16)).astype(jnp.float32)


def start_expert_forward(received, gate_weight, up_weight, down_weight):
    gate_terms = start_widen_rounded(jnp.dot(received, gate_weight, preferred_element_type=jnp.float32))
    up_terms = start_widen_rounded(jnp.dot(received, up_weight, preferred_element_type=jnp.float32))
    gate_pre, up_pre = (
        lax.psum(gate_terms.astype(jnp.bfloat16), "dp").astype(jnp.float32),
        lax.psum(up_terms.astype(jnp.bfloat16), "dp").astype(jnp.float32),
    )
    activated = (jax.nn.silu(gate_pre) * up_pre).astype(jnp.bfloat16)
    part_rows = jnp.dot(activated, down_weight, preferred_element_type=jnp.float32).astype(
        jnp.bfloat16
    )
    return (part_rows, (gate_pre, up_pre, activated))


def start_expert_backward(
    received, grad_recv, kept_state, gate_weight, up_weight, down_weight, grad_sums
):
    gate_pre, up_pre, activated = kept_state
    grad_terms = start_widen_rounded(start_contract_last(grad_recv, down_weight))
    grad_act = lax.psum(grad_terms.astype(jnp.bfloat16), "dp").astype(jnp.float32)
    sigmoid_gate = jax.nn.sigmoid(gate_pre)
    silu_gate = gate_pre * sigmoid_gate
    grad_gate_pre = (
        grad_act * up_pre * sigmoid_gate * (1.0 + gate_pre * (1.0 - sigmoid_gate))
    ).astype(jnp.bfloat16)
    grad_up_pre = (grad_act * silu_gate).astype(jnp.bfloat16)
    back_rows = (
        start_contract_last(grad_gate_pre, gate_weight) + start_contract_last(grad_up_pre, up_weight)
    ).astype(jnp.bfloat16)
    grad_gate = grad_sums[0] + start_contract_first(received, grad_gate_pre)
    grad_up = grad_sums[1] + start_contract_first(received, grad_up_pre)
    grad_down = grad_sums[2] + start_contract_first(activated, grad_recv)
    return (back_rows, (grad_gate, grad_up, grad_down))


def start_body(tokens, cotangent, gain, w_gate, w_up, w_down, route):
    pipe_count = lax.axis_size("pipe")
    dp_count = lax.axis_size("dp")
    expert_count = lax.axis_size("expert")
    section_index = lax.axis_index("pipe")
    gain_row = gain[0]
    gate_weight = w_gate[0, 0]
    up_weight = w_up[0, 0]
    down_weight = w_down[0, 0]
    route_table = route[0, :, :, 0]
    tile_count = route_table.shape[1]
    capacity = max(2, 3 * tile_count // (2 * expert_count))
    hidden = tokens[0]
    saved_ticks = []
    out_rows = hidden
    for pass_index in range(PASSES):
        micro_index = (section_index - pass_index + pipe_count) % pipe_count
        route_now = lax.dynamic_index_in_dim(route_table, micro_index, 0, keepdims=False)
        placed = start_slot_matrix(route_now, expert_count, capacity)
        normed, scaled, inverse = start_normalize(hidden, gain_row)
        received = start_send_out(start_into_slots(placed, normed, TILE, dp_count))
        part_rows, kept_state = start_expert_forward(received, gate_weight, up_weight, down_weight)
        ffn_rows = start_from_slots(placed, start_send_back(part_rows, dp_count, TILE))
        new_hidden = (hidden.astype(jnp.float32) + ffn_rows.astype(jnp.float32)).astype(
            jnp.bfloat16
        )
        saved_ticks.append((placed, scaled, inverse, received, kept_state))
        if pass_index + 1 < PASSES:
            hidden = start_shifted(new_hidden, "pipe", 1)
        else:
            out_rows = new_hidden
    grad_rows = cotangent[0]
    grad_sums = (
        jnp.zeros(gate_weight.shape, jnp.float32),
        jnp.zeros(up_weight.shape, jnp.float32),
        jnp.zeros(down_weight.shape, jnp.float32),
    )
    gain_sum = jnp.zeros(gain_row.shape, jnp.float32)
    entry_grad = grad_rows
    for pass_index in reversed(range(PASSES)):
        placed, scaled, inverse, received, kept_state = saved_ticks[pass_index]
        grad_recv = start_send_out(start_into_slots(placed, grad_rows, TILE, dp_count))
        back_rows, grad_sums = start_expert_backward(
            received, grad_recv, kept_state, gate_weight, up_weight, down_weight, grad_sums
        )
        grad_normed = start_from_slots(placed, start_send_back(back_rows, dp_count, TILE)).astype(jnp.float32)
        gain_sum = gain_sum + jnp.sum(grad_normed * scaled, axis=0)
        grad_scaled = grad_normed * gain_row
        grad_wide = inverse * (
            grad_scaled - scaled * jnp.mean(grad_scaled * scaled, axis=-1, keepdims=True)
        )
        grad_in = (grad_rows.astype(jnp.float32) + grad_wide).astype(jnp.bfloat16)
        if pass_index > 0:
            grad_rows = start_shifted(grad_in, "pipe", -1)
        else:
            entry_grad = grad_in
    gain_total = lax.psum(gain_sum, ("dp", "expert"))
    return (
        out_rows[None],
        entry_grad[None],
        gain_total[None],
        grad_sums[0].astype(jnp.bfloat16)[None, None],
        grad_sums[1].astype(jnp.bfloat16)[None, None],
        grad_sums[2].astype(jnp.bfloat16)[None, None],
    )


def start_solution(mesh):
    placed = (
        P("pipe", ("dp", "expert"), None),
        P("pipe", ("dp", "expert"), None),
        P("pipe", None),
        P("pipe", "expert", "dp", None),
        P("pipe", "expert", "dp", None),
        P("pipe", "expert", None, "dp"),
        P("pipe", None, ("dp", "expert"), None),
    )
    return jax.shard_map(
        start_body,
        mesh=mesh,
        in_specs=placed,
        out_specs=(
            P("pipe", ("dp", "expert"), None),
            P("pipe", ("dp", "expert"), None),
            P("pipe", None),
            P("pipe", "expert", "dp", None),
            P("pipe", "expert", "dp", None),
            P("pipe", "expert", None, "dp"),
        ),
        check_vma=False,
    )


def solution(mesh):
    if mesh.shape["expert"] != PAIR:
        return start_solution(mesh)
    placed = (
        P("pipe", ("dp", "expert"), None),
        P("pipe", ("dp", "expert"), None),
        P("pipe", None),
        P("pipe", "expert", "dp", None),
        P("pipe", "expert", "dp", None),
        P("pipe", "expert", None, "dp"),
        P("pipe", None, ("dp", "expert"), None),
    )
    return jax.shard_map(
        body,
        mesh=mesh,
        in_specs=placed,
        out_specs=placed[:2] + (P("pipe", None),) + placed[3:6],
        check_vma=False,
    )
```

```python
import jax
import jax.numpy as jnp
from jax import lax
from jax.experimental import pallas as pl
from jax.experimental.pallas import tpu as pltpu
from jax.sharding import PartitionSpec as P

TILE = 8
PASSES = 2
PAIR = 2
COLUMNS = 256
LANES = 128
VMEM_BYTES = 12 * 1024 * 1024


epsilon = 1e-06
bf16 = jnp.bfloat16
f32 = jnp.float32


def dot(former, latter, contract):
    return lax.dot_general(
        former, latter, ((contract[:1], contract[1:]), ((), ())), preferred_element_type=f32
    )


def partner_route(size, step):
    return [(i, i ^ step) for i in range(size)]


def swap(block, axis, step):
    return lax.ppermute(block, axis, partner_route(lax.axis_size(axis), step))


def shifted(block, axis, distance):
    size = lax.axis_size(axis)
    return lax.ppermute(block, axis, [(i, (i + distance) % size) for i in range(size)])


def quarter_of(rows, index, width):
    return lax.dynamic_slice_in_dim(rows, index * width, width, axis=-1)


def assemble(parts):
    here = lax.axis_index("dp")
    rows, width = parts[0].shape
    whole = jnp.zeros((rows, width * len(parts)), parts[0].dtype)
    for step, part in enumerate(parts):
        whole = lax.dynamic_update_slice_in_dim(whole, part, (here ^ step) * width, axis=1)
    return whole


def from_quarters(parts):
    return assemble(
        [swap(part, "dp", step) if step else part for step, part in enumerate(parts)]
    )


def gather_rows(rows, dp_count):
    return [rows] + [swap(rows, "dp", step) for step in range(1, dp_count)]


def after(value, *earlier):
    return lax.optimization_barrier((value,) + earlier)[0]


def columns_of(extent):
    return COLUMNS if extent % COLUMNS == 0 else extent


def kernel_call(body, operands, weights, out_shape, scratch):
    count, kept, made = len(operands), len(weights), len(out_shape)

    def call(*refs):
        operand_refs, refs = refs[:count], refs[count:]
        weight_refs, refs = refs[:kept], refs[kept:]
        body(operand_refs, weight_refs, refs[:made], refs[made:])

    in_vmem = pl.BlockSpec(memory_space=pltpu.VMEM)
    return pl.pallas_call(
        call,
        in_specs=[in_vmem] * (count + kept),
        out_specs=[in_vmem] * made,
        out_shape=out_shape,
        scratch_shapes=scratch,
        compiler_params=pltpu.CompilerParams(vmem_limit_bytes=VMEM_BYTES),
        cost_estimate=pl.CostEstimate(flops=0, bytes_accessed=0, transcendentals=0),
    )(*operands, *weights)


def resident(arrays):
    count = len(arrays)

    def call(*refs):
        arrivals = refs[-1]
        copies = [
            pltpu.make_async_copy(refs[i], refs[count + i], arrivals.at[i]) for i in range(count)
        ]
        for copy in copies:
            copy.start()
        for copy in copies:
            copy.wait()

    return pl.pallas_call(
        call,
        in_specs=[pl.BlockSpec(memory_space=pltpu.HBM)] * count,
        out_specs=[pl.BlockSpec(memory_space=pltpu.VMEM)] * count,
        out_shape=[pltpu.VMEM(a.shape, a.dtype) for a in arrays],
        scratch_shapes=[pltpu.SemaphoreType.DMA((count,))],
        compiler_params=pltpu.CompilerParams(vmem_limit_bytes=VMEM_BYTES),
        cost_estimate=pl.CostEstimate(
            flops=0,
            bytes_accessed=2 * sum(a.size * a.dtype.itemsize for a in arrays),
            transcendentals=0,
        ),
    )(*(pltpu.with_memory_space_constraint(a, pltpu.HBM) for a in arrays))


def store_parts(refs, columns, value):
    size = value.shape[0] // len(refs)
    for index, ref in enumerate(refs):
        ref[:, columns] = value[index * size : (index + 1) * size]


def each_tile(extent, visit):
    tile = columns_of(extent)

    def step(j, carry):
        visit(span(j, tile))
        return carry

    lax.fori_loop(0, extent // tile, step, 0)


def span(tile, size):
    return pl.ds(pl.multiple_of(tile * size, size), size)


def split_rows(rows_ref, mask_ref, other_ref, own_ref):
    rows = rows_ref[...]
    chosen = mask_ref[...] > 0.5
    own_ref[...] = jnp.where(chosen, rows, jnp.zeros_like(rows))
    other_ref[...] = jnp.where(chosen, jnp.zeros_like(rows), rows)


def hidden_parts(blocks, part_rows, gain_part, mask, gate_pair, up_pair, expert=None):
    width, units = gate_pair[0].shape
    routed = expert is not None
    block_rows = part_rows if routed else blocks[0].shape[0]
    rows = block_rows * len(blocks)
    parts_count = rows // part_rows
    passes = PASSES if routed else 0

    def body(operand_refs, weight_refs, out_refs, scratch):
        *block_refs, gain_ref, choice_ref = operand_refs
        part_refs, (other_rows, own_rows) = out_refs[:parts_count], out_refs[parts_count:][:2]
        mask_ref = out_refs[parts_count + 2] if routed else choice_ref
        (gained_ref,) = scratch
        for index, ref in enumerate(block_refs):
            place = slice(index * block_rows, (index + 1) * block_rows)
            block = ref[:block_rows]
            gained_ref[place] = (block.astype(f32) * gain_ref[...]).astype(bf16)
            if routed:
                out_refs[-1][place] = block
                tiles = block_rows // TILE
                row = lax.broadcasted_iota(jnp.int32, (block_rows, tiles), 0)
                first = TILE * lax.broadcasted_iota(jnp.int32, (block_rows, tiles), 1)
                chosen = ((row >= first) & (row < first + TILE)).astype(bf16)
                experts = dot(chosen, ref[block_rows:, :LANES], (1, 0)) - choice_ref[...]
                for k in range(passes):
                    near = jnp.abs(experts[:, k : k + 1]) < 0.5
                    out_refs[parts_count + 2 + k][place] = jnp.where(near, 1.0, 0.0)

        split_rows(gained_ref, mask_ref, other_rows, own_rows)
        for pair in range(2):

            def visit(columns, pair=pair):
                own, other = weight_refs[2 * pair : 2 * pair + 2]
                part = jnp.where(
                    mask_ref[...] > 0.5,
                    dot(gained_ref[...], own[:, columns], (1, 0)),
                    dot(gained_ref[...], other[:, columns], (1, 0)),
                ).astype(bf16)
                store_parts([ref.at[:, pair * units :] for ref in part_refs], columns, part)

            each_tile(units, visit)

    outs = kernel_call(
        body,
        (*blocks, gain_part, expert if routed else mask),
        (*gate_pair, *up_pair),
        [jax.ShapeDtypeStruct((part_rows, 2 * units), bf16)] * parts_count
        + [jax.ShapeDtypeStruct((rows, width), bf16)] * 2
        + [jax.ShapeDtypeStruct((rows, 1), f32)] * passes
        + [jax.ShapeDtypeStruct((rows, width), bf16)] * int(routed),
        [pltpu.VMEM((rows, width), bf16)],
    )
    return outs[:parts_count], outs[parts_count : parts_count + 2], outs[parts_count + 2 :]


def row_scale(blocks, features, summed):
    rows = blocks[0].shape[0]

    def body(operand_refs, weight_refs, out_refs, scratch):
        total = jnp.zeros((rows, 1), f32)
        for ref in operand_refs:
            wide = ref[...].astype(f32)
            if not summed:
                wide = jnp.sum(wide * wide, axis=-1, keepdims=True)
            total = total + wide
        out_refs[0][...] = lax.rsqrt(total / features + epsilon)

    (scale,) = kernel_call(body, blocks, (), [jax.ShapeDtypeStruct((rows, 1), f32)], [])
    return scale


def activate(parts, inverse):
    rows, both = parts[0].shape
    units = both // 2

    def body(operand_refs, weight_refs, out_refs, scratch):
        *part_refs, inverse_ref = operand_refs
        total = part_refs[0][...].astype(f32)
        for ref in part_refs[1:]:
            total = total + ref[...].astype(f32)
        total = total * inverse_ref[...]
        gate, up = total[:, :units], total[:, units:]
        out_refs[0][...] = gate
        out_refs[1][...] = up
        out_refs[2][...] = (gate / (1.0 + jnp.exp(-gate)) * up).astype(bf16)

    return kernel_call(
        body,
        (*parts, inverse),
        (),
        [jax.ShapeDtypeStruct((rows, units), f32)] * 2
        + [jax.ShapeDtypeStruct((rows, units), bf16)],
        [],
    )


def join(joined, refs, columns):
    size = refs[0].shape[0]
    for index, ref in enumerate(refs):
        joined[index * size : (index + 1) * size] = ref[:, columns]


def add_down(blocks, mask, down_pair, hidden, in_parts):
    count = len(blocks)
    part_rows, units = blocks[0].shape
    rows = part_rows * count
    width = down_pair[0].shape[1]
    out_count = count if in_parts else 1

    def body(operand_refs, weight_refs, out_refs, scratch):
        *block_refs, mask_ref, hidden_ref = operand_refs
        row_refs, square_refs = out_refs[:out_count], out_refs[out_count:-2]
        joined, square_ref = scratch
        join(joined, block_refs, slice(None))
        split_rows(joined, mask_ref, *out_refs[-2:])
        square_ref[...] = jnp.zeros_like(square_ref)
        own, other = weight_refs

        def visit(columns):
            ffn = jnp.where(
                mask_ref[...] > 0.5,
                dot(joined[...], own[:, columns], (1, 0)),
                dot(joined[...], other[:, columns], (1, 0)),
            ).astype(bf16)
            out = (hidden_ref[:, columns].astype(f32) + ffn.astype(f32)).astype(bf16)
            wide = out.astype(f32)
            square_ref[...] += jnp.sum(wide * wide, axis=-1, keepdims=True)
            store_parts(row_refs, columns, out)

        each_tile(width, visit)
        store_parts(square_refs, slice(None), square_ref[...])

    outs = kernel_call(
        body,
        (*blocks, mask, hidden),
        down_pair,
        [jax.ShapeDtypeStruct((rows // out_count, width), bf16)] * out_count
        + [jax.ShapeDtypeStruct((part_rows, 1), f32)] * count
        + [jax.ShapeDtypeStruct((rows, units), bf16)] * 2,
        [pltpu.VMEM((rows, units), bf16), pltpu.VMEM((rows, 1), f32)],
    )
    return outs[:out_count], outs[out_count:-2], outs[-2:]


def act_grad_parts(blocks, part_rows, mask, down_pair):
    rows = sum(block.shape[0] for block in blocks)
    parts_count = rows // part_rows
    units, width = down_pair[0].shape

    def body(operand_refs, weight_refs, out_refs, scratch):
        *block_refs, mask_ref = operand_refs
        *part_refs, grad_ref = out_refs
        own, other = weight_refs
        join(grad_ref, block_refs, slice(None))

        def visit(columns):
            part = jnp.where(
                mask_ref[...] > 0.5,
                dot(grad_ref[...], own[columns], (1, 1)),
                dot(grad_ref[...], other[columns], (1, 1)),
            ).astype(bf16)
            store_parts(part_refs, columns, part)

        each_tile(units, visit)

    outs = kernel_call(
        body,
        (*blocks, mask),
        down_pair,
        [jax.ShapeDtypeStruct((part_rows, units), bf16)] * parts_count
        + [jax.ShapeDtypeStruct((rows, width), bf16)],
        [],
    )
    return outs[:parts_count], outs[parts_count]


def hidden_grads(parts, gate, up, inverse, features):
    rows, units = gate.shape

    def body(operand_refs, weight_refs, out_refs, scratch):
        *part_refs, gate_ref, up_ref, inverse_ref = operand_refs
        (out_ref,) = out_refs
        grad_act = part_refs[0][...].astype(f32)
        for ref in part_refs[1:]:
            grad_act = grad_act + ref[...].astype(f32)
        gate_now, up_now, scale = gate_ref[...], up_ref[...], inverse_ref[...]
        sigmoid = 1.0 / (1.0 + jnp.exp(-gate_now))
        scaled = grad_act * scale
        gate_grad = scaled * up_now * sigmoid * (1.0 + gate_now * (1.0 - sigmoid))
        up_grad = scaled * (gate_now * sigmoid)
        shrink = jnp.sum(gate_grad * gate_now + up_grad * up_now, axis=-1, keepdims=True) * (
            scale / features
        )
        out_ref[:, :units] = gate_grad.astype(bf16)
        out_ref[:, units : 2 * units] = up_grad.astype(bf16)
        coarse = shrink.astype(bf16).astype(f32)
        lane = lax.broadcasted_iota(jnp.int32, (rows, LANES), 1)
        out_ref[:, 2 * units :] = jnp.where(
            lane == 0, coarse, jnp.where(lane == 1, shrink - coarse, 0.0)
        ).astype(bf16)

    (sent,) = kernel_call(
        body,
        (*parts, gate, up, inverse),
        [],
        [jax.ShapeDtypeStruct((rows, 2 * units + LANES), bf16)],
        [],
    )
    return sent


def input_grad(blocks, mask, gate_pair, up_pair, grad, hidden, gain_part, in_parts):
    count = len(blocks)
    part_rows = blocks[0].shape[0]
    rows = part_rows * count
    width, units = gate_pair[0].shape
    out_count = count if in_parts else 1

    def body(operand_refs, weight_refs, out_refs, scratch):
        *block_refs, mask_ref, grad_ref, hidden_ref, gain_ref = operand_refs
        *row_refs, sum_ref = out_refs
        joined, shrink = scratch
        join(joined, block_refs, slice(0, 2 * units))
        for index, ref in enumerate(block_refs):
            tail = ref[:, 2 * units :].astype(f32)
            shrink[index * part_rows : (index + 1) * part_rows] = jnp.sum(
                tail, axis=-1, keepdims=True
            )

        gate_own, gate_other, up_own, up_other = weight_refs

        def visit(columns):
            def back_of(gate, up):
                return dot(joined[:, :units], gate[columns], (1, 1)) + dot(
                    joined[:, units:], up[columns], (1, 1)
                )

            back = jnp.where(
                mask_ref[...] > 0.5, back_of(gate_own, up_own), back_of(gate_other, up_other)
            )
            wide = hidden_ref[:, columns].astype(f32)
            sum_ref[:, columns] = jnp.sum(back * wide, axis=0, keepdims=True)
            out = (
                grad_ref[:, columns].astype(f32)
                + back * gain_ref[:, columns]
                - wide * shrink[...]
            ).astype(bf16)
            store_parts(row_refs, columns, out)

        each_tile(width, visit)

    outs = kernel_call(
        body,
        (*blocks, mask, grad, hidden, gain_part),
        (*gate_pair, *up_pair),
        [jax.ShapeDtypeStruct((rows // out_count, width), bf16)] * out_count
        + [jax.ShapeDtypeStruct((1, width), f32)],
        [
            pltpu.VMEM((rows, 2 * units), bf16),
            pltpu.VMEM((rows, 1), f32),
        ],
    )
    return outs[:out_count], outs[out_count]


def body(tokens, cotangent, gain, w_gate, w_up, w_down, route):
    pipe_count = lax.axis_size("pipe")
    dp_count = lax.axis_size("dp")
    section = lax.axis_index("pipe")
    expert = lax.axis_index("expert")
    here = lax.axis_index("dp")
    features = tokens.shape[-1]
    width = features // dp_count
    units = w_gate.shape[-1]
    gain_part = lax.dynamic_slice_in_dim(gain, here * width, width, axis=1)

    groups = (slice(0, dp_count - 1), slice(dp_count - 1, dp_count))
    own_tokens = tokens[0]
    rows = own_tokens.shape[0]
    micro = [(section - k + pipe_count) % pipe_count for k in range(PASSES)]
    route_rows = jnp.stack(
        [lax.dynamic_index_in_dim(route[0, :, :, 0], m, 0, keepdims=False) for m in micro], axis=1
    ).astype(bf16)
    expert_id = jnp.full((1, LANES), expert, f32)
    route_rows = after(jnp.pad(route_rows, ((0, 0), (0, width - PASSES))), expert_id)

    def tokens_quarter(step):
        return jnp.concatenate([quarter_of(own_tokens, here ^ step, width), route_rows])

    def cotangent_quarter(step, *earlier):
        return quarter_of(after(cotangent[0], *earlier), here ^ step, width)

    def sent(parts):
        return [swap(part, "dp", step) if step else part for step, part in enumerate(parts)]

    def moved(pieces, distance):
        return [shifted(piece, "pipe", distance) for piece in pieces]

    def weight_grad(lefts, right, wanted):
        return dot(lefts[wanted], right, (0, 0))

    def stacked(pairs):
        return [jnp.concatenate(pieces) for pieces in zip(*pairs)]

    quarters = [tokens_quarter(step) for step in range(dp_count)]
    weights = [
        weight
        for own in (w_gate, w_up, w_down)
        for weight in (own[0, 0], swap(own[0, 0], "expert", 1))
    ]
    weights = resident(weights)
    gate_pair, up_pair, down_pair = weights[:2], weights[2:4], weights[4:]
    quarters[-1] = after(quarters[-1], *weights)
    blocks = sent(quarters)
    inverse = row_scale([own_tokens], features, False)

    parts, gained, masks, hidden = [], [], [], []
    for group in groups:
        made, scaled, (*choices, joined) = hidden_parts(
            blocks[group], rows, gain_part, None, gate_pair, up_pair, expert_id
        )
        parts += made
        gained.append(scaled)
        masks.append(choices)
        hidden.append(joined)
    masks = list(zip(*masks))
    gate, up, activated = activate(sent(parts), inverse)
    kept = [(hidden, gained, inverse, gate, up)]
    first_activated = gather_rows(activated, dp_count)
    next_hidden, squares, first_rows = [], [], []
    for group, mask, rows_in in zip(groups, masks[0], hidden):
        (out,), square, split = add_down(
            first_activated[group], mask, down_pair, rows_in, False
        )
        next_hidden.append(out)
        squares += square
        first_rows.append(split)
    hidden = moved(next_hidden, 1)
    grad_blocks = sent([cotangent_quarter(step, *next_hidden) for step in range(dp_count)])
    inverse = shifted(row_scale(sent(squares), features, True), "pipe", 1)
    act_parts, grad = [], []
    for group, mask in zip(groups, masks[1]):
        made, joined = act_grad_parts(grad_blocks[group], rows, mask, down_pair)
        act_parts += made
        grad.append(joined)
    act_parts = sent(act_parts)
    hidden[0] = after(hidden[0], inverse, *act_parts[1:-1])

    parts, gained = [], []
    for rows_in, mask in zip(hidden, masks[1]):
        made, scaled, _ = hidden_parts([rows_in], rows, gain_part, mask, gate_pair, up_pair)
        parts += made
        gained.append(scaled)
    gate, up, activated = activate(sent(parts), inverse)
    kept.append((hidden, gained, inverse, gate, up))

    gain_sum = jnp.zeros((1, width), f32)
    for k in reversed(range(PASSES)):
        hidden, gained, inverse, gate, up = kept[k]
        gained = stacked(gained)
        payload = hidden_grads(act_parts, gate, up, inverse, features)
        both_grad = gather_rows(payload, dp_count)
        joined = jnp.concatenate(both_grad)
        rights = [joined[:, :units], joined[:, units : 2 * units]]
        if k == 0:
            lefts = [gained, gained, stacked(first_rows)]
            rights.append(jnp.concatenate(grad))
            given = [
                (weight_grad(left, right, False) + soon.astype(f32)).astype(bf16)
                for left, right, soon in zip(lefts, rights, early[False])
            ]
            both_grad[1] = after(both_grad[1], given[2])
            received = [swap(value, "expert", 1) for value in given]
        else:
            last_activated = gather_rows(after(activated, *both_grad[1:]), dp_count)
        outs = []
        for group, choice, rows_in, grad_in in zip(groups, masks[k], hidden, grad):
            made, gain_term = input_grad(
                both_grad[group], choice, gate_pair, up_pair, grad_in, rows_in, gain_part, k == 0
            )
            outs += made
            gain_sum = gain_sum + gain_term
        if k > 0:
            last_grad = jnp.concatenate(grad)
            grad = moved(outs, -1)
            rights = [after(right, *outs) for right in rights]
            early = {
                wanted: [weight_grad(gained, right, wanted).astype(bf16) for right in rights]
                for wanted in (False, True)
            }
            out_parts, last_rows = [], []
            for group, choice, rows_in in zip(groups, masks[1], hidden):
                made, _, split = add_down(
                    last_activated[group], choice, down_pair, rows_in, True
                )
                out_parts += made
                last_rows.append(split)
            out_rows = from_quarters(out_parts)
            grad[0] = after(grad[0], out_rows, *early[False], *early[True])
            act_parts, joined = [], []
            for rows_in, choice in zip(grad, masks[0]):
                made, copied = act_grad_parts([rows_in], rows, choice, down_pair)
                act_parts += made
                joined.append(copied)
            grad = joined
            last_rows = stacked(last_rows)
            for wanted in (False, True):
                early[wanted].append(weight_grad(last_rows, last_grad, wanted).astype(bf16))
            act_parts = sent(act_parts)
            act_parts[1] = after(act_parts[1], early[False][2], early[True][2])

    returned = sent(outs)
    rights = [after(right, *outs) for right in rights]
    gain_rows = jnp.concatenate(gather_rows(after(gain_sum, *received), dp_count))
    gain_rows = gain_rows + swap(gain_rows, "expert", 1)
    gain_all = jnp.zeros((features,), f32)
    for step in range(dp_count):
        gain_all = lax.dynamic_update_slice_in_dim(
            gain_all, gain_rows[step], (here ^ step) * width, axis=0
        )
    grads = [
        (weight_grad(left, right, True) + soon.astype(f32) + other.astype(f32)).astype(bf16)
        for left, right, soon, other in zip(lefts, rights, early[True], received)
    ]
    returned = list(lax.optimization_barrier((*returned, *grads)))[:dp_count]
    entry = assemble(returned)
    return (
        out_rows[None],
        entry[None],
        gain_all[None],
        grads[0][None, None],
        grads[1][None, None],
        grads[2][None, None],
    )


def start_shifted(block, axis, distance):
    devices = range(lax.axis_size(axis))
    route = [((i - distance) % len(devices), i) for i in devices]
    return lax.ppermute(block, axis, route)


def start_contract_last(former, latter):
    return lax.dot_general(
        former, latter, (((1,), (1,)), ((), ())), preferred_element_type=jnp.float32
    )


def start_contract_first(former, latter):
    return lax.dot_general(
        former, latter, (((0,), (0,)), ((), ())), preferred_element_type=jnp.float32
    )


def start_normalize(hidden, gain_row):
    widened = hidden.astype(jnp.float32)
    inverse = lax.rsqrt(jnp.mean(widened * widened, axis=-1, keepdims=True) + epsilon)
    scaled = widened * inverse
    return ((scaled * gain_row).astype(jnp.bfloat16), scaled, inverse)


def start_slot_matrix(route_now, expert_count, capacity):
    tile_count = route_now.shape[0]
    expert_ids = jnp.arange(expert_count, dtype=jnp.int32)
    member = (route_now[None, :] == expert_ids[:, None]).astype(jnp.int32)
    earlier = jnp.cumsum(member, axis=1) - member
    rank_ids = jnp.arange(capacity, dtype=jnp.int32)
    placed = member[:, None, :] * (earlier[:, None, :] == rank_ids[None, :, None]).astype(jnp.int32)
    return placed.reshape(expert_count * capacity, tile_count)


def start_into_slots(placed, rows, tile_rows, dp_count):
    width = rows.shape[-1]
    tile_blocks = rows.reshape(placed.shape[1], tile_rows, dp_count, width // dp_count)
    return jnp.einsum(
        "st,trqd->qsrd",
        placed.astype(jnp.bfloat16),
        tile_blocks,
        preferred_element_type=jnp.float32,
    ).astype(jnp.bfloat16)


def start_from_slots(placed, slot_rows):
    merged = jnp.einsum(
        "st,qsrd->trqd", placed.astype(jnp.bfloat16), slot_rows, preferred_element_type=jnp.float32
    ).astype(jnp.bfloat16)
    return merged.reshape(merged.shape[0] * merged.shape[1], -1)


def start_send_out(slot_rows):
    quarter = slot_rows.shape[-1]
    flat = slot_rows.reshape((-1,) + slot_rows.shape[2:])
    arrived = lax.all_to_all(flat, ("dp", "expert"), split_axis=0, concat_axis=0, tiled=True)
    return arrived.reshape(-1, quarter)


def start_send_back(part_rows, dp_count, tile_rows):
    quarter = part_rows.shape[-1]
    flat = part_rows.reshape(-1, tile_rows, quarter)
    returned = lax.all_to_all(flat, ("dp", "expert"), split_axis=0, concat_axis=0, tiled=True)
    return returned.reshape(dp_count, -1, tile_rows, quarter)


def start_widen_rounded(values):
    return lax.optimization_barrier(values.astype(jnp.bfloat16)).astype(jnp.float32)


def start_expert_forward(received, gate_weight, up_weight, down_weight):
    gate_terms = start_widen_rounded(jnp.dot(received, gate_weight, preferred_element_type=jnp.float32))
    up_terms = start_widen_rounded(jnp.dot(received, up_weight, preferred_element_type=jnp.float32))
    gate_pre, up_pre = (
        lax.psum(gate_terms.astype(jnp.bfloat16), "dp").astype(jnp.float32),
        lax.psum(up_terms.astype(jnp.bfloat16), "dp").astype(jnp.float32),
    )
    activated = (jax.nn.silu(gate_pre) * up_pre).astype(jnp.bfloat16)
    part_rows = jnp.dot(activated, down_weight, preferred_element_type=jnp.float32).astype(
        jnp.bfloat16
    )
    return (part_rows, (gate_pre, up_pre, activated))


def start_expert_backward(
    received, grad_recv, kept_state, gate_weight, up_weight, down_weight, grad_sums
):
    gate_pre, up_pre, activated = kept_state
    grad_terms = start_widen_rounded(start_contract_last(grad_recv, down_weight))
    grad_act = lax.psum(grad_terms.astype(jnp.bfloat16), "dp").astype(jnp.float32)
    sigmoid_gate = jax.nn.sigmoid(gate_pre)
    silu_gate = gate_pre * sigmoid_gate
    grad_gate_pre = (
        grad_act * up_pre * sigmoid_gate * (1.0 + gate_pre * (1.0 - sigmoid_gate))
    ).astype(jnp.bfloat16)
    grad_up_pre = (grad_act * silu_gate).astype(jnp.bfloat16)
    back_rows = (
        start_contract_last(grad_gate_pre, gate_weight) + start_contract_last(grad_up_pre, up_weight)
    ).astype(jnp.bfloat16)
    grad_gate = grad_sums[0] + start_contract_first(received, grad_gate_pre)
    grad_up = grad_sums[1] + start_contract_first(received, grad_up_pre)
    grad_down = grad_sums[2] + start_contract_first(activated, grad_recv)
    return (back_rows, (grad_gate, grad_up, grad_down))


def start_body(tokens, cotangent, gain, w_gate, w_up, w_down, route):
    pipe_count = lax.axis_size("pipe")
    dp_count = lax.axis_size("dp")
    expert_count = lax.axis_size("expert")
    section_index = lax.axis_index("pipe")
    gain_row = gain[0]
    gate_weight = w_gate[0, 0]
    up_weight = w_up[0, 0]
    down_weight = w_down[0, 0]
    route_table = route[0, :, :, 0]
    tile_count = route_table.shape[1]
    capacity = max(2, 3 * tile_count // (2 * expert_count))
    hidden = tokens[0]
    saved_ticks = []
    out_rows = hidden
    for pass_index in range(PASSES):
        micro_index = (section_index - pass_index + pipe_count) % pipe_count
        route_now = lax.dynamic_index_in_dim(route_table, micro_index, 0, keepdims=False)
        placed = start_slot_matrix(route_now, expert_count, capacity)
        normed, scaled, inverse = start_normalize(hidden, gain_row)
        received = start_send_out(start_into_slots(placed, normed, TILE, dp_count))
        part_rows, kept_state = start_expert_forward(received, gate_weight, up_weight, down_weight)
        ffn_rows = start_from_slots(placed, start_send_back(part_rows, dp_count, TILE))
        new_hidden = (hidden.astype(jnp.float32) + ffn_rows.astype(jnp.float32)).astype(
            jnp.bfloat16
        )
        saved_ticks.append((placed, scaled, inverse, received, kept_state))
        if pass_index + 1 < PASSES:
            hidden = start_shifted(new_hidden, "pipe", 1)
        else:
            out_rows = new_hidden
    grad_rows = cotangent[0]
    grad_sums = (
        jnp.zeros(gate_weight.shape, jnp.float32),
        jnp.zeros(up_weight.shape, jnp.float32),
        jnp.zeros(down_weight.shape, jnp.float32),
    )
    gain_sum = jnp.zeros(gain_row.shape, jnp.float32)
    entry_grad = grad_rows
    for pass_index in reversed(range(PASSES)):
        placed, scaled, inverse, received, kept_state = saved_ticks[pass_index]
        grad_recv = start_send_out(start_into_slots(placed, grad_rows, TILE, dp_count))
        back_rows, grad_sums = start_expert_backward(
            received, grad_recv, kept_state, gate_weight, up_weight, down_weight, grad_sums
        )
        grad_normed = start_from_slots(placed, start_send_back(back_rows, dp_count, TILE)).astype(jnp.float32)
        gain_sum = gain_sum + jnp.sum(grad_normed * scaled, axis=0)
        grad_scaled = grad_normed * gain_row
        grad_wide = inverse * (
            grad_scaled - scaled * jnp.mean(grad_scaled * scaled, axis=-1, keepdims=True)
        )
        grad_in = (grad_rows.astype(jnp.float32) + grad_wide).astype(jnp.bfloat16)
        if pass_index > 0:
            grad_rows = start_shifted(grad_in, "pipe", -1)
        else:
            entry_grad = grad_in
    gain_total = lax.psum(gain_sum, ("dp", "expert"))
    return (
        out_rows[None],
        entry_grad[None],
        gain_total[None],
        grad_sums[0].astype(jnp.bfloat16)[None, None],
        grad_sums[1].astype(jnp.bfloat16)[None, None],
        grad_sums[2].astype(jnp.bfloat16)[None, None],
    )


def start_solution(mesh):
    placed = (
        P("pipe", ("dp", "expert"), None),
        P("pipe", ("dp", "expert"), None),
        P("pipe", None),
        P("pipe", "expert", "dp", None),
        P("pipe", "expert", "dp", None),
        P("pipe", "expert", None, "dp"),
        P("pipe", None, ("dp", "expert"), None),
    )
    return jax.shard_map(
        start_body,
        mesh=mesh,
        in_specs=placed,
        out_specs=(
            P("pipe", ("dp", "expert"), None),
            P("pipe", ("dp", "expert"), None),
            P("pipe", None),
            P("pipe", "expert", "dp", None),
            P("pipe", "expert", "dp", None),
            P("pipe", "expert", None, "dp"),
        ),
        check_vma=False,
    )


def solution(mesh):
    if mesh.shape["expert"] != PAIR:
        return start_solution(mesh)
    placed = (
        P("pipe", ("dp", "expert"), None),
        P("pipe", ("dp", "expert"), None),
        P("pipe", None),
        P("pipe", "expert", "dp", None),
        P("pipe", "expert", "dp", None),
        P("pipe", "expert", None, "dp"),
        P("pipe", None, ("dp", "expert"), None),
    )
    return jax.shard_map(
        body,
        mesh=mesh,
        in_specs=placed,
        out_specs=placed[:2] + (P("pipe", None),) + placed[3:6],
        check_vma=False,
    )
```

```python
import jax
import jax.numpy as jnp
from jax import lax
from jax.experimental import pallas as pl
from jax.experimental.pallas import tpu as pltpu
from jax.sharding import PartitionSpec as P

TILE = 8
PASSES = 2
PAIR = 2
COLUMNS = 256
LANES = 128
VMEM_BYTES = 12 * 1024 * 1024


epsilon = 1e-06
bf16 = jnp.bfloat16
f32 = jnp.float32


def dot(former, latter, contract):
    return lax.dot_general(
        former, latter, ((contract[:1], contract[1:]), ((), ())), preferred_element_type=f32
    )


def partner_route(size, step):
    return [(i, i ^ step) for i in range(size)]


def swap(block, axis, step):
    return lax.ppermute(block, axis, partner_route(lax.axis_size(axis), step))


def shifted(block, axis, distance):
    size = lax.axis_size(axis)
    return lax.ppermute(block, axis, [(i, (i + distance) % size) for i in range(size)])


def quarter_of(rows, index, width):
    return lax.dynamic_slice_in_dim(rows, index * width, width, axis=-1)


def assemble(parts):
    here = lax.axis_index("dp")
    rows, width = parts[0].shape
    whole = jnp.zeros((rows, width * len(parts)), parts[0].dtype)
    for step, part in enumerate(parts):
        whole = lax.dynamic_update_slice_in_dim(whole, part, (here ^ step) * width, axis=1)
    return whole


def from_quarters(parts):
    return assemble(
        [swap(part, "dp", step) if step else part for step, part in enumerate(parts)]
    )


def gather_rows(rows, dp_count):
    return [rows] + [swap(rows, "dp", step) for step in range(1, dp_count)]


def after(value, *earlier):
    return lax.optimization_barrier((value,) + earlier)[0]


def columns_of(extent):
    return COLUMNS if extent % COLUMNS == 0 else extent


def kernel_call(body, operands, weights, out_shape, scratch):
    count, kept, made = len(operands), len(weights), len(out_shape)
    rows = max(shape.shape[0] for shape in out_shape)

    def call(*refs):
        operand_refs, refs = refs[:count], refs[count:]
        weight_refs, refs = refs[:kept], refs[kept:]
        body(operand_refs, weight_refs, refs[:made], refs[made:])

    in_vmem = pl.BlockSpec(memory_space=pltpu.VMEM)
    return pl.pallas_call(
        call,
        in_specs=[in_vmem] * (count + kept),
        out_specs=[in_vmem] * made,
        out_shape=out_shape,
        scratch_shapes=scratch,
        compiler_params=pltpu.CompilerParams(vmem_limit_bytes=VMEM_BYTES),
        cost_estimate=pl.CostEstimate(
            flops=4 * rows * sum(weight.size for weight in weights) // 2,
            bytes_accessed=0,
            transcendentals=0,
        ),
    )(*operands, *weights)


def resident(arrays):
    count = len(arrays)

    def call(*refs):
        arrivals = refs[-1]
        copies = [
            pltpu.make_async_copy(refs[i], refs[count + i], arrivals.at[i]) for i in range(count)
        ]
        for copy in copies:
            copy.start()
        for copy in copies:
            copy.wait()

    return pl.pallas_call(
        call,
        in_specs=[pl.BlockSpec(memory_space=pltpu.HBM)] * count,
        out_specs=[pl.BlockSpec(memory_space=pltpu.VMEM)] * count,
        out_shape=[pltpu.VMEM(a.shape, a.dtype) for a in arrays],
        scratch_shapes=[pltpu.SemaphoreType.DMA((count,))],
        compiler_params=pltpu.CompilerParams(vmem_limit_bytes=VMEM_BYTES),
        cost_estimate=pl.CostEstimate(
            flops=0,
            bytes_accessed=2 * sum(a.size * a.dtype.itemsize for a in arrays),
            transcendentals=0,
        ),
    )(*(pltpu.with_memory_space_constraint(a, pltpu.HBM) for a in arrays))


def store_parts(refs, columns, value):
    size = value.shape[0] // len(refs)
    for index, ref in enumerate(refs):
        ref[:, columns] = value[index * size : (index + 1) * size]


def each_tile(extent, visit):
    tile = columns_of(extent)

    def step(j, carry):
        visit(span(j, tile))
        return carry

    lax.fori_loop(0, extent // tile, step, 0)


def span(tile, size):
    return pl.ds(pl.multiple_of(tile * size, size), size)


def split_rows(rows_ref, mask_ref, other_ref, own_ref):
    rows = rows_ref[...]
    chosen = mask_ref[...] > 0.5
    own_ref[...] = jnp.where(chosen, rows, jnp.zeros_like(rows))
    other_ref[...] = jnp.where(chosen, jnp.zeros_like(rows), rows)


def hidden_parts(blocks, part_rows, gain_part, mask, gate_pair, up_pair, expert=None):
    width, units = gate_pair[0].shape
    routed = expert is not None
    block_rows = part_rows if routed else blocks[0].shape[0]
    rows = block_rows * len(blocks)
    parts_count = rows // part_rows
    passes = PASSES if routed else 0

    def body(operand_refs, weight_refs, out_refs, scratch):
        *block_refs, gain_ref, choice_ref = operand_refs
        part_refs, (other_rows, own_rows) = out_refs[:parts_count], out_refs[parts_count:][:2]
        mask_ref = out_refs[parts_count + 2] if routed else choice_ref
        (gained_ref,) = scratch
        for index, ref in enumerate(block_refs):
            place = slice(index * block_rows, (index + 1) * block_rows)
            block = ref[:block_rows]
            gained_ref[place] = (block.astype(f32) * gain_ref[...]).astype(bf16)
            if routed:
                out_refs[-1][place] = block
                tiles = block_rows // TILE
                row = lax.broadcasted_iota(jnp.int32, (block_rows, tiles), 0)
                first = TILE * lax.broadcasted_iota(jnp.int32, (block_rows, tiles), 1)
                chosen = ((row >= first) & (row < first + TILE)).astype(bf16)
                experts = dot(chosen, ref[block_rows:, :LANES], (1, 0)) - choice_ref[...]
                for k in range(passes):
                    near = jnp.abs(experts[:, k : k + 1]) < 0.5
                    out_refs[parts_count + 2 + k][place] = jnp.where(near, 1.0, 0.0)

        split_rows(gained_ref, mask_ref, other_rows, own_rows)
        for pair in range(2):

            def visit(columns, pair=pair):
                own, other = weight_refs[2 * pair : 2 * pair + 2]
                part = jnp.where(
                    mask_ref[...] > 0.5,
                    dot(gained_ref[...], own[:, columns], (1, 0)),
                    dot(gained_ref[...], other[:, columns], (1, 0)),
                ).astype(bf16)
                store_parts([ref.at[:, pair * units :] for ref in part_refs], columns, part)

            each_tile(units, visit)

    outs = kernel_call(
        body,
        (*blocks, gain_part, expert if routed else mask),
        (*gate_pair, *up_pair),
        [jax.ShapeDtypeStruct((part_rows, 2 * units), bf16)] * parts_count
        + [jax.ShapeDtypeStruct((rows, width), bf16)] * 2
        + [jax.ShapeDtypeStruct((rows, 1), f32)] * passes
        + [jax.ShapeDtypeStruct((rows, width), bf16)] * int(routed),
        [pltpu.VMEM((rows, width), bf16)],
    )
    return outs[:parts_count], outs[parts_count : parts_count + 2], outs[parts_count + 2 :]


def row_scale(blocks, features, summed):
    rows = blocks[0].shape[0]

    def body(operand_refs, weight_refs, out_refs, scratch):
        total = jnp.zeros((rows, 1), f32)
        for ref in operand_refs:
            wide = ref[...].astype(f32)
            if not summed:
                wide = jnp.sum(wide * wide, axis=-1, keepdims=True)
            total = total + wide
        out_refs[0][...] = lax.rsqrt(total / features + epsilon)

    (scale,) = kernel_call(body, blocks, (), [jax.ShapeDtypeStruct((rows, 1), f32)], [])
    return scale


def activate(parts, inverse):
    rows, both = parts[0].shape
    units = both // 2

    def body(operand_refs, weight_refs, out_refs, scratch):
        *part_refs, inverse_ref = operand_refs
        total = part_refs[0][...].astype(f32)
        for ref in part_refs[1:]:
            total = total + ref[...].astype(f32)
        total = total * inverse_ref[...]
        gate, up = total[:, :units], total[:, units:]
        out_refs[0][...] = gate
        out_refs[1][...] = up
        out_refs[2][...] = (gate / (1.0 + jnp.exp(-gate)) * up).astype(bf16)

    return kernel_call(
        body,
        (*parts, inverse),
        (),
        [jax.ShapeDtypeStruct((rows, units), f32)] * 2
        + [jax.ShapeDtypeStruct((rows, units), bf16)],
        [],
    )


def join(joined, refs, columns):
    size = refs[0].shape[0]
    for index, ref in enumerate(refs):
        joined[index * size : (index + 1) * size] = ref[:, columns]


def add_down(blocks, mask, down_pair, hidden, in_parts):
    count = len(blocks)
    part_rows, units = blocks[0].shape
    rows = part_rows * count
    width = down_pair[0].shape[1]
    out_count = count if in_parts else 1

    def body(operand_refs, weight_refs, out_refs, scratch):
        *block_refs, mask_ref, hidden_ref = operand_refs
        row_refs, square_refs = out_refs[:out_count], out_refs[out_count:-2]
        joined, square_ref = scratch
        join(joined, block_refs, slice(None))
        split_rows(joined, mask_ref, *out_refs[-2:])
        square_ref[...] = jnp.zeros_like(square_ref)
        own, other = weight_refs

        def visit(columns):
            ffn = jnp.where(
                mask_ref[...] > 0.5,
                dot(joined[...], own[:, columns], (1, 0)),
                dot(joined[...], other[:, columns], (1, 0)),
            ).astype(bf16)
            out = (hidden_ref[:, columns].astype(f32) + ffn.astype(f32)).astype(bf16)
            wide = out.astype(f32)
            square_ref[...] += jnp.sum(wide * wide, axis=-1, keepdims=True)
            store_parts(row_refs, columns, out)

        each_tile(width, visit)
        store_parts(square_refs, slice(None), square_ref[...])

    outs = kernel_call(
        body,
        (*blocks, mask, hidden),
        down_pair,
        [jax.ShapeDtypeStruct((rows // out_count, width), bf16)] * out_count
        + [jax.ShapeDtypeStruct((part_rows, 1), f32)] * count
        + [jax.ShapeDtypeStruct((rows, units), bf16)] * 2,
        [pltpu.VMEM((rows, units), bf16), pltpu.VMEM((rows, 1), f32)],
    )
    return outs[:out_count], outs[out_count:-2], outs[-2:]


def act_grad_parts(blocks, part_rows, mask, down_pair):
    rows = sum(block.shape[0] for block in blocks)
    parts_count = rows // part_rows
    units, width = down_pair[0].shape

    def body(operand_refs, weight_refs, out_refs, scratch):
        *block_refs, mask_ref = operand_refs
        *part_refs, grad_ref = out_refs
        own, other = weight_refs
        join(grad_ref, block_refs, slice(None))

        def visit(columns):
            part = jnp.where(
                mask_ref[...] > 0.5,
                dot(grad_ref[...], own[columns], (1, 1)),
                dot(grad_ref[...], other[columns], (1, 1)),
            ).astype(bf16)
            store_parts(part_refs, columns, part)

        each_tile(units, visit)

    outs = kernel_call(
        body,
        (*blocks, mask),
        down_pair,
        [jax.ShapeDtypeStruct((part_rows, units), bf16)] * parts_count
        + [jax.ShapeDtypeStruct((rows, width), bf16)],
        [],
    )
    return outs[:parts_count], outs[parts_count]


def hidden_grads(parts, gate, up, inverse, features):
    rows, units = gate.shape

    def body(operand_refs, weight_refs, out_refs, scratch):
        *part_refs, gate_ref, up_ref, inverse_ref = operand_refs
        (out_ref,) = out_refs
        grad_act = part_refs[0][...].astype(f32)
        for ref in part_refs[1:]:
            grad_act = grad_act + ref[...].astype(f32)
        gate_now, up_now, scale = gate_ref[...], up_ref[...], inverse_ref[...]
        sigmoid = 1.0 / (1.0 + jnp.exp(-gate_now))
        scaled = grad_act * scale
        gate_grad = scaled * up_now * sigmoid * (1.0 + gate_now * (1.0 - sigmoid))
        up_grad = scaled * (gate_now * sigmoid)
        shrink = jnp.sum(gate_grad * gate_now + up_grad * up_now, axis=-1, keepdims=True) * (
            scale / features
        )
        out_ref[:, :units] = gate_grad.astype(bf16)
        out_ref[:, units : 2 * units] = up_grad.astype(bf16)
        coarse = shrink.astype(bf16).astype(f32)
        lane = lax.broadcasted_iota(jnp.int32, (rows, LANES), 1)
        out_ref[:, 2 * units :] = jnp.where(
            lane == 0, coarse, jnp.where(lane == 1, shrink - coarse, 0.0)
        ).astype(bf16)

    (sent,) = kernel_call(
        body,
        (*parts, gate, up, inverse),
        [],
        [jax.ShapeDtypeStruct((rows, 2 * units + LANES), bf16)],
        [],
    )
    return sent


def input_grad(blocks, mask, gate_pair, up_pair, grad, hidden, gain_part, in_parts):
    count = len(blocks)
    part_rows = blocks[0].shape[0]
    rows = part_rows * count
    width, units = gate_pair[0].shape
    out_count = count if in_parts else 1

    def body(operand_refs, weight_refs, out_refs, scratch):
        *block_refs, mask_ref, grad_ref, hidden_ref, gain_ref = operand_refs
        *row_refs, sum_ref = out_refs
        joined, shrink = scratch
        join(joined, block_refs, slice(0, 2 * units))
        for index, ref in enumerate(block_refs):
            tail = ref[:, 2 * units :].astype(f32)
            shrink[index * part_rows : (index + 1) * part_rows] = jnp.sum(
                tail, axis=-1, keepdims=True
            )

        gate_own, gate_other, up_own, up_other = weight_refs

        def visit(columns):
            def back_of(gate, up):
                return dot(joined[:, :units], gate[columns], (1, 1)) + dot(
                    joined[:, units:], up[columns], (1, 1)
                )

            back = jnp.where(
                mask_ref[...] > 0.5, back_of(gate_own, up_own), back_of(gate_other, up_other)
            )
            wide = hidden_ref[:, columns].astype(f32)
            sum_ref[:, columns] = jnp.sum(back * wide, axis=0, keepdims=True)
            out = (
                grad_ref[:, columns].astype(f32)
                + back * gain_ref[:, columns]
                - wide * shrink[...]
            ).astype(bf16)
            store_parts(row_refs, columns, out)

        each_tile(width, visit)

    outs = kernel_call(
        body,
        (*blocks, mask, grad, hidden, gain_part),
        (*gate_pair, *up_pair),
        [jax.ShapeDtypeStruct((rows // out_count, width), bf16)] * out_count
        + [jax.ShapeDtypeStruct((1, width), f32)],
        [
            pltpu.VMEM((rows, 2 * units), bf16),
            pltpu.VMEM((rows, 1), f32),
        ],
    )
    return outs[:out_count], outs[out_count]


def body(tokens, cotangent, gain, w_gate, w_up, w_down, route):
    pipe_count = lax.axis_size("pipe")
    dp_count = lax.axis_size("dp")
    section = lax.axis_index("pipe")
    expert = lax.axis_index("expert")
    here = lax.axis_index("dp")
    features = tokens.shape[-1]
    width = features // dp_count
    units = w_gate.shape[-1]
    gain_part = lax.dynamic_slice_in_dim(gain, here * width, width, axis=1)

    groups = (slice(0, dp_count - 1), slice(dp_count - 1, dp_count))
    own_tokens = tokens[0]
    rows = own_tokens.shape[0]
    micro = [(section - k + pipe_count) % pipe_count for k in range(PASSES)]
    route_rows = jnp.stack(
        [lax.dynamic_index_in_dim(route[0, :, :, 0], m, 0, keepdims=False) for m in micro], axis=1
    ).astype(bf16)
    expert_id = jnp.full((1, LANES), expert, f32)
    route_rows = after(jnp.pad(route_rows, ((0, 0), (0, width - PASSES))), expert_id)

    def tokens_quarter(step):
        return jnp.concatenate([quarter_of(own_tokens, here ^ step, width), route_rows])

    def cotangent_quarter(step, *earlier):
        return quarter_of(after(cotangent[0], *earlier), here ^ step, width)

    def sent(parts):
        return [swap(part, "dp", step) if step else part for step, part in enumerate(parts)]

    def moved(pieces, distance):
        return [shifted(piece, "pipe", distance) for piece in pieces]

    def weight_grad(lefts, right, wanted):
        return dot(lefts[wanted], right, (0, 0))

    def stacked(pairs):
        return [jnp.concatenate(pieces) for pieces in zip(*pairs)]

    quarters = [tokens_quarter(step) for step in range(dp_count)]
    weights = [
        weight
        for own in (w_gate, w_up, w_down)
        for weight in (own[0, 0], swap(own[0, 0], "expert", 1))
    ]
    weights = resident(weights)
    gate_pair, up_pair, down_pair = weights[:2], weights[2:4], weights[4:]
    quarters[-1] = after(quarters[-1], *weights)
    blocks = sent(quarters)
    inverse = row_scale([own_tokens], features, False)

    parts, gained, masks, hidden = [], [], [], []
    for group in groups:
        made, scaled, (*choices, joined) = hidden_parts(
            blocks[group], rows, gain_part, None, gate_pair, up_pair, expert_id
        )
        parts += made
        gained.append(scaled)
        masks.append(choices)
        hidden.append(joined)
    masks = list(zip(*masks))
    gate, up, activated = activate(sent(parts), inverse)
    kept = [(hidden, gained, inverse, gate, up)]
    first_activated = gather_rows(activated, dp_count)
    next_hidden, squares, first_rows = [], [], []
    for group, mask, rows_in in zip(groups, masks[0], hidden):
        (out,), square, split = add_down(
            first_activated[group], mask, down_pair, rows_in, False
        )
        next_hidden.append(out)
        squares += square
        first_rows.append(split)
    hidden = moved(next_hidden, 1)
    grad_blocks = sent([cotangent_quarter(step, next_hidden[0]) for step in range(dp_count)])
    squares = [after(square, *grad_blocks[1:-1]) for square in squares]
    inverse = shifted(row_scale(sent(squares), features, True), "pipe", 1)
    act_parts, grad = [], []
    for group, mask in zip(groups, masks[1]):
        made, joined = act_grad_parts(grad_blocks[group], rows, mask, down_pair)
        act_parts += made
        grad.append(joined)
    act_grads = act_parts
    act_parts = sent(act_parts)
    hidden[0] = after(hidden[0], inverse, *act_grads)

    parts, gained = [], []
    for rows_in, mask in zip(hidden, masks[1]):
        made, scaled, _ = hidden_parts([rows_in], rows, gain_part, mask, gate_pair, up_pair)
        parts += made
        gained.append(scaled)
    gate, up, activated = activate(sent(parts), inverse)
    kept.append((hidden, gained, inverse, gate, up))

    gain_sum = jnp.zeros((1, width), f32)
    for k in reversed(range(PASSES)):
        hidden, gained, inverse, gate, up = kept[k]
        gained = stacked(gained)
        payload = hidden_grads(act_parts, gate, up, inverse, features)
        both_grad = gather_rows(payload, dp_count)
        joined = jnp.concatenate(both_grad)
        rights = [joined[:, :units], joined[:, units : 2 * units]]
        if k == 0:
            lefts = [gained, gained, stacked(first_rows)]
            rights.append(jnp.concatenate(grad))
            given = [
                (weight_grad(left, right, False) + soon.astype(f32)).astype(bf16)
                for left, right, soon in zip(lefts, rights, early[False])
            ]
            both_grad[1] = after(both_grad[1], given[2])
            received = [swap(value, "expert", 1) for value in given]
        outs = []
        for group, choice, rows_in, grad_in in zip(groups, masks[k], hidden, grad):
            made, gain_term = input_grad(
                both_grad[group], choice, gate_pair, up_pair, grad_in, rows_in, gain_part, k == 0
            )
            outs += made
            gain_sum = gain_sum + gain_term
        if k > 0:
            last_grad = jnp.concatenate(grad)
            grad = moved(outs, -1)
            last_activated = gather_rows(after(activated, outs[0], grad[1]), dp_count)
            rights = [after(right, *outs) for right in rights]
            early = {
                wanted: [weight_grad(gained, right, wanted).astype(bf16) for right in rights]
                for wanted in (False, True)
            }
            out_parts, last_rows = [], []
            for group, choice, rows_in in zip(groups, masks[1], hidden):
                made, _, split = add_down(
                    last_activated[group], choice, down_pair, rows_in, True
                )
                out_parts += made
                last_rows.append(split)
            out_rows = from_quarters(out_parts)
            grad[0] = after(grad[0], out_rows, *early[False], *early[True])
            act_parts, joined = [], []
            for rows_in, choice in zip(grad, masks[0]):
                made, copied = act_grad_parts([rows_in], rows, choice, down_pair)
                act_parts += made
                joined.append(copied)
            grad = joined
            last_rows = stacked(last_rows)
            for wanted in (False, True):
                early[wanted].append(weight_grad(last_rows, last_grad, wanted).astype(bf16))
            act_parts = sent(act_parts)
            act_parts[1] = after(act_parts[1], early[False][2], early[True][2])

    returned = sent(outs)
    rights = [after(right, *outs) for right in rights]
    gain_rows = jnp.concatenate(gather_rows(after(gain_sum, *received), dp_count))
    gain_rows = gain_rows + swap(gain_rows, "expert", 1)
    gain_all = jnp.zeros((features,), f32)
    for step in range(dp_count):
        gain_all = lax.dynamic_update_slice_in_dim(
            gain_all, gain_rows[step], (here ^ step) * width, axis=0
        )
    grads = [
        (weight_grad(left, right, True) + soon.astype(f32) + other.astype(f32)).astype(bf16)
        for left, right, soon, other in zip(lefts, rights, early[True], received)
    ]
    returned = list(lax.optimization_barrier((*returned, *grads)))[:dp_count]
    entry = assemble(returned)
    return (
        out_rows[None],
        entry[None],
        gain_all[None],
        grads[0][None, None],
        grads[1][None, None],
        grads[2][None, None],
    )


def start_shifted(block, axis, distance):
    devices = range(lax.axis_size(axis))
    route = [((i - distance) % len(devices), i) for i in devices]
    return lax.ppermute(block, axis, route)


def start_contract_last(former, latter):
    return lax.dot_general(
        former, latter, (((1,), (1,)), ((), ())), preferred_element_type=jnp.float32
    )


def start_contract_first(former, latter):
    return lax.dot_general(
        former, latter, (((0,), (0,)), ((), ())), preferred_element_type=jnp.float32
    )


def start_normalize(hidden, gain_row):
    widened = hidden.astype(jnp.float32)
    inverse = lax.rsqrt(jnp.mean(widened * widened, axis=-1, keepdims=True) + epsilon)
    scaled = widened * inverse
    return ((scaled * gain_row).astype(jnp.bfloat16), scaled, inverse)


def start_slot_matrix(route_now, expert_count, capacity):
    tile_count = route_now.shape[0]
    expert_ids = jnp.arange(expert_count, dtype=jnp.int32)
    member = (route_now[None, :] == expert_ids[:, None]).astype(jnp.int32)
    earlier = jnp.cumsum(member, axis=1) - member
    rank_ids = jnp.arange(capacity, dtype=jnp.int32)
    placed = member[:, None, :] * (earlier[:, None, :] == rank_ids[None, :, None]).astype(jnp.int32)
    return placed.reshape(expert_count * capacity, tile_count)


def start_into_slots(placed, rows, tile_rows, dp_count):
    width = rows.shape[-1]
    tile_blocks = rows.reshape(placed.shape[1], tile_rows, dp_count, width // dp_count)
    return jnp.einsum(
        "st,trqd->qsrd",
        placed.astype(jnp.bfloat16),
        tile_blocks,
        preferred_element_type=jnp.float32,
    ).astype(jnp.bfloat16)


def start_from_slots(placed, slot_rows):
    merged = jnp.einsum(
        "st,qsrd->trqd", placed.astype(jnp.bfloat16), slot_rows, preferred_element_type=jnp.float32
    ).astype(jnp.bfloat16)
    return merged.reshape(merged.shape[0] * merged.shape[1], -1)


def start_send_out(slot_rows):
    quarter = slot_rows.shape[-1]
    flat = slot_rows.reshape((-1,) + slot_rows.shape[2:])
    arrived = lax.all_to_all(flat, ("dp", "expert"), split_axis=0, concat_axis=0, tiled=True)
    return arrived.reshape(-1, quarter)


def start_send_back(part_rows, dp_count, tile_rows):
    quarter = part_rows.shape[-1]
    flat = part_rows.reshape(-1, tile_rows, quarter)
    returned = lax.all_to_all(flat, ("dp", "expert"), split_axis=0, concat_axis=0, tiled=True)
    return returned.reshape(dp_count, -1, tile_rows, quarter)


def start_widen_rounded(values):
    return lax.optimization_barrier(values.astype(jnp.bfloat16)).astype(jnp.float32)


def start_expert_forward(received, gate_weight, up_weight, down_weight):
    gate_terms = start_widen_rounded(jnp.dot(received, gate_weight, preferred_element_type=jnp.float32))
    up_terms = start_widen_rounded(jnp.dot(received, up_weight, preferred_element_type=jnp.float32))
    gate_pre, up_pre = (
        lax.psum(gate_terms.astype(jnp.bfloat16), "dp").astype(jnp.float32),
        lax.psum(up_terms.astype(jnp.bfloat16), "dp").astype(jnp.float32),
    )
    activated = (jax.nn.silu(gate_pre) * up_pre).astype(jnp.bfloat16)
    part_rows = jnp.dot(activated, down_weight, preferred_element_type=jnp.float32).astype(
        jnp.bfloat16
    )
    return (part_rows, (gate_pre, up_pre, activated))


def start_expert_backward(
    received, grad_recv, kept_state, gate_weight, up_weight, down_weight, grad_sums
):
    gate_pre, up_pre, activated = kept_state
    grad_terms = start_widen_rounded(start_contract_last(grad_recv, down_weight))
    grad_act = lax.psum(grad_terms.astype(jnp.bfloat16), "dp").astype(jnp.float32)
    sigmoid_gate = jax.nn.sigmoid(gate_pre)
    silu_gate = gate_pre * sigmoid_gate
    grad_gate_pre = (
        grad_act * up_pre * sigmoid_gate * (1.0 + gate_pre * (1.0 - sigmoid_gate))
    ).astype(jnp.bfloat16)
    grad_up_pre = (grad_act * silu_gate).astype(jnp.bfloat16)
    back_rows = (
        start_contract_last(grad_gate_pre, gate_weight) + start_contract_last(grad_up_pre, up_weight)
    ).astype(jnp.bfloat16)
    grad_gate = grad_sums[0] + start_contract_first(received, grad_gate_pre)
    grad_up = grad_sums[1] + start_contract_first(received, grad_up_pre)
    grad_down = grad_sums[2] + start_contract_first(activated, grad_recv)
    return (back_rows, (grad_gate, grad_up, grad_down))


def start_body(tokens, cotangent, gain, w_gate, w_up, w_down, route):
    pipe_count = lax.axis_size("pipe")
    dp_count = lax.axis_size("dp")
    expert_count = lax.axis_size("expert")
    section_index = lax.axis_index("pipe")
    gain_row = gain[0]
    gate_weight = w_gate[0, 0]
    up_weight = w_up[0, 0]
    down_weight = w_down[0, 0]
    route_table = route[0, :, :, 0]
    tile_count = route_table.shape[1]
    capacity = max(2, 3 * tile_count // (2 * expert_count))
    hidden = tokens[0]
    saved_ticks = []
    out_rows = hidden
    for pass_index in range(PASSES):
        micro_index = (section_index - pass_index + pipe_count) % pipe_count
        route_now = lax.dynamic_index_in_dim(route_table, micro_index, 0, keepdims=False)
        placed = start_slot_matrix(route_now, expert_count, capacity)
        normed, scaled, inverse = start_normalize(hidden, gain_row)
        received = start_send_out(start_into_slots(placed, normed, TILE, dp_count))
        part_rows, kept_state = start_expert_forward(received, gate_weight, up_weight, down_weight)
        ffn_rows = start_from_slots(placed, start_send_back(part_rows, dp_count, TILE))
        new_hidden = (hidden.astype(jnp.float32) + ffn_rows.astype(jnp.float32)).astype(
            jnp.bfloat16
        )
        saved_ticks.append((placed, scaled, inverse, received, kept_state))
        if pass_index + 1 < PASSES:
            hidden = start_shifted(new_hidden, "pipe", 1)
        else:
            out_rows = new_hidden
    grad_rows = cotangent[0]
    grad_sums = (
        jnp.zeros(gate_weight.shape, jnp.float32),
        jnp.zeros(up_weight.shape, jnp.float32),
        jnp.zeros(down_weight.shape, jnp.float32),
    )
    gain_sum = jnp.zeros(gain_row.shape, jnp.float32)
    entry_grad = grad_rows
    for pass_index in reversed(range(PASSES)):
        placed, scaled, inverse, received, kept_state = saved_ticks[pass_index]
        grad_recv = start_send_out(start_into_slots(placed, grad_rows, TILE, dp_count))
        back_rows, grad_sums = start_expert_backward(
            received, grad_recv, kept_state, gate_weight, up_weight, down_weight, grad_sums
        )
        grad_normed = start_from_slots(placed, start_send_back(back_rows, dp_count, TILE)).astype(jnp.float32)
        gain_sum = gain_sum + jnp.sum(grad_normed * scaled, axis=0)
        grad_scaled = grad_normed * gain_row
        grad_wide = inverse * (
            grad_scaled - scaled * jnp.mean(grad_scaled * scaled, axis=-1, keepdims=True)
        )
        grad_in = (grad_rows.astype(jnp.float32) + grad_wide).astype(jnp.bfloat16)
        if pass_index > 0:
            grad_rows = start_shifted(grad_in, "pipe", -1)
        else:
            entry_grad = grad_in
    gain_total = lax.psum(gain_sum, ("dp", "expert"))
    return (
        out_rows[None],
        entry_grad[None],
        gain_total[None],
        grad_sums[0].astype(jnp.bfloat16)[None, None],
        grad_sums[1].astype(jnp.bfloat16)[None, None],
        grad_sums[2].astype(jnp.bfloat16)[None, None],
    )


def start_solution(mesh):
    placed = (
        P("pipe", ("dp", "expert"), None),
        P("pipe", ("dp", "expert"), None),
        P("pipe", None),
        P("pipe", "expert", "dp", None),
        P("pipe", "expert", "dp", None),
        P("pipe", "expert", None, "dp"),
        P("pipe", None, ("dp", "expert"), None),
    )
    return jax.shard_map(
        start_body,
        mesh=mesh,
        in_specs=placed,
        out_specs=(
            P("pipe", ("dp", "expert"), None),
            P("pipe", ("dp", "expert"), None),
            P("pipe", None),
            P("pipe", "expert", "dp", None),
            P("pipe", "expert", "dp", None),
            P("pipe", "expert", None, "dp"),
        ),
        check_vma=False,
    )


def solution(mesh):
    if mesh.shape["expert"] != PAIR:
        return start_solution(mesh)
    placed = (
        P("pipe", ("dp", "expert"), None),
        P("pipe", ("dp", "expert"), None),
        P("pipe", None),
        P("pipe", "expert", "dp", None),
        P("pipe", "expert", "dp", None),
        P("pipe", "expert", None, "dp"),
        P("pipe", None, ("dp", "expert"), None),
    )
    return jax.shard_map(
        body,
        mesh=mesh,
        in_specs=placed,
        out_specs=placed[:2] + (P("pipe", None),) + placed[3:6],
        check_vma=False,
    )
```

```python
import jax
import jax.numpy as jnp
from jax import lax
from jax.experimental import pallas as pl
from jax.experimental.pallas import tpu as pltpu
from jax.sharding import PartitionSpec as P

TILE = 8
PASSES = 2
PAIR = 2
COLUMNS = 256
LANES = 128
VMEM_BYTES = 12 * 1024 * 1024


epsilon = 1e-06
bf16 = jnp.bfloat16
f32 = jnp.float32


def dot(former, latter, contract):
    return lax.dot_general(
        former, latter, ((contract[:1], contract[1:]), ((), ())), preferred_element_type=f32
    )


def partner_route(size, step):
    return [(i, i ^ step) for i in range(size)]


def swap(block, axis, step):
    return lax.ppermute(block, axis, partner_route(lax.axis_size(axis), step))


def shifted(block, axis, distance):
    size = lax.axis_size(axis)
    return lax.ppermute(block, axis, [(i, (i + distance) % size) for i in range(size)])


def quarter_of(rows, index, width):
    return lax.dynamic_slice_in_dim(rows, index * width, width, axis=-1)


def assemble(parts):
    here = lax.axis_index("dp")
    rows, width = parts[0].shape
    whole = jnp.zeros((rows, width * len(parts)), parts[0].dtype)
    for step, part in enumerate(parts):
        whole = lax.dynamic_update_slice_in_dim(whole, part, (here ^ step) * width, axis=1)
    return whole


def from_quarters(parts):
    return assemble(
        [swap(part, "dp", step) if step else part for step, part in enumerate(parts)]
    )


def gather_rows(rows, dp_count):
    return [rows] + [swap(rows, "dp", step) for step in range(1, dp_count)]


def after(value, *earlier):
    return lax.optimization_barrier((value,) + earlier)[0]


def columns_of(extent):
    return COLUMNS if extent % COLUMNS == 0 else extent


def kernel_call(body, operands, weights, out_shape, scratch, weight_cost=1):
    count, kept, made = len(operands), len(weights), len(out_shape)
    rows = max(shape.shape[0] for shape in out_shape)

    def call(*refs):
        operand_refs, refs = refs[:count], refs[count:]
        weight_refs, refs = refs[:kept], refs[kept:]
        body(operand_refs, weight_refs, refs[:made], refs[made:])

    in_vmem = pl.BlockSpec(memory_space=pltpu.VMEM)
    return pl.pallas_call(
        call,
        in_specs=[in_vmem] * (count + kept),
        out_specs=[in_vmem] * made,
        out_shape=out_shape,
        scratch_shapes=scratch,
        compiler_params=pltpu.CompilerParams(vmem_limit_bytes=VMEM_BYTES),
        cost_estimate=pl.CostEstimate(
            flops=weight_cost * 2 * rows * sum(weight.size for weight in weights),
            bytes_accessed=0,
            transcendentals=0,
        ),
    )(*operands, *weights)


def resident(arrays):
    count = len(arrays)

    def call(*refs):
        arrivals = refs[-1]
        copies = [
            pltpu.make_async_copy(refs[i], refs[count + i], arrivals.at[i]) for i in range(count)
        ]
        for copy in copies:
            copy.start()
        for copy in copies:
            copy.wait()

    return pl.pallas_call(
        call,
        in_specs=[pl.BlockSpec(memory_space=pltpu.HBM)] * count,
        out_specs=[pl.BlockSpec(memory_space=pltpu.VMEM)] * count,
        out_shape=[pltpu.VMEM(a.shape, a.dtype) for a in arrays],
        scratch_shapes=[pltpu.SemaphoreType.DMA((count,))],
        compiler_params=pltpu.CompilerParams(vmem_limit_bytes=VMEM_BYTES),
        cost_estimate=pl.CostEstimate(
            flops=0,
            bytes_accessed=2 * sum(a.size * a.dtype.itemsize for a in arrays),
            transcendentals=0,
        ),
    )(*(pltpu.with_memory_space_constraint(a, pltpu.HBM) for a in arrays))


def store_parts(refs, columns, value):
    size = value.shape[0] // len(refs)
    for index, ref in enumerate(refs):
        ref[:, columns] = value[index * size : (index + 1) * size]


def each_tile(extent, visit):
    tile = columns_of(extent)

    def step(j, carry):
        visit(span(j, tile))
        return carry

    lax.fori_loop(0, extent // tile, step, 0)


def span(tile, size):
    return pl.ds(pl.multiple_of(tile * size, size), size)


def split_rows(rows_ref, mask_ref, other_ref, own_ref):
    rows = rows_ref[...]
    chosen = mask_ref[...] > 0.5
    own_ref[...] = jnp.where(chosen, rows, jnp.zeros_like(rows))
    other_ref[...] = jnp.where(chosen, jnp.zeros_like(rows), rows)


def hidden_parts(blocks, part_rows, gain_part, mask, gate_pair, up_pair, expert=None):
    width, units = gate_pair[0].shape
    routed = expert is not None
    block_rows = part_rows if routed else blocks[0].shape[0]
    rows = block_rows * len(blocks)
    parts_count = rows // part_rows
    passes = PASSES if routed else 0

    def body(operand_refs, weight_refs, out_refs, scratch):
        *block_refs, gain_ref, choice_ref = operand_refs
        part_refs, (other_rows, own_rows) = out_refs[:parts_count], out_refs[parts_count:][:2]
        mask_ref = out_refs[parts_count + 2] if routed else choice_ref
        (gained_ref,) = scratch
        for index, ref in enumerate(block_refs):
            place = slice(index * block_rows, (index + 1) * block_rows)
            block = ref[:block_rows]
            gained_ref[place] = (block.astype(f32) * gain_ref[...]).astype(bf16)
            if routed:
                out_refs[-1][place] = block
                tiles = block_rows // TILE
                row = lax.broadcasted_iota(jnp.int32, (block_rows, tiles), 0)
                first = TILE * lax.broadcasted_iota(jnp.int32, (block_rows, tiles), 1)
                chosen = ((row >= first) & (row < first + TILE)).astype(bf16)
                experts = dot(chosen, ref[block_rows:, :LANES], (1, 0)) - choice_ref[...]
                for k in range(passes):
                    near = jnp.abs(experts[:, k : k + 1]) < 0.5
                    out_refs[parts_count + 2 + k][place] = jnp.where(near, 1.0, 0.0)

        split_rows(gained_ref, mask_ref, other_rows, own_rows)
        for pair in range(2):

            def visit(columns, pair=pair):
                own, other = weight_refs[2 * pair : 2 * pair + 2]
                part = jnp.where(
                    mask_ref[...] > 0.5,
                    dot(gained_ref[...], own[:, columns], (1, 0)),
                    dot(gained_ref[...], other[:, columns], (1, 0)),
                ).astype(bf16)
                store_parts([ref.at[:, pair * units :] for ref in part_refs], columns, part)

            each_tile(units, visit)

    outs = kernel_call(
        body,
        (*blocks, gain_part, expert if routed else mask),
        (*gate_pair, *up_pair),
        [jax.ShapeDtypeStruct((part_rows, 2 * units), bf16)] * parts_count
        + [jax.ShapeDtypeStruct((rows, width), bf16)] * 2
        + [jax.ShapeDtypeStruct((rows, 1), f32)] * passes
        + [jax.ShapeDtypeStruct((rows, width), bf16)] * int(routed),
        [pltpu.VMEM((rows, width), bf16)],
    )
    return outs[:parts_count], outs[parts_count : parts_count + 2], outs[parts_count + 2 :]


def row_scale(blocks, features, summed):
    rows = blocks[0].shape[0]

    def body(operand_refs, weight_refs, out_refs, scratch):
        total = jnp.zeros((rows, 1), f32)
        for ref in operand_refs:
            wide = ref[...].astype(f32)
            if not summed:
                wide = jnp.sum(wide * wide, axis=-1, keepdims=True)
            total = total + wide
        out_refs[0][...] = lax.rsqrt(total / features + epsilon)

    (scale,) = kernel_call(body, blocks, (), [jax.ShapeDtypeStruct((rows, 1), f32)], [])
    return scale


def activate(parts, inverse):
    rows, both = parts[0].shape
    units = both // 2

    def body(operand_refs, weight_refs, out_refs, scratch):
        *part_refs, inverse_ref = operand_refs
        total = part_refs[0][...].astype(f32)
        for ref in part_refs[1:]:
            total = total + ref[...].astype(f32)
        total = total * inverse_ref[...]
        gate, up = total[:, :units], total[:, units:]
        out_refs[0][...] = gate
        out_refs[1][...] = up
        out_refs[2][...] = (gate / (1.0 + jnp.exp(-gate)) * up).astype(bf16)

    return kernel_call(
        body,
        (*parts, inverse),
        (),
        [jax.ShapeDtypeStruct((rows, units), f32)] * 2
        + [jax.ShapeDtypeStruct((rows, units), bf16)],
        [],
    )


def join(joined, refs, columns):
    size = refs[0].shape[0]
    for index, ref in enumerate(refs):
        joined[index * size : (index + 1) * size] = ref[:, columns]


def add_down(blocks, mask, down_pair, hidden, in_parts):
    count = len(blocks)
    part_rows, units = blocks[0].shape
    rows = part_rows * count
    width = down_pair[0].shape[1]
    out_count = count if in_parts else 1

    def body(operand_refs, weight_refs, out_refs, scratch):
        *block_refs, mask_ref, hidden_ref = operand_refs
        row_refs, square_refs = out_refs[:out_count], out_refs[out_count:-2]
        joined, square_ref = scratch
        join(joined, block_refs, slice(None))
        split_rows(joined, mask_ref, *out_refs[-2:])
        square_ref[...] = jnp.zeros_like(square_ref)
        own, other = weight_refs

        def visit(columns):
            ffn = jnp.where(
                mask_ref[...] > 0.5,
                dot(joined[...], own[:, columns], (1, 0)),
                dot(joined[...], other[:, columns], (1, 0)),
            ).astype(bf16)
            out = (hidden_ref[:, columns].astype(f32) + ffn.astype(f32)).astype(bf16)
            wide = out.astype(f32)
            square_ref[...] += jnp.sum(wide * wide, axis=-1, keepdims=True)
            store_parts(row_refs, columns, out)

        each_tile(width, visit)
        store_parts(square_refs, slice(None), square_ref[...])

    outs = kernel_call(
        body,
        (*blocks, mask, hidden),
        down_pair,
        [jax.ShapeDtypeStruct((rows // out_count, width), bf16)] * out_count
        + [jax.ShapeDtypeStruct((part_rows, 1), f32)] * count
        + [jax.ShapeDtypeStruct((rows, units), bf16)] * 2,
        [pltpu.VMEM((rows, units), bf16), pltpu.VMEM((rows, 1), f32)],
        weight_cost=0 if in_parts else 1,
    )
    return outs[:out_count], outs[out_count:-2], outs[-2:]


def act_grad_parts(blocks, part_rows, mask, down_pair):
    rows = sum(block.shape[0] for block in blocks)
    parts_count = rows // part_rows
    units, width = down_pair[0].shape

    def body(operand_refs, weight_refs, out_refs, scratch):
        *block_refs, mask_ref = operand_refs
        *part_refs, grad_ref = out_refs
        own, other = weight_refs
        join(grad_ref, block_refs, slice(None))

        def visit(columns):
            part = jnp.where(
                mask_ref[...] > 0.5,
                dot(grad_ref[...], own[columns], (1, 1)),
                dot(grad_ref[...], other[columns], (1, 1)),
            ).astype(bf16)
            store_parts(part_refs, columns, part)

        each_tile(units, visit)

    outs = kernel_call(
        body,
        (*blocks, mask),
        down_pair,
        [jax.ShapeDtypeStruct((part_rows, units), bf16)] * parts_count
        + [jax.ShapeDtypeStruct((rows, width), bf16)],
        [],
    )
    return outs[:parts_count], outs[parts_count]


def hidden_grads(parts, gate, up, inverse, features):
    rows, units = gate.shape

    def body(operand_refs, weight_refs, out_refs, scratch):
        *part_refs, gate_ref, up_ref, inverse_ref = operand_refs
        (out_ref,) = out_refs
        grad_act = part_refs[0][...].astype(f32)
        for ref in part_refs[1:]:
            grad_act = grad_act + ref[...].astype(f32)
        gate_now, up_now, scale = gate_ref[...], up_ref[...], inverse_ref[...]
        sigmoid = 1.0 / (1.0 + jnp.exp(-gate_now))
        scaled = grad_act * scale
        gate_grad = scaled * up_now * sigmoid * (1.0 + gate_now * (1.0 - sigmoid))
        up_grad = scaled * (gate_now * sigmoid)
        shrink = jnp.sum(gate_grad * gate_now + up_grad * up_now, axis=-1, keepdims=True) * (
            scale / features
        )
        out_ref[:, :units] = gate_grad.astype(bf16)
        out_ref[:, units : 2 * units] = up_grad.astype(bf16)
        coarse = shrink.astype(bf16).astype(f32)
        lane = lax.broadcasted_iota(jnp.int32, (rows, LANES), 1)
        out_ref[:, 2 * units :] = jnp.where(
            lane == 0, coarse, jnp.where(lane == 1, shrink - coarse, 0.0)
        ).astype(bf16)

    (sent,) = kernel_call(
        body,
        (*parts, gate, up, inverse),
        [],
        [jax.ShapeDtypeStruct((rows, 2 * units + LANES), bf16)],
        [],
    )
    return sent


def input_grad(blocks, mask, gate_pair, up_pair, grad, hidden, gain_part, in_parts):
    count = len(blocks)
    part_rows = blocks[0].shape[0]
    rows = part_rows * count
    width, units = gate_pair[0].shape
    out_count = count if in_parts else 1

    def body(operand_refs, weight_refs, out_refs, scratch):
        *block_refs, mask_ref, grad_ref, hidden_ref, gain_ref = operand_refs
        *row_refs, sum_ref = out_refs
        joined, shrink = scratch
        join(joined, block_refs, slice(0, 2 * units))
        for index, ref in enumerate(block_refs):
            tail = ref[:, 2 * units :].astype(f32)
            shrink[index * part_rows : (index + 1) * part_rows] = jnp.sum(
                tail, axis=-1, keepdims=True
            )

        gate_own, gate_other, up_own, up_other = weight_refs

        def visit(columns):
            def back_of(gate, up):
                return dot(joined[:, :units], gate[columns], (1, 1)) + dot(
                    joined[:, units:], up[columns], (1, 1)
                )

            back = jnp.where(
                mask_ref[...] > 0.5, back_of(gate_own, up_own), back_of(gate_other, up_other)
            )
            wide = hidden_ref[:, columns].astype(f32)
            sum_ref[:, columns] = jnp.sum(back * wide, axis=0, keepdims=True)
            out = (
                grad_ref[:, columns].astype(f32)
                + back * gain_ref[:, columns]
                - wide * shrink[...]
            ).astype(bf16)
            store_parts(row_refs, columns, out)

        each_tile(width, visit)

    outs = kernel_call(
        body,
        (*blocks, mask, grad, hidden, gain_part),
        (*gate_pair, *up_pair),
        [jax.ShapeDtypeStruct((rows // out_count, width), bf16)] * out_count
        + [jax.ShapeDtypeStruct((1, width), f32)],
        [
            pltpu.VMEM((rows, 2 * units), bf16),
            pltpu.VMEM((rows, 1), f32),
        ],
    )
    return outs[:out_count], outs[out_count]


def body(tokens, cotangent, gain, w_gate, w_up, w_down, route):
    pipe_count = lax.axis_size("pipe")
    dp_count = lax.axis_size("dp")
    section = lax.axis_index("pipe")
    expert = lax.axis_index("expert")
    here = lax.axis_index("dp")
    features = tokens.shape[-1]
    width = features // dp_count
    units = w_gate.shape[-1]
    gain_part = lax.dynamic_slice_in_dim(gain, here * width, width, axis=1)

    groups = (slice(0, dp_count - 1), slice(dp_count - 1, dp_count))
    own_tokens = tokens[0]
    rows = own_tokens.shape[0]
    micro = [(section - k + pipe_count) % pipe_count for k in range(PASSES)]
    route_rows = jnp.stack(
        [lax.dynamic_index_in_dim(route[0, :, :, 0], m, 0, keepdims=False) for m in micro], axis=1
    ).astype(bf16)
    expert_id = jnp.full((1, LANES), expert, f32)
    route_rows = after(jnp.pad(route_rows, ((0, 0), (0, width - PASSES))), expert_id)

    def tokens_quarter(step):
        return jnp.concatenate([quarter_of(own_tokens, here ^ step, width), route_rows])

    def cotangent_quarter(step, *earlier):
        return quarter_of(after(cotangent[0], *earlier), here ^ step, width)

    def sent(parts):
        return [swap(part, "dp", step) if step else part for step, part in enumerate(parts)]

    def moved(pieces, distance):
        return [shifted(piece, "pipe", distance) for piece in pieces]

    def weight_grad(lefts, right, wanted):
        return dot(lefts[wanted], right, (0, 0))

    def stacked(pairs):
        return [jnp.concatenate(pieces) for pieces in zip(*pairs)]

    quarters = [tokens_quarter(step) for step in range(dp_count)]
    weights = [
        weight
        for own in (w_gate, w_up, w_down)
        for weight in (own[0, 0], swap(own[0, 0], "expert", 1))
    ]
    weights = resident(weights)
    gate_pair, up_pair, down_pair = weights[:2], weights[2:4], weights[4:]
    quarters[-1] = after(quarters[-1], *weights)
    blocks = sent(quarters)
    inverse = row_scale([own_tokens], features, False)

    parts, gained, masks, hidden = [], [], [], []
    for group in groups:
        made, scaled, (*choices, joined) = hidden_parts(
            blocks[group], rows, gain_part, None, gate_pair, up_pair, expert_id
        )
        parts += made
        gained.append(scaled)
        masks.append(choices)
        hidden.append(joined)
    masks = list(zip(*masks))
    gate, up, activated = activate(sent(parts), inverse)
    kept = [(hidden, gained, inverse, gate, up)]
    first_activated = gather_rows(activated, dp_count)
    next_hidden, squares, first_rows = [], [], []
    for group, mask, rows_in in zip(groups, masks[0], hidden):
        (out,), square, split = add_down(
            first_activated[group], mask, down_pair, rows_in, False
        )
        next_hidden.append(out)
        squares += square
        first_rows.append(split)
    hidden = moved(next_hidden, 1)
    waited = [first_activated[1:-1]] * (dp_count - 1) + [next_hidden[:1]]
    grad_blocks = sent([cotangent_quarter(step, *waited[step]) for step in range(dp_count)])
    squares = [after(square, *grad_blocks[1:-1]) for square in squares]
    inverse = shifted(row_scale(sent(squares), features, True), "pipe", 1)
    act_parts, grad = [], []
    for group, mask in zip(groups, masks[1]):
        made, joined = act_grad_parts(grad_blocks[group], rows, mask, down_pair)
        act_parts += made
        grad.append(joined)
    act_grads = act_parts
    act_parts = sent(act_parts)
    hidden[0] = after(hidden[0], act_grads[0])

    parts, gained = [], []
    for rows_in, mask in zip(hidden, masks[1]):
        made, scaled, _ = hidden_parts([rows_in], rows, gain_part, mask, gate_pair, up_pair)
        parts += made
        gained.append(scaled)
    gate, up, activated = activate(sent(parts), inverse)
    kept.append((hidden, gained, inverse, gate, up))

    gain_sum = jnp.zeros((1, width), f32)
    for k in reversed(range(PASSES)):
        hidden, gained, inverse, gate, up = kept[k]
        gained = stacked(gained)
        payload = hidden_grads(act_parts, gate, up, inverse, features)
        both_grad = gather_rows(payload, dp_count)
        joined = jnp.concatenate(both_grad)
        rights = [joined[:, :units], joined[:, units : 2 * units]]
        if k == 0:
            lefts = [gained, gained, stacked(first_rows)]
            rights.append(jnp.concatenate(grad))
        outs = []
        for index in reversed(range(len(groups))):
            made, gain_term = input_grad(
                both_grad[groups[index]],
                masks[k][index],
                gate_pair,
                up_pair,
                grad[index],
                hidden[index],
                gain_part,
                k == 0,
            )
            outs = list(made) + outs
            gain_sum = gain_sum + gain_term
            if k == 0 and index > 0:
                both_grad[1] = after(both_grad[1], *early[False], *early[True])
                given = [
                    (weight_grad(left, after(right, made[0]), False) + soon.astype(f32)).astype(
                        bf16
                    )
                    for left, right, soon in zip(lefts, rights, early[False])
                ]
                both_grad[1] = after(both_grad[1], *given)
                received = [swap(value, "expert", 1) for value in given]
        if k > 0:
            last_grad = jnp.concatenate(grad)
            grad = moved(outs, -1)
            last_activated = gather_rows(after(activated, outs[0], grad[1]), dp_count)
            rights = [after(right, *last_activated[1:]) for right in rights]
            early = {
                wanted: [weight_grad(gained, right, wanted).astype(bf16) for right in rights]
                for wanted in (False, True)
            }
            out_parts, last_rows = [], []
            for group, choice, rows_in in zip(groups, masks[1], hidden):
                made, _, split = add_down(
                    last_activated[group], choice, down_pair, rows_in, True
                )
                out_parts += made
                last_rows.append(split)
            out_rows = from_quarters(out_parts)
            grad[0] = after(grad[0], out_rows)
            act_parts, joined = [], []
            for rows_in, choice in zip(grad, masks[0]):
                made, copied = act_grad_parts([rows_in], rows, choice, down_pair)
                act_parts += made
                joined.append(copied)
            grad = joined
            last_rows = stacked(last_rows)
            for wanted in (False, True):
                early[wanted].append(weight_grad(last_rows, last_grad, wanted).astype(bf16))
            act_parts = sent(act_parts)

    returned = sent(outs)
    rights = [after(right, *outs) for right in rights]
    gain_rows = jnp.concatenate(gather_rows(after(gain_sum, *received), dp_count))
    gain_rows = gain_rows + swap(gain_rows, "expert", 1)
    gain_all = jnp.zeros((features,), f32)
    for step in range(dp_count):
        gain_all = lax.dynamic_update_slice_in_dim(
            gain_all, gain_rows[step], (here ^ step) * width, axis=0
        )
    grads = [
        (weight_grad(left, right, True) + soon.astype(f32) + other.astype(f32)).astype(bf16)
        for left, right, soon, other in zip(lefts, rights, early[True], received)
    ]
    returned = list(lax.optimization_barrier((*returned, *grads)))[:dp_count]
    entry = assemble(returned)
    return (
        out_rows[None],
        entry[None],
        gain_all[None],
        grads[0][None, None],
        grads[1][None, None],
        grads[2][None, None],
    )


def start_shifted(block, axis, distance):
    devices = range(lax.axis_size(axis))
    route = [((i - distance) % len(devices), i) for i in devices]
    return lax.ppermute(block, axis, route)


def start_contract_last(former, latter):
    return lax.dot_general(
        former, latter, (((1,), (1,)), ((), ())), preferred_element_type=jnp.float32
    )


def start_contract_first(former, latter):
    return lax.dot_general(
        former, latter, (((0,), (0,)), ((), ())), preferred_element_type=jnp.float32
    )


def start_normalize(hidden, gain_row):
    widened = hidden.astype(jnp.float32)
    inverse = lax.rsqrt(jnp.mean(widened * widened, axis=-1, keepdims=True) + epsilon)
    scaled = widened * inverse
    return ((scaled * gain_row).astype(jnp.bfloat16), scaled, inverse)


def start_slot_matrix(route_now, expert_count, capacity):
    tile_count = route_now.shape[0]
    expert_ids = jnp.arange(expert_count, dtype=jnp.int32)
    member = (route_now[None, :] == expert_ids[:, None]).astype(jnp.int32)
    earlier = jnp.cumsum(member, axis=1) - member
    rank_ids = jnp.arange(capacity, dtype=jnp.int32)
    placed = member[:, None, :] * (earlier[:, None, :] == rank_ids[None, :, None]).astype(jnp.int32)
    return placed.reshape(expert_count * capacity, tile_count)


def start_into_slots(placed, rows, tile_rows, dp_count):
    width = rows.shape[-1]
    tile_blocks = rows.reshape(placed.shape[1], tile_rows, dp_count, width // dp_count)
    return jnp.einsum(
        "st,trqd->qsrd",
        placed.astype(jnp.bfloat16),
        tile_blocks,
        preferred_element_type=jnp.float32,
    ).astype(jnp.bfloat16)


def start_from_slots(placed, slot_rows):
    merged = jnp.einsum(
        "st,qsrd->trqd", placed.astype(jnp.bfloat16), slot_rows, preferred_element_type=jnp.float32
    ).astype(jnp.bfloat16)
    return merged.reshape(merged.shape[0] * merged.shape[1], -1)


def start_send_out(slot_rows):
    quarter = slot_rows.shape[-1]
    flat = slot_rows.reshape((-1,) + slot_rows.shape[2:])
    arrived = lax.all_to_all(flat, ("dp", "expert"), split_axis=0, concat_axis=0, tiled=True)
    return arrived.reshape(-1, quarter)


def start_send_back(part_rows, dp_count, tile_rows):
    quarter = part_rows.shape[-1]
    flat = part_rows.reshape(-1, tile_rows, quarter)
    returned = lax.all_to_all(flat, ("dp", "expert"), split_axis=0, concat_axis=0, tiled=True)
    return returned.reshape(dp_count, -1, tile_rows, quarter)


def start_widen_rounded(values):
    return lax.optimization_barrier(values.astype(jnp.bfloat16)).astype(jnp.float32)


def start_expert_forward(received, gate_weight, up_weight, down_weight):
    gate_terms = start_widen_rounded(jnp.dot(received, gate_weight, preferred_element_type=jnp.float32))
    up_terms = start_widen_rounded(jnp.dot(received, up_weight, preferred_element_type=jnp.float32))
    gate_pre, up_pre = (
        lax.psum(gate_terms.astype(jnp.bfloat16), "dp").astype(jnp.float32),
        lax.psum(up_terms.astype(jnp.bfloat16), "dp").astype(jnp.float32),
    )
    activated = (jax.nn.silu(gate_pre) * up_pre).astype(jnp.bfloat16)
    part_rows = jnp.dot(activated, down_weight, preferred_element_type=jnp.float32).astype(
        jnp.bfloat16
    )
    return (part_rows, (gate_pre, up_pre, activated))


def start_expert_backward(
    received, grad_recv, kept_state, gate_weight, up_weight, down_weight, grad_sums
):
    gate_pre, up_pre, activated = kept_state
    grad_terms = start_widen_rounded(start_contract_last(grad_recv, down_weight))
    grad_act = lax.psum(grad_terms.astype(jnp.bfloat16), "dp").astype(jnp.float32)
    sigmoid_gate = jax.nn.sigmoid(gate_pre)
    silu_gate = gate_pre * sigmoid_gate
    grad_gate_pre = (
        grad_act * up_pre * sigmoid_gate * (1.0 + gate_pre * (1.0 - sigmoid_gate))
    ).astype(jnp.bfloat16)
    grad_up_pre = (grad_act * silu_gate).astype(jnp.bfloat16)
    back_rows = (
        start_contract_last(grad_gate_pre, gate_weight) + start_contract_last(grad_up_pre, up_weight)
    ).astype(jnp.bfloat16)
    grad_gate = grad_sums[0] + start_contract_first(received, grad_gate_pre)
    grad_up = grad_sums[1] + start_contract_first(received, grad_up_pre)
    grad_down = grad_sums[2] + start_contract_first(activated, grad_recv)
    return (back_rows, (grad_gate, grad_up, grad_down))


def start_body(tokens, cotangent, gain, w_gate, w_up, w_down, route):
    pipe_count = lax.axis_size("pipe")
    dp_count = lax.axis_size("dp")
    expert_count = lax.axis_size("expert")
    section_index = lax.axis_index("pipe")
    gain_row = gain[0]
    gate_weight = w_gate[0, 0]
    up_weight = w_up[0, 0]
    down_weight = w_down[0, 0]
    route_table = route[0, :, :, 0]
    tile_count = route_table.shape[1]
    capacity = max(2, 3 * tile_count // (2 * expert_count))
    hidden = tokens[0]
    saved_ticks = []
    out_rows = hidden
    for pass_index in range(PASSES):
        micro_index = (section_index - pass_index + pipe_count) % pipe_count
        route_now = lax.dynamic_index_in_dim(route_table, micro_index, 0, keepdims=False)
        placed = start_slot_matrix(route_now, expert_count, capacity)
        normed, scaled, inverse = start_normalize(hidden, gain_row)
        received = start_send_out(start_into_slots(placed, normed, TILE, dp_count))
        part_rows, kept_state = start_expert_forward(received, gate_weight, up_weight, down_weight)
        ffn_rows = start_from_slots(placed, start_send_back(part_rows, dp_count, TILE))
        new_hidden = (hidden.astype(jnp.float32) + ffn_rows.astype(jnp.float32)).astype(
            jnp.bfloat16
        )
        saved_ticks.append((placed, scaled, inverse, received, kept_state))
        if pass_index + 1 < PASSES:
            hidden = start_shifted(new_hidden, "pipe", 1)
        else:
            out_rows = new_hidden
    grad_rows = cotangent[0]
    grad_sums = (
        jnp.zeros(gate_weight.shape, jnp.float32),
        jnp.zeros(up_weight.shape, jnp.float32),
        jnp.zeros(down_weight.shape, jnp.float32),
    )
    gain_sum = jnp.zeros(gain_row.shape, jnp.float32)
    entry_grad = grad_rows
    for pass_index in reversed(range(PASSES)):
        placed, scaled, inverse, received, kept_state = saved_ticks[pass_index]
        grad_recv = start_send_out(start_into_slots(placed, grad_rows, TILE, dp_count))
        back_rows, grad_sums = start_expert_backward(
            received, grad_recv, kept_state, gate_weight, up_weight, down_weight, grad_sums
        )
        grad_normed = start_from_slots(placed, start_send_back(back_rows, dp_count, TILE)).astype(jnp.float32)
        gain_sum = gain_sum + jnp.sum(grad_normed * scaled, axis=0)
        grad_scaled = grad_normed * gain_row
        grad_wide = inverse * (
            grad_scaled - scaled * jnp.mean(grad_scaled * scaled, axis=-1, keepdims=True)
        )
        grad_in = (grad_rows.astype(jnp.float32) + grad_wide).astype(jnp.bfloat16)
        if pass_index > 0:
            grad_rows = start_shifted(grad_in, "pipe", -1)
        else:
            entry_grad = grad_in
    gain_total = lax.psum(gain_sum, ("dp", "expert"))
    return (
        out_rows[None],
        entry_grad[None],
        gain_total[None],
        grad_sums[0].astype(jnp.bfloat16)[None, None],
        grad_sums[1].astype(jnp.bfloat16)[None, None],
        grad_sums[2].astype(jnp.bfloat16)[None, None],
    )


def start_solution(mesh):
    placed = (
        P("pipe", ("dp", "expert"), None),
        P("pipe", ("dp", "expert"), None),
        P("pipe", None),
        P("pipe", "expert", "dp", None),
        P("pipe", "expert", "dp", None),
        P("pipe", "expert", None, "dp"),
        P("pipe", None, ("dp", "expert"), None),
    )
    return jax.shard_map(
        start_body,
        mesh=mesh,
        in_specs=placed,
        out_specs=(
            P("pipe", ("dp", "expert"), None),
            P("pipe", ("dp", "expert"), None),
            P("pipe", None),
            P("pipe", "expert", "dp", None),
            P("pipe", "expert", "dp", None),
            P("pipe", "expert", None, "dp"),
        ),
        check_vma=False,
    )


def solution(mesh):
    if mesh.shape["expert"] != PAIR:
        return start_solution(mesh)
    placed = (
        P("pipe", ("dp", "expert"), None),
        P("pipe", ("dp", "expert"), None),
        P("pipe", None),
        P("pipe", "expert", "dp", None),
        P("pipe", "expert", "dp", None),
        P("pipe", "expert", None, "dp"),
        P("pipe", None, ("dp", "expert"), None),
    )
    return jax.shard_map(
        body,
        mesh=mesh,
        in_specs=placed,
        out_specs=placed[:2] + (P("pipe", None),) + placed[3:6],
        check_vma=False,
    )
```

```python
import jax
import jax.numpy as jnp
from jax import lax
from jax.experimental import pallas as pl
from jax.experimental.pallas import tpu as pltpu
from jax.sharding import PartitionSpec as P

TILE = 8
PASSES = 2
PAIR = 2
COLUMNS = 256
LANES = 128
VMEM_BYTES = 12 * 1024 * 1024


epsilon = 1e-06
bf16 = jnp.bfloat16
f32 = jnp.float32


def dot(former, latter, contract):
    return lax.dot_general(
        former, latter, ((contract[:1], contract[1:]), ((), ())), preferred_element_type=f32
    )


def partner_route(size, step):
    return [(i, i ^ step) for i in range(size)]


def swap(block, axis, step):
    return lax.ppermute(block, axis, partner_route(lax.axis_size(axis), step))


def shifted(block, axis, distance):
    size = lax.axis_size(axis)
    return lax.ppermute(block, axis, [(i, (i + distance) % size) for i in range(size)])


def quarter_of(rows, index, width):
    return lax.dynamic_slice_in_dim(rows, index * width, width, axis=-1)


def assemble(parts):
    here = lax.axis_index("dp")
    rows, width = parts[0].shape
    whole = jnp.zeros((rows, width * len(parts)), parts[0].dtype)
    for step, part in enumerate(parts):
        whole = lax.dynamic_update_slice_in_dim(whole, part, (here ^ step) * width, axis=1)
    return whole


def from_quarters(parts):
    return assemble(
        [swap(part, "dp", step) if step else part for step, part in enumerate(parts)]
    )


def gather_rows(rows, dp_count):
    return [rows] + [swap(rows, "dp", step) for step in range(1, dp_count)]


def after(value, *earlier):
    return lax.optimization_barrier((value,) + earlier)[0]


def columns_of(extent):
    return COLUMNS if extent % COLUMNS == 0 else extent


def kernel_call(body, operands, weights, out_shape, scratch, weight_cost=1):
    count, kept, made = len(operands), len(weights), len(out_shape)
    rows = max(shape.shape[0] for shape in out_shape)

    def call(*refs):
        operand_refs, refs = refs[:count], refs[count:]
        weight_refs, refs = refs[:kept], refs[kept:]
        body(operand_refs, weight_refs, refs[:made], refs[made:])

    in_vmem = pl.BlockSpec(memory_space=pltpu.VMEM)
    return pl.pallas_call(
        call,
        in_specs=[in_vmem] * (count + kept),
        out_specs=[in_vmem] * made,
        out_shape=out_shape,
        scratch_shapes=scratch,
        compiler_params=pltpu.CompilerParams(vmem_limit_bytes=VMEM_BYTES),
        cost_estimate=pl.CostEstimate(
            flops=weight_cost * 2 * rows * sum(weight.size for weight in weights),
            bytes_accessed=0,
            transcendentals=0,
        ),
    )(*operands, *weights)


def resident(arrays):
    count = len(arrays)

    def call(*refs):
        arrivals = refs[-1]
        copies = [
            pltpu.make_async_copy(refs[i], refs[count + i], arrivals.at[i]) for i in range(count)
        ]
        for copy in copies:
            copy.start()
        for copy in copies:
            copy.wait()

    return pl.pallas_call(
        call,
        in_specs=[pl.BlockSpec(memory_space=pltpu.HBM)] * count,
        out_specs=[pl.BlockSpec(memory_space=pltpu.VMEM)] * count,
        out_shape=[pltpu.VMEM(a.shape, a.dtype) for a in arrays],
        scratch_shapes=[pltpu.SemaphoreType.DMA((count,))],
        compiler_params=pltpu.CompilerParams(vmem_limit_bytes=VMEM_BYTES),
        cost_estimate=pl.CostEstimate(
            flops=0,
            bytes_accessed=2 * sum(a.size * a.dtype.itemsize for a in arrays),
            transcendentals=0,
        ),
    )(*(pltpu.with_memory_space_constraint(a, pltpu.HBM) for a in arrays))


def store_parts(refs, columns, value):
    size = value.shape[0] // len(refs)
    for index, ref in enumerate(refs):
        ref[:, columns] = value[index * size : (index + 1) * size]


def each_tile(extent, visit):
    tile = columns_of(extent)

    def step(j, carry):
        visit(span(j, tile))
        return carry

    lax.fori_loop(0, extent // tile, step, 0)


def span(tile, size):
    return pl.ds(pl.multiple_of(tile * size, size), size)


def split_rows(rows_ref, mask_ref, other_ref, own_ref):
    rows = rows_ref[...]
    chosen = mask_ref[...] > 0.5
    own_ref[...] = jnp.where(chosen, rows, jnp.zeros_like(rows))
    other_ref[...] = jnp.where(chosen, jnp.zeros_like(rows), rows)


def hidden_parts(blocks, part_rows, gain_part, mask, gate_pair, up_pair, expert=None):
    width, units = gate_pair[0].shape
    routed = expert is not None
    block_rows = part_rows if routed else blocks[0].shape[0]
    rows = block_rows * len(blocks)
    parts_count = rows // part_rows
    passes = PASSES if routed else 0

    def body(operand_refs, weight_refs, out_refs, scratch):
        *block_refs, gain_ref, choice_ref = operand_refs
        part_refs, (other_rows, own_rows) = out_refs[:parts_count], out_refs[parts_count:][:2]
        mask_ref = out_refs[parts_count + 2] if routed else choice_ref
        (gained_ref,) = scratch
        for index, ref in enumerate(block_refs):
            place = slice(index * block_rows, (index + 1) * block_rows)
            block = ref[:block_rows]
            gained_ref[place] = (block.astype(f32) * gain_ref[...]).astype(bf16)
            if routed:
                out_refs[-1][place] = block
                tiles = block_rows // TILE
                row = lax.broadcasted_iota(jnp.int32, (block_rows, tiles), 0)
                first = TILE * lax.broadcasted_iota(jnp.int32, (block_rows, tiles), 1)
                chosen = ((row >= first) & (row < first + TILE)).astype(bf16)
                experts = dot(chosen, ref[block_rows:, :LANES], (1, 0)) - choice_ref[...]
                for k in range(passes):
                    near = jnp.abs(experts[:, k : k + 1]) < 0.5
                    out_refs[parts_count + 2 + k][place] = jnp.where(near, 1.0, 0.0)

        split_rows(gained_ref, mask_ref, other_rows, own_rows)
        for pair in range(2):

            def visit(columns, pair=pair):
                own, other = weight_refs[2 * pair : 2 * pair + 2]
                part = jnp.where(
                    mask_ref[...] > 0.5,
                    dot(gained_ref[...], own[:, columns], (1, 0)),
                    dot(gained_ref[...], other[:, columns], (1, 0)),
                ).astype(bf16)
                store_parts([ref.at[:, pair * units :] for ref in part_refs], columns, part)

            each_tile(units, visit)

    outs = kernel_call(
        body,
        (*blocks, gain_part, expert if routed else mask),
        (*gate_pair, *up_pair),
        [jax.ShapeDtypeStruct((part_rows, 2 * units), bf16)] * parts_count
        + [jax.ShapeDtypeStruct((rows, width), bf16)] * 2
        + [jax.ShapeDtypeStruct((rows, 1), f32)] * passes
        + [jax.ShapeDtypeStruct((rows, width), bf16)] * int(routed),
        [pltpu.VMEM((rows, width), bf16)],
    )
    return outs[:parts_count], outs[parts_count : parts_count + 2], outs[parts_count + 2 :]


def row_scale(blocks, features, summed):
    rows = blocks[0].shape[0]

    def body(operand_refs, weight_refs, out_refs, scratch):
        total = jnp.zeros((rows, 1), f32)
        for ref in operand_refs:
            wide = ref[...].astype(f32)
            if not summed:
                wide = jnp.sum(wide * wide, axis=-1, keepdims=True)
            total = total + wide
        out_refs[0][...] = lax.rsqrt(total / features + epsilon)

    (scale,) = kernel_call(body, blocks, (), [jax.ShapeDtypeStruct((rows, 1), f32)], [])
    return scale


def activate(parts, inverse):
    rows, both = parts[0].shape
    units = both // 2

    def body(operand_refs, weight_refs, out_refs, scratch):
        *part_refs, inverse_ref = operand_refs
        total = part_refs[0][...].astype(f32)
        for ref in part_refs[1:]:
            total = total + ref[...].astype(f32)
        total = total * inverse_ref[...]
        gate, up = total[:, :units], total[:, units:]
        out_refs[0][...] = gate
        out_refs[1][...] = up
        out_refs[2][...] = (gate / (1.0 + jnp.exp(-gate)) * up).astype(bf16)

    return kernel_call(
        body,
        (*parts, inverse),
        (),
        [jax.ShapeDtypeStruct((rows, units), f32)] * 2
        + [jax.ShapeDtypeStruct((rows, units), bf16)],
        [],
    )


def join(joined, refs, columns):
    size = refs[0].shape[0]
    for index, ref in enumerate(refs):
        joined[index * size : (index + 1) * size] = ref[:, columns]


def add_down(blocks, mask, down_pair, hidden, in_parts):
    count = len(blocks)
    part_rows, units = blocks[0].shape
    rows = part_rows * count
    width = down_pair[0].shape[1]
    out_count = count if in_parts else 1

    def body(operand_refs, weight_refs, out_refs, scratch):
        *block_refs, mask_ref, hidden_ref = operand_refs
        row_refs, square_refs = out_refs[:out_count], out_refs[out_count:-2]
        joined, square_ref = scratch
        join(joined, block_refs, slice(None))
        split_rows(joined, mask_ref, *out_refs[-2:])
        square_ref[...] = jnp.zeros_like(square_ref)
        own, other = weight_refs

        def visit(columns):
            ffn = jnp.where(
                mask_ref[...] > 0.5,
                dot(joined[...], own[:, columns], (1, 0)),
                dot(joined[...], other[:, columns], (1, 0)),
            ).astype(bf16)
            out = (hidden_ref[:, columns].astype(f32) + ffn.astype(f32)).astype(bf16)
            wide = out.astype(f32)
            square_ref[...] += jnp.sum(wide * wide, axis=-1, keepdims=True)
            store_parts(row_refs, columns, out)

        each_tile(width, visit)
        store_parts(square_refs, slice(None), square_ref[...])

    outs = kernel_call(
        body,
        (*blocks, mask, hidden),
        down_pair,
        [jax.ShapeDtypeStruct((rows // out_count, width), bf16)] * out_count
        + [jax.ShapeDtypeStruct((part_rows, 1), f32)] * count
        + [jax.ShapeDtypeStruct((rows, units), bf16)] * 2,
        [pltpu.VMEM((rows, units), bf16), pltpu.VMEM((rows, 1), f32)],
        weight_cost=0 if in_parts else 1,
    )
    return outs[:out_count], outs[out_count:-2], outs[-2:]


def act_grad_parts(blocks, part_rows, mask, down_pair):
    rows = sum(block.shape[0] for block in blocks)
    parts_count = rows // part_rows
    units, width = down_pair[0].shape

    def body(operand_refs, weight_refs, out_refs, scratch):
        *block_refs, mask_ref = operand_refs
        *part_refs, grad_ref = out_refs
        own, other = weight_refs
        join(grad_ref, block_refs, slice(None))

        def visit(columns):
            part = jnp.where(
                mask_ref[...] > 0.5,
                dot(grad_ref[...], own[columns], (1, 1)),
                dot(grad_ref[...], other[columns], (1, 1)),
            ).astype(bf16)
            store_parts(part_refs, columns, part)

        each_tile(units, visit)

    outs = kernel_call(
        body,
        (*blocks, mask),
        down_pair,
        [jax.ShapeDtypeStruct((part_rows, units), bf16)] * parts_count
        + [jax.ShapeDtypeStruct((rows, width), bf16)],
        [],
    )
    return outs[:parts_count], outs[parts_count]


def hidden_grads(parts, gate, up, inverse, features):
    rows, units = gate.shape

    def body(operand_refs, weight_refs, out_refs, scratch):
        *part_refs, gate_ref, up_ref, inverse_ref = operand_refs
        (out_ref,) = out_refs
        grad_act = part_refs[0][...].astype(f32)
        for ref in part_refs[1:]:
            grad_act = grad_act + ref[...].astype(f32)
        gate_now, up_now, scale = gate_ref[...], up_ref[...], inverse_ref[...]
        sigmoid = 1.0 / (1.0 + jnp.exp(-gate_now))
        scaled = grad_act * scale
        gate_grad = scaled * up_now * sigmoid * (1.0 + gate_now * (1.0 - sigmoid))
        up_grad = scaled * (gate_now * sigmoid)
        shrink = jnp.sum(gate_grad * gate_now + up_grad * up_now, axis=-1, keepdims=True) * (
            scale / features
        )
        out_ref[:, :units] = gate_grad.astype(bf16)
        out_ref[:, units : 2 * units] = up_grad.astype(bf16)
        coarse = shrink.astype(bf16).astype(f32)
        lane = lax.broadcasted_iota(jnp.int32, (rows, LANES), 1)
        out_ref[:, 2 * units :] = jnp.where(
            lane == 0, coarse, jnp.where(lane == 1, shrink - coarse, 0.0)
        ).astype(bf16)

    (sent,) = kernel_call(
        body,
        (*parts, gate, up, inverse),
        [],
        [jax.ShapeDtypeStruct((rows, 2 * units + LANES), bf16)],
        [],
    )
    return sent


def input_grad(blocks, mask, gate_pair, up_pair, grad, hidden, gain_part, in_parts):
    count = len(blocks)
    part_rows = blocks[0].shape[0]
    rows = part_rows * count
    width, units = gate_pair[0].shape
    out_count = count if in_parts else 1

    def body(operand_refs, weight_refs, out_refs, scratch):
        *block_refs, mask_ref, grad_ref, hidden_ref, gain_ref = operand_refs
        *row_refs, sum_ref = out_refs
        joined, shrink = scratch
        join(joined, block_refs, slice(0, 2 * units))
        for index, ref in enumerate(block_refs):
            tail = ref[:, 2 * units :].astype(f32)
            shrink[index * part_rows : (index + 1) * part_rows] = jnp.sum(
                tail, axis=-1, keepdims=True
            )

        gate_own, gate_other, up_own, up_other = weight_refs

        def visit(columns):
            def back_of(gate, up):
                return dot(joined[:, :units], gate[columns], (1, 1)) + dot(
                    joined[:, units:], up[columns], (1, 1)
                )

            back = jnp.where(
                mask_ref[...] > 0.5, back_of(gate_own, up_own), back_of(gate_other, up_other)
            )
            wide = hidden_ref[:, columns].astype(f32)
            sum_ref[:, columns] = jnp.sum(back * wide, axis=0, keepdims=True)
            out = (
                grad_ref[:, columns].astype(f32)
                + back * gain_ref[:, columns]
                - wide * shrink[...]
            ).astype(bf16)
            store_parts(row_refs, columns, out)

        each_tile(width, visit)

    outs = kernel_call(
        body,
        (*blocks, mask, grad, hidden, gain_part),
        (*gate_pair, *up_pair),
        [jax.ShapeDtypeStruct((rows // out_count, width), bf16)] * out_count
        + [jax.ShapeDtypeStruct((1, width), f32)],
        [
            pltpu.VMEM((rows, 2 * units), bf16),
            pltpu.VMEM((rows, 1), f32),
        ],
    )
    return outs[:out_count], outs[out_count]


def body(tokens, cotangent, gain, w_gate, w_up, w_down, route):
    pipe_count = lax.axis_size("pipe")
    dp_count = lax.axis_size("dp")
    section = lax.axis_index("pipe")
    expert = lax.axis_index("expert")
    here = lax.axis_index("dp")
    features = tokens.shape[-1]
    width = features // dp_count
    units = w_gate.shape[-1]
    gain_part = lax.dynamic_slice_in_dim(gain, here * width, width, axis=1)

    groups = (slice(0, dp_count - 1), slice(dp_count - 1, dp_count))
    own_tokens = tokens[0]
    rows = own_tokens.shape[0]
    micro = [(section - k + pipe_count) % pipe_count for k in range(PASSES)]
    route_rows = jnp.stack(
        [lax.dynamic_index_in_dim(route[0, :, :, 0], m, 0, keepdims=False) for m in micro], axis=1
    ).astype(bf16)
    expert_id = jnp.full((1, LANES), expert, f32)
    route_rows = after(jnp.pad(route_rows, ((0, 0), (0, width - PASSES))), expert_id)

    def tokens_quarter(step):
        return jnp.concatenate([quarter_of(own_tokens, here ^ step, width), route_rows])

    def cotangent_quarter(step, *earlier):
        return quarter_of(after(cotangent[0], *earlier), here ^ step, width)

    def sent(parts):
        return [swap(part, "dp", step) if step else part for step, part in enumerate(parts)]

    def moved(pieces, distance):
        return [shifted(piece, "pipe", distance) for piece in pieces]

    def weight_grad(lefts, right, wanted):
        return dot(lefts[wanted], right, (0, 0))

    def stacked(pairs):
        return [jnp.concatenate(pieces) for pieces in zip(*pairs)]

    quarters = [tokens_quarter(step) for step in range(dp_count)]
    weights = [
        weight
        for own in (w_gate, w_up, w_down)
        for weight in (own[0, 0], swap(own[0, 0], "expert", 1))
    ]
    weights = resident(weights)
    gate_pair, up_pair, down_pair = weights[:2], weights[2:4], weights[4:]
    quarters[-1] = after(quarters[-1], *weights)
    blocks = sent(quarters)
    inverse = row_scale([own_tokens], features, False)

    parts, gained, masks, hidden = [], [], [], []
    for group in groups:
        made, scaled, (*choices, joined) = hidden_parts(
            blocks[group], rows, gain_part, None, gate_pair, up_pair, expert_id
        )
        parts += made
        gained.append(scaled)
        masks.append(choices)
        hidden.append(joined)
    masks = list(zip(*masks))
    gate, up, activated = activate(sent(parts), inverse)
    kept = [(hidden, gained, inverse, gate, up)]
    first_activated = gather_rows(activated, dp_count)
    next_hidden, squares, first_rows = [], [], []
    for index in reversed(range(len(groups))):
        near = first_activated[groups[index]]
        if next_hidden:
            near = [after(near[0], next_hidden[0]), *near[1:]]
        (out,), square, split = add_down(near, masks[0][index], down_pair, hidden[index], False)
        next_hidden.insert(0, out)
        squares = [*square, *squares]
        first_rows.insert(0, split)
    hidden = moved(next_hidden, 1)
    grad_blocks = sent([cotangent_quarter(step, next_hidden[0]) for step in range(dp_count)])
    squares = [after(square, *grad_blocks[1:-1]) for square in squares]
    inverse = shifted(row_scale(sent(squares), features, True), "pipe", 1)
    act_parts, grad = [], []
    for group, mask in zip(groups, masks[1]):
        made, joined = act_grad_parts(grad_blocks[group], rows, mask, down_pair)
        act_parts += made
        grad.append(joined)
    act_grads = act_parts
    act_parts = sent(act_parts)
    hidden[0] = after(hidden[0], act_grads[0])

    parts, gained = [], []
    for rows_in, mask in zip(hidden, masks[1]):
        made, scaled, _ = hidden_parts([rows_in], rows, gain_part, mask, gate_pair, up_pair)
        parts += made
        gained.append(scaled)
    gate, up, activated = activate(sent(parts), inverse)
    kept.append((hidden, gained, inverse, gate, up))

    gain_sum = jnp.zeros((1, width), f32)
    for k in reversed(range(PASSES)):
        hidden, gained, inverse, gate, up = kept[k]
        gained = stacked(gained)
        payload = hidden_grads(act_parts, gate, up, inverse, features)
        both_grad = gather_rows(payload, dp_count)
        joined = jnp.concatenate(both_grad)
        rights = [joined[:, :units], joined[:, units : 2 * units]]
        if k == 0:
            lefts = [gained, gained, stacked(first_rows)]
            rights.append(jnp.concatenate(grad))
        outs = []
        for index in reversed(range(len(groups))):
            made, gain_term = input_grad(
                both_grad[groups[index]],
                masks[k][index],
                gate_pair,
                up_pair,
                grad[index],
                hidden[index],
                gain_part,
                k == 0,
            )
            outs = list(made) + outs
            gain_sum = gain_sum + gain_term
            if k == 0 and index > 0:
                ready = [after(right, made[0]) for right in rights[:2]] + rights[2:]
                given = [
                    (weight_grad(left, right, False) + soon.astype(f32)).astype(bf16)
                    for left, right, soon in zip(lefts, ready, early[False])
                ]
                both_grad[1] = after(both_grad[1], *given)
                received = [swap(value, "expert", 1) for value in given]
        if k > 0:
            last_grad = jnp.concatenate(grad)
            grad = moved(outs, -1)
            last_activated = gather_rows(after(activated, both_grad[-1]), dp_count)
            rights = [after(right, *last_activated[1:]) for right in rights]
            early = {
                wanted: [weight_grad(gained, right, wanted).astype(bf16) for right in rights]
                for wanted in (False, True)
            }
            out_parts, last_rows = [], []
            for group, choice, rows_in in zip(groups, masks[1], hidden):
                made, _, split = add_down(
                    last_activated[group], choice, down_pair, rows_in, True
                )
                out_parts += made
                last_rows.append(split)
            out_rows = from_quarters(out_parts)
            grad[0] = after(grad[0], *out_parts, *early[False], *early[True])
            act_parts, joined = [], []
            for rows_in, choice in zip(grad, masks[0]):
                made, copied = act_grad_parts([rows_in], rows, choice, down_pair)
                act_parts += made
                joined.append(copied)
            grad = joined
            last_rows = stacked(last_rows)
            for wanted in (False, True):
                early[wanted].append(weight_grad(last_rows, last_grad, wanted).astype(bf16))
            act_parts = sent(act_parts)
            act_parts[1] = after(act_parts[1], early[False][2], early[True][2])

    returned = sent(outs)
    rights = [after(right, *outs) for right in rights]
    gain_sum = gain_sum + swap(gain_sum, "expert", 1)
    gain_rows = jnp.concatenate(gather_rows(after(gain_sum, *received), dp_count))
    gain_all = jnp.zeros((features,), f32)
    for step in range(dp_count):
        gain_all = lax.dynamic_update_slice_in_dim(
            gain_all, gain_rows[step], (here ^ step) * width, axis=0
        )
    grads = [
        (weight_grad(left, right, True) + soon.astype(f32) + other.astype(f32)).astype(bf16)
        for left, right, soon, other in zip(lefts, rights, early[True], received)
    ]
    returned = list(lax.optimization_barrier((*returned, *grads)))[:dp_count]
    entry = assemble(returned)
    return (
        out_rows[None],
        entry[None],
        gain_all[None],
        grads[0][None, None],
        grads[1][None, None],
        grads[2][None, None],
    )


def start_shifted(block, axis, distance):
    devices = range(lax.axis_size(axis))
    route = [((i - distance) % len(devices), i) for i in devices]
    return lax.ppermute(block, axis, route)


def start_contract_last(former, latter):
    return lax.dot_general(
        former, latter, (((1,), (1,)), ((), ())), preferred_element_type=jnp.float32
    )


def start_contract_first(former, latter):
    return lax.dot_general(
        former, latter, (((0,), (0,)), ((), ())), preferred_element_type=jnp.float32
    )


def start_normalize(hidden, gain_row):
    widened = hidden.astype(jnp.float32)
    inverse = lax.rsqrt(jnp.mean(widened * widened, axis=-1, keepdims=True) + epsilon)
    scaled = widened * inverse
    return ((scaled * gain_row).astype(jnp.bfloat16), scaled, inverse)


def start_slot_matrix(route_now, expert_count, capacity):
    tile_count = route_now.shape[0]
    expert_ids = jnp.arange(expert_count, dtype=jnp.int32)
    member = (route_now[None, :] == expert_ids[:, None]).astype(jnp.int32)
    earlier = jnp.cumsum(member, axis=1) - member
    rank_ids = jnp.arange(capacity, dtype=jnp.int32)
    placed = member[:, None, :] * (earlier[:, None, :] == rank_ids[None, :, None]).astype(jnp.int32)
    return placed.reshape(expert_count * capacity, tile_count)


def start_into_slots(placed, rows, tile_rows, dp_count):
    width = rows.shape[-1]
    tile_blocks = rows.reshape(placed.shape[1], tile_rows, dp_count, width // dp_count)
    return jnp.einsum(
        "st,trqd->qsrd",
        placed.astype(jnp.bfloat16),
        tile_blocks,
        preferred_element_type=jnp.float32,
    ).astype(jnp.bfloat16)


def start_from_slots(placed, slot_rows):
    merged = jnp.einsum(
        "st,qsrd->trqd", placed.astype(jnp.bfloat16), slot_rows, preferred_element_type=jnp.float32
    ).astype(jnp.bfloat16)
    return merged.reshape(merged.shape[0] * merged.shape[1], -1)


def start_send_out(slot_rows):
    quarter = slot_rows.shape[-1]
    flat = slot_rows.reshape((-1,) + slot_rows.shape[2:])
    arrived = lax.all_to_all(flat, ("dp", "expert"), split_axis=0, concat_axis=0, tiled=True)
    return arrived.reshape(-1, quarter)


def start_send_back(part_rows, dp_count, tile_rows):
    quarter = part_rows.shape[-1]
    flat = part_rows.reshape(-1, tile_rows, quarter)
    returned = lax.all_to_all(flat, ("dp", "expert"), split_axis=0, concat_axis=0, tiled=True)
    return returned.reshape(dp_count, -1, tile_rows, quarter)


def start_widen_rounded(values):
    return lax.optimization_barrier(values.astype(jnp.bfloat16)).astype(jnp.float32)


def start_expert_forward(received, gate_weight, up_weight, down_weight):
    gate_terms = start_widen_rounded(jnp.dot(received, gate_weight, preferred_element_type=jnp.float32))
    up_terms = start_widen_rounded(jnp.dot(received, up_weight, preferred_element_type=jnp.float32))
    gate_pre, up_pre = (
        lax.psum(gate_terms.astype(jnp.bfloat16), "dp").astype(jnp.float32),
        lax.psum(up_terms.astype(jnp.bfloat16), "dp").astype(jnp.float32),
    )
    activated = (jax.nn.silu(gate_pre) * up_pre).astype(jnp.bfloat16)
    part_rows = jnp.dot(activated, down_weight, preferred_element_type=jnp.float32).astype(
        jnp.bfloat16
    )
    return (part_rows, (gate_pre, up_pre, activated))


def start_expert_backward(
    received, grad_recv, kept_state, gate_weight, up_weight, down_weight, grad_sums
):
    gate_pre, up_pre, activated = kept_state
    grad_terms = start_widen_rounded(start_contract_last(grad_recv, down_weight))
    grad_act = lax.psum(grad_terms.astype(jnp.bfloat16), "dp").astype(jnp.float32)
    sigmoid_gate = jax.nn.sigmoid(gate_pre)
    silu_gate = gate_pre * sigmoid_gate
    grad_gate_pre = (
        grad_act * up_pre * sigmoid_gate * (1.0 + gate_pre * (1.0 - sigmoid_gate))
    ).astype(jnp.bfloat16)
    grad_up_pre = (grad_act * silu_gate).astype(jnp.bfloat16)
    back_rows = (
        start_contract_last(grad_gate_pre, gate_weight) + start_contract_last(grad_up_pre, up_weight)
    ).astype(jnp.bfloat16)
    grad_gate = grad_sums[0] + start_contract_first(received, grad_gate_pre)
    grad_up = grad_sums[1] + start_contract_first(received, grad_up_pre)
    grad_down = grad_sums[2] + start_contract_first(activated, grad_recv)
    return (back_rows, (grad_gate, grad_up, grad_down))


def start_body(tokens, cotangent, gain, w_gate, w_up, w_down, route):
    pipe_count = lax.axis_size("pipe")
    dp_count = lax.axis_size("dp")
    expert_count = lax.axis_size("expert")
    section_index = lax.axis_index("pipe")
    gain_row = gain[0]
    gate_weight = w_gate[0, 0]
    up_weight = w_up[0, 0]
    down_weight = w_down[0, 0]
    route_table = route[0, :, :, 0]
    tile_count = route_table.shape[1]
    capacity = max(2, 3 * tile_count // (2 * expert_count))
    hidden = tokens[0]
    saved_ticks = []
    out_rows = hidden
    for pass_index in range(PASSES):
        micro_index = (section_index - pass_index + pipe_count) % pipe_count
        route_now = lax.dynamic_index_in_dim(route_table, micro_index, 0, keepdims=False)
        placed = start_slot_matrix(route_now, expert_count, capacity)
        normed, scaled, inverse = start_normalize(hidden, gain_row)
        received = start_send_out(start_into_slots(placed, normed, TILE, dp_count))
        part_rows, kept_state = start_expert_forward(received, gate_weight, up_weight, down_weight)
        ffn_rows = start_from_slots(placed, start_send_back(part_rows, dp_count, TILE))
        new_hidden = (hidden.astype(jnp.float32) + ffn_rows.astype(jnp.float32)).astype(
            jnp.bfloat16
        )
        saved_ticks.append((placed, scaled, inverse, received, kept_state))
        if pass_index + 1 < PASSES:
            hidden = start_shifted(new_hidden, "pipe", 1)
        else:
            out_rows = new_hidden
    grad_rows = cotangent[0]
    grad_sums = (
        jnp.zeros(gate_weight.shape, jnp.float32),
        jnp.zeros(up_weight.shape, jnp.float32),
        jnp.zeros(down_weight.shape, jnp.float32),
    )
    gain_sum = jnp.zeros(gain_row.shape, jnp.float32)
    entry_grad = grad_rows
    for pass_index in reversed(range(PASSES)):
        placed, scaled, inverse, received, kept_state = saved_ticks[pass_index]
        grad_recv = start_send_out(start_into_slots(placed, grad_rows, TILE, dp_count))
        back_rows, grad_sums = start_expert_backward(
            received, grad_recv, kept_state, gate_weight, up_weight, down_weight, grad_sums
        )
        grad_normed = start_from_slots(placed, start_send_back(back_rows, dp_count, TILE)).astype(jnp.float32)
        gain_sum = gain_sum + jnp.sum(grad_normed * scaled, axis=0)
        grad_scaled = grad_normed * gain_row
        grad_wide = inverse * (
            grad_scaled - scaled * jnp.mean(grad_scaled * scaled, axis=-1, keepdims=True)
        )
        grad_in = (grad_rows.astype(jnp.float32) + grad_wide).astype(jnp.bfloat16)
        if pass_index > 0:
            grad_rows = start_shifted(grad_in, "pipe", -1)
        else:
            entry_grad = grad_in
    gain_total = lax.psum(gain_sum, ("dp", "expert"))
    return (
        out_rows[None],
        entry_grad[None],
        gain_total[None],
        grad_sums[0].astype(jnp.bfloat16)[None, None],
        grad_sums[1].astype(jnp.bfloat16)[None, None],
        grad_sums[2].astype(jnp.bfloat16)[None, None],
    )


def start_solution(mesh):
    placed = (
        P("pipe", ("dp", "expert"), None),
        P("pipe", ("dp", "expert"), None),
        P("pipe", None),
        P("pipe", "expert", "dp", None),
        P("pipe", "expert", "dp", None),
        P("pipe", "expert", None, "dp"),
        P("pipe", None, ("dp", "expert"), None),
    )
    return jax.shard_map(
        start_body,
        mesh=mesh,
        in_specs=placed,
        out_specs=(
            P("pipe", ("dp", "expert"), None),
            P("pipe", ("dp", "expert"), None),
            P("pipe", None),
            P("pipe", "expert", "dp", None),
            P("pipe", "expert", "dp", None),
            P("pipe", "expert", None, "dp"),
        ),
        check_vma=False,
    )


def solution(mesh):
    if mesh.shape["expert"] != PAIR:
        return start_solution(mesh)
    placed = (
        P("pipe", ("dp", "expert"), None),
        P("pipe", ("dp", "expert"), None),
        P("pipe", None),
        P("pipe", "expert", "dp", None),
        P("pipe", "expert", "dp", None),
        P("pipe", "expert", None, "dp"),
        P("pipe", None, ("dp", "expert"), None),
    )
    return jax.shard_map(
        body,
        mesh=mesh,
        in_specs=placed,
        out_specs=placed[:2] + (P("pipe", None),) + placed[3:6],
        check_vma=False,
    )
```

```python
import jax
import jax.numpy as jnp
from jax import lax
from jax.experimental import pallas as pl
from jax.experimental.pallas import tpu as pltpu
from jax.sharding import PartitionSpec as P

TILE = 8
PASSES = 2
PAIR = 2
COLUMNS = 256
LANES = 128
VMEM_BYTES = 12 * 1024 * 1024


epsilon = 1e-06
bf16 = jnp.bfloat16
f32 = jnp.float32


def dot(former, latter, contract):
    return lax.dot_general(
        former, latter, ((contract[:1], contract[1:]), ((), ())), preferred_element_type=f32
    )


def partner_route(size, step):
    return [(i, i ^ step) for i in range(size)]


def swap(block, axis, step):
    return lax.ppermute(block, axis, partner_route(lax.axis_size(axis), step))


def shifted(block, axis, distance):
    size = lax.axis_size(axis)
    return lax.ppermute(block, axis, [(i, (i + distance) % size) for i in range(size)])


def quarter_of(rows, index, width):
    return lax.dynamic_slice_in_dim(rows, index * width, width, axis=-1)


def assemble(parts):
    here = lax.axis_index("dp")
    rows, width = parts[0].shape
    whole = jnp.zeros((rows, width * len(parts)), parts[0].dtype)
    for step, part in enumerate(parts):
        whole = lax.dynamic_update_slice_in_dim(whole, part, (here ^ step) * width, axis=1)
    return whole


def from_quarters(parts):
    return assemble(
        [swap(part, "dp", step) if step else part for step, part in enumerate(parts)]
    )


def gather_rows(rows, dp_count):
    return [rows] + [swap(rows, "dp", step) for step in range(1, dp_count)]


def after(value, *earlier):
    return lax.optimization_barrier((value,) + earlier)[0]


def columns_of(extent):
    return COLUMNS if extent % COLUMNS == 0 else extent


def kernel_call(body, operands, weights, out_shape, scratch, weight_cost=1):
    count, kept, made = len(operands), len(weights), len(out_shape)
    rows = max(shape.shape[0] for shape in out_shape)

    def call(*refs):
        operand_refs, refs = refs[:count], refs[count:]
        weight_refs, refs = refs[:kept], refs[kept:]
        body(operand_refs, weight_refs, refs[:made], refs[made:])

    in_vmem = pl.BlockSpec(memory_space=pltpu.VMEM)
    return pl.pallas_call(
        call,
        in_specs=[in_vmem] * (count + kept),
        out_specs=[in_vmem] * made,
        out_shape=out_shape,
        scratch_shapes=scratch,
        compiler_params=pltpu.CompilerParams(vmem_limit_bytes=VMEM_BYTES),
        cost_estimate=pl.CostEstimate(
            flops=weight_cost * 2 * rows * sum(weight.size for weight in weights),
            bytes_accessed=0,
            transcendentals=0,
        ),
    )(*operands, *weights)


def resident(arrays):
    count = len(arrays)

    def call(*refs):
        arrivals = refs[-1]
        copies = [
            pltpu.make_async_copy(refs[i], refs[count + i], arrivals.at[i]) for i in range(count)
        ]
        for copy in copies:
            copy.start()
        for copy in copies:
            copy.wait()

    return pl.pallas_call(
        call,
        in_specs=[pl.BlockSpec(memory_space=pltpu.HBM)] * count,
        out_specs=[pl.BlockSpec(memory_space=pltpu.VMEM)] * count,
        out_shape=[pltpu.VMEM(a.shape, a.dtype) for a in arrays],
        scratch_shapes=[pltpu.SemaphoreType.DMA((count,))],
        compiler_params=pltpu.CompilerParams(vmem_limit_bytes=VMEM_BYTES),
        cost_estimate=pl.CostEstimate(
            flops=0,
            bytes_accessed=2 * sum(a.size * a.dtype.itemsize for a in arrays),
            transcendentals=0,
        ),
    )(*(pltpu.with_memory_space_constraint(a, pltpu.HBM) for a in arrays))


def store_parts(refs, columns, value):
    size = value.shape[0] // len(refs)
    for index, ref in enumerate(refs):
        ref[:, columns] = value[index * size : (index + 1) * size]


def each_tile(extent, visit):
    tile = columns_of(extent)

    def step(j, carry):
        visit(span(j, tile))
        return carry

    lax.fori_loop(0, extent // tile, step, 0)


def span(tile, size):
    return pl.ds(pl.multiple_of(tile * size, size), size)


def split_rows(rows_ref, mask_ref, other_ref, own_ref):
    rows = rows_ref[...]
    chosen = mask_ref[...] > 0.5
    own_ref[...] = jnp.where(chosen, rows, jnp.zeros_like(rows))
    other_ref[...] = jnp.where(chosen, jnp.zeros_like(rows), rows)


def hidden_parts(blocks, part_rows, gain_part, mask, gate_pair, up_pair, expert=None):
    width, units = gate_pair[0].shape
    routed = expert is not None
    block_rows = part_rows if routed else blocks[0].shape[0]
    rows = block_rows * len(blocks)
    parts_count = rows // part_rows
    passes = PASSES if routed else 0

    def body(operand_refs, weight_refs, out_refs, scratch):
        *block_refs, gain_ref, choice_ref = operand_refs
        part_refs, (other_rows, own_rows) = out_refs[:parts_count], out_refs[parts_count:][:2]
        mask_ref = out_refs[parts_count + 2] if routed else choice_ref
        (gained_ref,) = scratch
        for index, ref in enumerate(block_refs):
            place = slice(index * block_rows, (index + 1) * block_rows)
            block = ref[:block_rows]
            gained_ref[place] = (block.astype(f32) * gain_ref[...]).astype(bf16)
            if routed:
                out_refs[-1][place] = block
                tiles = block_rows // TILE
                row = lax.broadcasted_iota(jnp.int32, (block_rows, tiles), 0)
                first = TILE * lax.broadcasted_iota(jnp.int32, (block_rows, tiles), 1)
                chosen = ((row >= first) & (row < first + TILE)).astype(bf16)
                experts = dot(chosen, ref[block_rows:, :LANES], (1, 0)) - choice_ref[...]
                for k in range(passes):
                    near = jnp.abs(experts[:, k : k + 1]) < 0.5
                    out_refs[parts_count + 2 + k][place] = jnp.where(near, 1.0, 0.0)

        split_rows(gained_ref, mask_ref, other_rows, own_rows)
        for pair in range(2):

            def visit(columns, pair=pair):
                own, other = weight_refs[2 * pair : 2 * pair + 2]
                part = jnp.where(
                    mask_ref[...] > 0.5,
                    dot(gained_ref[...], own[:, columns], (1, 0)),
                    dot(gained_ref[...], other[:, columns], (1, 0)),
                ).astype(bf16)
                store_parts([ref.at[:, pair * units :] for ref in part_refs], columns, part)

            each_tile(units, visit)

    outs = kernel_call(
        body,
        (*blocks, gain_part, expert if routed else mask),
        (*gate_pair, *up_pair),
        [jax.ShapeDtypeStruct((part_rows, 2 * units), bf16)] * parts_count
        + [jax.ShapeDtypeStruct((rows, width), bf16)] * 2
        + [jax.ShapeDtypeStruct((rows, 1), f32)] * passes
        + [jax.ShapeDtypeStruct((rows, width), bf16)] * int(routed),
        [pltpu.VMEM((rows, width), bf16)],
    )
    return outs[:parts_count], outs[parts_count : parts_count + 2], outs[parts_count + 2 :]


def row_scale(blocks, features, summed):
    rows = blocks[0].shape[0]

    def body(operand_refs, weight_refs, out_refs, scratch):
        total = jnp.zeros((rows, 1), f32)
        for ref in operand_refs:
            wide = ref[...].astype(f32)
            if not summed:
                wide = jnp.sum(wide * wide, axis=-1, keepdims=True)
            total = total + wide
        out_refs[0][...] = lax.rsqrt(total / features + epsilon)

    (scale,) = kernel_call(body, blocks, (), [jax.ShapeDtypeStruct((rows, 1), f32)], [])
    return scale


def activate(parts, inverse):
    rows, both = parts[0].shape
    units = both // 2

    def body(operand_refs, weight_refs, out_refs, scratch):
        *part_refs, inverse_ref = operand_refs
        total = part_refs[0][...].astype(f32)
        for ref in part_refs[1:]:
            total = total + ref[...].astype(f32)
        total = total * inverse_ref[...]
        gate, up = total[:, :units], total[:, units:]
        out_refs[0][...] = gate
        out_refs[1][...] = up
        out_refs[2][...] = (gate / (1.0 + jnp.exp(-gate)) * up).astype(bf16)

    return kernel_call(
        body,
        (*parts, inverse),
        (),
        [jax.ShapeDtypeStruct((rows, units), f32)] * 2
        + [jax.ShapeDtypeStruct((rows, units), bf16)],
        [],
    )


def join(joined, refs, columns):
    size = refs[0].shape[0]
    for index, ref in enumerate(refs):
        joined[index * size : (index + 1) * size] = ref[:, columns]


def add_down(blocks, mask, down_pair, hidden, in_parts):
    count = len(blocks)
    part_rows, units = blocks[0].shape
    rows = part_rows * count
    width = down_pair[0].shape[1]
    out_count = count if in_parts else 1

    def body(operand_refs, weight_refs, out_refs, scratch):
        *block_refs, mask_ref, hidden_ref = operand_refs
        row_refs, square_refs = out_refs[:out_count], out_refs[out_count:-2]
        joined, square_ref = scratch
        join(joined, block_refs, slice(None))
        split_rows(joined, mask_ref, *out_refs[-2:])
        square_ref[...] = jnp.zeros_like(square_ref)
        own, other = weight_refs

        def visit(columns):
            ffn = jnp.where(
                mask_ref[...] > 0.5,
                dot(joined[...], own[:, columns], (1, 0)),
                dot(joined[...], other[:, columns], (1, 0)),
            ).astype(bf16)
            out = (hidden_ref[:, columns].astype(f32) + ffn.astype(f32)).astype(bf16)
            wide = out.astype(f32)
            square_ref[...] += jnp.sum(wide * wide, axis=-1, keepdims=True)
            store_parts(row_refs, columns, out)

        each_tile(width, visit)
        store_parts(square_refs, slice(None), square_ref[...])

    outs = kernel_call(
        body,
        (*blocks, mask, hidden),
        down_pair,
        [jax.ShapeDtypeStruct((rows // out_count, width), bf16)] * out_count
        + [jax.ShapeDtypeStruct((part_rows, 1), f32)] * count
        + [jax.ShapeDtypeStruct((rows, units), bf16)] * 2,
        [pltpu.VMEM((rows, units), bf16), pltpu.VMEM((rows, 1), f32)],
        weight_cost=0 if in_parts else 1,
    )
    return outs[:out_count], outs[out_count:-2], outs[-2:]


def act_grad_parts(blocks, part_rows, mask, down_pair):
    rows = sum(block.shape[0] for block in blocks)
    parts_count = rows // part_rows
    units, width = down_pair[0].shape

    def body(operand_refs, weight_refs, out_refs, scratch):
        *block_refs, mask_ref = operand_refs
        *part_refs, grad_ref = out_refs
        own, other = weight_refs
        join(grad_ref, block_refs, slice(None))

        def visit(columns):
            part = jnp.where(
                mask_ref[...] > 0.5,
                dot(grad_ref[...], own[columns], (1, 1)),
                dot(grad_ref[...], other[columns], (1, 1)),
            ).astype(bf16)
            store_parts(part_refs, columns, part)

        each_tile(units, visit)

    outs = kernel_call(
        body,
        (*blocks, mask),
        down_pair,
        [jax.ShapeDtypeStruct((part_rows, units), bf16)] * parts_count
        + [jax.ShapeDtypeStruct((rows, width), bf16)],
        [],
    )
    return outs[:parts_count], outs[parts_count]


def hidden_grads(parts, gate, up, inverse, features):
    rows, units = gate.shape

    def body(operand_refs, weight_refs, out_refs, scratch):
        *part_refs, gate_ref, up_ref, inverse_ref = operand_refs
        (out_ref,) = out_refs
        grad_act = part_refs[0][...].astype(f32)
        for ref in part_refs[1:]:
            grad_act = grad_act + ref[...].astype(f32)
        gate_now, up_now, scale = gate_ref[...], up_ref[...], inverse_ref[...]
        sigmoid = 1.0 / (1.0 + jnp.exp(-gate_now))
        scaled = grad_act * scale
        gate_grad = scaled * up_now * sigmoid * (1.0 + gate_now * (1.0 - sigmoid))
        up_grad = scaled * (gate_now * sigmoid)
        shrink = jnp.sum(gate_grad * gate_now + up_grad * up_now, axis=-1, keepdims=True) * (
            scale / features
        )
        out_ref[:, :units] = gate_grad.astype(bf16)
        out_ref[:, units : 2 * units] = up_grad.astype(bf16)
        coarse = shrink.astype(bf16).astype(f32)
        lane = lax.broadcasted_iota(jnp.int32, (rows, LANES), 1)
        out_ref[:, 2 * units :] = jnp.where(
            lane == 0, coarse, jnp.where(lane == 1, shrink - coarse, 0.0)
        ).astype(bf16)

    (sent,) = kernel_call(
        body,
        (*parts, gate, up, inverse),
        [],
        [jax.ShapeDtypeStruct((rows, 2 * units + LANES), bf16)],
        [],
    )
    return sent


def input_grad(blocks, mask, gate_pair, up_pair, grad, hidden, gain_part, in_parts):
    count = len(blocks)
    part_rows = blocks[0].shape[0]
    rows = part_rows * count
    width, units = gate_pair[0].shape
    out_count = count if in_parts else 1

    def body(operand_refs, weight_refs, out_refs, scratch):
        *block_refs, mask_ref, grad_ref, hidden_ref, gain_ref = operand_refs
        *row_refs, sum_ref = out_refs
        joined, shrink = scratch
        join(joined, block_refs, slice(0, 2 * units))
        for index, ref in enumerate(block_refs):
            tail = ref[:, 2 * units :].astype(f32)
            shrink[index * part_rows : (index + 1) * part_rows] = jnp.sum(
                tail, axis=-1, keepdims=True
            )

        gate_own, gate_other, up_own, up_other = weight_refs

        def visit(columns):
            def back_of(gate, up):
                return dot(joined[:, :units], gate[columns], (1, 1)) + dot(
                    joined[:, units:], up[columns], (1, 1)
                )

            back = jnp.where(
                mask_ref[...] > 0.5, back_of(gate_own, up_own), back_of(gate_other, up_other)
            )
            wide = hidden_ref[:, columns].astype(f32)
            sum_ref[:, columns] = jnp.sum(back * wide, axis=0, keepdims=True)
            out = (
                grad_ref[:, columns].astype(f32)
                + back * gain_ref[:, columns]
                - wide * shrink[...]
            ).astype(bf16)
            store_parts(row_refs, columns, out)

        each_tile(width, visit)

    outs = kernel_call(
        body,
        (*blocks, mask, grad, hidden, gain_part),
        (*gate_pair, *up_pair),
        [jax.ShapeDtypeStruct((rows // out_count, width), bf16)] * out_count
        + [jax.ShapeDtypeStruct((1, width), f32)],
        [
            pltpu.VMEM((rows, 2 * units), bf16),
            pltpu.VMEM((rows, 1), f32),
        ],
    )
    return outs[:out_count], outs[out_count]


def body(tokens, cotangent, gain, w_gate, w_up, w_down, route):
    pipe_count = lax.axis_size("pipe")
    dp_count = lax.axis_size("dp")
    section = lax.axis_index("pipe")
    expert = lax.axis_index("expert")
    here = lax.axis_index("dp")
    features = tokens.shape[-1]
    width = features // dp_count
    units = w_gate.shape[-1]
    gain_part = lax.dynamic_slice_in_dim(gain, here * width, width, axis=1)

    groups = (slice(0, dp_count - 1), slice(dp_count - 1, dp_count))
    own_tokens = tokens[0]
    rows = own_tokens.shape[0]
    micro = [(section - k + pipe_count) % pipe_count for k in range(PASSES)]
    route_rows = jnp.stack(
        [lax.dynamic_index_in_dim(route[0, :, :, 0], m, 0, keepdims=False) for m in micro], axis=1
    ).astype(bf16)
    expert_id = jnp.full((1, LANES), expert, f32)
    route_rows = after(jnp.pad(route_rows, ((0, 0), (0, width - PASSES))), expert_id)

    def tokens_quarter(step):
        return jnp.concatenate([quarter_of(own_tokens, here ^ step, width), route_rows])

    def cotangent_quarter(step, *earlier):
        return quarter_of(after(cotangent[0], *earlier), here ^ step, width)

    def sent(parts):
        return [swap(part, "dp", step) if step else part for step, part in enumerate(parts)]

    def moved(pieces, distance):
        return [shifted(piece, "pipe", distance) for piece in pieces]

    def weight_grad(lefts, right, wanted):
        return dot(lefts[wanted], right, (0, 0))

    def stacked(pairs):
        return [jnp.concatenate(pieces) for pieces in zip(*pairs)]

    quarters = [tokens_quarter(step) for step in range(dp_count)]
    weights = [
        weight
        for own in (w_gate, w_up, w_down)
        for weight in (own[0, 0], swap(own[0, 0], "expert", 1))
    ]
    weights = resident(weights)
    gate_pair, up_pair, down_pair = weights[:2], weights[2:4], weights[4:]
    quarters[-1] = after(quarters[-1], *weights)
    blocks = sent(quarters)
    inverse = row_scale([own_tokens], features, False)

    parts, gained, masks, hidden = [], [], [], []
    for group in groups:
        made, scaled, (*choices, joined) = hidden_parts(
            blocks[group], rows, gain_part, None, gate_pair, up_pair, expert_id
        )
        parts += made
        gained.append(scaled)
        masks.append(choices)
        hidden.append(joined)
    masks = list(zip(*masks))
    gate, up, activated = activate(sent(parts), inverse)
    kept = [(hidden, gained, inverse, gate, up)]
    first_activated = gather_rows(activated, dp_count)
    next_hidden, squares, first_rows = [], [], []
    for index in reversed(range(len(groups))):
        near = first_activated[groups[index]]
        if next_hidden:
            near = [after(near[0], next_hidden[0]), *near[1:]]
        (out,), square, split = add_down(near, masks[0][index], down_pair, hidden[index], False)
        next_hidden.insert(0, out)
        squares = [*square, *squares]
        first_rows.insert(0, split)
    hidden = moved(next_hidden, 1)
    grad_blocks = sent([cotangent_quarter(step, next_hidden[0]) for step in range(dp_count)])
    squares = [after(square, grad_blocks[-1]) for square in squares]
    inverse = shifted(row_scale(sent(squares), features, True), "pipe", 1)
    act_parts, grad = [], []
    for group, mask in zip(groups, masks[1]):
        made, joined = act_grad_parts(grad_blocks[group], rows, mask, down_pair)
        act_parts += made
        grad.append(joined)
    act_grads = act_parts
    act_parts = sent(act_parts)
    hidden[0] = after(hidden[0], act_grads[0])

    parts, gained = [], []
    for rows_in, mask in zip(hidden, masks[1]):
        if parts:
            rows_in = after(rows_in, parts[0])
        made, scaled, _ = hidden_parts([rows_in], rows, gain_part, mask, gate_pair, up_pair)
        parts += made
        gained.append(scaled)
    gate, up, activated = activate(sent(parts), inverse)
    kept.append((hidden, gained, inverse, gate, up))

    gain_sum = jnp.zeros((1, width), f32)
    for k in reversed(range(PASSES)):
        hidden, gained, inverse, gate, up = kept[k]
        gained = stacked(gained)
        payload = hidden_grads(act_parts, gate, up, inverse, features)
        both_grad = gather_rows(payload, dp_count)
        joined = jnp.concatenate(both_grad)
        rights = [joined[:, :units], joined[:, units : 2 * units]]
        if k == 0:
            lefts = [gained, gained, stacked(first_rows)]
            rights.append(jnp.concatenate(grad))
        outs = []
        for index in reversed(range(len(groups))):
            made, gain_term = input_grad(
                both_grad[groups[index]],
                masks[k][index],
                gate_pair,
                up_pair,
                grad[index],
                hidden[index],
                gain_part,
                k == 0,
            )
            outs = list(made) + outs
            gain_sum = gain_sum + gain_term
            if k == 0 and index > 0:
                ready = [after(right, made[0]) for right in rights[:2]] + rights[2:]
                given = [
                    (weight_grad(left, right, False) + soon.astype(f32)).astype(bf16)
                    for left, right, soon in zip(lefts, ready, early[False])
                ]
                both_grad[1] = after(both_grad[1], *given)
                received = [swap(value, "expert", 1) for value in given]
        if k > 0:
            last_grad = jnp.concatenate(grad)
            grad = moved(outs, -1)
            last_activated = gather_rows(after(activated, both_grad[-1]), dp_count)
            rights = [after(right, *last_activated[1:]) for right in rights]
            early = {
                wanted: [weight_grad(gained, right, wanted).astype(bf16) for right in rights]
                for wanted in (False, True)
            }
            out_parts, last_rows = [], []
            for group, choice, rows_in in zip(groups, masks[1], hidden):
                made, _, split = add_down(
                    last_activated[group], choice, down_pair, rows_in, True
                )
                out_parts += made
                last_rows.append(split)
            out_rows = from_quarters(out_parts)
            grad[0] = after(grad[0], *out_parts, *early[False], *early[True])
            act_parts, joined = [], []
            for rows_in, choice in zip(grad, masks[0]):
                made, copied = act_grad_parts([rows_in], rows, choice, down_pair)
                act_parts += made
                joined.append(copied)
            grad = joined
            last_rows = stacked(last_rows)
            for wanted in (False, True):
                early[wanted].append(weight_grad(last_rows, last_grad, wanted).astype(bf16))
            act_parts = sent(act_parts)
            act_parts[1] = after(act_parts[1], early[False][2], early[True][2])

    returned = sent(outs)
    rights = [after(right, *outs) for right in rights]
    gain_sum = gain_sum + swap(gain_sum, "expert", 1)
    gain_rows = jnp.concatenate(gather_rows(after(gain_sum, *received), dp_count))
    gain_all = jnp.zeros((features,), f32)
    for step in range(dp_count):
        gain_all = lax.dynamic_update_slice_in_dim(
            gain_all, gain_rows[step], (here ^ step) * width, axis=0
        )
    grads = [
        (weight_grad(left, right, True) + soon.astype(f32) + other.astype(f32)).astype(bf16)
        for left, right, soon, other in zip(lefts, rights, early[True], received)
    ]
    returned = list(lax.optimization_barrier((*returned, *grads)))[:dp_count]
    entry = assemble(returned)
    return (
        out_rows[None],
        entry[None],
        gain_all[None],
        grads[0][None, None],
        grads[1][None, None],
        grads[2][None, None],
    )


def start_shifted(block, axis, distance):
    devices = range(lax.axis_size(axis))
    route = [((i - distance) % len(devices), i) for i in devices]
    return lax.ppermute(block, axis, route)


def start_contract_last(former, latter):
    return lax.dot_general(
        former, latter, (((1,), (1,)), ((), ())), preferred_element_type=jnp.float32
    )


def start_contract_first(former, latter):
    return lax.dot_general(
        former, latter, (((0,), (0,)), ((), ())), preferred_element_type=jnp.float32
    )


def start_normalize(hidden, gain_row):
    widened = hidden.astype(jnp.float32)
    inverse = lax.rsqrt(jnp.mean(widened * widened, axis=-1, keepdims=True) + epsilon)
    scaled = widened * inverse
    return ((scaled * gain_row).astype(jnp.bfloat16), scaled, inverse)


def start_slot_matrix(route_now, expert_count, capacity):
    tile_count = route_now.shape[0]
    expert_ids = jnp.arange(expert_count, dtype=jnp.int32)
    member = (route_now[None, :] == expert_ids[:, None]).astype(jnp.int32)
    earlier = jnp.cumsum(member, axis=1) - member
    rank_ids = jnp.arange(capacity, dtype=jnp.int32)
    placed = member[:, None, :] * (earlier[:, None, :] == rank_ids[None, :, None]).astype(jnp.int32)
    return placed.reshape(expert_count * capacity, tile_count)


def start_into_slots(placed, rows, tile_rows, dp_count):
    width = rows.shape[-1]
    tile_blocks = rows.reshape(placed.shape[1], tile_rows, dp_count, width // dp_count)
    return jnp.einsum(
        "st,trqd->qsrd",
        placed.astype(jnp.bfloat16),
        tile_blocks,
        preferred_element_type=jnp.float32,
    ).astype(jnp.bfloat16)


def start_from_slots(placed, slot_rows):
    merged = jnp.einsum(
        "st,qsrd->trqd", placed.astype(jnp.bfloat16), slot_rows, preferred_element_type=jnp.float32
    ).astype(jnp.bfloat16)
    return merged.reshape(merged.shape[0] * merged.shape[1], -1)


def start_send_out(slot_rows):
    quarter = slot_rows.shape[-1]
    flat = slot_rows.reshape((-1,) + slot_rows.shape[2:])
    arrived = lax.all_to_all(flat, ("dp", "expert"), split_axis=0, concat_axis=0, tiled=True)
    return arrived.reshape(-1, quarter)


def start_send_back(part_rows, dp_count, tile_rows):
    quarter = part_rows.shape[-1]
    flat = part_rows.reshape(-1, tile_rows, quarter)
    returned = lax.all_to_all(flat, ("dp", "expert"), split_axis=0, concat_axis=0, tiled=True)
    return returned.reshape(dp_count, -1, tile_rows, quarter)


def start_widen_rounded(values):
    return lax.optimization_barrier(values.astype(jnp.bfloat16)).astype(jnp.float32)


def start_expert_forward(received, gate_weight, up_weight, down_weight):
    gate_terms = start_widen_rounded(jnp.dot(received, gate_weight, preferred_element_type=jnp.float32))
    up_terms = start_widen_rounded(jnp.dot(received, up_weight, preferred_element_type=jnp.float32))
    gate_pre, up_pre = (
        lax.psum(gate_terms.astype(jnp.bfloat16), "dp").astype(jnp.float32),
        lax.psum(up_terms.astype(jnp.bfloat16), "dp").astype(jnp.float32),
    )
    activated = (jax.nn.silu(gate_pre) * up_pre).astype(jnp.bfloat16)
    part_rows = jnp.dot(activated, down_weight, preferred_element_type=jnp.float32).astype(
        jnp.bfloat16
    )
    return (part_rows, (gate_pre, up_pre, activated))


def start_expert_backward(
    received, grad_recv, kept_state, gate_weight, up_weight, down_weight, grad_sums
):
    gate_pre, up_pre, activated = kept_state
    grad_terms = start_widen_rounded(start_contract_last(grad_recv, down_weight))
    grad_act = lax.psum(grad_terms.astype(jnp.bfloat16), "dp").astype(jnp.float32)
    sigmoid_gate = jax.nn.sigmoid(gate_pre)
    silu_gate = gate_pre * sigmoid_gate
    grad_gate_pre = (
        grad_act * up_pre * sigmoid_gate * (1.0 + gate_pre * (1.0 - sigmoid_gate))
    ).astype(jnp.bfloat16)
    grad_up_pre = (grad_act * silu_gate).astype(jnp.bfloat16)
    back_rows = (
        start_contract_last(grad_gate_pre, gate_weight) + start_contract_last(grad_up_pre, up_weight)
    ).astype(jnp.bfloat16)
    grad_gate = grad_sums[0] + start_contract_first(received, grad_gate_pre)
    grad_up = grad_sums[1] + start_contract_first(received, grad_up_pre)
    grad_down = grad_sums[2] + start_contract_first(activated, grad_recv)
    return (back_rows, (grad_gate, grad_up, grad_down))


def start_body(tokens, cotangent, gain, w_gate, w_up, w_down, route):
    pipe_count = lax.axis_size("pipe")
    dp_count = lax.axis_size("dp")
    expert_count = lax.axis_size("expert")
    section_index = lax.axis_index("pipe")
    gain_row = gain[0]
    gate_weight = w_gate[0, 0]
    up_weight = w_up[0, 0]
    down_weight = w_down[0, 0]
    route_table = route[0, :, :, 0]
    tile_count = route_table.shape[1]
    capacity = max(2, 3 * tile_count // (2 * expert_count))
    hidden = tokens[0]
    saved_ticks = []
    out_rows = hidden
    for pass_index in range(PASSES):
        micro_index = (section_index - pass_index + pipe_count) % pipe_count
        route_now = lax.dynamic_index_in_dim(route_table, micro_index, 0, keepdims=False)
        placed = start_slot_matrix(route_now, expert_count, capacity)
        normed, scaled, inverse = start_normalize(hidden, gain_row)
        received = start_send_out(start_into_slots(placed, normed, TILE, dp_count))
        part_rows, kept_state = start_expert_forward(received, gate_weight, up_weight, down_weight)
        ffn_rows = start_from_slots(placed, start_send_back(part_rows, dp_count, TILE))
        new_hidden = (hidden.astype(jnp.float32) + ffn_rows.astype(jnp.float32)).astype(
            jnp.bfloat16
        )
        saved_ticks.append((placed, scaled, inverse, received, kept_state))
        if pass_index + 1 < PASSES:
            hidden = start_shifted(new_hidden, "pipe", 1)
        else:
            out_rows = new_hidden
    grad_rows = cotangent[0]
    grad_sums = (
        jnp.zeros(gate_weight.shape, jnp.float32),
        jnp.zeros(up_weight.shape, jnp.float32),
        jnp.zeros(down_weight.shape, jnp.float32),
    )
    gain_sum = jnp.zeros(gain_row.shape, jnp.float32)
    entry_grad = grad_rows
    for pass_index in reversed(range(PASSES)):
        placed, scaled, inverse, received, kept_state = saved_ticks[pass_index]
        grad_recv = start_send_out(start_into_slots(placed, grad_rows, TILE, dp_count))
        back_rows, grad_sums = start_expert_backward(
            received, grad_recv, kept_state, gate_weight, up_weight, down_weight, grad_sums
        )
        grad_normed = start_from_slots(placed, start_send_back(back_rows, dp_count, TILE)).astype(jnp.float32)
        gain_sum = gain_sum + jnp.sum(grad_normed * scaled, axis=0)
        grad_scaled = grad_normed * gain_row
        grad_wide = inverse * (
            grad_scaled - scaled * jnp.mean(grad_scaled * scaled, axis=-1, keepdims=True)
        )
        grad_in = (grad_rows.astype(jnp.float32) + grad_wide).astype(jnp.bfloat16)
        if pass_index > 0:
            grad_rows = start_shifted(grad_in, "pipe", -1)
        else:
            entry_grad = grad_in
    gain_total = lax.psum(gain_sum, ("dp", "expert"))
    return (
        out_rows[None],
        entry_grad[None],
        gain_total[None],
        grad_sums[0].astype(jnp.bfloat16)[None, None],
        grad_sums[1].astype(jnp.bfloat16)[None, None],
        grad_sums[2].astype(jnp.bfloat16)[None, None],
    )


def start_solution(mesh):
    placed = (
        P("pipe", ("dp", "expert"), None),
        P("pipe", ("dp", "expert"), None),
        P("pipe", None),
        P("pipe", "expert", "dp", None),
        P("pipe", "expert", "dp", None),
        P("pipe", "expert", None, "dp"),
        P("pipe", None, ("dp", "expert"), None),
    )
    return jax.shard_map(
        start_body,
        mesh=mesh,
        in_specs=placed,
        out_specs=(
            P("pipe", ("dp", "expert"), None),
            P("pipe", ("dp", "expert"), None),
            P("pipe", None),
            P("pipe", "expert", "dp", None),
            P("pipe", "expert", "dp", None),
            P("pipe", "expert", None, "dp"),
        ),
        check_vma=False,
    )


def solution(mesh):
    if mesh.shape["expert"] != PAIR:
        return start_solution(mesh)
    placed = (
        P("pipe", ("dp", "expert"), None),
        P("pipe", ("dp", "expert"), None),
        P("pipe", None),
        P("pipe", "expert", "dp", None),
        P("pipe", "expert", "dp", None),
        P("pipe", "expert", None, "dp"),
        P("pipe", None, ("dp", "expert"), None),
    )
    return jax.shard_map(
        body,
        mesh=mesh,
        in_specs=placed,
        out_specs=placed[:2] + (P("pipe", None),) + placed[3:6],
        check_vma=False,
    )
```

```python
import jax
import jax.numpy as jnp
from jax import lax
from jax.experimental import pallas as pl
from jax.experimental.pallas import tpu as pltpu
from jax.sharding import PartitionSpec as P

TILE = 8
PASSES = 2
PAIR = 2
COLUMNS = 256
LANES = 128
VMEM_BYTES = 12 * 1024 * 1024


epsilon = 1e-06
bf16 = jnp.bfloat16
f32 = jnp.float32


def dot(former, latter, contract):
    return lax.dot_general(
        former, latter, ((contract[:1], contract[1:]), ((), ())), preferred_element_type=f32
    )


def partner_route(size, step):
    return [(i, i ^ step) for i in range(size)]


def swap(block, axis, step):
    return lax.ppermute(block, axis, partner_route(lax.axis_size(axis), step))


def shifted(block, axis, distance):
    size = lax.axis_size(axis)
    return lax.ppermute(block, axis, [(i, (i + distance) % size) for i in range(size)])


def quarter_of(rows, index, width):
    return lax.dynamic_slice_in_dim(rows, index * width, width, axis=-1)


def assemble(parts):
    here = lax.axis_index("dp")
    rows, width = parts[0].shape
    whole = jnp.zeros((rows, width * len(parts)), parts[0].dtype)
    for step, part in enumerate(parts):
        whole = lax.dynamic_update_slice_in_dim(whole, part, (here ^ step) * width, axis=1)
    return whole


def from_quarters(parts):
    return assemble(
        [swap(part, "dp", step) if step else part for step, part in enumerate(parts)]
    )


def gather_rows(rows, dp_count):
    return [rows] + [swap(rows, "dp", step) for step in range(1, dp_count)]


def after(value, *earlier):
    return lax.optimization_barrier((value,) + earlier)[0]


def columns_of(extent):
    return COLUMNS if extent % COLUMNS == 0 else extent


def kernel_call(body, operands, weights, out_shape, scratch, weight_cost=1):
    count, kept, made = len(operands), len(weights), len(out_shape)
    rows = max(shape.shape[0] for shape in out_shape)

    def call(*refs):
        operand_refs, refs = refs[:count], refs[count:]
        weight_refs, refs = refs[:kept], refs[kept:]
        body(operand_refs, weight_refs, refs[:made], refs[made:])

    in_vmem = pl.BlockSpec(memory_space=pltpu.VMEM)
    return pl.pallas_call(
        call,
        in_specs=[in_vmem] * (count + kept),
        out_specs=[in_vmem] * made,
        out_shape=out_shape,
        scratch_shapes=scratch,
        compiler_params=pltpu.CompilerParams(vmem_limit_bytes=VMEM_BYTES),
        cost_estimate=pl.CostEstimate(
            flops=weight_cost * 2 * rows * sum(weight.size for weight in weights),
            bytes_accessed=0,
            transcendentals=0,
        ),
    )(*operands, *weights)


def resident(arrays):
    count = len(arrays)

    def call(*refs):
        arrivals = refs[-1]
        copies = [
            pltpu.make_async_copy(refs[i], refs[count + i], arrivals.at[i]) for i in range(count)
        ]
        for copy in copies:
            copy.start()
        for copy in copies:
            copy.wait()

    return pl.pallas_call(
        call,
        in_specs=[pl.BlockSpec(memory_space=pltpu.HBM)] * count,
        out_specs=[pl.BlockSpec(memory_space=pltpu.VMEM)] * count,
        out_shape=[pltpu.VMEM(a.shape, a.dtype) for a in arrays],
        scratch_shapes=[pltpu.SemaphoreType.DMA((count,))],
        compiler_params=pltpu.CompilerParams(vmem_limit_bytes=VMEM_BYTES),
        cost_estimate=pl.CostEstimate(
            flops=0,
            bytes_accessed=2 * sum(a.size * a.dtype.itemsize for a in arrays),
            transcendentals=0,
        ),
    )(*(pltpu.with_memory_space_constraint(a, pltpu.HBM) for a in arrays))


def store_parts(refs, columns, value):
    size = value.shape[0] // len(refs)
    for index, ref in enumerate(refs):
        ref[:, columns] = value[index * size : (index + 1) * size]


def each_tile(extent, visit):
    tile = columns_of(extent)

    def step(j, carry):
        visit(span(j, tile))
        return carry

    lax.fori_loop(0, extent // tile, step, 0)


def span(tile, size):
    return pl.ds(pl.multiple_of(tile * size, size), size)


def in_lanes(scalar):
    coarse = scalar.astype(bf16).astype(f32)
    lane = lax.broadcasted_iota(jnp.int32, (scalar.shape[0], LANES), 1)
    return jnp.where(lane == 0, coarse, jnp.where(lane == 1, scalar - coarse, 0.0)).astype(bf16)


def split_rows(rows_ref, mask_ref, other_ref, own_ref):
    rows = rows_ref[...]
    chosen = mask_ref[...] > 0.5
    own_ref[...] = jnp.where(chosen, rows, jnp.zeros_like(rows))
    other_ref[...] = jnp.where(chosen, jnp.zeros_like(rows), rows)


def hidden_parts(blocks, part_rows, gain_part, mask, gate_pair, up_pair, expert=None):
    width, units = gate_pair[0].shape
    routed = expert is not None
    block_rows = part_rows if routed else blocks[0].shape[0]
    rows = block_rows * len(blocks)
    parts_count = rows // part_rows
    passes = PASSES if routed else 0

    def body(operand_refs, weight_refs, out_refs, scratch):
        *block_refs, gain_ref, choice_ref = operand_refs
        part_refs, (other_rows, own_rows) = out_refs[:parts_count], out_refs[parts_count:][:2]
        mask_ref = out_refs[parts_count + 2] if routed else choice_ref
        (gained_ref,) = scratch
        for index, ref in enumerate(block_refs):
            place = slice(index * block_rows, (index + 1) * block_rows)
            block = ref[:block_rows]
            wide = block.astype(f32)
            gained_ref[place] = (wide * gain_ref[...]).astype(bf16)
            if not routed:
                squares = jnp.sum(wide * wide, axis=-1, keepdims=True)
                tails = [ref.at[:, 2 * units :] for ref in part_refs]
                store_parts(tails, slice(None), in_lanes(squares))
            if routed:
                out_refs[-1][place] = block
                tiles = block_rows // TILE
                row = lax.broadcasted_iota(jnp.int32, (block_rows, tiles), 0)
                first = TILE * lax.broadcasted_iota(jnp.int32, (block_rows, tiles), 1)
                chosen = ((row >= first) & (row < first + TILE)).astype(bf16)
                experts = dot(chosen, ref[block_rows:, :LANES], (1, 0)) - choice_ref[...]
                for k in range(passes):
                    near = jnp.abs(experts[:, k : k + 1]) < 0.5
                    out_refs[parts_count + 2 + k][place] = jnp.where(near, 1.0, 0.0)

        split_rows(gained_ref, mask_ref, other_rows, own_rows)
        for pair in range(2):

            def visit(columns, pair=pair):
                own, other = weight_refs[2 * pair : 2 * pair + 2]
                part = jnp.where(
                    mask_ref[...] > 0.5,
                    dot(gained_ref[...], own[:, columns], (1, 0)),
                    dot(gained_ref[...], other[:, columns], (1, 0)),
                ).astype(bf16)
                store_parts([ref.at[:, pair * units :] for ref in part_refs], columns, part)

            each_tile(units, visit)

    outs = kernel_call(
        body,
        (*blocks, gain_part, expert if routed else mask),
        (*gate_pair, *up_pair),
        [jax.ShapeDtypeStruct((part_rows, 2 * units + LANES * int(not routed)), bf16)]
        * parts_count
        + [jax.ShapeDtypeStruct((rows, width), bf16)] * 2
        + [jax.ShapeDtypeStruct((rows, 1), f32)] * passes
        + [jax.ShapeDtypeStruct((rows, width), bf16)] * int(routed),
        [pltpu.VMEM((rows, width), bf16)],
    )
    return outs[:parts_count], outs[parts_count : parts_count + 2], outs[parts_count + 2 :]


def row_scale(block):
    rows, features = block.shape

    def body(operand_refs, weight_refs, out_refs, scratch):
        wide = operand_refs[0][...].astype(f32)
        total = jnp.sum(wide * wide, axis=-1, keepdims=True)
        out_refs[0][...] = lax.rsqrt(total / features + epsilon)

    (scale,) = kernel_call(body, (block,), (), [jax.ShapeDtypeStruct((rows, 1), f32)], [])
    return scale


def activate(parts, units, features, inverse=None):
    rows = parts[0].shape[0]
    count = len(parts)

    def body(operand_refs, weight_refs, out_refs, scratch):
        part_refs = operand_refs[:count]
        total = part_refs[0][...].astype(f32)
        for ref in part_refs[1:]:
            total = total + ref[...].astype(f32)
        if inverse is None:
            squares = jnp.sum(total[:, 2 * units :], axis=-1, keepdims=True)
            scale = lax.rsqrt(squares / features + epsilon)
        else:
            scale = operand_refs[-1][...]
        gate, up = total[:, :units] * scale, total[:, units : 2 * units] * scale
        out_refs[0][...] = gate
        out_refs[1][...] = up
        out_refs[2][...] = (gate / (1.0 + jnp.exp(-gate)) * up).astype(bf16)
        out_refs[3][...] = scale

    return kernel_call(
        body,
        tuple(parts) + (() if inverse is None else (inverse,)),
        (),
        [jax.ShapeDtypeStruct((rows, units), f32)] * 2
        + [jax.ShapeDtypeStruct((rows, units), bf16), jax.ShapeDtypeStruct((rows, 1), f32)],
        [],
    )


def join(joined, refs, columns):
    size = refs[0].shape[0]
    for index, ref in enumerate(refs):
        joined[index * size : (index + 1) * size] = ref[:, columns]


def add_down(blocks, mask, down_pair, hidden, in_parts):
    count = len(blocks)
    part_rows, units = blocks[0].shape
    rows = part_rows * count
    width = down_pair[0].shape[1]
    out_count = count if in_parts else 1

    def body(operand_refs, weight_refs, out_refs, scratch):
        *block_refs, mask_ref, hidden_ref = operand_refs
        row_refs = out_refs[:out_count]
        (joined,) = scratch
        join(joined, block_refs, slice(None))
        split_rows(joined, mask_ref, *out_refs[-2:])
        own, other = weight_refs

        def visit(columns):
            ffn = jnp.where(
                mask_ref[...] > 0.5,
                dot(joined[...], own[:, columns], (1, 0)),
                dot(joined[...], other[:, columns], (1, 0)),
            ).astype(bf16)
            out = (hidden_ref[:, columns].astype(f32) + ffn.astype(f32)).astype(bf16)
            store_parts(row_refs, columns, out)

        each_tile(width, visit)

    outs = kernel_call(
        body,
        (*blocks, mask, hidden),
        down_pair,
        [jax.ShapeDtypeStruct((rows // out_count, width), bf16)] * out_count
        + [jax.ShapeDtypeStruct((rows, units), bf16)] * 2,
        [pltpu.VMEM((rows, units), bf16)],
        weight_cost=0 if in_parts else 1,
    )
    return outs[:out_count], outs[-2:]


def act_grad_parts(blocks, part_rows, mask, down_pair):
    rows = sum(block.shape[0] for block in blocks)
    parts_count = rows // part_rows
    units, width = down_pair[0].shape

    def body(operand_refs, weight_refs, out_refs, scratch):
        *block_refs, mask_ref = operand_refs
        *part_refs, grad_ref = out_refs
        own, other = weight_refs
        join(grad_ref, block_refs, slice(None))

        def visit(columns):
            part = jnp.where(
                mask_ref[...] > 0.5,
                dot(grad_ref[...], own[columns], (1, 1)),
                dot(grad_ref[...], other[columns], (1, 1)),
            ).astype(bf16)
            store_parts(part_refs, columns, part)

        each_tile(units, visit)

    outs = kernel_call(
        body,
        (*blocks, mask),
        down_pair,
        [jax.ShapeDtypeStruct((part_rows, units), bf16)] * parts_count
        + [jax.ShapeDtypeStruct((rows, width), bf16)],
        [],
    )
    return outs[:parts_count], outs[parts_count]


def hidden_grads(parts, gate, up, inverse, features):
    rows, units = gate.shape

    def body(operand_refs, weight_refs, out_refs, scratch):
        *part_refs, gate_ref, up_ref, inverse_ref = operand_refs
        (out_ref,) = out_refs
        grad_act = part_refs[0][...].astype(f32)
        for ref in part_refs[1:]:
            grad_act = grad_act + ref[...].astype(f32)
        gate_now, up_now, scale = gate_ref[...], up_ref[...], inverse_ref[...]
        sigmoid = 1.0 / (1.0 + jnp.exp(-gate_now))
        scaled = grad_act * scale
        gate_grad = scaled * up_now * sigmoid * (1.0 + gate_now * (1.0 - sigmoid))
        up_grad = scaled * (gate_now * sigmoid)
        shrink = jnp.sum(gate_grad * gate_now + up_grad * up_now, axis=-1, keepdims=True) * (
            scale / features
        )
        out_ref[:, :units] = gate_grad.astype(bf16)
        out_ref[:, units : 2 * units] = up_grad.astype(bf16)
        out_ref[:, 2 * units :] = in_lanes(shrink)

    (sent,) = kernel_call(
        body,
        (*parts, gate, up, inverse),
        [],
        [jax.ShapeDtypeStruct((rows, 2 * units + LANES), bf16)],
        [],
    )
    return sent


def input_grad(blocks, mask, gate_pair, up_pair, grad, hidden, gain_part, in_parts):
    count = len(blocks)
    part_rows = blocks[0].shape[0]
    rows = part_rows * count
    width, units = gate_pair[0].shape
    out_count = count if in_parts else 1

    def body(operand_refs, weight_refs, out_refs, scratch):
        *block_refs, mask_ref, grad_ref, hidden_ref, gain_ref = operand_refs
        *row_refs, sum_ref = out_refs
        joined, shrink = scratch
        join(joined, block_refs, slice(0, 2 * units))
        for index, ref in enumerate(block_refs):
            tail = ref[:, 2 * units :].astype(f32)
            shrink[index * part_rows : (index + 1) * part_rows] = jnp.sum(
                tail, axis=-1, keepdims=True
            )

        gate_own, gate_other, up_own, up_other = weight_refs

        def visit(columns):
            def back_of(gate, up):
                return dot(joined[:, :units], gate[columns], (1, 1)) + dot(
                    joined[:, units:], up[columns], (1, 1)
                )

            back = jnp.where(
                mask_ref[...] > 0.5, back_of(gate_own, up_own), back_of(gate_other, up_other)
            )
            wide = hidden_ref[:, columns].astype(f32)
            sum_ref[:, columns] = jnp.sum(back * wide, axis=0, keepdims=True)
            out = (
                grad_ref[:, columns].astype(f32)
                + back * gain_ref[:, columns]
                - wide * shrink[...]
            ).astype(bf16)
            store_parts(row_refs, columns, out)

        each_tile(width, visit)

    outs = kernel_call(
        body,
        (*blocks, mask, grad, hidden, gain_part),
        (*gate_pair, *up_pair),
        [jax.ShapeDtypeStruct((rows // out_count, width), bf16)] * out_count
        + [jax.ShapeDtypeStruct((1, width), f32)],
        [
            pltpu.VMEM((rows, 2 * units), bf16),
            pltpu.VMEM((rows, 1), f32),
        ],
    )
    return outs[:out_count], outs[out_count]


def body(tokens, cotangent, gain, w_gate, w_up, w_down, route):
    pipe_count = lax.axis_size("pipe")
    dp_count = lax.axis_size("dp")
    section = lax.axis_index("pipe")
    expert = lax.axis_index("expert")
    here = lax.axis_index("dp")
    features = tokens.shape[-1]
    width = features // dp_count
    units = w_gate.shape[-1]
    gain_part = lax.dynamic_slice_in_dim(gain, here * width, width, axis=1)

    groups = (slice(0, dp_count - 1), slice(dp_count - 1, dp_count))
    own_tokens = tokens[0]
    rows = own_tokens.shape[0]
    micro = [(section - k + pipe_count) % pipe_count for k in range(PASSES)]
    route_rows = jnp.stack(
        [lax.dynamic_index_in_dim(route[0, :, :, 0], m, 0, keepdims=False) for m in micro], axis=1
    ).astype(bf16)
    expert_id = jnp.full((1, LANES), expert, f32)
    route_rows = after(jnp.pad(route_rows, ((0, 0), (0, width - PASSES))), expert_id)

    def tokens_quarter(step):
        return jnp.concatenate([quarter_of(own_tokens, here ^ step, width), route_rows])

    def cotangent_quarter(step, *earlier):
        return quarter_of(after(cotangent[0], *earlier), here ^ step, width)

    def sent(parts):
        return [swap(part, "dp", step) if step else part for step, part in enumerate(parts)]

    def moved(pieces, distance):
        return [shifted(piece, "pipe", distance) for piece in pieces]

    def weight_grad(lefts, right, wanted):
        return dot(lefts[wanted], right, (0, 0))

    def stacked(pairs):
        return [jnp.concatenate(pieces) for pieces in zip(*pairs)]

    quarters = [tokens_quarter(step) for step in range(dp_count)]
    weights = [
        weight
        for own in (w_gate, w_up, w_down)
        for weight in (own[0, 0], swap(own[0, 0], "expert", 1))
    ]
    weights = resident(weights)
    gate_pair, up_pair, down_pair = weights[:2], weights[2:4], weights[4:]
    quarters[-1] = after(quarters[-1], *weights)
    blocks = sent(quarters)
    inverse = row_scale(own_tokens)

    parts, gained, masks, hidden = [], [], [], []
    for group in groups:
        made, scaled, (*choices, joined) = hidden_parts(
            blocks[group], rows, gain_part, None, gate_pair, up_pair, expert_id
        )
        parts += made
        gained.append(scaled)
        masks.append(choices)
        hidden.append(joined)
    masks = list(zip(*masks))
    gate, up, activated, _ = activate(sent(parts), units, features, inverse)
    kept = [(hidden, gained, inverse, gate, up)]
    first_activated = gather_rows(activated, dp_count)
    next_hidden, first_rows = [], []
    for index in reversed(range(len(groups))):
        near = first_activated[groups[index]]
        if next_hidden:
            near = [after(near[0], next_hidden[0]), *near[1:]]
        (out,), split = add_down(near, masks[0][index], down_pair, hidden[index], False)
        next_hidden.insert(0, out)
        first_rows.insert(0, split)
    hidden = moved(next_hidden, 1)
    grad_blocks = sent([cotangent_quarter(step, next_hidden[0]) for step in range(dp_count)])
    act_parts, grad = [], []
    for group, mask in zip(groups, masks[1]):
        made, joined = act_grad_parts(grad_blocks[group], rows, mask, down_pair)
        act_parts += made
        grad.append(joined)
    act_grads = act_parts
    act_parts = sent(act_parts)
    hidden[0] = after(hidden[0], act_grads[0])

    parts, gained = [], []
    for rows_in, mask in zip(hidden, masks[1]):
        if parts:
            rows_in = after(rows_in, parts[0])
        made, scaled, _ = hidden_parts([rows_in], rows, gain_part, mask, gate_pair, up_pair)
        parts += made
        gained.append(scaled)
    gate, up, activated, inverse = activate(sent(parts), units, features)
    kept.append((hidden, gained, inverse, gate, up))

    gain_sum = jnp.zeros((1, width), f32)
    for k in reversed(range(PASSES)):
        hidden, gained, inverse, gate, up = kept[k]
        gained = stacked(gained)
        payload = hidden_grads(act_parts, gate, up, inverse, features)
        both_grad = gather_rows(payload, dp_count)
        joined = jnp.concatenate(both_grad)
        rights = [joined[:, :units], joined[:, units : 2 * units]]
        if k == 0:
            lefts = [gained, gained, stacked(first_rows)]
            rights.append(jnp.concatenate(grad))
        outs = []
        for index in reversed(range(len(groups))):
            made, gain_term = input_grad(
                both_grad[groups[index]],
                masks[k][index],
                gate_pair,
                up_pair,
                grad[index],
                hidden[index],
                gain_part,
                k == 0,
            )
            outs = list(made) + outs
            gain_sum = gain_sum + gain_term
            if k == 0 and index > 0:
                ready = [after(right, made[0]) for right in rights[:2]] + rights[2:]
                given = [
                    (weight_grad(left, right, False) + soon.astype(f32)).astype(bf16)
                    for left, right, soon in zip(lefts, ready, early[False])
                ]
                both_grad[1] = after(both_grad[1], *given)
                received = [swap(value, "expert", 1) for value in given]
        if k > 0:
            last_grad = jnp.concatenate(grad)
            grad = moved(outs, -1)
            last_activated = gather_rows(after(activated, both_grad[-1]), dp_count)
            rights = [after(right, *last_activated[1:]) for right in rights]
            early = {
                wanted: [weight_grad(gained, right, wanted).astype(bf16) for right in rights]
                for wanted in (False, True)
            }
            out_parts, last_rows = [], []
            for group, choice, rows_in in zip(groups, masks[1], hidden):
                made, split = add_down(
                    last_activated[group], choice, down_pair, rows_in, True
                )
                out_parts += made
                last_rows.append(split)
            out_rows = from_quarters(out_parts)
            grad[0] = after(grad[0], *out_parts, *early[False], *early[True])
            act_parts, joined = [], []
            for rows_in, choice in zip(grad, masks[0]):
                made, copied = act_grad_parts([rows_in], rows, choice, down_pair)
                act_parts += made
                joined.append(copied)
            grad = joined
            last_rows = stacked(last_rows)
            for wanted in (False, True):
                early[wanted].append(weight_grad(last_rows, last_grad, wanted).astype(bf16))
            act_parts = sent(act_parts)
            act_parts[1] = after(act_parts[1], early[False][2], early[True][2])

    returned = sent(outs)
    rights = [after(right, *outs) for right in rights]
    gain_sum = gain_sum + swap(gain_sum, "expert", 1)
    gain_rows = jnp.concatenate(gather_rows(after(gain_sum, *received), dp_count))
    gain_all = jnp.zeros((features,), f32)
    for step in range(dp_count):
        gain_all = lax.dynamic_update_slice_in_dim(
            gain_all, gain_rows[step], (here ^ step) * width, axis=0
        )
    grads = [
        (weight_grad(left, right, True) + soon.astype(f32) + other.astype(f32)).astype(bf16)
        for left, right, soon, other in zip(lefts, rights, early[True], received)
    ]
    returned = list(lax.optimization_barrier((*returned, *grads)))[:dp_count]
    entry = assemble(returned)
    return (
        out_rows[None],
        entry[None],
        gain_all[None],
        grads[0][None, None],
        grads[1][None, None],
        grads[2][None, None],
    )


def start_shifted(block, axis, distance):
    devices = range(lax.axis_size(axis))
    route = [((i - distance) % len(devices), i) for i in devices]
    return lax.ppermute(block, axis, route)


def start_contract_last(former, latter):
    return lax.dot_general(
        former, latter, (((1,), (1,)), ((), ())), preferred_element_type=jnp.float32
    )


def start_contract_first(former, latter):
    return lax.dot_general(
        former, latter, (((0,), (0,)), ((), ())), preferred_element_type=jnp.float32
    )


def start_normalize(hidden, gain_row):
    widened = hidden.astype(jnp.float32)
    inverse = lax.rsqrt(jnp.mean(widened * widened, axis=-1, keepdims=True) + epsilon)
    scaled = widened * inverse
    return ((scaled * gain_row).astype(jnp.bfloat16), scaled, inverse)


def start_slot_matrix(route_now, expert_count, capacity):
    tile_count = route_now.shape[0]
    expert_ids = jnp.arange(expert_count, dtype=jnp.int32)
    member = (route_now[None, :] == expert_ids[:, None]).astype(jnp.int32)
    earlier = jnp.cumsum(member, axis=1) - member
    rank_ids = jnp.arange(capacity, dtype=jnp.int32)
    placed = member[:, None, :] * (earlier[:, None, :] == rank_ids[None, :, None]).astype(jnp.int32)
    return placed.reshape(expert_count * capacity, tile_count)


def start_into_slots(placed, rows, tile_rows, dp_count):
    width = rows.shape[-1]
    tile_blocks = rows.reshape(placed.shape[1], tile_rows, dp_count, width // dp_count)
    return jnp.einsum(
        "st,trqd->qsrd",
        placed.astype(jnp.bfloat16),
        tile_blocks,
        preferred_element_type=jnp.float32,
    ).astype(jnp.bfloat16)


def start_from_slots(placed, slot_rows):
    merged = jnp.einsum(
        "st,qsrd->trqd", placed.astype(jnp.bfloat16), slot_rows, preferred_element_type=jnp.float32
    ).astype(jnp.bfloat16)
    return merged.reshape(merged.shape[0] * merged.shape[1], -1)


def start_send_out(slot_rows):
    quarter = slot_rows.shape[-1]
    flat = slot_rows.reshape((-1,) + slot_rows.shape[2:])
    arrived = lax.all_to_all(flat, ("dp", "expert"), split_axis=0, concat_axis=0, tiled=True)
    return arrived.reshape(-1, quarter)


def start_send_back(part_rows, dp_count, tile_rows):
    quarter = part_rows.shape[-1]
    flat = part_rows.reshape(-1, tile_rows, quarter)
    returned = lax.all_to_all(flat, ("dp", "expert"), split_axis=0, concat_axis=0, tiled=True)
    return returned.reshape(dp_count, -1, tile_rows, quarter)


def start_widen_rounded(values):
    return lax.optimization_barrier(values.astype(jnp.bfloat16)).astype(jnp.float32)


def start_expert_forward(received, gate_weight, up_weight, down_weight):
    gate_terms = start_widen_rounded(jnp.dot(received, gate_weight, preferred_element_type=jnp.float32))
    up_terms = start_widen_rounded(jnp.dot(received, up_weight, preferred_element_type=jnp.float32))
    gate_pre, up_pre = (
        lax.psum(gate_terms.astype(jnp.bfloat16), "dp").astype(jnp.float32),
        lax.psum(up_terms.astype(jnp.bfloat16), "dp").astype(jnp.float32),
    )
    activated = (jax.nn.silu(gate_pre) * up_pre).astype(jnp.bfloat16)
    part_rows = jnp.dot(activated, down_weight, preferred_element_type=jnp.float32).astype(
        jnp.bfloat16
    )
    return (part_rows, (gate_pre, up_pre, activated))


def start_expert_backward(
    received, grad_recv, kept_state, gate_weight, up_weight, down_weight, grad_sums
):
    gate_pre, up_pre, activated = kept_state
    grad_terms = start_widen_rounded(start_contract_last(grad_recv, down_weight))
    grad_act = lax.psum(grad_terms.astype(jnp.bfloat16), "dp").astype(jnp.float32)
    sigmoid_gate = jax.nn.sigmoid(gate_pre)
    silu_gate = gate_pre * sigmoid_gate
    grad_gate_pre = (
        grad_act * up_pre * sigmoid_gate * (1.0 + gate_pre * (1.0 - sigmoid_gate))
    ).astype(jnp.bfloat16)
    grad_up_pre = (grad_act * silu_gate).astype(jnp.bfloat16)
    back_rows = (
        start_contract_last(grad_gate_pre, gate_weight) + start_contract_last(grad_up_pre, up_weight)
    ).astype(jnp.bfloat16)
    grad_gate = grad_sums[0] + start_contract_first(received, grad_gate_pre)
    grad_up = grad_sums[1] + start_contract_first(received, grad_up_pre)
    grad_down = grad_sums[2] + start_contract_first(activated, grad_recv)
    return (back_rows, (grad_gate, grad_up, grad_down))


def start_body(tokens, cotangent, gain, w_gate, w_up, w_down, route):
    pipe_count = lax.axis_size("pipe")
    dp_count = lax.axis_size("dp")
    expert_count = lax.axis_size("expert")
    section_index = lax.axis_index("pipe")
    gain_row = gain[0]
    gate_weight = w_gate[0, 0]
    up_weight = w_up[0, 0]
    down_weight = w_down[0, 0]
    route_table = route[0, :, :, 0]
    tile_count = route_table.shape[1]
    capacity = max(2, 3 * tile_count // (2 * expert_count))
    hidden = tokens[0]
    saved_ticks = []
    out_rows = hidden
    for pass_index in range(PASSES):
        micro_index = (section_index - pass_index + pipe_count) % pipe_count
        route_now = lax.dynamic_index_in_dim(route_table, micro_index, 0, keepdims=False)
        placed = start_slot_matrix(route_now, expert_count, capacity)
        normed, scaled, inverse = start_normalize(hidden, gain_row)
        received = start_send_out(start_into_slots(placed, normed, TILE, dp_count))
        part_rows, kept_state = start_expert_forward(received, gate_weight, up_weight, down_weight)
        ffn_rows = start_from_slots(placed, start_send_back(part_rows, dp_count, TILE))
        new_hidden = (hidden.astype(jnp.float32) + ffn_rows.astype(jnp.float32)).astype(
            jnp.bfloat16
        )
        saved_ticks.append((placed, scaled, inverse, received, kept_state))
        if pass_index + 1 < PASSES:
            hidden = start_shifted(new_hidden, "pipe", 1)
        else:
            out_rows = new_hidden
    grad_rows = cotangent[0]
    grad_sums = (
        jnp.zeros(gate_weight.shape, jnp.float32),
        jnp.zeros(up_weight.shape, jnp.float32),
        jnp.zeros(down_weight.shape, jnp.float32),
    )
    gain_sum = jnp.zeros(gain_row.shape, jnp.float32)
    entry_grad = grad_rows
    for pass_index in reversed(range(PASSES)):
        placed, scaled, inverse, received, kept_state = saved_ticks[pass_index]
        grad_recv = start_send_out(start_into_slots(placed, grad_rows, TILE, dp_count))
        back_rows, grad_sums = start_expert_backward(
            received, grad_recv, kept_state, gate_weight, up_weight, down_weight, grad_sums
        )
        grad_normed = start_from_slots(placed, start_send_back(back_rows, dp_count, TILE)).astype(jnp.float32)
        gain_sum = gain_sum + jnp.sum(grad_normed * scaled, axis=0)
        grad_scaled = grad_normed * gain_row
        grad_wide = inverse * (
            grad_scaled - scaled * jnp.mean(grad_scaled * scaled, axis=-1, keepdims=True)
        )
        grad_in = (grad_rows.astype(jnp.float32) + grad_wide).astype(jnp.bfloat16)
        if pass_index > 0:
            grad_rows = start_shifted(grad_in, "pipe", -1)
        else:
            entry_grad = grad_in
    gain_total = lax.psum(gain_sum, ("dp", "expert"))
    return (
        out_rows[None],
        entry_grad[None],
        gain_total[None],
        grad_sums[0].astype(jnp.bfloat16)[None, None],
        grad_sums[1].astype(jnp.bfloat16)[None, None],
        grad_sums[2].astype(jnp.bfloat16)[None, None],
    )


def start_solution(mesh):
    placed = (
        P("pipe", ("dp", "expert"), None),
        P("pipe", ("dp", "expert"), None),
        P("pipe", None),
        P("pipe", "expert", "dp", None),
        P("pipe", "expert", "dp", None),
        P("pipe", "expert", None, "dp"),
        P("pipe", None, ("dp", "expert"), None),
    )
    return jax.shard_map(
        start_body,
        mesh=mesh,
        in_specs=placed,
        out_specs=(
            P("pipe", ("dp", "expert"), None),
            P("pipe", ("dp", "expert"), None),
            P("pipe", None),
            P("pipe", "expert", "dp", None),
            P("pipe", "expert", "dp", None),
            P("pipe", "expert", None, "dp"),
        ),
        check_vma=False,
    )


def solution(mesh):
    if mesh.shape["expert"] != PAIR:
        return start_solution(mesh)
    placed = (
        P("pipe", ("dp", "expert"), None),
        P("pipe", ("dp", "expert"), None),
        P("pipe", None),
        P("pipe", "expert", "dp", None),
        P("pipe", "expert", "dp", None),
        P("pipe", "expert", None, "dp"),
        P("pipe", None, ("dp", "expert"), None),
    )
    return jax.shard_map(
        body,
        mesh=mesh,
        in_specs=placed,
        out_specs=placed[:2] + (P("pipe", None),) + placed[3:6],
        check_vma=False,
    )
```

```python
import jax
import jax.numpy as jnp
from jax import lax
from jax.experimental import pallas as pl
from jax.experimental.pallas import tpu as pltpu
from jax.sharding import PartitionSpec as P

TILE = 8
PASSES = 2
PAIR = 2
COLUMNS = 256
LANES = 128
VMEM_BYTES = 12 * 1024 * 1024


epsilon = 1e-06
bf16 = jnp.bfloat16
f32 = jnp.float32


def dot(former, latter, contract):
    return lax.dot_general(
        former, latter, ((contract[:1], contract[1:]), ((), ())), preferred_element_type=f32
    )


def partner_route(size, step):
    return [(i, i ^ step) for i in range(size)]


def swap(block, axis, step):
    return lax.ppermute(block, axis, partner_route(lax.axis_size(axis), step))


def shifted(block, axis, distance):
    size = lax.axis_size(axis)
    return lax.ppermute(block, axis, [(i, (i + distance) % size) for i in range(size)])


def quarter_of(rows, index, width):
    return lax.dynamic_slice_in_dim(rows, index * width, width, axis=-1)


def assemble(parts):
    here = lax.axis_index("dp")
    rows, width = parts[0].shape
    whole = jnp.zeros((rows, width * len(parts)), parts[0].dtype)
    for step, part in enumerate(parts):
        whole = lax.dynamic_update_slice_in_dim(whole, part, (here ^ step) * width, axis=1)
    return whole


def from_quarters(parts):
    return assemble(
        [swap(part, "dp", step) if step else part for step, part in enumerate(parts)]
    )


def gather_rows(rows, dp_count):
    return [rows] + [swap(rows, "dp", step) for step in range(1, dp_count)]


def after(value, *earlier):
    return lax.optimization_barrier((value,) + earlier)[0]


def columns_of(extent):
    return COLUMNS if extent % COLUMNS == 0 else extent


def kernel_call(body, operands, weights, out_shape, scratch, weight_cost=1):
    count, kept, made = len(operands), len(weights), len(out_shape)
    rows = max(shape.shape[0] for shape in out_shape)

    def call(*refs):
        operand_refs, refs = refs[:count], refs[count:]
        weight_refs, refs = refs[:kept], refs[kept:]
        body(operand_refs, weight_refs, refs[:made], refs[made:])

    in_vmem = pl.BlockSpec(memory_space=pltpu.VMEM)
    return pl.pallas_call(
        call,
        in_specs=[in_vmem] * (count + kept),
        out_specs=[in_vmem] * made,
        out_shape=out_shape,
        scratch_shapes=scratch,
        compiler_params=pltpu.CompilerParams(vmem_limit_bytes=VMEM_BYTES),
        cost_estimate=pl.CostEstimate(
            flops=weight_cost * 2 * rows * sum(weight.size for weight in weights),
            bytes_accessed=0,
            transcendentals=0,
        ),
    )(*operands, *weights)


def resident(arrays):
    count = len(arrays)

    def call(*refs):
        arrivals = refs[-1]
        copies = [
            pltpu.make_async_copy(refs[i], refs[count + i], arrivals.at[i]) for i in range(count)
        ]
        for copy in copies:
            copy.start()
        for copy in copies:
            copy.wait()

    return pl.pallas_call(
        call,
        in_specs=[pl.BlockSpec(memory_space=pltpu.HBM)] * count,
        out_specs=[pl.BlockSpec(memory_space=pltpu.VMEM)] * count,
        out_shape=[pltpu.VMEM(a.shape, a.dtype) for a in arrays],
        scratch_shapes=[pltpu.SemaphoreType.DMA((count,))],
        compiler_params=pltpu.CompilerParams(vmem_limit_bytes=VMEM_BYTES),
        cost_estimate=pl.CostEstimate(
            flops=0,
            bytes_accessed=2 * sum(a.size * a.dtype.itemsize for a in arrays),
            transcendentals=0,
        ),
    )(*(pltpu.with_memory_space_constraint(a, pltpu.HBM) for a in arrays))


def store_parts(refs, columns, value):
    size = value.shape[0] // len(refs)
    for index, ref in enumerate(refs):
        ref[:, columns] = value[index * size : (index + 1) * size]


def each_tile(extent, visit):
    tile = columns_of(extent)

    def step(j, carry):
        visit(span(j, tile))
        return carry

    lax.fori_loop(0, extent // tile, step, 0)


def span(tile, size):
    return pl.ds(pl.multiple_of(tile * size, size), size)


def in_lanes(scalar):
    coarse = scalar.astype(bf16).astype(f32)
    lane = lax.broadcasted_iota(jnp.int32, (scalar.shape[0], LANES), 1)
    return jnp.where(lane == 0, coarse, jnp.where(lane == 1, scalar - coarse, 0.0)).astype(bf16)


def split_rows(rows_ref, mask_ref, other_ref, own_ref):
    rows = rows_ref[...]
    chosen = mask_ref[...] > 0.5
    own_ref[...] = jnp.where(chosen, rows, jnp.zeros_like(rows))
    other_ref[...] = jnp.where(chosen, jnp.zeros_like(rows), rows)


def hidden_parts(blocks, part_rows, gain_part, mask, gate_pair, up_pair, expert=None):
    width, units = gate_pair[0].shape
    routed = expert is not None
    block_rows = part_rows if routed else blocks[0].shape[0]
    rows = block_rows * len(blocks)
    parts_count = rows // part_rows
    passes = PASSES if routed else 0

    def body(operand_refs, weight_refs, out_refs, scratch):
        *block_refs, gain_ref, choice_ref = operand_refs
        part_refs, (other_rows, own_rows) = out_refs[:parts_count], out_refs[parts_count:][:2]
        mask_ref = out_refs[parts_count + 2] if routed else choice_ref
        (gained_ref,) = scratch
        for index, ref in enumerate(block_refs):
            place = slice(index * block_rows, (index + 1) * block_rows)
            block = ref[:block_rows]
            wide = block.astype(f32)
            gained_ref[place] = (wide * gain_ref[...]).astype(bf16)
            if not routed:
                squares = jnp.sum(wide * wide, axis=-1, keepdims=True)
                tails = [ref.at[:, 2 * units :] for ref in part_refs]
                store_parts(tails, slice(None), in_lanes(squares))
            if routed:
                out_refs[-1][place] = block
                tiles = block_rows // TILE
                row = lax.broadcasted_iota(jnp.int32, (block_rows, tiles), 0)
                first = TILE * lax.broadcasted_iota(jnp.int32, (block_rows, tiles), 1)
                chosen = ((row >= first) & (row < first + TILE)).astype(bf16)
                experts = dot(chosen, ref[block_rows:, :LANES], (1, 0)) - choice_ref[...]
                for k in range(passes):
                    near = jnp.abs(experts[:, k : k + 1]) < 0.5
                    out_refs[parts_count + 2 + k][place] = jnp.where(near, 1.0, 0.0)

        split_rows(gained_ref, mask_ref, other_rows, own_rows)
        for pair in range(2):

            def visit(columns, pair=pair):
                own, other = weight_refs[2 * pair : 2 * pair + 2]
                part = jnp.where(
                    mask_ref[...] > 0.5,
                    dot(gained_ref[...], own[:, columns], (1, 0)),
                    dot(gained_ref[...], other[:, columns], (1, 0)),
                ).astype(bf16)
                store_parts([ref.at[:, pair * units :] for ref in part_refs], columns, part)

            each_tile(units, visit)

    outs = kernel_call(
        body,
        (*blocks, gain_part, expert if routed else mask),
        (*gate_pair, *up_pair),
        [jax.ShapeDtypeStruct((part_rows, 2 * units + LANES * int(not routed)), bf16)]
        * parts_count
        + [jax.ShapeDtypeStruct((rows, width), bf16)] * 2
        + [jax.ShapeDtypeStruct((rows, 1), f32)] * passes
        + [jax.ShapeDtypeStruct((rows, width), bf16)] * int(routed),
        [pltpu.VMEM((rows, width), bf16)],
    )
    return outs[:parts_count], outs[parts_count : parts_count + 2], outs[parts_count + 2 :]


def row_scale(block):
    rows, features = block.shape

    def body(operand_refs, weight_refs, out_refs, scratch):
        wide = operand_refs[0][...].astype(f32)
        total = jnp.sum(wide * wide, axis=-1, keepdims=True)
        out_refs[0][...] = lax.rsqrt(total / features + epsilon)

    (scale,) = kernel_call(body, (block,), (), [jax.ShapeDtypeStruct((rows, 1), f32)], [])
    return scale


def activate(parts, units, features, inverse=None):
    rows = parts[0].shape[0]
    count = len(parts)

    def body(operand_refs, weight_refs, out_refs, scratch):
        part_refs = operand_refs[:count]
        total = part_refs[0][...].astype(f32)
        for ref in part_refs[1:]:
            total = total + ref[...].astype(f32)
        if inverse is None:
            squares = jnp.sum(total[:, 2 * units :], axis=-1, keepdims=True)
            scale = lax.rsqrt(squares / features + epsilon)
        else:
            scale = operand_refs[-1][...]
        gate, up = total[:, :units] * scale, total[:, units : 2 * units] * scale
        out_refs[0][...] = gate
        out_refs[1][...] = up
        out_refs[2][...] = (gate / (1.0 + jnp.exp(-gate)) * up).astype(bf16)
        out_refs[3][...] = scale

    return kernel_call(
        body,
        tuple(parts) + (() if inverse is None else (inverse,)),
        (),
        [jax.ShapeDtypeStruct((rows, units), f32)] * 2
        + [jax.ShapeDtypeStruct((rows, units), bf16), jax.ShapeDtypeStruct((rows, 1), f32)],
        [],
    )


def join(joined, refs, columns):
    size = refs[0].shape[0]
    for index, ref in enumerate(refs):
        joined[index * size : (index + 1) * size] = ref[:, columns]


def add_down(blocks, mask, down_pair, hidden, in_parts):
    count = len(blocks)
    part_rows, units = blocks[0].shape
    rows = part_rows * count
    width = down_pair[0].shape[1]
    out_count = count if in_parts else 1

    def body(operand_refs, weight_refs, out_refs, scratch):
        *block_refs, mask_ref, hidden_ref = operand_refs
        row_refs = out_refs[:out_count]
        (joined,) = scratch
        join(joined, block_refs, slice(None))
        split_rows(joined, mask_ref, *out_refs[-2:])
        own, other = weight_refs

        def visit(columns):
            ffn = jnp.where(
                mask_ref[...] > 0.5,
                dot(joined[...], own[:, columns], (1, 0)),
                dot(joined[...], other[:, columns], (1, 0)),
            ).astype(bf16)
            out = (hidden_ref[:, columns].astype(f32) + ffn.astype(f32)).astype(bf16)
            store_parts(row_refs, columns, out)

        each_tile(width, visit)

    outs = kernel_call(
        body,
        (*blocks, mask, hidden),
        down_pair,
        [jax.ShapeDtypeStruct((rows // out_count, width), bf16)] * out_count
        + [jax.ShapeDtypeStruct((rows, units), bf16)] * 2,
        [pltpu.VMEM((rows, units), bf16)],
        weight_cost=0 if in_parts else 1,
    )
    return outs[:out_count], outs[-2:]


def act_grad_parts(blocks, part_rows, mask, down_pair):
    rows = sum(block.shape[0] for block in blocks)
    parts_count = rows // part_rows
    units, width = down_pair[0].shape

    def body(operand_refs, weight_refs, out_refs, scratch):
        *block_refs, mask_ref = operand_refs
        *part_refs, grad_ref = out_refs
        own, other = weight_refs
        join(grad_ref, block_refs, slice(None))

        def visit(columns):
            part = jnp.where(
                mask_ref[...] > 0.5,
                dot(grad_ref[...], own[columns], (1, 1)),
                dot(grad_ref[...], other[columns], (1, 1)),
            ).astype(bf16)
            store_parts(part_refs, columns, part)

        each_tile(units, visit)

    outs = kernel_call(
        body,
        (*blocks, mask),
        down_pair,
        [jax.ShapeDtypeStruct((part_rows, units), bf16)] * parts_count
        + [jax.ShapeDtypeStruct((rows, width), bf16)],
        [],
    )
    return outs[:parts_count], outs[parts_count]


def hidden_grads(parts, gate, up, inverse, features):
    rows, units = gate.shape

    def body(operand_refs, weight_refs, out_refs, scratch):
        *part_refs, gate_ref, up_ref, inverse_ref = operand_refs
        (out_ref,) = out_refs
        grad_act = part_refs[0][...].astype(f32)
        for ref in part_refs[1:]:
            grad_act = grad_act + ref[...].astype(f32)
        gate_now, up_now, scale = gate_ref[...], up_ref[...], inverse_ref[...]
        sigmoid = 1.0 / (1.0 + jnp.exp(-gate_now))
        scaled = grad_act * scale
        gate_grad = scaled * up_now * sigmoid * (1.0 + gate_now * (1.0 - sigmoid))
        up_grad = scaled * (gate_now * sigmoid)
        shrink = jnp.sum(gate_grad * gate_now + up_grad * up_now, axis=-1, keepdims=True) * (
            scale / features
        )
        out_ref[:, :units] = gate_grad.astype(bf16)
        out_ref[:, units : 2 * units] = up_grad.astype(bf16)
        out_ref[:, 2 * units :] = in_lanes(shrink)

    (sent,) = kernel_call(
        body,
        (*parts, gate, up, inverse),
        [],
        [jax.ShapeDtypeStruct((rows, 2 * units + LANES), bf16)],
        [],
    )
    return sent


def input_grad(blocks, mask, gate_pair, up_pair, grad, hidden, gain_part, in_parts):
    count = len(blocks)
    part_rows = blocks[0].shape[0]
    rows = part_rows * count
    width, units = gate_pair[0].shape
    out_count = count if in_parts else 1

    def body(operand_refs, weight_refs, out_refs, scratch):
        *block_refs, mask_ref, grad_ref, hidden_ref, gain_ref = operand_refs
        *row_refs, sum_ref = out_refs
        joined, shrink = scratch
        join(joined, block_refs, slice(0, 2 * units))
        for index, ref in enumerate(block_refs):
            tail = ref[:, 2 * units :].astype(f32)
            shrink[index * part_rows : (index + 1) * part_rows] = jnp.sum(
                tail, axis=-1, keepdims=True
            )

        gate_own, gate_other, up_own, up_other = weight_refs

        def visit(columns):
            def back_of(gate, up):
                return dot(joined[:, :units], gate[columns], (1, 1)) + dot(
                    joined[:, units:], up[columns], (1, 1)
                )

            back = jnp.where(
                mask_ref[...] > 0.5, back_of(gate_own, up_own), back_of(gate_other, up_other)
            )
            wide = hidden_ref[:, columns].astype(f32)
            sum_ref[:, columns] = jnp.sum(back * wide, axis=0, keepdims=True)
            out = (
                grad_ref[:, columns].astype(f32)
                + back * gain_ref[:, columns]
                - wide * shrink[...]
            ).astype(bf16)
            store_parts(row_refs, columns, out)

        each_tile(width, visit)

    outs = kernel_call(
        body,
        (*blocks, mask, grad, hidden, gain_part),
        (*gate_pair, *up_pair),
        [jax.ShapeDtypeStruct((rows // out_count, width), bf16)] * out_count
        + [jax.ShapeDtypeStruct((1, width), f32)],
        [
            pltpu.VMEM((rows, 2 * units), bf16),
            pltpu.VMEM((rows, 1), f32),
        ],
    )
    return outs[:out_count], outs[out_count]


def body(tokens, cotangent, gain, w_gate, w_up, w_down, route):
    pipe_count = lax.axis_size("pipe")
    dp_count = lax.axis_size("dp")
    section = lax.axis_index("pipe")
    expert = lax.axis_index("expert")
    here = lax.axis_index("dp")
    features = tokens.shape[-1]
    width = features // dp_count
    units = w_gate.shape[-1]
    gain_part = lax.dynamic_slice_in_dim(gain, here * width, width, axis=1)

    groups = (slice(0, dp_count - 1), slice(dp_count - 1, dp_count))
    own_tokens = tokens[0]
    rows = own_tokens.shape[0]
    micro = [(section - k + pipe_count) % pipe_count for k in range(PASSES)]
    route_rows = jnp.stack(
        [lax.dynamic_index_in_dim(route[0, :, :, 0], m, 0, keepdims=False) for m in micro], axis=1
    ).astype(bf16)
    expert_id = jnp.full((1, LANES), expert, f32)
    route_rows = after(jnp.pad(route_rows, ((0, 0), (0, width - PASSES))), expert_id)

    def tokens_quarter(step):
        return jnp.concatenate([quarter_of(own_tokens, here ^ step, width), route_rows])

    def cotangent_quarter(step, *earlier):
        return quarter_of(after(cotangent[0], *earlier), here ^ step, width)

    def sent(parts):
        return [swap(part, "dp", step) if step else part for step, part in enumerate(parts)]

    def moved(pieces, distance):
        return [shifted(piece, "pipe", distance) for piece in pieces]

    def weight_grad(lefts, right, wanted):
        return dot(lefts[wanted], right, (0, 0))

    def stacked(pairs):
        return [jnp.concatenate(pieces) for pieces in zip(*pairs)]

    quarters = [tokens_quarter(step) for step in range(dp_count)]
    weights = [
        weight
        for own in (w_gate, w_up, w_down)
        for weight in (own[0, 0], swap(own[0, 0], "expert", 1))
    ]
    weights = resident(weights)
    gate_pair, up_pair, down_pair = weights[:2], weights[2:4], weights[4:]
    quarters[-1] = after(quarters[-1], *weights)
    blocks = sent(quarters)
    inverse = row_scale(own_tokens)

    parts, gained, masks, hidden = [], [], [], []
    for group in groups:
        made, scaled, (*choices, joined) = hidden_parts(
            blocks[group], rows, gain_part, None, gate_pair, up_pair, expert_id
        )
        parts += made
        gained.append(scaled)
        masks.append(choices)
        hidden.append(joined)
    masks = list(zip(*masks))
    gate, up, activated, _ = activate(sent(parts), units, features, inverse)
    kept = [(hidden, gained, inverse, gate, up)]
    first_activated = gather_rows(activated, dp_count)
    next_hidden, first_rows = [], []
    for index in reversed(range(len(groups))):
        near = first_activated[groups[index]]
        if next_hidden:
            near = [after(near[0], next_hidden[0]), *near[1:]]
        (out,), split = add_down(near, masks[0][index], down_pair, hidden[index], False)
        next_hidden.insert(0, out)
        first_rows.insert(0, split)
    hidden = moved(next_hidden, 1)
    grad_blocks = sent([cotangent_quarter(step, next_hidden[0]) for step in range(dp_count)])
    act_parts, grad = [], []
    for group, mask in zip(groups, masks[1]):
        made, joined = act_grad_parts(grad_blocks[group], rows, mask, down_pair)
        act_parts += made
        grad.append(joined)
    act_grads = act_parts
    act_parts = sent(act_parts)
    hidden[0] = after(hidden[0], act_grads[0])

    parts, gained = [], []
    for rows_in, mask in zip(hidden, masks[1]):
        if parts:
            parts = sent(parts)
            rows_in = after(rows_in, parts[1])
        made, scaled, _ = hidden_parts([rows_in], rows, gain_part, mask, gate_pair, up_pair)
        parts += made
        gained.append(scaled)
    parts[-1] = swap(parts[-1], "dp", dp_count - 1)
    gate, up, activated, inverse = activate(parts, units, features)
    kept.append((hidden, gained, inverse, gate, up))

    gain_sum = jnp.zeros((1, width), f32)
    for k in reversed(range(PASSES)):
        hidden, gained, inverse, gate, up = kept[k]
        gained = stacked(gained)
        payload = hidden_grads(act_parts, gate, up, inverse, features)
        both_grad = gather_rows(payload, dp_count)
        joined = jnp.concatenate(both_grad)
        rights = [joined[:, :units], joined[:, units : 2 * units]]
        if k == 0:
            lefts = [gained, gained, stacked(first_rows)]
            rights.append(jnp.concatenate(grad))
        outs = []
        for index in reversed(range(len(groups))):
            made, gain_term = input_grad(
                both_grad[groups[index]],
                masks[k][index],
                gate_pair,
                up_pair,
                grad[index],
                hidden[index],
                gain_part,
                k == 0,
            )
            outs = list(made) + outs
            gain_sum = gain_sum + gain_term
            if k == 0 and index > 0:
                ready = [after(right, made[0]) for right in rights[:2]] + rights[2:]
                given = [
                    (weight_grad(left, right, False) + soon.astype(f32)).astype(bf16)
                    for left, right, soon in zip(lefts, ready, early[False])
                ]
                both_grad[1] = after(both_grad[1], *given)
                received = [swap(value, "expert", 1) for value in given]
        if k > 0:
            last_grad = jnp.concatenate(grad)
            grad = moved(outs, -1)
            last_activated = gather_rows(after(activated, both_grad[-1]), dp_count)
            rights = [after(right, *last_activated[1:]) for right in rights]
            early = {
                wanted: [weight_grad(gained, right, wanted).astype(bf16) for right in rights]
                for wanted in (False, True)
            }
            out_parts, last_rows = [], []
            for group, choice, rows_in in zip(groups, masks[1], hidden):
                made, split = add_down(
                    last_activated[group], choice, down_pair, rows_in, True
                )
                out_parts += made
                last_rows.append(split)
            out_rows = from_quarters(out_parts)
            grad[0] = after(grad[0], *out_parts, *early[False], *early[True])
            act_parts, joined = [], []
            for rows_in, choice in zip(grad, masks[0]):
                made, copied = act_grad_parts([rows_in], rows, choice, down_pair)
                act_parts += made
                joined.append(copied)
            grad = joined
            last_rows = stacked(last_rows)
            for wanted in (False, True):
                early[wanted].append(weight_grad(last_rows, last_grad, wanted).astype(bf16))
            act_parts = sent(act_parts)
            act_parts[1] = after(act_parts[1], early[False][2], early[True][2])

    returned = sent(outs)
    rights = [after(right, *outs) for right in rights]
    gain_sum = gain_sum + swap(gain_sum, "expert", 1)
    gain_rows = jnp.concatenate(gather_rows(after(gain_sum, *received), dp_count))
    gain_all = jnp.zeros((features,), f32)
    for step in range(dp_count):
        gain_all = lax.dynamic_update_slice_in_dim(
            gain_all, gain_rows[step], (here ^ step) * width, axis=0
        )
    grads = [
        (weight_grad(left, right, True) + soon.astype(f32) + other.astype(f32)).astype(bf16)
        for left, right, soon, other in zip(lefts, rights, early[True], received)
    ]
    returned = list(lax.optimization_barrier((*returned, *grads)))[:dp_count]
    entry = assemble(returned)
    return (
        out_rows[None],
        entry[None],
        gain_all[None],
        grads[0][None, None],
        grads[1][None, None],
        grads[2][None, None],
    )


def start_shifted(block, axis, distance):
    devices = range(lax.axis_size(axis))
    route = [((i - distance) % len(devices), i) for i in devices]
    return lax.ppermute(block, axis, route)


def start_contract_last(former, latter):
    return lax.dot_general(
        former, latter, (((1,), (1,)), ((), ())), preferred_element_type=jnp.float32
    )


def start_contract_first(former, latter):
    return lax.dot_general(
        former, latter, (((0,), (0,)), ((), ())), preferred_element_type=jnp.float32
    )


def start_normalize(hidden, gain_row):
    widened = hidden.astype(jnp.float32)
    inverse = lax.rsqrt(jnp.mean(widened * widened, axis=-1, keepdims=True) + epsilon)
    scaled = widened * inverse
    return ((scaled * gain_row).astype(jnp.bfloat16), scaled, inverse)


def start_slot_matrix(route_now, expert_count, capacity):
    tile_count = route_now.shape[0]
    expert_ids = jnp.arange(expert_count, dtype=jnp.int32)
    member = (route_now[None, :] == expert_ids[:, None]).astype(jnp.int32)
    earlier = jnp.cumsum(member, axis=1) - member
    rank_ids = jnp.arange(capacity, dtype=jnp.int32)
    placed = member[:, None, :] * (earlier[:, None, :] == rank_ids[None, :, None]).astype(jnp.int32)
    return placed.reshape(expert_count * capacity, tile_count)


def start_into_slots(placed, rows, tile_rows, dp_count):
    width = rows.shape[-1]
    tile_blocks = rows.reshape(placed.shape[1], tile_rows, dp_count, width // dp_count)
    return jnp.einsum(
        "st,trqd->qsrd",
        placed.astype(jnp.bfloat16),
        tile_blocks,
        preferred_element_type=jnp.float32,
    ).astype(jnp.bfloat16)


def start_from_slots(placed, slot_rows):
    merged = jnp.einsum(
        "st,qsrd->trqd", placed.astype(jnp.bfloat16), slot_rows, preferred_element_type=jnp.float32
    ).astype(jnp.bfloat16)
    return merged.reshape(merged.shape[0] * merged.shape[1], -1)


def start_send_out(slot_rows):
    quarter = slot_rows.shape[-1]
    flat = slot_rows.reshape((-1,) + slot_rows.shape[2:])
    arrived = lax.all_to_all(flat, ("dp", "expert"), split_axis=0, concat_axis=0, tiled=True)
    return arrived.reshape(-1, quarter)


def start_send_back(part_rows, dp_count, tile_rows):
    quarter = part_rows.shape[-1]
    flat = part_rows.reshape(-1, tile_rows, quarter)
    returned = lax.all_to_all(flat, ("dp", "expert"), split_axis=0, concat_axis=0, tiled=True)
    return returned.reshape(dp_count, -1, tile_rows, quarter)


def start_widen_rounded(values):
    return lax.optimization_barrier(values.astype(jnp.bfloat16)).astype(jnp.float32)


def start_expert_forward(received, gate_weight, up_weight, down_weight):
    gate_terms = start_widen_rounded(jnp.dot(received, gate_weight, preferred_element_type=jnp.float32))
    up_terms = start_widen_rounded(jnp.dot(received, up_weight, preferred_element_type=jnp.float32))
    gate_pre, up_pre = (
        lax.psum(gate_terms.astype(jnp.bfloat16), "dp").astype(jnp.float32),
        lax.psum(up_terms.astype(jnp.bfloat16), "dp").astype(jnp.float32),
    )
    activated = (jax.nn.silu(gate_pre) * up_pre).astype(jnp.bfloat16)
    part_rows = jnp.dot(activated, down_weight, preferred_element_type=jnp.float32).astype(
        jnp.bfloat16
    )
    return (part_rows, (gate_pre, up_pre, activated))


def start_expert_backward(
    received, grad_recv, kept_state, gate_weight, up_weight, down_weight, grad_sums
):
    gate_pre, up_pre, activated = kept_state
    grad_terms = start_widen_rounded(start_contract_last(grad_recv, down_weight))
    grad_act = lax.psum(grad_terms.astype(jnp.bfloat16), "dp").astype(jnp.float32)
    sigmoid_gate = jax.nn.sigmoid(gate_pre)
    silu_gate = gate_pre * sigmoid_gate
    grad_gate_pre = (
        grad_act * up_pre * sigmoid_gate * (1.0 + gate_pre * (1.0 - sigmoid_gate))
    ).astype(jnp.bfloat16)
    grad_up_pre = (grad_act * silu_gate).astype(jnp.bfloat16)
    back_rows = (
        start_contract_last(grad_gate_pre, gate_weight) + start_contract_last(grad_up_pre, up_weight)
    ).astype(jnp.bfloat16)
    grad_gate = grad_sums[0] + start_contract_first(received, grad_gate_pre)
    grad_up = grad_sums[1] + start_contract_first(received, grad_up_pre)
    grad_down = grad_sums[2] + start_contract_first(activated, grad_recv)
    return (back_rows, (grad_gate, grad_up, grad_down))


def start_body(tokens, cotangent, gain, w_gate, w_up, w_down, route):
    pipe_count = lax.axis_size("pipe")
    dp_count = lax.axis_size("dp")
    expert_count = lax.axis_size("expert")
    section_index = lax.axis_index("pipe")
    gain_row = gain[0]
    gate_weight = w_gate[0, 0]
    up_weight = w_up[0, 0]
    down_weight = w_down[0, 0]
    route_table = route[0, :, :, 0]
    tile_count = route_table.shape[1]
    capacity = max(2, 3 * tile_count // (2 * expert_count))
    hidden = tokens[0]
    saved_ticks = []
    out_rows = hidden
    for pass_index in range(PASSES):
        micro_index = (section_index - pass_index + pipe_count) % pipe_count
        route_now = lax.dynamic_index_in_dim(route_table, micro_index, 0, keepdims=False)
        placed = start_slot_matrix(route_now, expert_count, capacity)
        normed, scaled, inverse = start_normalize(hidden, gain_row)
        received = start_send_out(start_into_slots(placed, normed, TILE, dp_count))
        part_rows, kept_state = start_expert_forward(received, gate_weight, up_weight, down_weight)
        ffn_rows = start_from_slots(placed, start_send_back(part_rows, dp_count, TILE))
        new_hidden = (hidden.astype(jnp.float32) + ffn_rows.astype(jnp.float32)).astype(
            jnp.bfloat16
        )
        saved_ticks.append((placed, scaled, inverse, received, kept_state))
        if pass_index + 1 < PASSES:
            hidden = start_shifted(new_hidden, "pipe", 1)
        else:
            out_rows = new_hidden
    grad_rows = cotangent[0]
    grad_sums = (
        jnp.zeros(gate_weight.shape, jnp.float32),
        jnp.zeros(up_weight.shape, jnp.float32),
        jnp.zeros(down_weight.shape, jnp.float32),
    )
    gain_sum = jnp.zeros(gain_row.shape, jnp.float32)
    entry_grad = grad_rows
    for pass_index in reversed(range(PASSES)):
        placed, scaled, inverse, received, kept_state = saved_ticks[pass_index]
        grad_recv = start_send_out(start_into_slots(placed, grad_rows, TILE, dp_count))
        back_rows, grad_sums = start_expert_backward(
            received, grad_recv, kept_state, gate_weight, up_weight, down_weight, grad_sums
        )
        grad_normed = start_from_slots(placed, start_send_back(back_rows, dp_count, TILE)).astype(jnp.float32)
        gain_sum = gain_sum + jnp.sum(grad_normed * scaled, axis=0)
        grad_scaled = grad_normed * gain_row
        grad_wide = inverse * (
            grad_scaled - scaled * jnp.mean(grad_scaled * scaled, axis=-1, keepdims=True)
        )
        grad_in = (grad_rows.astype(jnp.float32) + grad_wide).astype(jnp.bfloat16)
        if pass_index > 0:
            grad_rows = start_shifted(grad_in, "pipe", -1)
        else:
            entry_grad = grad_in
    gain_total = lax.psum(gain_sum, ("dp", "expert"))
    return (
        out_rows[None],
        entry_grad[None],
        gain_total[None],
        grad_sums[0].astype(jnp.bfloat16)[None, None],
        grad_sums[1].astype(jnp.bfloat16)[None, None],
        grad_sums[2].astype(jnp.bfloat16)[None, None],
    )


def start_solution(mesh):
    placed = (
        P("pipe", ("dp", "expert"), None),
        P("pipe", ("dp", "expert"), None),
        P("pipe", None),
        P("pipe", "expert", "dp", None),
        P("pipe", "expert", "dp", None),
        P("pipe", "expert", None, "dp"),
        P("pipe", None, ("dp", "expert"), None),
    )
    return jax.shard_map(
        start_body,
        mesh=mesh,
        in_specs=placed,
        out_specs=(
            P("pipe", ("dp", "expert"), None),
            P("pipe", ("dp", "expert"), None),
            P("pipe", None),
            P("pipe", "expert", "dp", None),
            P("pipe", "expert", "dp", None),
            P("pipe", "expert", None, "dp"),
        ),
        check_vma=False,
    )


def solution(mesh):
    if mesh.shape["expert"] != PAIR:
        return start_solution(mesh)
    placed = (
        P("pipe", ("dp", "expert"), None),
        P("pipe", ("dp", "expert"), None),
        P("pipe", None),
        P("pipe", "expert", "dp", None),
        P("pipe", "expert", "dp", None),
        P("pipe", "expert", None, "dp"),
        P("pipe", None, ("dp", "expert"), None),
    )
    return jax.shard_map(
        body,
        mesh=mesh,
        in_specs=placed,
        out_specs=placed[:2] + (P("pipe", None),) + placed[3:6],
        check_vma=False,
    )
```
